32 devices in a mesh: ctx: 16 (over z, x, core), head: 2 (over y).
Axes of the slice: x: 2, y: 2, z: 4, core: 2. Of those that a mesh axis runs over, the one named last changes fastest.
Arguments:
- kv_latent: bfloat16 [8192, 576], P('ctx'), may hold values from -4 to 4
- queries: bfloat16 [8192, 3072], P('ctx', 'head'), may hold values from -22 to 22
- grad_out: bfloat16 [8192, 2048], P('ctx', 'head'), may hold values from -6 to 6
- kv_up_weight: bfloat16 [512, 4096], P(None, 'head'), may hold values from -0.25 to 0.25
- doc_ids: int32 [8192], replicated, may hold values from 0 to 7, never falling along the last dimension, each value on 1 to 1536 neighbouring positions
Outputs:
- grad_queries: bfloat16 [8192, 3072], P('ctx', 'head')
- grad_latent: bfloat16 [8192, 576], P('ctx')
- grad_weight: float32 [512, 4096], P('ctx', 'head')
The draws below stay inside these ranges and needn't reach their ends.
Inputs may be any that keep to these rules, and one draw needn't show every extreme that they name: `doc_ids`: document ids never fall along the sequence; every document has 1 to 1536 tokens, and one has exactly 1536.
All inputs are finite; a program needn't handle non-finite values.
Results may differ from the reference program's by a relative error of at most 0.0076.
Values may be sent and summed in bfloat16 or wider, within the bound.
No kernel may reach another device: no remote copies, remote signals or barrier semaphores. Data moves between devices by JAX's collectives and lax.ppermute only.
A program may use at most 128 MiB of HBM per device.

```python
import math
import jax
import jax.numpy as jnp
import numpy as np
from jax import lax

HEADS = 16
NOPE = 128
ROPE = 64
VDIM = 128
LATENT = 512
TOK_DEV = 512
REACH = 3
TOKENS = 8192
DOCS = 8
DOC_MOST = 1536


def draw_kv_latent(key, part):
    inner_key = jax.random.fold_in(key, 1)
    values = jnp.clip(jax.random.normal(inner_key, (TOKENS, LATENT + ROPE), jnp.float32), -4.0, 4.0)
    return values.astype(jnp.bfloat16)


def draw_queries(key, part):
    inner_key = jax.random.fold_in(key, 2)
    values = jnp.clip(jax.random.normal(inner_key, (TOKENS, HEADS * (NOPE + ROPE)), jnp.float32), -4.0, 4.0)
    return values.astype(jnp.bfloat16)


def block_scale(own_key, extent, cuts, smallest, top_value):
    def one(axis_at, blocks):
        heights = jax.random.uniform(jax.random.fold_in(jax.random.fold_in(own_key, 6), axis_at), (blocks,), jnp.float32, smallest / len(cuts), top_value / len(cuts))
        return jnp.repeat(jnp.exp(heights), extent[axis_at] // blocks).reshape((-1,) + (1,) * (len(extent) - axis_at - 1))

    gain = one(*cuts[0])
    for cut in cuts[1:]:
        gain = gain * one(*cut)
    return gain


def length_profile(count, total, most, skew):
    portions = [(1 << 20) // math.isqrt(grade ** skew) + 1 for grade in range(2, count + 1)]
    surplus, counts = total - most - (count - 1), [1] * (count - 1)
    while surplus > 0:
        movable = [i for i in range(count - 1) if counts[i] < most]
        mass, left = sum([portions[i] for i in movable]), surplus
        for i in movable:
            more = min(most - counts[i], max(1, left * portions[i] // mass), surplus)
            counts[i] = counts[i] + more
            surplus = surplus - more
    return np.array([most] + counts)


def ragged(own_key, amount, total, reach, slope):
    if amount == 2:
        one = jax.random.randint(own_key, (), max(1, total - reach), min(reach, total - 1) + 1)
        return jnp.stack([one, total - one])
    lengths = jnp.asarray(length_profile(amount, total, reach, slope), jnp.int32)
    twos = (amount - 1) // 2
    source_of, receiver = lengths[1:1 + 2 * twos:2], lengths[2:2 + 2 * twos:2]
    margin = jnp.minimum(source_of - 1, reach - receiver)
    shifted = jax.random.randint(jax.random.fold_in(own_key, 1), (twos,), 0, 1 << 20) % (margin + 1)
    lengths = lengths.at[1:1 + 2 * twos:2].set(source_of - shifted).at[2:2 + 2 * twos:2].set(receiver + shifted)
    return lengths[jax.random.permutation(jax.random.fold_in(own_key, 2), amount)]


def normal_values(stream_key, dims, spread, reach, pieces=(), held_as=jnp.bfloat16):
    drawn = spread * jax.random.normal(stream_key, dims, jnp.float32)
    if pieces:
        drawn = drawn * block_scale(stream_key, dims, pieces, -0.22, 0.18)
    return jnp.clip(drawn, -reach, reach).astype(held_as)


def setup_inputs(seed: int = 0) -> dict:
    streams_of = jax.random.split(jax.random.key(seed), 6)
    kv_latent = draw_kv_latent(jax.random.fold_in(streams_of[5], 71), 0)
    queries = draw_queries(jax.random.fold_in(streams_of[5], 71), 0)
    grad_out = normal_values(streams_of[2], (TOKENS, HEADS * VDIM), 1.0, 6.0, ((0, 16), (1, 2)))
    kv_up_weight = normal_values(streams_of[3], (LATENT, HEADS * (NOPE + VDIM)), LATENT ** -0.5, 0.25, ((1, 2),))
    doc_ids = jnp.searchsorted(jnp.cumsum(ragged(streams_of[4], DOCS, TOKENS, DOC_MOST, 1)), jnp.arange(TOKENS), side="right").astype(jnp.int32)
    return {"kv_latent": kv_latent, "queries": queries, "grad_out": grad_out, "kv_up_weight": kv_up_weight, "doc_ids": doc_ids}


masked_score = -1e+30

def reference(kv_latent, queries, grad_out, kv_up_weight, doc_ids):
    score_scale = 1.0 / math.sqrt(NOPE + ROPE)
    span = (REACH + 1) * TOK_DEV
    latent = kv_latent[:, :LATENT]
    rope_keys = kv_latent[:, LATENT:].astype(jnp.float32)
    lifted = jnp.dot(latent, kv_up_weight, preferred_element_type=jnp.float32).astype(jnp.bfloat16)
    lifted = lifted.reshape(TOKENS, HEADS, NOPE + VDIM).astype(jnp.float32)
    head_queries = queries.reshape(TOKENS, HEADS, NOPE + ROPE).astype(jnp.float32)
    head_grads = grad_out.reshape(TOKENS, HEADS, VDIM).astype(jnp.float32)

    def one_block(carry, block_index):
        key_total, rope_total = carry
        query_start = (block_index * TOK_DEV).astype(jnp.int32)
        key_start = jnp.maximum(query_start - REACH * TOK_DEV, 0).astype(jnp.int32)
        query_rows = lax.dynamic_slice_in_dim(head_queries, query_start, TOK_DEV, 0)
        out_rows = lax.dynamic_slice_in_dim(head_grads, query_start, TOK_DEV, 0)
        key_rows = lax.dynamic_slice_in_dim(lifted, key_start, span, 0)
        rope_rows = lax.dynamic_slice_in_dim(rope_keys, key_start, span, 0)
        query_pos = query_start + jnp.arange(TOK_DEV, dtype=jnp.int32)
        key_pos = key_start + jnp.arange(span, dtype=jnp.int32)
        query_docs = lax.dynamic_slice_in_dim(doc_ids, query_start, TOK_DEV)
        key_docs = lax.dynamic_slice_in_dim(doc_ids, key_start, span)
        visible = (query_docs[:, None] == key_docs[None, :]) & (key_pos[None, :] <= query_pos[:, None])
        key_nope = key_rows[:, :, :NOPE]
        values = key_rows[:, :, NOPE:]
        query_nope = query_rows[:, :, :NOPE]
        query_rope = query_rows[:, :, NOPE:]
        scores = score_scale * (jnp.einsum('thd,khd->htk', query_nope, key_nope) + jnp.einsum('thd,kd->htk', query_rope, rope_rows))
        scores = jnp.where(visible[None], scores, masked_score)
        row_top = lax.optimization_barrier(jnp.max(scores, axis=2))
        log_total = row_top + jnp.log(lax.optimization_barrier(jnp.sum(jnp.exp(scores - row_top[:, :, None]), axis=2)))
        weights = jnp.where(visible[None], jnp.exp(scores - log_total[:, :, None]), 0.0)
        grad_probs = jnp.einsum('thd,khd->htk', out_rows, values)
        delta = lax.optimization_barrier(jnp.sum(weights * grad_probs, axis=2))
        grad_scores = lax.optimization_barrier((weights * (grad_probs - delta[:, :, None])).astype(jnp.bfloat16)).astype(jnp.float32)
        weights_low = lax.optimization_barrier(weights.astype(jnp.bfloat16)).astype(jnp.float32)
        grad_query = score_scale * jnp.concatenate([jnp.einsum('htk,khd->thd', grad_scores, key_nope), jnp.einsum('htk,kd->thd', grad_scores, rope_rows)], axis=2)
        grad_keys = score_scale * jnp.einsum('htk,thd->khd', grad_scores, query_nope)
        grad_values = jnp.einsum('htk,thd->khd', weights_low, out_rows)
        grad_rope = score_scale * jnp.einsum('htk,thd->kd', grad_scores, query_rope)
        block_kv = jnp.concatenate([grad_keys, grad_values], axis=2)
        key_total = lax.dynamic_update_slice_in_dim(key_total, lax.dynamic_slice_in_dim(key_total, key_start, span, 0) + block_kv, key_start, 0)
        rope_total = lax.dynamic_update_slice_in_dim(rope_total, lax.dynamic_slice_in_dim(rope_total, key_start, span, 0) + grad_rope, key_start, 0)
        return ((key_total, rope_total), grad_query)
    start_sums = (jnp.zeros((TOKENS, HEADS, NOPE + VDIM), jnp.float32), jnp.zeros((TOKENS, ROPE), jnp.float32))
    (key_total, rope_total), query_grads = lax.scan(one_block, start_sums, jnp.arange(TOKENS // TOK_DEV, dtype=jnp.int32))
    grad_queries = query_grads.reshape(TOKENS, HEADS * (NOPE + ROPE)).astype(jnp.bfloat16)
    kv_grad = key_total.reshape(TOKENS, HEADS * (NOPE + VDIM)).astype(jnp.bfloat16)
    latent_grad = jnp.dot(kv_grad, kv_up_weight.T, preferred_element_type=jnp.float32)
    grad_latent = jnp.concatenate([latent_grad, rope_total], axis=1).astype(jnp.bfloat16)
    grad_weight = jnp.dot(latent.T, kv_grad, preferred_element_type=jnp.float32)
    return (grad_queries, grad_latent, grad_weight)
```

```python
import functools
import math

import jax
import jax.numpy as jnp
from jax import lax
from jax.experimental import pallas as pl
from jax.experimental.pallas import tpu as pltpu
from jax.sharding import PartitionSpec as P

NOPE = 128
ROPE = 64
VDIM = 128
LATENT = 512
REACH = 3
QK = NOPE + ROPE
KV = NOPE + VDIM
TILE = 256
GROUPS = 2

MASKED = -1e30
FLOOR = -1e20
SCALE = 1.0 / math.sqrt(QK)
SCALE2 = SCALE * math.log2(math.e)

NT = (((1,), (1,)), ((), ()))
NN = (((1,), (0,)), ((), ()))


def dot(a, b, dims=NN):
    return lax.dot_general(a, b, dims, preferred_element_type=jnp.float32)


def attention_kernel(
    rows,
    place_ref, start_ref, q_ref, do_ref, w_ref, lat0, lat1, lat2, lat3,
    dq_ref, gw_ref, x0_ref, x1_ref, x2_ref, x3_ref,
    lat_ref, lat_t_ref, bias_ref, e_ref, g_ref, k_ref, top_ref, dq_acc, gw_acc, x_acc, sems,
):
    step = pl.program_id(0)
    tiles_block = rows // TILE
    tiles = (REACH + 1) * tiles_block
    first_start = place_ref[REACH + 1]

    def window_base(t):
        return place_ref[t // tiles_block] + lax.rem(t, tiles_block) * TILE

    def active(t):
        return window_base(t) + TILE > first_start

    def tile_rows(t):
        return pl.ds(pl.multiple_of(t * TILE, TILE), TILE)

    @pl.when(step == 0)
    def _():
        copies = [
            pltpu.make_async_copy(source, lat_ref.at[pl.ds(i * rows, rows)], sems.at[i])
            for i, source in enumerate((lat0, lat1, lat2, lat3))
        ]
        for copy in copies:
            copy.start()
        x_acc[...] = jnp.zeros_like(x_acc)
        start = start_ref[...]
        last_seen = REACH * rows + lax.broadcasted_iota(jnp.int32, (1, rows), 1)

        def fill(t, carry):
            base = window_base(t)
            key = lax.broadcasted_iota(jnp.int32, (TILE, rows), 0)
            seen = (key >= start - base) & (key <= last_seen - base)
            bias_ref[tile_rows(t), :] = jnp.where(seen, 0.0, MASKED)
            return carry

        lax.fori_loop(0, tiles, fill, 0)
        for copy in copies:
            copy.wait()
        for i in range(REACH + 1):
            part = slice(i * rows, (i + 1) * rows)
            lat_t_ref[:, part] = lat_ref[part, :LATENT].T

    gw_acc[...] = jnp.zeros_like(gw_acc)
    dq_acc[...] = jnp.zeros_like(dq_acc)
    heads = range(2)
    q = [q_ref[:, h * QK : (h + 1) * QK] for h in heads]
    do = [do_ref[:, h * VDIM : (h + 1) * VDIM] for h in heads]

    def first_pass(t, carry):
        def run(carry):
            part = tile_rows(t)
            latent = lat_ref[part, :LATENT]
            rope = lat_ref[part, LATENT:]
            bias = bias_ref[part, :]
            out = []
            for h in heads:
                top, mass, cross = carry[h]
                lifted = dot(latent, w_ref[:, h * KV : (h + 1) * KV]).astype(jnp.bfloat16)
                key = jnp.concatenate([lifted[:, :NOPE], rope], axis=1)
                k_ref[h, part, :] = key
                scores = dot(key, q[h], NT) * SCALE2 + bias
                grads = dot(lifted[:, NOPE:], do[h], NT)
                new_top = jnp.maximum(top, jnp.max(scores, axis=0, keepdims=True))
                weights = jnp.exp2(scores - new_top)
                factor = jnp.exp2(top - new_top)
                mass = mass * factor + jnp.sum(weights, axis=0, keepdims=True)
                cross = cross * factor + jnp.sum(weights * grads, axis=0, keepdims=True)
                e_ref[h, part, :] = weights
                g_ref[h, part, :] = grads
                top_ref[h, pl.ds(t, 1), :] = new_top
                out.append((new_top, mass, cross))
            return tuple(out)

        return lax.cond(active(t), run, lambda c: c, carry)

    zero = jnp.zeros((1, rows), jnp.float32)
    stats = lax.fori_loop(0, tiles, first_pass, ((zero + FLOOR, zero, zero),) * 2)
    inverse = [1.0 / mass for _, mass, _ in stats]
    delta = [cross * inv for (_, _, cross), inv in zip(stats, inverse)]

    def second_pass(t, carry):
        @pl.when(active(t))
        def _():
            part = tile_rows(t)
            pieces = []
            for h in heads:
                factor = jnp.exp2(top_ref[h, pl.ds(t, 1), :] - stats[h][0]) * inverse[h]
                probs = e_ref[h, part, :] * factor
                low = probs.astype(jnp.bfloat16)
                dscore = (probs * (g_ref[h, part, :] - delta[h])).astype(jnp.bfloat16)
                dvalue = dot(low, do[h])
                dkey = dot(dscore, q[h]) * SCALE
                own = slice(h * QK, (h + 1) * QK)
                dq_acc[own, :] += dot(k_ref[h, part, :].T, dscore)
                x_acc[part, LATENT:] += dkey[:, NOPE:]
                pieces += [dkey[:, :NOPE].astype(jnp.bfloat16), dvalue.astype(jnp.bfloat16)]
            grads = jnp.concatenate(pieces, axis=1)
            x_acc[part, :LATENT] += dot(grads, w_ref[...], NT)
            gw_acc[...] += dot(lat_t_ref[:, part], grads)

        return carry

    lax.fori_loop(0, tiles, second_pass, 0)
    dq_ref[...] = (dq_acc[...] * SCALE).T.astype(dq_ref.dtype)
    gw_ref[...] = gw_acc[...].astype(gw_ref.dtype)

    @pl.when(step == pl.num_programs(0) - 1)
    def _():
        for i, out in enumerate((x0_ref, x1_ref, x2_ref, x3_ref)):
            out[...] = x_acc[i * rows : (i + 1) * rows, :].astype(out.dtype)


def attention(place, start, queries, grad_out, weight, blocks, group, groups):
    rows = queries.shape[0]
    heads = weight.shape[1] // KV
    pairs = heads // 2 // groups
    first = group * pairs
    window = (REACH + 1) * rows
    width = LATENT + ROPE
    low, full = jnp.bfloat16, jnp.float32

    def pair_cols(size, base):
        return pl.BlockSpec((rows, 2 * size), lambda i: (0, base + i))

    whole = pl.BlockSpec((rows, width), lambda i: (0, 0))
    flops = 2 * pairs * 2 * rows * window * (3 * QK + 2 * VDIM) * 2
    return pl.pallas_call(
        functools.partial(attention_kernel, rows),
        grid=(pairs,),
        in_specs=[
            pl.BlockSpec(memory_space=pltpu.SMEM),
            pl.BlockSpec((1, rows), lambda i: (0, 0)),
            pair_cols(QK, first),
            pair_cols(VDIM, first),
            pl.BlockSpec((LATENT, 2 * KV), lambda i: (0, first + i)),
        ]
        + [pl.BlockSpec(memory_space=pl.ANY)] * (REACH + 1),
        out_specs=[
            pair_cols(QK, 0),
            pl.BlockSpec((LATENT, 2 * KV), lambda i: (0, i)),
        ]
        + [whole] * (REACH + 1),
        out_shape=[
            jax.ShapeDtypeStruct((rows, pairs * 2 * QK), low),
            jax.ShapeDtypeStruct((LATENT, pairs * 2 * KV), low),
        ]
        + [jax.ShapeDtypeStruct((rows, width), full)] * (REACH + 1),
        scratch_shapes=[
            pltpu.VMEM((window, width), low),
            pltpu.VMEM((LATENT, window), low),
            pltpu.VMEM((window, rows), full),
            pltpu.VMEM((2, window, rows), full),
            pltpu.VMEM((2, window, rows), full),
            pltpu.VMEM((2, window, QK), low),
            pltpu.VMEM((2, window // TILE, rows), full),
            pltpu.VMEM((2 * QK, rows), full),
            pltpu.VMEM((LATENT, 2 * KV), full),
            pltpu.VMEM((window, width), full),
            pltpu.SemaphoreType.DMA((REACH + 1,)),
        ],
        compiler_params=pltpu.CompilerParams(
            dimension_semantics=("arbitrary",), vmem_limit_bytes=56 * 1024 * 1024
        ),
        cost_estimate=pl.CostEstimate(
            flops=flops, bytes_accessed=16 * 1024 * 1024, transcendentals=0
        ),
        name="attention",
    )(place, start, queries, grad_out, weight, *blocks)


def permute(value, axis, target):
    count = lax.axis_size(axis)
    pairs = [(s, target(s)) for s in range(count) if 0 <= target(s) < count]
    return lax.ppermute(value, axis, pairs)


def local(kv_latent, queries, grad_out, kv_up_weight, doc_ids):
    rows = kv_latent.shape[0]
    index = lax.axis_index("ctx")
    first_row = index * rows
    odd = lax.rem(index, 2)

    far = permute(kv_latent, "ctx", lambda s: s + 2)
    mixed = permute(kv_latent, "ctx", lambda s: s + 3 if s % 2 else s + 1)
    swapped = permute(far, "ctx", lambda s: s ^ 1)
    blocks = (swapped, far, mixed, kv_latent)
    place_blocks = [rows * 2 * (1 - odd), rows, rows * 2 * odd, REACH * rows]

    padded = jnp.pad(doc_ids, (REACH * rows, 0), constant_values=-1)
    window_docs = lax.dynamic_slice_in_dim(padded, first_row, (REACH + 1) * rows)
    my_docs = window_docs[REACH * rows :]
    start = jnp.sum((window_docs[:, None] < my_docs[None, :]).astype(jnp.int32), axis=0)
    place = jnp.stack([jnp.asarray(p, jnp.int32) for p in place_blocks] + [start[0]])

    grad_queries, grad_weight, partial = [], [], None
    groups = min(GROUPS, kv_up_weight.shape[1] // (2 * KV))
    for group in range(groups):
        dq, gw, *parts = attention(
            place, start[None], queries, grad_out, kv_up_weight, blocks, group, groups
        )
        grad_queries.append(dq)
        grad_weight.append(
            lax.psum_scatter(gw, "ctx", scatter_dimension=0, tiled=True).astype(jnp.float32)
        )
        partial = parts if partial is None else [a + b for a, b in zip(partial, parts)]

    low = jnp.bfloat16
    to_swap, to_far, to_mixed, total = partial
    from_mixed = permute(to_mixed.astype(low), "ctx", lambda s: s - 1 if s % 2 else s - 3)
    from_swap = permute(to_swap.astype(low), "ctx", lambda s: s ^ 1)
    far_sum = (to_far + from_swap.astype(jnp.float32)).astype(low)
    from_far = permute(far_sum, "ctx", lambda s: s - 2)
    total = total + from_mixed.astype(jnp.float32) + from_far.astype(jnp.float32)
    mine = total.astype(low)
    size = lax.axis_size("head")
    for turn in range(1, size):
        other = lax.ppermute(mine, "head", [(s, (s + turn) % size) for s in range(size)])
        total = total + other.astype(jnp.float32)
    return (
        jnp.concatenate(grad_queries, axis=1),
        total.astype(low),
        jnp.concatenate(grad_weight, axis=1),
    )


def solution(mesh):
    return jax.shard_map(
        local,
        mesh=mesh,
        in_specs=(P("ctx", None), P("ctx", "head"), P("ctx", "head"), P(None, "head"), P()),
        out_specs=(P("ctx", "head"), P("ctx", None), P("ctx", "head")),
        check_vma=False,
    )
```

```python
import functools
import math

import jax
import jax.numpy as jnp
from jax import lax
from jax.experimental import pallas as pl
from jax.experimental.pallas import tpu as pltpu
from jax.sharding import PartitionSpec as P

NOPE = 128
ROPE = 64
VDIM = 128
LATENT = 512
REACH = 3
QK = NOPE + ROPE
KV = NOPE + VDIM
WIDTH = LATENT + ROPE
TILE = 256
GROUPS = 2

MASKED = -1e30
FLOOR = -1e20
SCALE = 1.0 / math.sqrt(QK)
SCALE2 = SCALE * math.log2(math.e)

NT = (((1,), (1,)), ((), ()))
NN = (((1,), (0,)), ((), ()))


def dot(a, b, dims=NN):
    return lax.dot_general(a, b, dims, preferred_element_type=jnp.float32)


def attention_kernel(rows, ranks, initial, final, *refs):
    index_ref, docs_sref, docs_ref, q_ref, do_ref, w_ref, lat0, lat1, lat2, lat3, *refs = refs
    if not initial:
        _, x_in, *refs = refs
    dq_ref, keep_ref, send_ref, *refs = refs
    x_outs, refs = (refs[: REACH + 1], refs[REACH + 1 :]) if final else (refs[:1], refs[1:])
    (lat_ref, lat_t_ref, bias_ref, e_ref, g_ref, k_ref, top_ref, dq_acc, gw_acc, x_acc, r_acc,
     sems, x_sem) = refs

    step = pl.program_id(0)
    index = index_ref[0]
    odd = lax.rem(index, 2)
    first_row = index * rows
    tiles_block = rows // TILE
    tiles = (REACH + 1) * tiles_block
    first_doc = docs_sref[first_row]

    def window_base(t):
        block = t // tiles_block
        base = jnp.where(block == 1, rows, REACH * rows)
        base = jnp.where(block == 0, rows * 2 * (1 - odd), base)
        base = jnp.where(block == 2, rows * 2 * odd, base)
        return base + lax.rem(t, tiles_block) * TILE

    def active(t):
        position = first_row - REACH * rows + window_base(t)
        last_doc = docs_sref[jnp.maximum(position, 0) + TILE - 1]
        return (position >= 0) & (last_doc >= first_doc)

    def tile_rows(t):
        return pl.ds(pl.multiple_of(t * TILE, TILE), TILE)

    @pl.when(step == 0)
    def _():
        copies = [
            pltpu.make_async_copy(source, lat_t_ref.at[:, pl.ds(i * rows, rows)], sems.at[i])
            for i, source in enumerate((lat0, lat1, lat2, lat3))
        ]
        for copy in copies:
            copy.start()
        if initial:
            x_acc[...] = jnp.zeros_like(x_acc)
        else:
            x_copy = pltpu.make_async_copy(x_in, x_acc, x_sem)
            x_copy.start()
        r_acc[...] = jnp.zeros_like(r_acc)
        my_docs = docs_ref[:, pl.ds(pl.multiple_of(first_row, rows), rows)]
        last_seen = REACH * rows + lax.broadcasted_iota(jnp.int32, (1, rows), 1)

        def fill(t, carry):
            @pl.when(active(t))
            def _():
                base = window_base(t)
                position = pl.multiple_of(first_row - REACH * rows + base, TILE)
                key_docs = docs_ref[:, pl.ds(position, TILE)]
                key_docs = jnp.broadcast_to(key_docs, (128, TILE)).T[:, :1]
                key = lax.broadcasted_iota(jnp.int32, (TILE, rows), 0)
                seen = (key_docs == my_docs) & (key <= last_seen - base)
                bias_ref[tile_rows(t), :] = jnp.where(seen, 0.0, MASKED)

            return carry

        lax.fori_loop(0, tiles, fill, 0)
        for copy in copies:
            copy.wait()
        for i in range(REACH + 1):
            part = slice(i * rows, (i + 1) * rows)
            lat_ref[part, :] = lat_t_ref[:, part].T
        if not initial:
            x_copy.wait()

    gw_acc[...] = jnp.zeros_like(gw_acc)
    dq_acc[...] = jnp.zeros_like(dq_acc)
    heads = range(2)
    q = [q_ref[:, h * QK : (h + 1) * QK] for h in heads]
    do = [do_ref[:, h * VDIM : (h + 1) * VDIM] for h in heads]

    def first_pass(t, carry):
        def run(carry):
            part = tile_rows(t)
            latent = lat_ref[part, :LATENT]
            rope = lat_ref[part, LATENT:]
            bias = bias_ref[part, :]
            out = []
            for h in heads:
                top, mass, cross = carry[h]
                lifted = dot(latent, w_ref[:, h * KV : (h + 1) * KV]).astype(jnp.bfloat16)
                key = jnp.concatenate([lifted[:, :NOPE], rope], axis=1)
                k_ref[h, part, :] = key
                scores = dot(key, q[h], NT) * SCALE2 + bias
                grads = dot(lifted[:, NOPE:], do[h], NT)
                new_top = jnp.maximum(top, jnp.max(scores, axis=0, keepdims=True))
                weights = jnp.exp2(scores - new_top)
                factor = jnp.exp2(top - new_top)
                mass = mass * factor + jnp.sum(weights, axis=0, keepdims=True)
                cross = cross * factor + jnp.sum(weights * grads, axis=0, keepdims=True)
                e_ref[h, part, :] = weights
                g_ref[h, part, :] = grads
                top_ref[h, pl.ds(t, 1), :] = new_top
                out.append((new_top, mass, cross))
            return tuple(out)

        return lax.cond(active(t), run, lambda c: c, carry)

    zero = jnp.zeros((1, rows), jnp.float32)
    stats = lax.fori_loop(0, tiles, first_pass, ((zero + FLOOR, zero, zero),) * 2)
    inverse = [1.0 / mass for _, mass, _ in stats]
    delta = [cross * inv for (_, _, cross), inv in zip(stats, inverse)]

    def second_pass(t, carry):
        @pl.when(active(t))
        def _():
            part = tile_rows(t)
            pieces = []
            for h in heads:
                factor = jnp.exp2(top_ref[h, pl.ds(t, 1), :] - stats[h][0]) * inverse[h]
                probs = e_ref[h, part, :] * factor
                low = probs.astype(jnp.bfloat16)
                dscore = (probs * (g_ref[h, part, :] - delta[h])).astype(jnp.bfloat16)
                dvalue = dot(low, do[h])
                dkey = dot(dscore, q[h]) * SCALE
                own = slice(h * QK, (h + 1) * QK)
                dq_acc[own, :] += dot(k_ref[h, part, :].T, dscore)
                r_acc[part, :] += dkey[:, NOPE:]
                pieces += [dkey[:, :NOPE].astype(jnp.bfloat16), dvalue.astype(jnp.bfloat16)]
            grads = jnp.concatenate(pieces, axis=1)
            x_acc[:LATENT, part] += dot(w_ref[...], grads, NT)
            gw_acc[...] += dot(lat_t_ref[:LATENT, part], grads)

        return carry

    lax.fori_loop(0, tiles, second_pass, 0)
    dq_ref[...] = (dq_acc[...] * SCALE).T.astype(dq_ref.dtype)
    share = LATENT // ranks
    for i in range(ranks // 2):
        for out, half in ((keep_ref, odd), (send_ref, 1 - odd)):
            source = pl.multiple_of(2 * i * share + half * share, share)
            out[i * share : (i + 1) * share, :] = gw_acc[pl.ds(source, share), :].astype(out.dtype)

    @pl.when(step == pl.num_programs(0) - 1)
    def _():
        x_acc[LATENT:, :] += r_acc[...].T
        if final:
            for i, out in enumerate(x_outs):
                out[...] = x_acc[:, i * rows : (i + 1) * rows].astype(out.dtype)
        else:
            x_copy = pltpu.make_async_copy(x_acc, x_outs[0], x_sem)
            x_copy.start()
            x_copy.wait()


def attention(index, doc_ids, queries, grad_out, weight, blocks, state, group, groups, ranks):
    rows = queries.shape[0]
    heads = weight.shape[1] // KV
    pairs = heads // 2 // groups
    first = group * pairs
    window = (REACH + 1) * rows
    low, full = jnp.bfloat16, jnp.float32
    initial, final = group == 0, group == groups - 1
    anywhere = pl.BlockSpec(memory_space=pl.ANY)
    scalars = pl.BlockSpec(memory_space=pltpu.SMEM)

    def pair_cols(height, size):
        return pl.BlockSpec((height, 2 * size), lambda i: (0, first + i))

    half = pl.BlockSpec((LATENT // 2, 2 * KV), lambda i: (0, i))
    half_shape = jax.ShapeDtypeStruct((LATENT // 2, pairs * 2 * KV), low)
    flops = 2 * pairs * 2 * rows * window * (3 * QK + 2 * VDIM) * 2
    return pl.pallas_call(
        functools.partial(attention_kernel, rows, ranks, initial, final),
        grid=(pairs,),
        in_specs=[
            scalars,
            scalars,
            pl.BlockSpec((1, doc_ids.shape[0]), lambda i: (0, 0)),
            pair_cols(rows, QK),
            pair_cols(rows, VDIM),
            pair_cols(LATENT, KV),
        ]
        + [anywhere] * (REACH + 1 + len(state)),
        out_specs=[pair_cols(rows, QK), half, half]
        + ([pl.BlockSpec((WIDTH, rows), lambda i: (0, 0))] * (REACH + 1) if final else [anywhere]),
        out_shape=[jax.ShapeDtypeStruct(queries.shape, low), half_shape, half_shape]
        + (
            [jax.ShapeDtypeStruct((WIDTH, rows), low)] * (REACH + 1)
            if final
            else [jax.ShapeDtypeStruct((WIDTH, window), full)]
        ),
        input_output_aliases={} if initial else {6 + REACH + 1: 0},
        scratch_shapes=[
            pltpu.VMEM((window, WIDTH), low),
            pltpu.VMEM((WIDTH, window), low),
            pltpu.VMEM((window, rows), full),
            pltpu.VMEM((2, window, rows), full),
            pltpu.VMEM((2, window, rows), full),
            pltpu.VMEM((2, window, QK), low),
            pltpu.VMEM((2, window // TILE, rows), full),
            pltpu.VMEM((2 * QK, rows), full),
            pltpu.VMEM((LATENT, 2 * KV), full),
            pltpu.VMEM((WIDTH, window), full),
            pltpu.VMEM((window, ROPE), full),
            pltpu.SemaphoreType.DMA((REACH + 1,)),
            pltpu.SemaphoreType.DMA,
        ],
        compiler_params=pltpu.CompilerParams(
            dimension_semantics=("arbitrary",), vmem_limit_bytes=56 * 1024 * 1024
        ),
        cost_estimate=pl.CostEstimate(
            flops=flops, bytes_accessed=16 * 1024 * 1024, transcendentals=0
        ),
        name="attention",
    )(index, doc_ids, doc_ids[None], queries, grad_out, weight, *blocks, *state)


def permute(value, axis, target):
    count = lax.axis_size(axis)
    pairs = [(s, target(s)) for s in range(count) if 0 <= target(s) < count]
    return lax.ppermute(value, axis, pairs)


def local(kv_latent, queries, grad_out, kv_up_weight, doc_ids):
    ranks = lax.axis_size("ctx")
    index = lax.axis_index("ctx").astype(jnp.int32)[None]
    low, full = jnp.bfloat16, jnp.float32

    latent = kv_latent.T
    far = permute(latent, "ctx", lambda s: s + 2)
    mixed = permute(latent, "ctx", lambda s: s + 3 if s % 2 else s + 1)
    swapped = permute(far, "ctx", lambda s: s ^ 1)
    blocks = (swapped, far, mixed, latent)

    groups = min(GROUPS, kv_up_weight.shape[1] // (2 * KV))
    chips = [list(range(parity, ranks, 2)) for parity in range(2)]
    state, grad_weight = (), []
    for group in range(groups):
        grad_queries, keep, send, *parts = attention(
            index, doc_ids, queries, grad_out, kv_up_weight, blocks, state, group, groups, ranks
        )
        both = keep.astype(full) + permute(send, "ctx", lambda s: s ^ 1).astype(full)
        both = both.astype(low)
        if group < groups - 1:
            both, *parts = lax.optimization_barrier((both, *parts))
        state = (grad_queries, *parts)
        grad_weight.append(
            lax.psum_scatter(
                both, "ctx", scatter_dimension=0, axis_index_groups=chips, tiled=True
            ).astype(full)
        )

    to_swap, to_far, to_mixed, mine = parts
    from_mixed = permute(to_mixed, "ctx", lambda s: s - 1 if s % 2 else s - 3)
    from_swap = permute(to_swap, "ctx", lambda s: s ^ 1)
    far_sum = (to_far.astype(full) + from_swap.astype(full)).astype(low)
    from_far = permute(far_sum, "ctx", lambda s: s - 2)
    total = mine.astype(full) + from_mixed.astype(full) + from_far.astype(full)
    mine = total.astype(low)
    size = lax.axis_size("head")
    for turn in range(1, size):
        other = lax.ppermute(mine, "head", [(s, (s + turn) % size) for s in range(size)])
        total = total + other.astype(full)
    return grad_queries, total.astype(low).T, jnp.concatenate(grad_weight, axis=1)


def solution(mesh):
    return jax.shard_map(
        local,
        mesh=mesh,
        in_specs=(P("ctx", None), P("ctx", "head"), P("ctx", "head"), P(None, "head"), P()),
        out_specs=(P("ctx", "head"), P("ctx", None), P("ctx", "head")),
        check_vma=False,
    )
```

```python
import functools
import math

import jax
import jax.numpy as jnp
from jax import lax
from jax.experimental import pallas as pl
from jax.experimental.pallas import tpu as pltpu
from jax.sharding import PartitionSpec as P

NOPE = 128
ROPE = 64
VDIM = 128
LATENT = 512
REACH = 3
QK = NOPE + ROPE
KV = NOPE + VDIM
WIDTH = LATENT + ROPE
TILE = 256

MASKED = -1e30
FLOOR = -1e20
SCALE = 1.0 / math.sqrt(QK)
SCALE2 = SCALE * math.log2(math.e)

NT = (((1,), (1,)), ((), ()))
NN = (((1,), (0,)), ((), ()))


def dot(a, b, dims=NN):
    return lax.dot_general(a, b, dims, preferred_element_type=jnp.float32)


def attention_kernel(rows, ranks, initial, final, *refs):
    index_ref, docs_sref, docs_ref, q_ref, do_ref, w_ref, lat0, lat1, lat2, lat3, *refs = refs
    if not initial:
        _, x_in, *refs = refs
    dq_ref, keep_ref, send_ref, *refs = refs
    x_outs, refs = (refs[: REACH + 1], refs[REACH + 1 :]) if final else (refs[:1], refs[1:])
    (lat_ref, lat_t_ref, bias_ref, e_ref, g_ref, k_ref, top_ref, dq_acc, gw_acc, x_acc, r_acc,
     sems, x_sem) = refs

    step = pl.program_id(0)
    index = index_ref[0]
    odd = lax.rem(index, 2)
    first_row = index * rows
    tiles_block = rows // TILE
    tiles = (REACH + 1) * tiles_block
    first_doc = docs_sref[first_row]

    def window_base(t):
        block = t // tiles_block
        base = jnp.where(block == 1, rows, REACH * rows)
        base = jnp.where(block == 0, rows * 2 * (1 - odd), base)
        base = jnp.where(block == 2, rows * 2 * odd, base)
        return base + lax.rem(t, tiles_block) * TILE

    def active(t):
        position = first_row - REACH * rows + window_base(t)
        last_doc = docs_sref[jnp.maximum(position, 0) + TILE - 1]
        return (position >= 0) & (last_doc >= first_doc)

    def tile_rows(t):
        return pl.ds(pl.multiple_of(t * TILE, TILE), TILE)

    @pl.when(step == 0)
    def _():
        copies = [
            pltpu.make_async_copy(source, lat_t_ref.at[:, pl.ds(i * rows, rows)], sems.at[i])
            for i, source in enumerate((lat0, lat1, lat2, lat3))
        ]
        for copy in copies:
            copy.start()
        if initial:
            x_acc[...] = jnp.zeros_like(x_acc)
        else:
            x_copy = pltpu.make_async_copy(x_in, x_acc, x_sem)
            x_copy.start()
        r_acc[...] = jnp.zeros_like(r_acc)
        my_docs = docs_ref[:, pl.ds(pl.multiple_of(first_row, rows), rows)]
        last_seen = REACH * rows + lax.broadcasted_iota(jnp.int32, (1, rows), 1)

        def fill(t, carry):
            @pl.when(active(t))
            def _():
                base = window_base(t)
                position = pl.multiple_of(first_row - REACH * rows + base, TILE)
                key_docs = docs_ref[:, pl.ds(position, TILE)]
                key_docs = jnp.broadcast_to(key_docs, (128, TILE)).T[:, :1]
                key = lax.broadcasted_iota(jnp.int32, (TILE, rows), 0)
                seen = (key_docs == my_docs) & (key <= last_seen - base)
                bias_ref[tile_rows(t), :] = jnp.where(seen, 0.0, MASKED)

            return carry

        lax.fori_loop(0, tiles, fill, 0)
        for copy in copies:
            copy.wait()
        for i in range(REACH + 1):
            part = slice(i * rows, (i + 1) * rows)
            lat_ref[part, :] = lat_t_ref[:, part].T
        if not initial:
            x_copy.wait()

    gw_acc[...] = jnp.zeros_like(gw_acc)
    dq_acc[...] = jnp.zeros_like(dq_acc)
    heads = range(2)
    q = [q_ref[:, h * QK : (h + 1) * QK] for h in heads]
    do = [do_ref[:, h * VDIM : (h + 1) * VDIM] for h in heads]

    def first_pass(t, carry):
        def run(carry):
            part = tile_rows(t)
            latent = lat_ref[part, :LATENT]
            rope = lat_ref[part, LATENT:]
            bias = bias_ref[part, :]
            out = []
            for h in heads:
                top, mass, cross = carry[h]
                lifted = dot(latent, w_ref[:, h * KV : (h + 1) * KV]).astype(jnp.bfloat16)
                key = jnp.concatenate([lifted[:, :NOPE], rope], axis=1)
                k_ref[h, part, :] = key
                scores = dot(key, q[h], NT) * SCALE2 + bias
                grads = dot(lifted[:, NOPE:], do[h], NT)
                new_top = jnp.maximum(top, jnp.max(scores, axis=0, keepdims=True))
                weights = jnp.exp2(scores - new_top)
                factor = jnp.exp2(top - new_top)
                mass = mass * factor + jnp.sum(weights, axis=0, keepdims=True)
                cross = cross * factor + jnp.sum(weights * grads, axis=0, keepdims=True)
                e_ref[h, part, :] = weights
                g_ref[h, part, :] = grads
                top_ref[h, pl.ds(t, 1), :] = new_top
                out.append((new_top, mass, cross))
            return tuple(out)

        return lax.cond(active(t), run, lambda c: c, carry)

    zero = jnp.zeros((1, rows), jnp.float32)
    stats = lax.fori_loop(0, tiles, first_pass, ((zero + FLOOR, zero, zero),) * 2)
    inverse = [1.0 / mass for _, mass, _ in stats]
    delta = [cross * inv for (_, _, cross), inv in zip(stats, inverse)]

    def second_pass(t, carry):
        @pl.when(active(t))
        def _():
            part = tile_rows(t)
            pieces = []
            for h in heads:
                factor = jnp.exp2(top_ref[h, pl.ds(t, 1), :] - stats[h][0]) * inverse[h]
                probs = e_ref[h, part, :] * factor
                low = probs.astype(jnp.bfloat16)
                dscore = (probs * (g_ref[h, part, :] - delta[h])).astype(jnp.bfloat16)
                dvalue = dot(low, do[h])
                dkey = dot(dscore, q[h]) * SCALE
                own = slice(h * QK, (h + 1) * QK)
                dq_acc[own, :] += dot(k_ref[h, part, :].T, dscore)
                r_acc[part, :] += dkey[:, NOPE:]
                pieces += [dkey[:, :NOPE].astype(jnp.bfloat16), dvalue.astype(jnp.bfloat16)]
            grads = jnp.concatenate(pieces, axis=1)
            x_acc[:LATENT, part] += dot(w_ref[...], grads, NT)
            gw_acc[...] += dot(lat_t_ref[:LATENT, part], grads)

        return carry

    lax.fori_loop(0, tiles, second_pass, 0)
    dq_ref[...] = (dq_acc[...] * SCALE).T.astype(dq_ref.dtype)
    share = LATENT // ranks
    for i in range(ranks // 2):
        for out, half in ((keep_ref, odd), (send_ref, 1 - odd)):
            source = pl.multiple_of(2 * i * share + half * share, share)
            out[i * share : (i + 1) * share, :] = gw_acc[pl.ds(source, share), :].astype(out.dtype)

    @pl.when(step == pl.num_programs(0) - 1)
    def _():
        x_acc[LATENT:, :] += r_acc[...].T
        if final:
            for i, out in enumerate(x_outs):
                out[...] = x_acc[:, i * rows : (i + 1) * rows].astype(out.dtype)
        else:
            x_copy = pltpu.make_async_copy(x_acc, x_outs[0], x_sem)
            x_copy.start()
            x_copy.wait()


def attention(index, doc_ids, queries, grad_out, weight, blocks, state, span, total, ranks):
    rows = queries.shape[0]
    first, pairs = span[0], span[1] - span[0]
    window = (REACH + 1) * rows
    low, full = jnp.bfloat16, jnp.float32
    initial, final = span[0] == 0, span[1] == total
    anywhere = pl.BlockSpec(memory_space=pl.ANY)
    scalars = pl.BlockSpec(memory_space=pltpu.SMEM)

    def pair_cols(height, size):
        return pl.BlockSpec((height, 2 * size), lambda i: (0, first + i))

    half = pl.BlockSpec((LATENT // 2, 2 * KV), lambda i: (0, i))
    half_shape = jax.ShapeDtypeStruct((LATENT // 2, pairs * 2 * KV), low)
    flops = 2 * pairs * 2 * rows * window * (3 * QK + 2 * VDIM) * 2
    return pl.pallas_call(
        functools.partial(attention_kernel, rows, ranks, initial, final),
        grid=(pairs,),
        in_specs=[
            scalars,
            scalars,
            pl.BlockSpec((1, doc_ids.shape[0]), lambda i: (0, 0)),
            pair_cols(rows, QK),
            pair_cols(rows, VDIM),
            pair_cols(LATENT, KV),
        ]
        + [anywhere] * (REACH + 1 + len(state)),
        out_specs=[pair_cols(rows, QK), half, half]
        + ([pl.BlockSpec((WIDTH, rows), lambda i: (0, 0))] * (REACH + 1) if final else [anywhere]),
        out_shape=[jax.ShapeDtypeStruct(queries.shape, low), half_shape, half_shape]
        + (
            [jax.ShapeDtypeStruct((WIDTH, rows), low)] * (REACH + 1)
            if final
            else [jax.ShapeDtypeStruct((WIDTH, window), full)]
        ),
        input_output_aliases={} if initial else {6 + REACH + 1: 0},
        scratch_shapes=[
            pltpu.VMEM((window, WIDTH), low),
            pltpu.VMEM((WIDTH, window), low),
            pltpu.VMEM((window, rows), full),
            pltpu.VMEM((2, window, rows), full),
            pltpu.VMEM((2, window, rows), full),
            pltpu.VMEM((2, window, QK), low),
            pltpu.VMEM((2, window // TILE, rows), full),
            pltpu.VMEM((2 * QK, rows), full),
            pltpu.VMEM((LATENT, 2 * KV), full),
            pltpu.VMEM((WIDTH, window), full),
            pltpu.VMEM((window, ROPE), full),
            pltpu.SemaphoreType.DMA((REACH + 1,)),
            pltpu.SemaphoreType.DMA,
        ],
        compiler_params=pltpu.CompilerParams(
            dimension_semantics=("arbitrary",), vmem_limit_bytes=56 * 1024 * 1024
        ),
        cost_estimate=pl.CostEstimate(
            flops=flops, bytes_accessed=16 * 1024 * 1024, transcendentals=0
        ),
        name="attention",
    )(index, doc_ids, doc_ids[None], queries, grad_out, weight, *blocks, *state)


def permute(value, axis, target):
    count = lax.axis_size(axis)
    pairs = [(s, target(s)) for s in range(count) if 0 <= target(s) < count]
    return lax.ppermute(value, axis, pairs)


def local(kv_latent, queries, grad_out, kv_up_weight, doc_ids):
    ranks = lax.axis_size("ctx")
    index = lax.axis_index("ctx").astype(jnp.int32)[None]
    low, full = jnp.bfloat16, jnp.float32

    latent = kv_latent.T
    far = permute(latent, "ctx", lambda s: s + 2)
    mixed = permute(latent, "ctx", lambda s: s + 3 if s % 2 else s + 1)
    swapped = permute(far, "ctx", lambda s: s ^ 1)
    blocks = (swapped, far, mixed, latent)

    pairs = kv_up_weight.shape[1] // (2 * KV)
    spans = [(0, pairs - 1), (pairs - 1, pairs)] if pairs > 1 else [(0, pairs)]
    chips = [list(range(parity, ranks, 2)) for parity in range(2)]
    state, arrived = (), []
    for span in spans:
        grad_queries, keep, send, *parts = attention(
            index, doc_ids, queries, grad_out, kv_up_weight, blocks, state, span, pairs, ranks
        )
        if arrived:
            arrived[-1], send, *parts = lax.optimization_barrier((arrived[-1], send, *parts))
        both = keep.astype(full) + permute(send, "ctx", lambda s: s ^ 1).astype(full)
        both = both.astype(low)
        if span[1] < pairs:
            both, *parts = lax.optimization_barrier((both, *parts))
        state = (grad_queries, *parts)
        arrived.append(lax.all_to_all(both, "ctx", 0, 0, axis_index_groups=chips, tiled=True))
    grad_weight = [
        jnp.sum(pieces.reshape(ranks // 2, LATENT // ranks, -1).astype(full), axis=0)
        for pieces in arrived
    ]

    to_swap, to_far, to_mixed, mine = parts
    from_mixed = permute(to_mixed, "ctx", lambda s: s - 1 if s % 2 else s - 3)
    from_swap = permute(to_swap, "ctx", lambda s: s ^ 1)
    far_sum = (to_far.astype(full) + from_swap.astype(full)).astype(low)
    from_far = permute(far_sum, "ctx", lambda s: s - 2)
    total = mine.astype(full) + from_mixed.astype(full) + from_far.astype(full)
    mine = total.astype(low)
    size = lax.axis_size("head")
    for turn in range(1, size):
        other = lax.ppermute(mine, "head", [(s, (s + turn) % size) for s in range(size)])
        total = total + other.astype(full)
    return grad_queries, total.astype(low).T, jnp.concatenate(grad_weight, axis=1)


def solution(mesh):
    return jax.shard_map(
        local,
        mesh=mesh,
        in_specs=(P("ctx", None), P("ctx", "head"), P("ctx", "head"), P(None, "head"), P()),
        out_specs=(P("ctx", "head"), P("ctx", None), P("ctx", "head")),
        check_vma=False,
    )
```

```python
import functools
import math

import jax
import jax.numpy as jnp
from jax import lax
from jax.experimental import pallas as pl
from jax.experimental.pallas import tpu as pltpu
from jax.sharding import PartitionSpec as P

NOPE = 128
ROPE = 64
VDIM = 128
LATENT = 512
REACH = 3
QK = NOPE + ROPE
KV = NOPE + VDIM
WIDTH = LATENT + ROPE
TILE = 512
LANES = 128

MASKED = -1e30
FLOOR = -1e20
SCALE = 1.0 / math.sqrt(QK)
SCALE2 = SCALE * math.log2(math.e)

NT = (((1,), (1,)), ((), ()))
NN = (((1,), (0,)), ((), ()))


def dot(a, b, dims=NN):
    return lax.dot_general(a, b, dims, preferred_element_type=jnp.float32)


def attention_kernel(rows, ranks, initial, final, *refs):
    index_ref, docs_sref, docs_ref, q_ref, do_ref, w_ref, lat0, lat1, lat2, lat3, *refs = refs
    if not initial:
        _, x_in, *refs = refs
    dq_ref, keep_ref, send_ref, *refs = refs
    x_outs, refs = (refs[: REACH + 1], refs[REACH + 1 :]) if final else (refs[:1], refs[1:])
    (lat_ref, lat_t_ref, bias_ref, e_ref, g_ref, k_ref, top_ref, dq_acc, gw_acc, x_acc, r_acc,
     sems, x_sem) = refs

    step = pl.program_id(0)
    index = index_ref[0]
    odd = lax.rem(index, 2)
    first_row = index * rows
    tiles_block = rows // TILE
    tiles = (REACH + 1) * tiles_block
    first_doc = docs_sref[first_row]

    def window_base(t):
        block = t // tiles_block
        base = jnp.where(block == 1, rows, REACH * rows)
        base = jnp.where(block == 0, rows * 2 * (1 - odd), base)
        base = jnp.where(block == 2, rows * 2 * odd, base)
        return base + lax.rem(t, tiles_block) * TILE

    def active(t):
        position = first_row - REACH * rows + window_base(t)
        last_doc = docs_sref[jnp.maximum(position, 0) + TILE - 1]
        return (position >= 0) & (last_doc >= first_doc)

    def tile_rows(t):
        return pl.ds(pl.multiple_of(t * TILE, TILE), TILE)

    @pl.when(step == 0)
    def _():
        copies = [
            pltpu.make_async_copy(source, lat_t_ref.at[:, pl.ds(i * rows, rows)], sems.at[i])
            for i, source in enumerate((lat0, lat1, lat2, lat3))
        ]
        for copy in copies:
            copy.start()
        if initial:
            x_acc[...] = jnp.zeros_like(x_acc)
        else:
            x_copy = pltpu.make_async_copy(x_in, x_acc, x_sem)
            x_copy.start()
        r_acc[...] = jnp.zeros_like(r_acc)
        my_docs = docs_ref[:, pl.ds(pl.multiple_of(first_row, rows), rows)]
        last_seen = REACH * rows + lax.broadcasted_iota(jnp.int32, (1, rows), 1)

        def fill(t, carry):
            @pl.when(active(t))
            def _():
                base = window_base(t)
                position = pl.multiple_of(first_row - REACH * rows + base, TILE)
                key_docs = docs_ref[:, pl.ds(position, TILE)]
                key_docs = jnp.broadcast_to(key_docs, (128, TILE)).T[:, :1]
                key = lax.broadcasted_iota(jnp.int32, (TILE, rows), 0)
                seen = (key_docs == my_docs) & (key <= last_seen - base)
                bias_ref[tile_rows(t), :] = jnp.where(seen, 0.0, MASKED)

            return carry

        lax.fori_loop(0, tiles, fill, 0)
        for copy in copies:
            copy.wait()
        for i in range(REACH + 1):
            part = slice(i * rows, (i + 1) * rows)
            lat_ref[part, :] = lat_t_ref[:, part].T
        if not initial:
            x_copy.wait()

    gw_acc[...] = jnp.zeros_like(gw_acc)
    dq_acc[...] = jnp.zeros_like(dq_acc)
    heads = range(2)
    q = [q_ref[:, h * QK : (h + 1) * QK] for h in heads]
    do = [do_ref[:, h * VDIM : (h + 1) * VDIM] for h in heads]

    def first_pass(t, carry):
        def run(carry):
            part = tile_rows(t)
            latent = lat_ref[part, :LATENT]
            rope = lat_ref[part, LATENT:]
            out = []
            for h in heads:
                top, mass, cross = carry[h]
                lifted = dot(latent, w_ref[:, h * KV : (h + 1) * KV]).astype(jnp.bfloat16)
                key = jnp.concatenate([lifted[:, :NOPE], rope], axis=1)
                k_ref[h, part, :] = key
                raw = dot(key, q[h], NT)
                grads = dot(lifted[:, NOPE:], do[h], NT)
                g_ref[h, part, :] = grads
                tops, masses, crosses = [], [], []
                for c in range(0, rows, LANES):
                    cols = slice(c, c + LANES)
                    scores = raw[:, cols] * SCALE2 + bias_ref[part, cols]
                    old_top = top[:, cols]
                    new_top = jnp.maximum(old_top, jnp.max(scores, axis=0, keepdims=True))
                    weights = jnp.exp2(scores - new_top)
                    e_ref[h, part, cols] = weights
                    factor = jnp.exp2(old_top - new_top)
                    tops.append(new_top)
                    masses.append(mass[:, cols] * factor + jnp.sum(weights, axis=0, keepdims=True))
                    crosses.append(
                        cross[:, cols] * factor
                        + jnp.sum(weights * grads[:, cols], axis=0, keepdims=True)
                    )
                new_top, mass, cross = (
                    jnp.concatenate(pieces, axis=1) for pieces in (tops, masses, crosses)
                )
                top_ref[h, pl.ds(t, 1), :] = new_top
                out.append((new_top, mass, cross))
            return tuple(out)

        return lax.cond(active(t), run, lambda c: c, carry)

    zero = jnp.zeros((1, rows), jnp.float32)
    stats = lax.fori_loop(0, tiles, first_pass, ((zero + FLOOR, zero, zero),) * 2)
    inverse = [1.0 / mass for _, mass, _ in stats]
    delta = [cross * inv for (_, _, cross), inv in zip(stats, inverse)]

    def second_pass(t, carry):
        @pl.when(active(t))
        def _():
            part = tile_rows(t)
            pieces = []
            for h in heads:
                factor = jnp.exp2(top_ref[h, pl.ds(t, 1), :] - stats[h][0]) * inverse[h]
                lows, dscores = [], []
                for c in range(0, rows, LANES):
                    cols = slice(c, c + LANES)
                    probs = e_ref[h, part, cols] * factor[:, cols]
                    dscore = probs * (g_ref[h, part, cols] - delta[h][:, cols])
                    lows.append(probs.astype(jnp.bfloat16))
                    dscores.append(dscore.astype(jnp.bfloat16))
                low = jnp.concatenate(lows, axis=1)
                dscore = jnp.concatenate(dscores, axis=1)
                dvalue = dot(low, do[h])
                dkey = dot(dscore, q[h]) * SCALE
                own = slice(h * QK, (h + 1) * QK)
                dq_acc[own, :] += dot(k_ref[h, part, :].T, dscore)
                r_acc[part, :] += dkey[:, NOPE:]
                pieces += [dkey[:, :NOPE].astype(jnp.bfloat16), dvalue.astype(jnp.bfloat16)]
            grads = jnp.concatenate(pieces, axis=1)
            x_acc[:LATENT, part] += dot(w_ref[...], grads, NT)
            gw_acc[...] += dot(lat_t_ref[:LATENT, part], grads)

        return carry

    lax.fori_loop(0, tiles, second_pass, 0)
    dq_ref[...] = (dq_acc[...] * SCALE).T.astype(dq_ref.dtype)
    share = LATENT // ranks
    for i in range(ranks // 2):
        for out, half in ((keep_ref, odd), (send_ref, 1 - odd)):
            source = pl.multiple_of(2 * i * share + half * share, share)
            out[i * share : (i + 1) * share, :] = gw_acc[pl.ds(source, share), :].astype(out.dtype)

    @pl.when(step == pl.num_programs(0) - 1)
    def _():
        x_acc[LATENT:, :] += r_acc[...].T
        if final:
            for i, out in enumerate(x_outs):
                out[...] = x_acc[:, i * rows : (i + 1) * rows].astype(out.dtype)
        else:
            x_copy = pltpu.make_async_copy(x_acc, x_outs[0], x_sem)
            x_copy.start()
            x_copy.wait()


def attention(index, doc_ids, queries, grad_out, weight, blocks, state, span, total, ranks):
    rows = queries.shape[0]
    first, pairs = span[0], span[1] - span[0]
    window = (REACH + 1) * rows
    low, full = jnp.bfloat16, jnp.float32
    initial, final = span[0] == 0, span[1] == total
    anywhere = pl.BlockSpec(memory_space=pl.ANY)
    scalars = pl.BlockSpec(memory_space=pltpu.SMEM)

    def pair_cols(height, size):
        return pl.BlockSpec((height, 2 * size), lambda i: (0, first + i))

    half = pl.BlockSpec((LATENT // 2, 2 * KV), lambda i: (0, i))
    half_shape = jax.ShapeDtypeStruct((LATENT // 2, pairs * 2 * KV), low)
    flops = 2 * pairs * 2 * rows * window * (3 * QK + 2 * VDIM) * 2
    return pl.pallas_call(
        functools.partial(attention_kernel, rows, ranks, initial, final),
        grid=(pairs,),
        in_specs=[
            scalars,
            scalars,
            pl.BlockSpec((1, doc_ids.shape[0]), lambda i: (0, 0)),
            pair_cols(rows, QK),
            pair_cols(rows, VDIM),
            pair_cols(LATENT, KV),
        ]
        + [anywhere] * (REACH + 1 + len(state)),
        out_specs=[pair_cols(rows, QK), half, half]
        + ([pl.BlockSpec((WIDTH, rows), lambda i: (0, 0))] * (REACH + 1) if final else [anywhere]),
        out_shape=[jax.ShapeDtypeStruct(queries.shape, low), half_shape, half_shape]
        + (
            [jax.ShapeDtypeStruct((WIDTH, rows), low)] * (REACH + 1)
            if final
            else [jax.ShapeDtypeStruct((WIDTH, window), full)]
        ),
        input_output_aliases={} if initial else {6 + REACH + 1: 0},
        scratch_shapes=[
            pltpu.VMEM((window, WIDTH), low),
            pltpu.VMEM((WIDTH, window), low),
            pltpu.VMEM((window, rows), full),
            pltpu.VMEM((2, window, rows), full),
            pltpu.VMEM((2, window, rows), full),
            pltpu.VMEM((2, window, QK), low),
            pltpu.VMEM((2, window // TILE, rows), full),
            pltpu.VMEM((2 * QK, rows), full),
            pltpu.VMEM((LATENT, 2 * KV), full),
            pltpu.VMEM((WIDTH, window), full),
            pltpu.VMEM((window, ROPE), full),
            pltpu.SemaphoreType.DMA((REACH + 1,)),
            pltpu.SemaphoreType.DMA,
        ],
        compiler_params=pltpu.CompilerParams(
            dimension_semantics=("arbitrary",), vmem_limit_bytes=56 * 1024 * 1024
        ),
        cost_estimate=pl.CostEstimate(
            flops=flops, bytes_accessed=16 * 1024 * 1024, transcendentals=0
        ),
        name="attention",
    )(index, doc_ids, doc_ids[None], queries, grad_out, weight, *blocks, *state)


def permute(value, axis, target):
    count = lax.axis_size(axis)
    pairs = [(s, target(s)) for s in range(count) if 0 <= target(s) < count]
    return lax.ppermute(value, axis, pairs)


def local(kv_latent, queries, grad_out, kv_up_weight, doc_ids):
    ranks = lax.axis_size("ctx")
    index = lax.axis_index("ctx").astype(jnp.int32)[None]
    low, full = jnp.bfloat16, jnp.float32

    latent = kv_latent.T
    far = permute(latent, "ctx", lambda s: s + 2)
    mixed = permute(latent, "ctx", lambda s: s + 3 if s % 2 else s + 1)
    swapped = permute(far, "ctx", lambda s: s ^ 1)
    blocks = (swapped, far, mixed, latent)

    pairs = kv_up_weight.shape[1] // (2 * KV)
    spans = [(0, pairs - 1), (pairs - 1, pairs)] if pairs > 1 else [(0, pairs)]
    chips = [list(range(parity, ranks, 2)) for parity in range(2)]
    state, arrived = (), []
    for span in spans:
        grad_queries, keep, send, *parts = attention(
            index, doc_ids, queries, grad_out, kv_up_weight, blocks, state, span, pairs, ranks
        )
        if arrived:
            arrived[-1], send, *parts = lax.optimization_barrier((arrived[-1], send, *parts))
        both = keep.astype(full) + permute(send, "ctx", lambda s: s ^ 1).astype(full)
        both = both.astype(low)
        if span[1] < pairs:
            both, *parts = lax.optimization_barrier((both, *parts))
        state = (grad_queries, *parts)
        arrived.append(lax.all_to_all(both, "ctx", 0, 0, axis_index_groups=chips, tiled=True))
    grad_weight = [
        jnp.sum(pieces.reshape(ranks // 2, LATENT // ranks, -1).astype(full), axis=0)
        for pieces in arrived
    ]

    to_swap, to_far, to_mixed, mine = parts
    from_mixed = permute(to_mixed, "ctx", lambda s: s - 1 if s % 2 else s - 3)
    from_swap = permute(to_swap, "ctx", lambda s: s ^ 1)
    far_sum = (to_far.astype(full) + from_swap.astype(full)).astype(low)
    from_far = permute(far_sum, "ctx", lambda s: s - 2)
    total = mine.astype(full) + from_mixed.astype(full) + from_far.astype(full)
    mine = total.astype(low)
    size = lax.axis_size("head")
    for turn in range(1, size):
        other = lax.ppermute(mine, "head", [(s, (s + turn) % size) for s in range(size)])
        total = total + other.astype(full)
    return grad_queries, total.astype(low).T, jnp.concatenate(grad_weight, axis=1)


def solution(mesh):
    return jax.shard_map(
        local,
        mesh=mesh,
        in_specs=(P("ctx", None), P("ctx", "head"), P("ctx", "head"), P(None, "head"), P()),
        out_specs=(P("ctx", "head"), P("ctx", None), P("ctx", "head")),
        check_vma=False,
    )
```

```python
import functools
import math

import jax
import jax.numpy as jnp
from jax import lax
from jax.experimental import pallas as pl
from jax.experimental.pallas import tpu as pltpu
from jax.sharding import PartitionSpec as P

NOPE = 128
ROPE = 64
VDIM = 128
LATENT = 512
REACH = 3
QK = NOPE + ROPE
KV = NOPE + VDIM
WIDTH = LATENT + ROPE
LANES = 128

MASKED = -1e30
FLOOR = -1e20
SCALE = 1.0 / math.sqrt(QK)
SCALE2 = SCALE * math.log2(math.e)

NT = (((1,), (1,)), ((), ()))
NN = (((1,), (0,)), ((), ()))


def dot(a, b, dims=NN):
    return lax.dot_general(a, b, dims, preferred_element_type=jnp.float32)


def attention_kernel(rows, ranks, *refs):
    (index_ref, docs_sref, docs_ref, qa_ref, doa_ref, wa_ref, qc_ref, doc_ref, wc_ref,
     lat0, lat1, lat2, lat3, dq_ref, keep_ref, send_ref, x0_ref, x1_ref, x2_ref, x3_ref,
     lat_ref, lat_t_ref, bias_ref, e_ref, g_ref, k_ref, top_ref, run_ref, end_ref,
     dq_acc, gw_acc, x_acc, r_acc, sems) = refs

    step, last = pl.program_id(0), pl.num_programs(0) - 1
    index = index_ref[0]
    odd = lax.rem(index, 2)
    first_row = index * rows
    first_doc = docs_sref[first_row]
    heads = range(2)

    def window_base(t):
        base = jnp.where(t == 1, rows, REACH * rows)
        base = jnp.where(t == 0, rows * 2 * (1 - odd), base)
        return jnp.where(t == 2, rows * 2 * odd, base)

    def active(t):
        position = first_row - REACH * rows + window_base(t)
        last_doc = docs_sref[jnp.maximum(position, 0) + rows - 1]
        return (position >= 0) & (last_doc >= first_doc)

    def block_rows(t):
        return pl.ds(pl.multiple_of(t * rows, rows), rows)

    def each_block(body):
        def visit(t, carry):
            @pl.when(active(t))
            def _():
                body(t)

            return carry

        lax.fori_loop(0, REACH + 1, visit, 0)

    def fill_bias(t):
        base = window_base(t)
        my_docs = docs_ref[:, pl.ds(pl.multiple_of(first_row, rows), rows)]
        last_seen = REACH * rows + lax.broadcasted_iota(jnp.int32, (1, rows), 1)
        position = pl.multiple_of(first_row - REACH * rows + base, rows)
        key_docs = docs_ref[:, pl.ds(position, rows)]
        key_docs = jnp.broadcast_to(key_docs, (128, rows)).T[:, :1]
        key = lax.broadcasted_iota(jnp.int32, (rows, rows), 0)
        seen = (key_docs == my_docs) & (key <= last_seen - base)
        bias_ref[block_rows(t), :] = jnp.where(seen, 0.0, MASKED)

    @pl.when(step == 0)
    def _():
        copies = [
            pltpu.make_async_copy(source, lat_t_ref.at[:, pl.ds(i * rows, rows)], sems.at[i])
            for i, source in enumerate((lat0, lat1, lat2, lat3))
        ]
        for copy in copies:
            copy.start()
        x_acc[...] = jnp.zeros_like(x_acc)
        r_acc[...] = jnp.zeros_like(r_acc)
        each_block(fill_bias)
        for copy in copies:
            copy.wait()
        for i in range(REACH + 1):
            part = slice(i * rows, (i + 1) * rows)
            lat_ref[part, :] = lat_t_ref[:, part].T

    def take_probs(t):
        part = block_rows(t)
        out = []
        for h in heads:
            factor = jnp.exp2(top_ref[h, t, 0:1, :] - end_ref[h, 0:1, :]) * end_ref[h, 1:2, :]
            delta = end_ref[h, 2:3, :]
            lows, dscores = [], []
            for c in range(0, rows, LANES):
                cols = slice(c, c + LANES)
                probs = e_ref[h, part, cols] * factor[:, cols]
                dscore = probs * (g_ref[h, part, cols] - delta[:, cols])
                lows.append(probs.astype(jnp.bfloat16))
                dscores.append(dscore.astype(jnp.bfloat16))
            out.append(
                (
                    jnp.concatenate(lows, axis=1),
                    jnp.concatenate(dscores, axis=1),
                    k_ref[h, part, :].T,
                )
            )
        return out

    def add_grads(t, taken):
        part = block_rows(t)
        pieces = []
        for h in heads:
            low, dscore, key_t = taken[h]
            dvalue = dot(low, doc_ref[:, h * VDIM : (h + 1) * VDIM])
            dkey = dot(dscore, qc_ref[:, h * QK : (h + 1) * QK]) * SCALE
            dq_acc[h * QK : (h + 1) * QK, :] += dot(key_t, dscore)
            r_acc[part, :] += dkey[:, NOPE:]
            pieces += [dkey[:, :NOPE].astype(jnp.bfloat16), dvalue.astype(jnp.bfloat16)]
        grads = jnp.concatenate(pieces, axis=1)
        x_acc[:LATENT, part] += dot(wc_ref[...], grads, NT)
        gw_acc[...] += dot(lat_t_ref[:LATENT, part], grads)

    def make_scores(t):
        part = block_rows(t)
        latent = lat_ref[part, :LATENT]
        rope = lat_ref[part, LATENT:]
        out = []
        for h in heads:
            lifted = dot(latent, wa_ref[:, h * KV : (h + 1) * KV]).astype(jnp.bfloat16)
            key = jnp.concatenate([lifted[:, :NOPE], rope], axis=1)
            raw = dot(key, qa_ref[:, h * QK : (h + 1) * QK], NT)
            grads = dot(lifted[:, NOPE:], doa_ref[:, h * VDIM : (h + 1) * VDIM], NT)
            out.append((key, raw, grads))
        return out

    def keep_scores(t, made):
        part = block_rows(t)
        for h in heads:
            key, raw, grads = made[h]
            k_ref[h, part, :] = key
            g_ref[h, part, :] = grads
            for c in range(0, rows, LANES):
                cols = slice(c, c + LANES)
                scores = raw[:, cols] * SCALE2 + bias_ref[part, cols]
                old_top = run_ref[h, 0:1, cols]
                new_top = jnp.maximum(old_top, jnp.max(scores, axis=0, keepdims=True))
                weights = jnp.exp2(scores - new_top)
                e_ref[h, part, cols] = weights
                factor = jnp.exp2(old_top - new_top)
                run_ref[h, 0:1, cols] = new_top
                run_ref[h, 1:2, cols] = run_ref[h, 1:2, cols] * factor + jnp.sum(
                    weights, axis=0, keepdims=True
                )
                run_ref[h, 2:3, cols] = run_ref[h, 2:3, cols] * factor + jnp.sum(
                    weights * grads[:, cols], axis=0, keepdims=True
                )
                top_ref[h, t, 0:1, cols] = new_top

    @pl.when(step > 0)
    def _():
        for h in heads:
            inverse = 1.0 / run_ref[h, 1:2, :]
            end_ref[h, 0:1, :] = run_ref[h, 0:1, :]
            end_ref[h, 1:2, :] = inverse
            end_ref[h, 2:3, :] = run_ref[h, 2:3, :] * inverse
        gw_acc[...] = jnp.zeros_like(gw_acc)
        dq_acc[...] = jnp.zeros_like(dq_acc)

    for h in heads:
        run_ref[h, 0:1, :] = jnp.full((1, rows), FLOOR, jnp.float32)
        run_ref[h, 1:3, :] = jnp.zeros((2, rows), jnp.float32)

    @pl.when(step == 0)
    def _():
        each_block(lambda t: keep_scores(t, make_scores(t)))

    @pl.when((step > 0) & (step < last))
    def _():
        def both(t):
            taken = take_probs(t)
            made = make_scores(t)
            add_grads(t, taken)
            keep_scores(t, made)

        each_block(both)

    @pl.when(step == last)
    def _():
        each_block(lambda t: add_grads(t, take_probs(t)))

    @pl.when(step > 0)
    def _():
        dq_ref[...] = (dq_acc[...] * SCALE).T.astype(dq_ref.dtype)
        share = LATENT // ranks
        quarter = LATENT // 4
        own_x = lax.rem(index // 2, 2)
        for i in range(ranks // 4):
            for out, core in ((keep_ref, odd), (send_ref, 1 - odd)):
                for where, x in ((0, own_x), (quarter, 1 - own_x)):
                    source = pl.multiple_of((4 * i + 2 * x + core) * share, share)
                    out[where + i * share : where + (i + 1) * share, :] = gw_acc[
                        pl.ds(source, share), :
                    ].astype(out.dtype)

    @pl.when(step == last)
    def _():
        x_acc[LATENT:, :] = r_acc[...].T
        for i, out in enumerate((x0_ref, x1_ref, x2_ref, x3_ref)):
            out[...] = x_acc[:, i * rows : (i + 1) * rows].astype(out.dtype)


def attention(index, doc_ids, queries, grad_out, weight, blocks, ranks):
    rows = queries.shape[0]
    pairs = weight.shape[1] // (2 * KV)
    window = (REACH + 1) * rows
    low, full = jnp.bfloat16, jnp.float32
    scalars = pl.BlockSpec(memory_space=pltpu.SMEM)

    def pair_cols(height, size, pair):
        return pl.BlockSpec((height, 2 * size), lambda i: (0, pair(i)))

    def inputs(pair):
        return [
            pair_cols(rows, QK, pair), pair_cols(rows, VDIM, pair), pair_cols(LATENT, KV, pair)
        ]

    def ahead(i):
        return jnp.minimum(i, pairs - 1)

    def behind(i):
        return jnp.maximum(i - 1, 0)

    half = pair_cols(LATENT // 2, KV, behind)
    half_shape = jax.ShapeDtypeStruct((LATENT // 2, pairs * 2 * KV), low)
    flops = 2 * pairs * 2 * rows * window * (3 * QK + 2 * VDIM) * 2
    return pl.pallas_call(
        functools.partial(attention_kernel, rows, ranks),
        grid=(pairs + 1,),
        in_specs=[scalars, scalars, pl.BlockSpec((1, doc_ids.shape[0]), lambda i: (0, 0))]
        + inputs(ahead)
        + inputs(behind)
        + [pl.BlockSpec(memory_space=pl.ANY)] * (REACH + 1),
        out_specs=[pair_cols(rows, QK, behind), half, half]
        + [pl.BlockSpec((WIDTH, rows), lambda i: (0, 0))] * (REACH + 1),
        out_shape=[jax.ShapeDtypeStruct(queries.shape, low), half_shape, half_shape]
        + [jax.ShapeDtypeStruct((WIDTH, rows), low)] * (REACH + 1),
        scratch_shapes=[
            pltpu.VMEM((window, WIDTH), low),
            pltpu.VMEM((WIDTH, window), low),
            pltpu.VMEM((window, rows), full),
            pltpu.VMEM((2, window, rows), full),
            pltpu.VMEM((2, window, rows), full),
            pltpu.VMEM((2, window, QK), low),
            pltpu.VMEM((2, REACH + 1, 8, rows), full),
            pltpu.VMEM((2, 8, rows), full),
            pltpu.VMEM((2, 8, rows), full),
            pltpu.VMEM((2 * QK, rows), full),
            pltpu.VMEM((LATENT, 2 * KV), full),
            pltpu.VMEM((WIDTH, window), full),
            pltpu.VMEM((window, ROPE), full),
            pltpu.SemaphoreType.DMA((REACH + 1,)),
        ],
        compiler_params=pltpu.CompilerParams(
            dimension_semantics=("arbitrary",), vmem_limit_bytes=56 * 1024 * 1024
        ),
        cost_estimate=pl.CostEstimate(
            flops=flops, bytes_accessed=16 * 1024 * 1024, transcendentals=0
        ),
        name="attention",
    )(index, doc_ids, doc_ids[None], *(queries, grad_out, weight) * 2, *blocks)


def permute(value, axis, target):
    count = lax.axis_size(axis)
    pairs = [(s, target(s)) for s in range(count) if 0 <= target(s) < count]
    return lax.ppermute(value, axis, pairs)


def local(kv_latent, queries, grad_out, kv_up_weight, doc_ids):
    ranks = lax.axis_size("ctx")
    index = lax.axis_index("ctx").astype(jnp.int32)[None]
    low, full = jnp.bfloat16, jnp.float32

    latent = kv_latent.T
    far = permute(latent, "ctx", lambda s: s + 2)
    mixed = permute(latent, "ctx", lambda s: s + 3 if s % 2 else s + 1)
    swapped = permute(far, "ctx", lambda s: s ^ 1)
    blocks = (swapped, far, mixed, latent)

    grad_queries, keep, send, to_swap, to_far, to_mixed, mine = attention(
        index, doc_ids, queries, grad_out, kv_up_weight, blocks, ranks
    )

    chip = keep.astype(full) + permute(send, "ctx", lambda s: s ^ 1).astype(full)
    quarter = LATENT // 4
    from_x = permute(chip[quarter:].astype(low), "ctx", lambda s: s ^ 2)
    plane = (chip[:quarter] + from_x.astype(full)).astype(low)
    columns = [list(range(first, ranks, 4)) for first in range(4)]
    pieces = lax.all_to_all(plane, "ctx", 0, 0, axis_index_groups=columns, tiled=True)
    grad_weight = jnp.sum(pieces.reshape(ranks // 4, LATENT // ranks, -1).astype(full), axis=0)

    from_mixed = permute(to_mixed, "ctx", lambda s: s - 1 if s % 2 else s - 3)
    from_swap = permute(to_swap, "ctx", lambda s: s ^ 1)
    far_sum = (to_far.astype(full) + from_swap.astype(full)).astype(low)
    from_far = permute(far_sum, "ctx", lambda s: s - 2)
    total = mine.astype(full) + from_mixed.astype(full) + from_far.astype(full)
    mine = total.astype(low)
    size = lax.axis_size("head")
    for turn in range(1, size):
        other = lax.ppermute(mine, "head", [(s, (s + turn) % size) for s in range(size)])
        total = total + other.astype(full)
    return grad_queries, total.astype(low).T, grad_weight


def solution(mesh):
    return jax.shard_map(
        local,
        mesh=mesh,
        in_specs=(P("ctx", None), P("ctx", "head"), P("ctx", "head"), P(None, "head"), P()),
        out_specs=(P("ctx", "head"), P("ctx", None), P("ctx", "head")),
        check_vma=False,
    )
```

```python
import functools
import math

import jax
import jax.numpy as jnp
from jax import lax
from jax.experimental import pallas as pl
from jax.experimental.pallas import tpu as pltpu
from jax.sharding import PartitionSpec as P

NOPE = 128
ROPE = 64
VDIM = 128
LATENT = 512
REACH = 3
QK = NOPE + ROPE
KV = NOPE + VDIM
WIDTH = LATENT + ROPE
LANES = 128

MASKED = -1e30
FLOOR = -1e20
SCALE = 1.0 / math.sqrt(QK)
SCALE2 = SCALE * math.log2(math.e)

NT = (((1,), (1,)), ((), ()))
NN = (((1,), (0,)), ((), ()))


def dot(a, b, dims=NN):
    return lax.dot_general(a, b, dims, preferred_element_type=jnp.float32)


def head_cols(h, size):
    return slice(h * size, (h + 1) * size)


def score_block(h, latent, q_ref, do_ref, w_ref, bias, run_ref, keep):
    rows = q_ref.shape[0]
    lifted = dot(latent[:, :LATENT], w_ref[:, head_cols(h, KV)]).astype(jnp.bfloat16)
    key = jnp.concatenate([lifted[:, :NOPE], latent[:, LATENT:]], axis=1)
    raw = dot(key, q_ref[:, head_cols(h, QK)], NT)
    grads = dot(lifted[:, NOPE:], do_ref[:, head_cols(h, VDIM)], NT)
    for c in range(0, rows, LANES):
        cols = slice(c, c + LANES)
        scores = raw[:, cols] * SCALE2 + bias(cols)
        old_top = run_ref[h, 0:1, cols]
        new_top = jnp.maximum(old_top, jnp.max(scores, axis=0, keepdims=True))
        weights = jnp.exp2(scores - new_top)
        factor = jnp.exp2(old_top - new_top)
        run_ref[h, 0:1, cols] = new_top
        run_ref[h, 1:2, cols] = run_ref[h, 1:2, cols] * factor + jnp.sum(
            weights, axis=0, keepdims=True
        )
        run_ref[h, 2:3, cols] = run_ref[h, 2:3, cols] * factor + jnp.sum(
            weights * grads[:, cols], axis=0, keepdims=True
        )
        keep(cols, weights, grads[:, cols], new_top)
    return key


def grad_block(h, weights, grads, key, top, end_ref, q_t, do_t, dq_acc, first):
    rows = do_t.shape[1]
    factor = jnp.exp2(top - end_ref[h, 0:1, :]) * end_ref[h, 1:2, :]
    delta = end_ref[h, 2:3, :]
    lows, dscores = [], []
    for c in range(0, rows, LANES):
        cols = slice(c, c + LANES)
        probs = weights(cols) * factor[:, cols]
        lows.append(probs.astype(jnp.bfloat16))
        dscores.append((probs * (grads(cols) - delta[:, cols])).astype(jnp.bfloat16))
    low = jnp.concatenate(lows, axis=1)
    dscore = jnp.concatenate(dscores, axis=1)
    dvalue = dot(do_t[head_cols(h, VDIM), :], low, NT)
    dkey = dot(q_t[head_cols(h, QK), :], dscore, NT) * SCALE
    own = head_cols(h, QK)
    dq = dot(key.T, dscore)
    dq_acc[own, :] = dq + (first[own, :] if first is not None else dq_acc[own, :])
    columns = [dkey[:NOPE].astype(jnp.bfloat16), dvalue.astype(jnp.bfloat16)]
    return columns, dkey[NOPE:]


def start_stats(run_ref):
    rows = run_ref.shape[2]
    for h in range(2):
        run_ref[h, 0:1, :] = jnp.full((1, rows), FLOOR, jnp.float32)
        run_ref[h, 1:8, :] = jnp.zeros((7, rows), jnp.float32)


def own_score_kernel(
    index_ref, docs_ref, q_ref, do_ref, w_ref, lat_t_ref,
    e_ref, g_ref, k_ref, run_ref, lat_ref, bias_ref,
):
    rows = q_ref.shape[0]

    @pl.when(pl.program_id(0) == 0)
    def _():
        lat_ref[...] = lat_t_ref[...].T
        first_row = pl.multiple_of(index_ref[0] * rows, rows)
        docs = docs_ref[:, pl.ds(first_row, rows)]
        key_docs = jnp.broadcast_to(docs, (128, rows)).T[:, :1]
        key = lax.broadcasted_iota(jnp.int32, (rows, rows), 0)
        query = lax.broadcasted_iota(jnp.int32, (rows, rows), 1)
        bias_ref[...] = jnp.where((key_docs == docs) & (key <= query), 0.0, MASKED)

    start_stats(run_ref)
    for h in range(2):

        def keep(cols, weights, grads, new_top):
            e_ref[h, :, cols] = weights
            g_ref[h, :, cols] = grads

        k_ref[h, :, :] = score_block(
            h, lat_ref[...], q_ref, do_ref, w_ref, lambda cols: bias_ref[:, cols], run_ref, keep
        )


def earlier_kernel(
    index_ref, docs_sref, docs_ref, q_ref, do_ref, w_ref, own_run_ref, lat0, lat1, lat2,
    dq_ref, gw_ref, end_ref, x0_ref, x1_ref, x2_ref,
    lat_ref, lat_t_ref, bias_ref, e_ref, g_ref, k_ref, top_ref, run_ref, x_acc, sems,
):
    step = pl.program_id(0)
    rows = q_ref.shape[0]
    index = index_ref[0]
    odd = lax.rem(index, 2)
    first_row = index * rows
    first_doc = docs_sref[first_row]
    heads = range(2)

    def block_start(t):
        back = jnp.where(t == 1, 2, jnp.where(t == 0, 1 + 2 * odd, 3 - 2 * odd))
        return first_row - back * rows

    def active(t):
        start = block_start(t)
        return (start >= 0) & (docs_sref[jnp.maximum(start, 0) + rows - 1] >= first_doc)

    def block_rows(t):
        return pl.ds(pl.multiple_of(t * rows, rows), rows)

    def each_block(body):
        def visit(t, carry):
            @pl.when(active(t))
            def _():
                body(t)

            return carry

        lax.fori_loop(0, REACH, visit, 0)

    def fill_bias(t):
        my_docs = docs_ref[:, pl.ds(pl.multiple_of(first_row, rows), rows)]
        key_docs = docs_ref[:, pl.ds(pl.multiple_of(block_start(t), rows), rows)]
        key_docs = jnp.broadcast_to(key_docs, (128, rows)).T[:, :1]
        bias_ref[block_rows(t), :] = jnp.where(key_docs == my_docs, 0.0, MASKED)

    @pl.when(step == 0)
    def _():
        copies = [
            pltpu.make_async_copy(source, lat_t_ref.at[:, pl.ds(i * rows, rows)], sems.at[i])
            for i, source in enumerate((lat0, lat1, lat2))
        ]
        for copy in copies:
            copy.start()
        x_acc[...] = jnp.zeros_like(x_acc)
        each_block(fill_bias)
        for copy in copies:
            copy.wait()
        for i in range(REACH):
            part = slice(i * rows, (i + 1) * rows)
            lat_ref[part, :] = lat_t_ref[:, part].T

    gw_ref[...] = jnp.zeros_like(gw_ref)
    dq_ref[...] = jnp.zeros_like(dq_ref)
    run_ref[...] = own_run_ref[...]

    def first_pass(t):
        part = block_rows(t)
        latent = lat_ref[part, :]
        for h in heads:

            def keep(cols, weights, grads, new_top):
                e_ref[h, part, cols] = weights
                g_ref[h, part, cols] = grads
                top_ref[h, t, 0:1, cols] = new_top

            k_ref[h, part, :] = score_block(
                h, latent, q_ref, do_ref, w_ref, lambda cols: bias_ref[part, cols], run_ref, keep
            )

    each_block(first_pass)
    for h in heads:
        inverse = 1.0 / run_ref[h, 1:2, :]
        end_ref[h, 0:1, :] = run_ref[h, 0:1, :]
        end_ref[h, 1:2, :] = inverse
        end_ref[h, 2:3, :] = run_ref[h, 2:3, :] * inverse
        end_ref[h, 3:8, :] = jnp.zeros((5, rows), jnp.float32)
    q_t, do_t = q_ref[...].T, do_ref[...].T

    def second_pass(t):
        part = block_rows(t)
        columns, rope = [], 0.0
        for h in heads:
            made, turn = grad_block(
                h, lambda cols: e_ref[h, part, cols], lambda cols: g_ref[h, part, cols],
                k_ref[h, part, :], top_ref[h, t, 0:1, :], end_ref, q_t, do_t, dq_ref, None,
            )
            columns += made
            rope = rope + turn
        grads = jnp.concatenate(columns, axis=0)
        x_acc[:LATENT, part] += dot(w_ref[...], grads)
        x_acc[LATENT:, part] += rope
        gw_ref[...] += dot(lat_t_ref[:LATENT, part], grads, NT)

    each_block(second_pass)

    @pl.when(step == pl.num_programs(0) - 1)
    def _():
        for i, out in enumerate((x0_ref, x1_ref, x2_ref)):
            out[...] = x_acc[:, i * rows : (i + 1) * rows].astype(out.dtype)


def own_grad_kernel(
    ranks,
    index_ref, q_ref, do_ref, w_ref, lat_t_ref, e_ref, g_ref, k_ref, run_ref, end_ref,
    dq_in, gw_in, dq_ref, keep_ref, send_ref, x_ref, dq_acc, gw_acc, x_acc,
):
    step = pl.program_id(0)
    index = index_ref[0]

    @pl.when(step == 0)
    def _():
        x_acc[...] = jnp.zeros_like(x_acc)

    q_t, do_t = q_ref[...].T, do_ref[...].T
    columns = []
    for h in range(2):
        made, turn = grad_block(
            h, lambda cols: e_ref[h, :, cols], lambda cols: g_ref[h, :, cols],
            k_ref[h, :, :], run_ref[h, 0:1, :], end_ref, q_t, do_t, dq_acc, dq_in,
        )
        columns += made
        x_acc[LATENT:, :] += turn
    grads = jnp.concatenate(columns, axis=0)
    gw_acc[...] = gw_in[...] + dot(lat_t_ref[:LATENT, :], grads, NT)
    x_acc[:LATENT, :] += dot(w_ref[...], grads)
    dq_ref[...] = (dq_acc[...] * SCALE).T.astype(dq_ref.dtype)

    share, quarter = LATENT // ranks, LATENT // 4
    own_core, own_x = lax.rem(index, 2), lax.rem(index // 2, 2)
    for i in range(ranks // 4):
        for out, core in ((keep_ref, own_core), (send_ref, 1 - own_core)):
            for where, x in ((0, own_x), (quarter, 1 - own_x)):
                source = pl.multiple_of((4 * i + 2 * x + core) * share, share)
                out[where + i * share : where + (i + 1) * share, :] = gw_acc[
                    pl.ds(source, share), :
                ].astype(out.dtype)

    @pl.when(step == pl.num_programs(0) - 1)
    def _():
        x_ref[...] = x_acc[...].astype(x_ref.dtype)


def pair_cols(height, size):
    return pl.BlockSpec((height, 2 * size), lambda i: (0, i))


def pair_heads(*shape):
    return pl.BlockSpec((2, *shape), lambda i: (i, 0, 0))


def fixed(*shape):
    return pl.BlockSpec(shape, lambda i: (0, 0))


SCALARS = pl.BlockSpec(memory_space=pltpu.SMEM)


def call(body, pairs, flops, in_specs, out_specs, out_shape, scratch, name):
    return pl.pallas_call(
        body,
        grid=(pairs,),
        in_specs=in_specs,
        out_specs=out_specs,
        out_shape=[jax.ShapeDtypeStruct(shape, kind) for shape, kind in out_shape],
        scratch_shapes=scratch,
        compiler_params=pltpu.CompilerParams(
            dimension_semantics=("arbitrary",), vmem_limit_bytes=56 * 1024 * 1024
        ),
        cost_estimate=pl.CostEstimate(
            flops=flops, bytes_accessed=16 * 1024 * 1024, transcendentals=0
        ),
        name=name,
    )


def own_scores(index, docs, queries, grad_out, weight, latent):
    rows = queries.shape[0]
    pairs = weight.shape[1] // (2 * KV)
    low, full = jnp.bfloat16, jnp.float32
    return call(
        own_score_kernel,
        pairs,
        2 * pairs * rows * rows * 2 * (QK + VDIM + KV),
        [
            SCALARS, fixed(1, docs.shape[1]), pair_cols(rows, QK), pair_cols(rows, VDIM),
            pair_cols(LATENT, KV), fixed(WIDTH, rows),
        ],
        [pair_heads(rows, rows), pair_heads(rows, rows), pair_heads(rows, QK), pair_heads(8, rows)],
        [
            ((2 * pairs, rows, rows), full),
            ((2 * pairs, rows, rows), full),
            ((2 * pairs, rows, QK), low),
            ((2 * pairs, 8, rows), full),
        ],
        [pltpu.VMEM((rows, WIDTH), low), pltpu.VMEM((rows, rows), full)],
        "own_scores",
    )(index, docs, queries, grad_out, weight, latent)


def earlier_blocks(index, doc_ids, docs, queries, grad_out, weight, run, blocks):
    rows = queries.shape[0]
    pairs = weight.shape[1] // (2 * KV)
    window = REACH * rows
    low, full = jnp.bfloat16, jnp.float32
    return call(
        earlier_kernel,
        pairs,
        2 * pairs * rows * window * 2 * (3 * QK + 2 * VDIM + 3 * KV),
        [
            SCALARS, SCALARS, fixed(1, docs.shape[1]), pair_cols(rows, QK), pair_cols(rows, VDIM),
            pair_cols(LATENT, KV), pair_heads(8, rows),
        ]
        + [pl.BlockSpec(memory_space=pl.ANY)] * REACH,
        [
            pl.BlockSpec((2 * QK, rows), lambda i: (i, 0)), pair_cols(LATENT, KV),
            pair_heads(8, rows),
        ]
        + [fixed(WIDTH, rows)] * REACH,
        [
            ((pairs * 2 * QK, rows), full),
            ((LATENT, pairs * 2 * KV), full),
            ((2 * pairs, 8, rows), full),
        ]
        + [((WIDTH, rows), low)] * REACH,
        [
            pltpu.VMEM((window, WIDTH), low),
            pltpu.VMEM((WIDTH, window), low),
            pltpu.VMEM((window, rows), full),
            pltpu.VMEM((2, window, rows), full),
            pltpu.VMEM((2, window, rows), full),
            pltpu.VMEM((2, window, QK), low),
            pltpu.VMEM((2, REACH, 8, rows), full),
            pltpu.VMEM((2, 8, rows), full),
            pltpu.VMEM((WIDTH, window), full),
            pltpu.SemaphoreType.DMA((REACH,)),
        ],
        "earlier_blocks",
    )(index, doc_ids, docs, queries, grad_out, weight, run, *blocks)


def own_grads(index, queries, grad_out, weight, latent, kept, end, dq, gw, ranks):
    rows = queries.shape[0]
    pairs = weight.shape[1] // (2 * KV)
    low, full = jnp.bfloat16, jnp.float32
    half = pair_cols(LATENT // 2, KV)
    return call(
        functools.partial(own_grad_kernel, ranks),
        pairs,
        2 * pairs * rows * rows * 2 * (2 * QK + VDIM + 2 * KV),
        [
            SCALARS, pair_cols(rows, QK), pair_cols(rows, VDIM), pair_cols(LATENT, KV),
            fixed(WIDTH, rows), pair_heads(rows, rows), pair_heads(rows, rows),
            pair_heads(rows, QK), pair_heads(8, rows), pair_heads(8, rows),
            pl.BlockSpec((2 * QK, rows), lambda i: (i, 0)), pair_cols(LATENT, KV),
        ],
        [pair_cols(rows, QK), half, half, fixed(WIDTH, rows)],
        [
            (queries.shape, low),
            ((LATENT // 2, pairs * 2 * KV), low),
            ((LATENT // 2, pairs * 2 * KV), low),
            ((WIDTH, rows), low),
        ],
        [
            pltpu.VMEM((2 * QK, rows), full),
            pltpu.VMEM((LATENT, 2 * KV), full),
            pltpu.VMEM((WIDTH, rows), full),
        ],
        "own_grads",
    )(index, queries, grad_out, weight, latent, *kept, end, dq, gw)


def permute(value, axis, target):
    count = lax.axis_size(axis)
    pairs = [(s, target(s)) for s in range(count) if 0 <= target(s) < count]
    return lax.ppermute(value, axis, pairs)


def local(kv_latent, queries, grad_out, kv_up_weight, doc_ids):
    ranks = lax.axis_size("ctx")
    index = lax.axis_index("ctx").astype(jnp.int32)[None]
    low, full = jnp.bfloat16, jnp.float32
    docs = doc_ids[None]

    latent = kv_latent.T
    far = permute(latent, "ctx", lambda s: s + 2)
    mixed = permute(latent, "ctx", lambda s: s + 3 if s % 2 else s + 1)
    *kept, run = own_scores(index, docs, queries, grad_out, kv_up_weight, latent)
    far, run = lax.optimization_barrier((far, run))
    swapped = permute(far, "ctx", lambda s: s ^ 1)

    dq, gw, end, to_swap, to_far, to_mixed = earlier_blocks(
        index, doc_ids, docs, queries, grad_out, kv_up_weight, run, (swapped, far, mixed)
    )
    from_mixed = permute(to_mixed, "ctx", lambda s: s - 1 if s % 2 else s - 3)
    from_swap = permute(to_swap, "ctx", lambda s: s ^ 1)
    far_sum = (to_far.astype(full) + from_swap.astype(full)).astype(low)
    far_sum, gw = lax.optimization_barrier((far_sum, gw))
    from_far = permute(far_sum, "ctx", lambda s: s - 2)
    grad_queries, keep, send, mine = own_grads(
        index, queries, grad_out, kv_up_weight, latent, (*kept, run), end, dq, gw, ranks
    )

    from_far, from_mixed, send = lax.optimization_barrier((from_far, from_mixed, send))

    chip = keep.astype(full) + permute(send, "ctx", lambda s: s ^ 1).astype(full)
    quarter = LATENT // 4
    from_x = permute(chip[quarter:].astype(low), "ctx", lambda s: s ^ 2)
    plane = (chip[:quarter] + from_x.astype(full)).astype(low)
    columns = [list(range(first, ranks, 4)) for first in range(4)]
    pieces = lax.all_to_all(plane, "ctx", 0, 0, axis_index_groups=columns, tiled=True)
    grad_weight = jnp.sum(pieces.reshape(ranks // 4, LATENT // ranks, -1).astype(full), axis=0)

    total = mine.astype(full) + from_mixed.astype(full) + from_far.astype(full)
    mine = total.astype(low)
    size = lax.axis_size("head")
    for turn in range(1, size):
        other = lax.ppermute(mine, "head", [(s, (s + turn) % size) for s in range(size)])
        total = total + other.astype(full)
    return grad_queries, total.astype(low).T, grad_weight


def solution(mesh):
    return jax.shard_map(
        local,
        mesh=mesh,
        in_specs=(P("ctx", None), P("ctx", "head"), P("ctx", "head"), P(None, "head"), P()),
        out_specs=(P("ctx", "head"), P("ctx", None), P("ctx", "head")),
        check_vma=False,
    )
```

```python
import functools
import math

import jax
import jax.numpy as jnp
from jax import lax
from jax.experimental import pallas as pl
from jax.experimental.pallas import tpu as pltpu
from jax.sharding import PartitionSpec as P

NOPE = 128
ROPE = 64
VDIM = 128
LATENT = 512
REACH = 3
QK = NOPE + ROPE
KV = NOPE + VDIM
WIDTH = LATENT + ROPE
LANES = 128

MASKED = -1e30
FLOOR = -1e20
SCALE = 1.0 / math.sqrt(QK)
SCALE2 = SCALE * math.log2(math.e)

NT = (((1,), (1,)), ((), ()))
NN = (((1,), (0,)), ((), ()))


def dot(a, b, dims=NN):
    return lax.dot_general(a, b, dims, preferred_element_type=jnp.float32)


def head_cols(h, size):
    return slice(h * size, (h + 1) * size)


def fold(value, combine):
    return combine(value.reshape(-1, 8, value.shape[1]), axis=0)


def score_block(latent, q_ref, do_ref, w_ref, bias, run_ref, raw_ref, graw_ref, k_out, keep):
    rows = q_ref.shape[0]
    for h in range(2):
        lifted = dot(latent[:, :LATENT], w_ref[:, head_cols(h, KV)]).astype(jnp.bfloat16)
        key = jnp.concatenate([lifted[:, :NOPE], latent[:, LATENT:]], axis=1)
        k_out(h, key)
        raw_ref[h] = dot(key, q_ref[:, head_cols(h, QK)], NT)
        graw_ref[h] = dot(lifted[:, NOPE:], do_ref[:, head_cols(h, VDIM)], NT)
    for h in range(2):
        for c in range(0, rows, LANES):
            cols = slice(c, c + LANES)

            def scores(part):
                return raw_ref[h, part, cols] * SCALE2 + bias(part, cols)

            pieces = [slice(r, r + LANES) for r in range(0, rows, LANES)]
            high = None
            for part in pieces:
                piece = fold(scores(part), jnp.max)
                high = piece if high is None else jnp.maximum(high, piece)
            old_top = run_ref[h, 0:1, cols]
            new_top = jnp.maximum(old_top, jnp.max(high, axis=0, keepdims=True))
            mass, cross = 0.0, 0.0
            for part in pieces:
                weights = jnp.exp2(scores(part) - new_top)
                grads = graw_ref[h, part, cols]
                keep(h, part, cols, weights.astype(jnp.bfloat16), grads.astype(jnp.bfloat16))
                mass = mass + fold(weights, jnp.sum)
                cross = cross + fold(weights * grads, jnp.sum)
            factor = jnp.exp2(old_top - new_top)
            run_ref[h, 0:1, cols] = new_top
            run_ref[h, 1:2, cols] = run_ref[h, 1:2, cols] * factor + jnp.sum(
                mass, axis=0, keepdims=True
            )
            run_ref[h, 2:3, cols] = run_ref[h, 2:3, cols] * factor + jnp.sum(
                cross, axis=0, keepdims=True
            )


def grad_block(kept, key, top, end_ref, q_t, do_t, low_ref, ds_ref, dq_acc):
    rows = do_t.shape[1]
    for h in range(2):
        factor = jnp.exp2(top(h) - end_ref[h, 0:1, :]) * end_ref[h, 1:2, :]
        delta = end_ref[h, 2:3, :]
        for c in range(0, rows, LANES):
            cols = slice(c, c + LANES)
            for r in range(0, rows, LANES):
                part = slice(r, r + LANES)
                weights, grads = kept(h, part, cols)
                probs = weights.astype(jnp.float32) * factor[:, cols]
                low_ref[h, part, cols] = probs.astype(jnp.bfloat16)
                ds_ref[h, part, cols] = (
                    probs * (grads.astype(jnp.float32) - delta[:, cols])
                ).astype(jnp.bfloat16)
    columns, rope = [], 0.0
    for h in range(2):
        dvalue = dot(do_t[head_cols(h, VDIM), :], low_ref[h], NT)
        dkey = dot(q_t[head_cols(h, QK), :], ds_ref[h], NT) * SCALE
        dq_acc[head_cols(h, QK), :] += dot(key(h).T, ds_ref[h])
        columns += [dkey[:NOPE].astype(jnp.bfloat16), dvalue.astype(jnp.bfloat16)]
        rope = rope + dkey[NOPE:]
    return jnp.concatenate(columns, axis=0), rope


def start_stats(run_ref):
    rows = run_ref.shape[2]
    for h in range(2):
        run_ref[h, 0:1, :] = jnp.full((1, rows), FLOOR, jnp.float32)
        run_ref[h, 1:8, :] = jnp.zeros((7, rows), jnp.float32)


def own_score_kernel(
    index_ref, docs_ref, q_ref, do_ref, w_ref, lat_t_ref,
    e_ref, g_ref, k_ref, run_ref, lat_ref, bias_ref, raw_ref, graw_ref,
):
    rows = q_ref.shape[0]

    @pl.when(pl.program_id(0) == 0)
    def _():
        lat_ref[...] = lat_t_ref[...].T
        first_row = pl.multiple_of(index_ref[0] * rows, rows)
        docs = docs_ref[:, pl.ds(first_row, rows)]
        key_docs = jnp.broadcast_to(docs, (128, rows)).T[:, :1]
        key = lax.broadcasted_iota(jnp.int32, (rows, rows), 0)
        query = lax.broadcasted_iota(jnp.int32, (rows, rows), 1)
        bias_ref[...] = jnp.where((key_docs == docs) & (key <= query), 0.0, MASKED)

    start_stats(run_ref)

    def k_out(h, key):
        k_ref[h] = key

    def keep(h, part, cols, weights, grads):
        e_ref[h, part, cols] = weights
        g_ref[h, part, cols] = grads

    score_block(
        lat_ref[...], q_ref, do_ref, w_ref, lambda part, cols: bias_ref[part, cols], run_ref,
        raw_ref, graw_ref, k_out, keep,
    )


def main_kernel(
    ranks,
    index_ref, docs_sref, docs_ref, q_ref, do_ref, w_ref, own_e, own_g, own_k, own_run,
    lat0, lat1, lat2, lat3,
    dq_ref, keep_ref, send_ref, x0_ref, x1_ref, x2_ref, x3_ref,
    lat_ref, lat_t_ref, bias_ref, e_ref, g_ref, k_ref, top_ref, run_ref, end_ref,
    raw_ref, graw_ref, low_ref, ds_ref, dq_acc, gw_acc, x_acc, sems,
):
    step = pl.program_id(0)
    rows = q_ref.shape[0]
    index = index_ref[0]
    own_core, own_x = lax.rem(index, 2), lax.rem(index // 2, 2)
    first_row = index * rows
    first_doc = docs_sref[first_row]

    def block_start(t):
        back = jnp.where(t == 1, 2, jnp.where(t == 0, 1 + 2 * own_core, 3 - 2 * own_core))
        return first_row - back * rows

    def active(t):
        start = block_start(t)
        return (start >= 0) & (docs_sref[jnp.maximum(start, 0) + rows - 1] >= first_doc)

    def block_rows(t):
        return pl.ds(pl.multiple_of(t * rows, rows), rows)

    def piece_rows(t, part):
        size = part.stop - part.start
        return pl.ds(pl.multiple_of(t * rows + part.start, size), size)

    def each_block(body):
        def visit(t, carry):
            @pl.when(active(t))
            def _():
                body(t)

            return carry

        lax.fori_loop(0, REACH, visit, 0)

    def fill_bias(t):
        my_docs = docs_ref[:, pl.ds(pl.multiple_of(first_row, rows), rows)]
        key_docs = docs_ref[:, pl.ds(pl.multiple_of(block_start(t), rows), rows)]
        key_docs = jnp.broadcast_to(key_docs, (128, rows)).T[:, :1]
        bias_ref[block_rows(t), :] = jnp.where(key_docs == my_docs, 0.0, MASKED)

    @pl.when(step == 0)
    def _():
        copies = [
            pltpu.make_async_copy(source, lat_t_ref.at[:, pl.ds(i * rows, rows)], sems.at[i])
            for i, source in enumerate((lat0, lat1, lat2, lat3))
        ]
        for copy in copies:
            copy.start()
        x_acc[...] = jnp.zeros_like(x_acc)
        each_block(fill_bias)
        for copy in copies:
            copy.wait()
        for i in range(REACH):
            part = slice(i * rows, (i + 1) * rows)
            lat_ref[part, :] = lat_t_ref[:, part].T

    gw_acc[...] = jnp.zeros_like(gw_acc)
    dq_acc[...] = jnp.zeros_like(dq_acc)
    run_ref[...] = own_run[...]

    def first_pass(t):
        def k_out(h, key):
            k_ref[h, block_rows(t), :] = key

        def keep(h, part, cols, weights, grads):
            e_ref[h, piece_rows(t, part), cols] = weights
            g_ref[h, piece_rows(t, part), cols] = grads

        score_block(
            lat_ref[block_rows(t), :], q_ref, do_ref, w_ref,
            lambda part, cols: bias_ref[piece_rows(t, part), cols], run_ref,
            raw_ref, graw_ref, k_out, keep,
        )
        for h in range(2):
            top_ref[h, t, 0:1, :] = run_ref[h, 0:1, :]

    each_block(first_pass)
    for h in range(2):
        inverse = 1.0 / run_ref[h, 1:2, :]
        end_ref[h, 0:1, :] = run_ref[h, 0:1, :]
        end_ref[h, 1:2, :] = inverse
        end_ref[h, 2:3, :] = run_ref[h, 2:3, :] * inverse
    q_t, do_t = q_ref[...].T, do_ref[...].T

    def add_block(part, kept, key, top):
        grads, rope = grad_block(kept, key, top, end_ref, q_t, do_t, low_ref, ds_ref, dq_acc)
        x_acc[:LATENT, part] += dot(w_ref[...], grads)
        x_acc[LATENT:, part] += rope
        gw_acc[...] += dot(lat_t_ref[:LATENT, part], grads, NT)

    def second_pass(t):
        def kept(h, part, cols):
            return e_ref[h, piece_rows(t, part), cols], g_ref[h, piece_rows(t, part), cols]

        add_block(
            block_rows(t), kept, lambda h: k_ref[h, block_rows(t), :],
            lambda h: top_ref[h, t, 0:1, :],
        )

    each_block(second_pass)
    add_block(
        slice(REACH * rows, (REACH + 1) * rows),
        lambda h, part, cols: (own_e[h, part, cols], own_g[h, part, cols]),
        lambda h: own_k[h],
        lambda h: own_run[h, 0:1, :],
    )
    dq_ref[...] = (dq_acc[...] * SCALE).T.astype(dq_ref.dtype)

    share, quarter = LATENT // ranks, LATENT // 4
    for i in range(ranks // 4):
        for out, core in ((keep_ref, own_core), (send_ref, 1 - own_core)):
            for where, x in ((0, own_x), (quarter, 1 - own_x)):
                source = pl.multiple_of((4 * i + 2 * x + core) * share, share)
                out[where + i * share : where + (i + 1) * share, :] = gw_acc[
                    pl.ds(source, share), :
                ].astype(out.dtype)

    @pl.when(step == pl.num_programs(0) - 1)
    def _():
        for i, out in enumerate((x0_ref, x1_ref, x2_ref, x3_ref)):
            out[...] = x_acc[:, i * rows : (i + 1) * rows].astype(out.dtype)


def pair_cols(height, size):
    return pl.BlockSpec((height, 2 * size), lambda i: (0, i))


def pair_heads(*shape):
    return pl.BlockSpec((2, *shape), lambda i: (i, 0, 0))


def fixed(*shape):
    return pl.BlockSpec(shape, lambda i: (0, 0))


SCALARS = pl.BlockSpec(memory_space=pltpu.SMEM)


def call(body, pairs, flops, in_specs, out_specs, out_shape, scratch, name):
    return pl.pallas_call(
        body,
        grid=(pairs,),
        in_specs=in_specs,
        out_specs=out_specs,
        out_shape=[jax.ShapeDtypeStruct(shape, kind) for shape, kind in out_shape],
        scratch_shapes=scratch,
        compiler_params=pltpu.CompilerParams(
            dimension_semantics=("arbitrary",), vmem_limit_bytes=56 * 1024 * 1024
        ),
        cost_estimate=pl.CostEstimate(
            flops=flops, bytes_accessed=16 * 1024 * 1024, transcendentals=0
        ),
        name=name,
    )


def own_scores(index, docs, queries, grad_out, weight, latent):
    rows = queries.shape[0]
    pairs = weight.shape[1] // (2 * KV)
    low, full = jnp.bfloat16, jnp.float32
    return call(
        own_score_kernel,
        pairs,
        2 * pairs * rows * rows * 2 * (QK + VDIM + KV),
        [
            SCALARS, fixed(1, docs.shape[1]), pair_cols(rows, QK), pair_cols(rows, VDIM),
            pair_cols(LATENT, KV), fixed(WIDTH, rows),
        ],
        [pair_heads(rows, rows), pair_heads(rows, rows), pair_heads(rows, QK), pair_heads(8, rows)],
        [
            ((2 * pairs, rows, rows), low),
            ((2 * pairs, rows, rows), low),
            ((2 * pairs, rows, QK), low),
            ((2 * pairs, 8, rows), full),
        ],
        [
            pltpu.VMEM((rows, WIDTH), low),
            pltpu.VMEM((rows, rows), full),
            pltpu.VMEM((2, rows, rows), full),
            pltpu.VMEM((2, rows, rows), full),
        ],
        "own_scores",
    )(index, docs, queries, grad_out, weight, latent)


def attention(index, doc_ids, docs, queries, grad_out, weight, kept, blocks, ranks):
    rows = queries.shape[0]
    pairs = weight.shape[1] // (2 * KV)
    window = REACH * rows
    low, full = jnp.bfloat16, jnp.float32
    half = pair_cols(LATENT // 2, KV)
    return call(
        functools.partial(main_kernel, ranks),
        pairs,
        2 * pairs * rows * window * 2 * (3 * QK + 2 * VDIM + 3 * KV),
        [
            SCALARS, SCALARS, fixed(1, docs.shape[1]), pair_cols(rows, QK), pair_cols(rows, VDIM),
            pair_cols(LATENT, KV), pair_heads(rows, rows), pair_heads(rows, rows),
            pair_heads(rows, QK), pair_heads(8, rows),
        ]
        + [pl.BlockSpec(memory_space=pl.ANY)] * (REACH + 1),
        [pair_cols(rows, QK), half, half] + [fixed(WIDTH, rows)] * (REACH + 1),
        [
            (queries.shape, low),
            ((LATENT // 2, pairs * 2 * KV), low),
            ((LATENT // 2, pairs * 2 * KV), low),
        ]
        + [((WIDTH, rows), low)] * (REACH + 1),
        [
            pltpu.VMEM((window, WIDTH), low),
            pltpu.VMEM((WIDTH, window + rows), low),
            pltpu.VMEM((window, rows), full),
            pltpu.VMEM((2, window, rows), low),
            pltpu.VMEM((2, window, rows), low),
            pltpu.VMEM((2, window, QK), low),
            pltpu.VMEM((2, REACH, 8, rows), full),
            pltpu.VMEM((2, 8, rows), full),
            pltpu.VMEM((2, 8, rows), full),
            pltpu.VMEM((2, rows, rows), full),
            pltpu.VMEM((2, rows, rows), full),
            pltpu.VMEM((2, rows, rows), low),
            pltpu.VMEM((2, rows, rows), low),
            pltpu.VMEM((2 * QK, rows), full),
            pltpu.VMEM((LATENT, 2 * KV), full),
            pltpu.VMEM((WIDTH, window + rows), full),
            pltpu.SemaphoreType.DMA((REACH + 1,)),
        ],
        "attention",
    )(index, doc_ids, docs, queries, grad_out, weight, *kept, *blocks)


def permute(value, axis, target):
    count = lax.axis_size(axis)
    pairs = [(s, target(s)) for s in range(count) if 0 <= target(s) < count]
    return lax.ppermute(value, axis, pairs)


def local(kv_latent, queries, grad_out, kv_up_weight, doc_ids):
    ranks = lax.axis_size("ctx")
    index = lax.axis_index("ctx").astype(jnp.int32)[None]
    low, full = jnp.bfloat16, jnp.float32
    docs = doc_ids[None]

    latent = kv_latent.T
    far = permute(latent, "ctx", lambda s: s + 2)
    mixed = permute(latent, "ctx", lambda s: s + 3 if s % 2 else s + 1)
    *kept, run = own_scores(index, docs, queries, grad_out, kv_up_weight, latent)
    far, run = lax.optimization_barrier((far, run))
    swapped = permute(far, "ctx", lambda s: s ^ 1)

    grad_queries, keep, send, to_swap, to_far, to_mixed, mine = attention(
        index, doc_ids, docs, queries, grad_out, kv_up_weight, (*kept, run),
        (swapped, far, mixed, latent), ranks,
    )

    chip = keep.astype(full) + permute(send, "ctx", lambda s: s ^ 1).astype(full)
    quarter = LATENT // 4
    to_x = chip[quarter:].astype(low)
    from_swap = permute(to_swap, "ctx", lambda s: s ^ 1)
    to_x, from_swap = lax.optimization_barrier((to_x, from_swap))
    from_x = permute(to_x, "ctx", lambda s: s ^ 2)
    plane = (chip[:quarter] + from_x.astype(full)).astype(low)
    columns = [list(range(first, ranks, 4)) for first in range(4)]
    pieces = lax.all_to_all(plane, "ctx", 0, 0, axis_index_groups=columns, tiled=True)
    grad_weight = jnp.sum(pieces.reshape(ranks // 4, LATENT // ranks, -1).astype(full), axis=0)

    far_sum = (to_far.astype(full) + from_swap.astype(full)).astype(low)
    from_far = permute(far_sum, "ctx", lambda s: s - 2)
    from_mixed = permute(to_mixed, "ctx", lambda s: s - 1 if s % 2 else s - 3)
    total = mine.astype(full) + from_mixed.astype(full) + from_far.astype(full)
    mine = total.astype(low)
    size = lax.axis_size("head")
    for turn in range(1, size):
        other = lax.ppermute(mine, "head", [(s, (s + turn) % size) for s in range(size)])
        total = total + other.astype(full)
    return grad_queries, total.astype(low).T, grad_weight


def solution(mesh):
    return jax.shard_map(
        local,
        mesh=mesh,
        in_specs=(P("ctx", None), P("ctx", "head"), P("ctx", "head"), P(None, "head"), P()),
        out_specs=(P("ctx", "head"), P("ctx", None), P("ctx", "head")),
        check_vma=False,
    )
```

```python
import functools
import math

import jax
import jax.numpy as jnp
from jax import lax
from jax.experimental import pallas as pl
from jax.experimental.pallas import tpu as pltpu
from jax.sharding import PartitionSpec as P

NOPE = 128
ROPE = 64
VDIM = 128
LATENT = 512
REACH = 3
QK = NOPE + ROPE
KV = NOPE + VDIM
WIDTH = LATENT + ROPE
LANES = 128

MASKED = -1e30
FLOOR = -1e20
SCALE = 1.0 / math.sqrt(QK)
SCALE2 = SCALE * math.log2(math.e)

NT = (((1,), (1,)), ((), ()))
NN = (((1,), (0,)), ((), ()))


def dot(a, b, dims=NN):
    return lax.dot_general(a, b, dims, preferred_element_type=jnp.float32)


def head_cols(h, size):
    return slice(h * size, (h + 1) * size)


def fold(value, combine):
    return combine(value.reshape(-1, 8, value.shape[1]), axis=0)


def fold(value, combine):
    return combine(value.reshape(-1, 8, value.shape[1]), axis=0)


def lift(latent, w_ref, k_out, v_out):
    for h in range(w_ref.shape[1] // KV):
        lifted = dot(latent[:, :LATENT], w_ref[:, head_cols(h, KV)]).astype(jnp.bfloat16)
        k_out(h, jnp.concatenate([lifted[:, :NOPE], latent[:, LATENT:]], axis=1))
        v_out(h, lifted[:, NOPE:])


def score_block(key, value, q_ref, do_ref, bounds, run_ref, raw_ref, graw_ref, keep):
    rows = do_ref.shape[0]
    heads = range(do_ref.shape[1] // VDIM)
    lower, upper = bounds
    for h in heads:
        raw_ref[h] = dot(key(h), q_ref[:, head_cols(h, QK)], NT)
        graw_ref[h] = dot(value(h), do_ref[:, head_cols(h, VDIM)], NT)
    index = lax.broadcasted_iota(jnp.int32, (LANES, LANES), 0)
    pieces = [slice(r, r + LANES) for r in range(0, rows, LANES)]
    for h in heads:
        for c in range(0, rows, LANES):
            cols = slice(c, c + LANES)

            def scores(part):
                place = index + part.start
                seen = (place >= lower[:, cols]) & (place <= upper[:, cols])
                return jnp.where(seen, raw_ref[h, part, cols] * SCALE2, MASKED)

            high = None
            for part in pieces:
                piece = fold(scores(part), jnp.max)
                high = piece if high is None else jnp.maximum(high, piece)
            old_top = run_ref[h, 0:1, cols]
            new_top = jnp.maximum(old_top, jnp.max(high, axis=0, keepdims=True))
            mass, cross = 0.0, 0.0
            for part in pieces:
                weights = jnp.exp2(scores(part) - new_top)
                grads = graw_ref[h, part, cols]
                keep(h, part, cols, weights.astype(jnp.bfloat16), grads.astype(jnp.bfloat16))
                mass = mass + fold(weights, jnp.sum)
                cross = cross + fold(weights * grads, jnp.sum)
            factor = jnp.exp2(old_top - new_top)
            run_ref[h, 0:1, cols] = new_top
            run_ref[h, 1:2, cols] = run_ref[h, 1:2, cols] * factor + jnp.sum(
                mass, axis=0, keepdims=True
            )
            run_ref[h, 2:3, cols] = run_ref[h, 2:3, cols] * factor + jnp.sum(
                cross, axis=0, keepdims=True
            )


def grad_block(kept, key, top, end_ref, q_t, do_t, low_ref, ds_ref, dq_acc, d_acc, r_add):
    rows = do_t.shape[1]
    heads = range(do_t.shape[0] // VDIM)
    for h in heads:
        factor = jnp.exp2(top(h) - end_ref[h, 0:1, :]) * end_ref[h, 1:2, :]
        delta = end_ref[h, 2:3, :]
        for c in range(0, rows, LANES):
            cols = slice(c, c + LANES)
            for r in range(0, rows, LANES):
                part = slice(r, r + LANES)
                weights, grads = kept(h, part, cols)
                probs = weights.astype(jnp.float32) * factor[:, cols]
                low_ref[h, part, cols] = probs.astype(jnp.bfloat16)
                ds_ref[h, part, cols] = (
                    probs * (grads.astype(jnp.float32) - delta[:, cols])
                ).astype(jnp.bfloat16)
    rope = 0.0
    for h in heads:
        dvalue = dot(do_t[head_cols(h, VDIM), :], low_ref[h], NT)
        dkey = dot(q_t[head_cols(h, QK), :], ds_ref[h], NT) * SCALE
        dq_acc[head_cols(h, QK), :] += dot(key(h).T, ds_ref[h])
        d_acc[h * KV : h * KV + NOPE, :] += dkey[:NOPE]
        d_acc[h * KV + NOPE : (h + 1) * KV, :] += dvalue
        rope = rope + dkey[NOPE:]
    r_add(rope)


def start_stats(run_ref):
    count, rows = run_ref.shape[0], run_ref.shape[2]
    for h in range(count):
        run_ref[h, 0:1, :] = jnp.full((1, rows), FLOOR, jnp.float32)
        run_ref[h, 1:8, :] = jnp.zeros((7, rows), jnp.float32)


def chip_place(index_ref):
    core = lax.rem(index_ref[0], 2)
    return core, index_ref[0] - core


def order_pair(out_ref, core, own, other):
    out_ref[core] = own[...]
    out_ref[1 - core] = other[...]


LOCAL = ((1, REACH), (0, REACH), (1, REACH + 1))


def query_bounds(start_ref, chip, j, t, rows):
    lower = start_ref[j, 0:1, :] - (chip + t - REACH) * rows
    upper = lax.broadcasted_iota(jnp.int32, (1, rows), 1) + (j + REACH - t) * rows
    return lower, upper


def find_starts(docs_ref, start_ref, chip, rows):
    for j in range(2):
        my_docs = docs_ref[:, pl.ds(pl.multiple_of((chip + j) * rows, rows), rows)]
        start_ref[j, 0:1, :] = jnp.maximum(chip - REACH, 0) * rows + jnp.zeros((1, rows), jnp.int32)

        def count(t, carry):
            block = chip + t - REACH

            @pl.when(block >= 0)
            def _():
                key_docs = docs_ref[:, pl.ds(pl.multiple_of(block * rows, rows), rows)]
                key_docs = jnp.broadcast_to(key_docs, (128, rows)).T[:, :1]
                before = jnp.where(key_docs < my_docs, 1.0, 0.0)
                start_ref[j, 0:1, :] += jnp.sum(before, axis=0, keepdims=True).astype(jnp.int32)

            return carry

        lax.fori_loop(0, REACH + 2, count, 0)


def local_kernel(
    index_ref, docs_ref, q0, do0, q1, do1, w_ref, lat0, lat1,
    e_ref, g_ref, k_ref, run_ref, top_ref,
    q_ref, do_ref, lat_ref, v_ref, start_ref, raw_ref, graw_ref,
):
    rows = q0.shape[0]
    core, chip = chip_place(index_ref)
    heads = w_ref.shape[1] // KV

    @pl.when(pl.program_id(0) == 0)
    def _():
        lat_ref[core] = lat0[...].T
        lat_ref[1 - core] = lat1[...].T
        find_starts(docs_ref, start_ref, chip, rows)

    order_pair(q_ref, core, q0, q1)
    order_pair(do_ref, core, do0, do1)
    for j in range(2):

        def k_out(h, key):
            k_ref[0, j * heads + h] = key

        def v_out(h, value):
            v_ref[j * heads + h] = value

        lift(lat_ref[j], w_ref, k_out, v_out)
        start_stats(run_ref.at[0, pl.ds(j * heads, heads)])
    for n, (j, t) in enumerate(LOCAL):
        slot = t - REACH

        def keep(h, part, cols, weights, grads):
            e_ref[0, n * heads + h, part, cols] = weights
            g_ref[0, n * heads + h, part, cols] = grads

        run = run_ref.at[0, pl.ds(j * heads, heads)]
        score_block(
            lambda h: k_ref[0, slot * heads + h], lambda h: v_ref[slot * heads + h],
            q_ref.at[j], do_ref.at[j], query_bounds(start_ref, chip, j, t, rows), run,
            raw_ref, graw_ref, keep,
        )
        for h in range(heads):
            top_ref[0, n * heads + h] = run[h]


def main_kernel(
    ranks,
    index_ref, docs_sref, docs_ref, q0, do0, q1, do1, w_ref,
    all_e, all_g, local_k, local_run, local_top,
    lat_far, lat_swap, lat_mixed, lat_passed, lat_own, lat_other,
    dq0_ref, dq1_ref, keep_ref, send_ref, x_old, x_far, x_swap, x_own, x_other,
    q_ref, do_ref, lat_ref, lat_t_ref, start_ref, e_ref, g_ref, k_ref, v_ref, top_ref,
    run_ref, end_ref, raw_ref, graw_ref, low_ref, ds_ref, dq_acc, d_acc, gw_acc, x_acc,
    local_e, local_g, sems, kept_sems,
):
    step = pl.program_id(0)
    rows = q0.shape[0]
    heads = w_ref.shape[1] // KV
    blocks = REACH + 2
    kept_copies = [
        pltpu.make_async_copy(all_e.at[step], local_e, kept_sems.at[0]),
        pltpu.make_async_copy(all_g.at[step], local_g, kept_sems.at[1]),
    ]
    for copy in kept_copies:
        copy.start()
    core, chip = chip_place(index_ref)

    def active(j, t):
        block = chip + t - REACH
        last_doc = docs_sref[jnp.maximum(block, 0) * rows + rows - 1]
        return (block >= 0) & (last_doc >= docs_sref[(chip + j) * rows])

    def block_rows(t):
        return pl.ds(pl.multiple_of(t * rows, rows), rows)

    def piece_rows(t, part):
        size = part.stop - part.start
        return pl.ds(pl.multiple_of(t * rows + part.start, size), size)

    def loop(first, last, when, body):
        def visit(t, carry):
            @pl.when(when(t))
            def _():
                body(t)

            return carry

        lax.fori_loop(first, last, visit, 0)

    @pl.when(step == 0)
    def _():
        places = [(lat_far, 1 + core), (lat_swap, 2 - core), (lat_own, REACH + core),
                  (lat_other, REACH + 1 - core)]
        copies = [
            pltpu.make_async_copy(source, lat_t_ref.at[:, block_rows(t)], sems.at[i])
            for i, (source, t) in enumerate(places)
        ]
        first = lat_t_ref.at[:, block_rows(0)]
        oldest = pltpu.make_async_copy(lat_mixed, first, sems.at[4])
        passed = pltpu.make_async_copy(lat_passed, first, sems.at[4])
        for copy in copies:
            copy.start()
        pl.when(core == 0)(oldest.start)
        pl.when(core == 1)(passed.start)
        x_acc[...] = jnp.zeros_like(x_acc)
        find_starts(docs_ref, start_ref, chip, rows)
        for copy in copies:
            copy.wait()
        oldest.wait()
        for t in range(REACH):
            part = slice(t * rows, (t + 1) * rows)
            lat_ref[part, :] = lat_t_ref[:, part].T

    order_pair(q_ref, core, q0, q1)
    order_pair(do_ref, core, do0, do1)
    gw_acc[...] = jnp.zeros_like(gw_acc)
    dq_acc[...] = jnp.zeros_like(dq_acc)
    d_acc[...] = jnp.zeros_like(d_acc)

    def lift_block(t):
        def k_out(h, key):
            k_ref[h, block_rows(t), :] = key

        def v_out(h, value):
            v_ref[h, block_rows(t), :] = value

        lift(lat_ref[block_rows(t), :], w_ref, k_out, v_out)

    loop(0, REACH, lambda t: active(0, t) | active(1, t), lift_block)

    for j in range(2):
        for h in range(heads):
            run_ref[h] = local_run[0, j * heads + h]

        def first_pass(t):
            def keep(h, part, cols, weights, grads):
                e_ref[h, piece_rows(t, part), cols] = weights
                g_ref[h, piece_rows(t, part), cols] = grads

            score_block(
                lambda h: k_ref[h, block_rows(t), :], lambda h: v_ref[h, block_rows(t), :],
                q_ref.at[j], do_ref.at[j], query_bounds(start_ref, chip, j, t, rows), run_ref,
                raw_ref, graw_ref, keep,
            )
            for h in range(heads):
                top_ref[h, t] = run_ref[h]

        loop(j, REACH, lambda t: active(j, t), first_pass)
        for h in range(heads):
            inverse = 1.0 / run_ref[h, 1:2, :]
            end_ref[h, 0:1, :] = run_ref[h, 0:1, :]
            end_ref[h, 1:2, :] = inverse
            end_ref[h, 2:3, :] = run_ref[h, 2:3, :] * inverse
        q_t, do_t = q_ref[j].T, do_ref[j].T

        def add(t, part, kept, key, top):
            def r_add(rope):
                x_acc[LATENT:, part] += rope

            grad_block(
                kept, key, top, end_ref, q_t, do_t, low_ref, ds_ref, dq_acc.at[j], d_acc.at[t],
                r_add,
            )

        def second_pass(t):
            def kept(h, part, cols):
                return e_ref[h, piece_rows(t, part), cols], g_ref[h, piece_rows(t, part), cols]

            add(
                t, block_rows(t), kept, lambda h: k_ref[h, block_rows(t), :],
                lambda h: top_ref[h, t, 0:1, :],
            )

        loop(j, REACH, lambda t: active(j, t), second_pass)
        if j == 0:
            for copy in kept_copies:
                copy.wait()
        for n, (query, t) in enumerate(LOCAL):
            if query == j:
                add(
                    t, slice(t * rows, (t + 1) * rows),
                    lambda h, part, cols: (
                        local_e[n * heads + h, part, cols], local_g[n * heads + h, part, cols]
                    ),
                    lambda h: local_k[0, (t - REACH) * heads + h],
                    lambda h: local_top[0, n * heads + h, 0:1, :],
                )

    def project(t):
        part = block_rows(t)
        grads = d_acc[t].astype(jnp.bfloat16)
        x_acc[:LATENT, part] += dot(w_ref[...], grads)
        gw_acc[...] += dot(lat_t_ref[:LATENT, part], grads, NT)

    loop(0, blocks, lambda t: (t >= REACH) | active(0, t) | active(1, t), project)
    dq0_ref[...] = (dq_acc[core] * SCALE).T.astype(dq0_ref.dtype)
    dq1_ref[...] = (dq_acc[1 - core] * SCALE).T.astype(dq1_ref.dtype)

    share = 2 * (LATENT // ranks)
    own_x = lax.rem(index_ref[0] // 2, 2)
    for i in range(ranks // 4):
        for out, x in ((keep_ref, own_x), (send_ref, 1 - own_x)):
            source = pl.multiple_of((2 * i + x) * share, share)
            out[i * share : (i + 1) * share, :] = gw_acc[pl.ds(source, share), :].astype(out.dtype)

    @pl.when(step == pl.num_programs(0) - 1)
    def _():
        places = ((x_old, 0), (x_far, 1 + core), (x_swap, 2 - core), (x_own, REACH + core),
                  (x_other, REACH + 1 - core))
        copies = []
        for i, (out, t) in enumerate(places):
            part = block_rows(t)
            lat_t_ref[:, part] = x_acc[:, part].astype(lat_t_ref.dtype)
            copies.append(pltpu.make_async_copy(lat_t_ref.at[:, part], out, sems.at[i]))
            copies[-1].start()
        for copy in copies:
            copy.wait()


def step_cols(height, size):
    return pl.BlockSpec((height, size), lambda i: (0, i))


def step_block(*shape):
    return pl.BlockSpec((1, *shape), lambda i: (i, 0, 0, 0))


def fixed(*shape):
    return pl.BlockSpec(shape, lambda i: (0, 0))


SCALARS = pl.BlockSpec(memory_space=pltpu.SMEM)
ANYWHERE = pl.BlockSpec(memory_space=pl.ANY)


def call(body, steps, flops, in_specs, outs, scratch, name):
    return pl.pallas_call(
        body,
        grid=(steps,),
        in_specs=in_specs,
        out_specs=[spec for spec, _, _ in outs],
        out_shape=[jax.ShapeDtypeStruct(shape, kind) for _, shape, kind in outs],
        scratch_shapes=[pltpu.VMEM(*entry) if isinstance(entry, tuple) else entry for entry in scratch],
        compiler_params=pltpu.CompilerParams(
            dimension_semantics=("arbitrary",), vmem_limit_bytes=58 * 1024 * 1024
        ),
        cost_estimate=pl.CostEstimate(
            flops=flops, bytes_accessed=16 * 1024 * 1024, transcendentals=0
        ),
        name=name,
    )


def local_scores(index, docs, pairs, weight, latents, heads, steps):
    rows = pairs[0].shape[0]
    low, full = jnp.bfloat16, jnp.float32
    count = len(LOCAL) * heads
    return call(
        local_kernel,
        steps,
        2 * steps * heads * rows * rows * (3 * (QK + VDIM) + 2 * KV),
        [
            SCALARS, fixed(1, docs.shape[1]),
            *[step_cols(rows, heads * QK), step_cols(rows, heads * VDIM)] * 2,
            step_cols(LATENT, heads * KV), fixed(WIDTH, rows), fixed(WIDTH, rows),
        ],
        [
            (step_block(count, rows, rows), (steps, count, rows, rows), low),
            (step_block(count, rows, rows), (steps, count, rows, rows), low),
            (step_block(2 * heads, rows, QK), (steps, 2 * heads, rows, QK), low),
            (step_block(2 * heads, 8, rows), (steps, 2 * heads, 8, rows), full),
            (step_block(count, 8, rows), (steps, count, 8, rows), full),
        ],
        [
            ((2, rows, heads * QK), low),
            ((2, rows, heads * VDIM), low),
            ((2, rows, WIDTH), low),
            ((2 * heads, rows, VDIM), low),
            ((2, 8, rows), jnp.int32),
            ((heads, rows, rows), full),
            ((heads, rows, rows), full),
        ],
        "local_scores",
    )(index, docs, *pairs, weight, *latents)


def attention(index, doc_ids, docs, pairs, weight, kept, latents, heads, steps, ranks):
    rows = pairs[0].shape[0]
    low, full = jnp.bfloat16, jnp.float32
    count = len(LOCAL) * heads
    window = (REACH + 2) * rows
    far = REACH * rows
    half = (LATENT // 2, steps * heads * KV)
    return call(
        functools.partial(main_kernel, ranks),
        steps,
        2 * steps * heads * rows * rows * (5 * (QK + VDIM) + 8 * (2 * QK + VDIM) + 13 * KV),
        [
            SCALARS, SCALARS, fixed(1, docs.shape[1]),
            *[step_cols(rows, heads * QK), step_cols(rows, heads * VDIM)] * 2,
            step_cols(LATENT, heads * KV),
            ANYWHERE, ANYWHERE, step_block(2 * heads, rows, QK), step_block(2 * heads, 8, rows),
            step_block(count, 8, rows),
        ]
        + [ANYWHERE] * len(latents),
        [(step_cols(rows, heads * QK), (rows, steps * heads * QK), low)] * 2
        + [(step_cols(LATENT // 2, heads * KV), half, low)] * 2
        + [(ANYWHERE, (WIDTH, rows), low)] * (REACH + 2),
        [
            ((2, rows, heads * QK), low),
            ((2, rows, heads * VDIM), low),
            ((far, WIDTH), low),
            ((WIDTH, window), low),
            ((2, 8, rows), jnp.int32),
            ((heads, far, rows), low),
            ((heads, far, rows), low),
            ((heads, far, QK), low),
            ((heads, far, VDIM), low),
            ((heads, REACH, 8, rows), full),
            ((heads, 8, rows), full),
            ((heads, 8, rows), full),
            ((heads, rows, rows), full),
            ((heads, rows, rows), full),
            ((heads, rows, rows), low),
            ((heads, rows, rows), low),
            ((2, heads * QK, rows), full),
            ((REACH + 2, heads * KV, rows), full),
            ((LATENT, heads * KV), full),
            ((WIDTH, window), full),
            ((count, rows, rows), low),
            ((count, rows, rows), low),
            pltpu.SemaphoreType.DMA((5,)),
            pltpu.SemaphoreType.DMA((2,)),
        ],
        "attention",
    )(index, doc_ids, docs, *pairs, weight, *kept, *latents)


def permute(value, axis, target):
    count = lax.axis_size(axis)
    pairs = [(s, target(s)) for s in range(count) if 0 <= target(s) < count]
    return lax.ppermute(value, axis, pairs)


def local(kv_latent, queries, grad_out, kv_up_weight, doc_ids):
    ranks = lax.axis_size("ctx")
    position = lax.axis_index("ctx").astype(jnp.int32)
    index, core = position[None], lax.rem(position, 2)
    low, full = jnp.bfloat16, jnp.float32
    docs = doc_ids[None]
    core_heads = kv_up_weight.shape[1] // KV // 2
    heads = min(2, core_heads)
    steps = core_heads // heads

    def own_heads(value, which):
        size = value.shape[1] // 2
        return lax.dynamic_slice_in_dim(value, which * size, size, axis=1)

    def across(value):
        return permute(value, "ctx", lambda s: s ^ 1)

    latent = kv_latent.T
    far = permute(latent, "ctx", lambda s: s + 2)
    mixed = permute(latent, "ctx", lambda s: s + 3 if s % 2 else -1)
    other = across(latent)
    pairs = (
        own_heads(queries, core),
        own_heads(grad_out, core),
        across(own_heads(queries, 1 - core)),
        across(own_heads(grad_out, 1 - core)),
    )
    weight = own_heads(kv_up_weight, core)
    *kept, top = local_scores(index, docs, pairs, weight, (latent, other), heads, steps)
    far, mixed, top = lax.optimization_barrier((far, mixed, top))
    swapped = across(far)
    passed = permute(mixed, "ctx", lambda s: -1 if s % 2 else s + 1)

    dq_own, dq_other, keep, send, to_old, to_far, to_swap, mine, to_other = attention(
        index, doc_ids, docs, pairs, weight, (*kept, top),
        (far, swapped, mixed, passed, latent, other), heads, steps, ranks,
    )

    from_x = permute(send, "ctx", lambda s: s ^ 2)
    from_swap = across(to_swap)
    from_other = across(to_other)
    from_old = permute(to_old, "ctx", lambda s: s - 1 if s % 2 else -1)
    far_sum = (to_far.astype(full) + from_swap.astype(full)).astype(low)
    old_sum = (to_old.astype(full) + from_old.astype(full)).astype(low)
    from_x, far_sum, old_sum = lax.optimization_barrier((from_x, far_sum, old_sum))
    from_far = permute(far_sum, "ctx", lambda s: s - 2)
    from_mixed = permute(old_sum, "ctx", lambda s: -1 if s % 2 else s - 3)
    plane = (keep.astype(full) + from_x.astype(full)).astype(low)
    columns = [list(range(first, ranks, 4)) for first in range(4)]
    pieces = lax.all_to_all(plane, "ctx", 0, 0, axis_index_groups=columns, tiled=True)
    share = LATENT // ranks
    summed = jnp.sum(pieces.reshape(ranks // 4, 2 * share, -1).astype(full), axis=0)

    def in_order(own, received):
        first = jnp.where(core == 0, own, received)
        second = jnp.where(core == 0, received, own)
        return jnp.concatenate([first, second], axis=1)

    rows_own = lax.dynamic_slice_in_dim(summed, core * share, share, axis=0)
    rows_other = lax.dynamic_slice_in_dim(summed, (1 - core) * share, share, axis=0)
    grad_weight = in_order(rows_own, across(rows_other))
    grad_queries = in_order(dq_own, across(dq_other))

    total = mine.astype(full) + from_other.astype(full)
    total = total + from_mixed.astype(full) + from_far.astype(full)
    mine = total.astype(low)
    size = lax.axis_size("head")
    for turn in range(1, size):
        other = lax.ppermute(mine, "head", [(s, (s + turn) % size) for s in range(size)])
        total = total + other.astype(full)
    return grad_queries, total.astype(low).T, grad_weight


def solution(mesh):
    return jax.shard_map(
        local,
        mesh=mesh,
        in_specs=(P("ctx", None), P("ctx", "head"), P("ctx", "head"), P(None, "head"), P()),
        out_specs=(P("ctx", "head"), P("ctx", None), P("ctx", "head")),
        check_vma=False,
    )
```

```python
import functools
import math

import jax
import jax.numpy as jnp
from jax import lax
from jax.experimental import pallas as pl
from jax.experimental.pallas import tpu as pltpu
from jax.sharding import PartitionSpec as P

NOPE = 128
ROPE = 64
VDIM = 128
LATENT = 512
REACH = 3
QK = NOPE + ROPE
KV = NOPE + VDIM
WIDTH = LATENT + ROPE
LANES = 128

MASKED = -1e30
FLOOR = -1e20
SCALE = 1.0 / math.sqrt(QK)
SCALE2 = SCALE * math.log2(math.e)

NT = (((1,), (1,)), ((), ()))
NN = (((1,), (0,)), ((), ()))


def dot(a, b, dims=NN):
    return lax.dot_general(a, b, dims, preferred_element_type=jnp.float32)


def head_cols(h, size):
    return slice(h * size, (h + 1) * size)


def fold(value, combine):
    return combine(value.reshape(-1, 8, value.shape[1]), axis=0)


def fold(value, combine):
    return combine(value.reshape(-1, 8, value.shape[1]), axis=0)


def lift(latent, w_ref, k_out, v_out):
    for h in range(w_ref.shape[1] // KV):
        lifted = dot(latent[:, :LATENT], w_ref[:, head_cols(h, KV)]).astype(jnp.bfloat16)
        k_out(h, jnp.concatenate([lifted[:, :NOPE], latent[:, LATENT:]], axis=1))
        v_out(h, lifted[:, NOPE:])


def score_block(key, value, q_ref, do_ref, bounds, run_ref, raw_ref, graw_ref, keep):
    rows = do_ref.shape[0]
    heads = range(do_ref.shape[1] // VDIM)
    lower, upper = bounds
    for h in heads:
        raw_ref[h] = dot(key(h), q_ref[:, head_cols(h, QK)], NT)
        graw_ref[h] = dot(value(h), do_ref[:, head_cols(h, VDIM)], NT)
    index = lax.broadcasted_iota(jnp.int32, (LANES, LANES), 0)
    pieces = [slice(r, r + LANES) for r in range(0, rows, LANES)]
    for h in heads:
        for c in range(0, rows, LANES):
            cols = slice(c, c + LANES)

            def scores(part):
                place = index + part.start
                seen = (place >= lower[:, cols]) & (place <= upper[:, cols])
                return jnp.where(seen, raw_ref[h, part, cols] * SCALE2, MASKED)

            high = None
            for part in pieces:
                piece = fold(scores(part), jnp.max)
                high = piece if high is None else jnp.maximum(high, piece)
            old_top = run_ref[h, 0:1, cols]
            new_top = jnp.maximum(old_top, jnp.max(high, axis=0, keepdims=True))
            mass, cross = 0.0, 0.0
            for part in pieces:
                weights = jnp.exp2(scores(part) - new_top)
                grads = graw_ref[h, part, cols]
                keep(h, part, cols, weights.astype(jnp.bfloat16), grads.astype(jnp.bfloat16))
                mass = mass + fold(weights, jnp.sum)
                cross = cross + fold(weights * grads, jnp.sum)
            factor = jnp.exp2(old_top - new_top)
            run_ref[h, 0:1, cols] = new_top
            run_ref[h, 1:2, cols] = run_ref[h, 1:2, cols] * factor + jnp.sum(
                mass, axis=0, keepdims=True
            )
            run_ref[h, 2:3, cols] = run_ref[h, 2:3, cols] * factor + jnp.sum(
                cross, axis=0, keepdims=True
            )


def grad_block(kept, key, top, end_ref, q_t, do_t, low_ref, ds_ref, dq_acc, d_acc, r_add):
    rows = do_t.shape[1]
    heads = range(do_t.shape[0] // VDIM)
    for h in heads:
        factor = jnp.exp2(top(h) - end_ref[h, 0:1, :]) * end_ref[h, 1:2, :]
        delta = end_ref[h, 2:3, :]
        for c in range(0, rows, LANES):
            cols = slice(c, c + LANES)
            for r in range(0, rows, LANES):
                part = slice(r, r + LANES)
                weights, grads = kept(h, part, cols)
                probs = weights.astype(jnp.float32) * factor[:, cols]
                low_ref[h, part, cols] = probs.astype(jnp.bfloat16)
                ds_ref[h, part, cols] = (
                    probs * (grads.astype(jnp.float32) - delta[:, cols])
                ).astype(jnp.bfloat16)
    rope = 0.0
    for h in heads:
        dvalue = dot(do_t[head_cols(h, VDIM), :], low_ref[h], NT)
        dkey = dot(q_t[head_cols(h, QK), :], ds_ref[h], NT) * SCALE
        dq_acc[head_cols(h, QK), :] += dot(key(h).T, ds_ref[h])
        d_acc[h * KV : h * KV + NOPE, :] += dkey[:NOPE]
        d_acc[h * KV + NOPE : (h + 1) * KV, :] += dvalue
        rope = rope + dkey[NOPE:]
    r_add(rope)


def start_stats(run_ref):
    count, rows = run_ref.shape[0], run_ref.shape[2]
    for h in range(count):
        run_ref[h, 0:1, :] = jnp.full((1, rows), FLOOR, jnp.float32)
        run_ref[h, 1:8, :] = jnp.zeros((7, rows), jnp.float32)


def chip_place(index_ref):
    core = lax.rem(index_ref[0], 2)
    return core, index_ref[0] - core


def order_pair(out_ref, core, own, other):
    out_ref[core] = own[...]
    out_ref[1 - core] = other[...]


LOCAL = ((1, REACH), (0, REACH), (1, REACH + 1))


def query_bounds(start_ref, chip, j, t, rows):
    lower = start_ref[j, 0:1, :] - (chip + t - REACH) * rows
    upper = lax.broadcasted_iota(jnp.int32, (1, rows), 1) + (j + REACH - t) * rows
    return lower, upper


def find_starts(docs_ref, start_ref, chip, rows):
    for j in range(2):
        block = chip + j
        my_docs = docs_ref[:, pl.ds(pl.multiple_of(block * rows, rows), rows)]
        first_doc = my_docs[:, :1]
        key_docs = jnp.broadcast_to(my_docs, (128, rows)).T[:, :1]
        inside = jnp.sum(jnp.where(key_docs < my_docs, 1.0, 0.0), axis=0, keepdims=True)
        before = jnp.zeros((1, rows), jnp.float32)
        for back in range(1, REACH + 1):
            earlier = jnp.maximum(block - back, 0)
            docs = docs_ref[:, pl.ds(pl.multiple_of(earlier * rows, rows), rows)]
            same = (docs == first_doc) & (block >= back)
            before = before + jnp.where(same, 1.0, 0.0)
        before = jnp.sum(before, axis=1, keepdims=True)
        start = jnp.where(my_docs == first_doc, -before, inside).astype(jnp.int32)
        start_ref[j, 0:1, :] = start + block * rows


def local_kernel(
    index_ref, docs_ref, q0, do0, q1, do1, w_ref, lat0, lat1,
    e_ref, g_ref, k_ref, run_ref, top_ref, start_ref,
    q_ref, do_ref, lat_ref, v_ref, raw_ref, graw_ref,
):
    rows = q0.shape[0]
    core, chip = chip_place(index_ref)
    heads = w_ref.shape[1] // KV

    @pl.when(pl.program_id(0) == 0)
    def _():
        lat_ref[core] = lat0[...].T
        lat_ref[1 - core] = lat1[...].T
        find_starts(docs_ref, start_ref, chip, rows)

    order_pair(q_ref, core, q0, q1)
    order_pair(do_ref, core, do0, do1)
    for j in range(2):

        def k_out(h, key):
            k_ref[0, j * heads + h] = key

        def v_out(h, value):
            v_ref[j * heads + h] = value

        lift(lat_ref[j], w_ref, k_out, v_out)
        start_stats(run_ref.at[0, pl.ds(j * heads, heads)])
    for n, (j, t) in enumerate(LOCAL):
        slot = t - REACH

        def keep(h, part, cols, weights, grads):
            e_ref[0, n * heads + h, part, cols] = weights
            g_ref[0, n * heads + h, part, cols] = grads

        run = run_ref.at[0, pl.ds(j * heads, heads)]
        score_block(
            lambda h: k_ref[0, slot * heads + h], lambda h: v_ref[slot * heads + h],
            q_ref.at[j], do_ref.at[j], query_bounds(start_ref, chip, j, t, rows), run,
            raw_ref, graw_ref, keep,
        )
        for h in range(heads):
            top_ref[0, n * heads + h] = run[h]


def main_kernel(ranks, steps, index_ref, docs_sref, q0, do0, q1, do1, w_ref, *refs):
    kept, refs = [refs[5 * n : 5 * n + 5] for n in range(steps)], refs[5 * steps :]
    main_body(ranks, index_ref, docs_sref, q0, do0, q1, do1, w_ref, kept, *refs)


def main_body(
    ranks, index_ref, docs_sref, q0, do0, q1, do1, w_ref, kept_steps, start_ref,
    lat_far, lat_swap, lat_mixed, lat_passed, lat_own, lat_other,
    dq0_ref, dq1_ref, keep_ref, send_ref, x_old, x_far, x_swap, x_own, x_other,
    q_ref, do_ref, lat_ref, lat_t_ref, e_ref, g_ref, k_ref, v_ref, top_ref,
    run_ref, end_ref, raw_ref, graw_ref, low_ref, ds_ref, dq_acc, d_acc, gw_acc, x_acc,
    local_e, local_g, local_k, local_run, local_top, sems, kept_sems,
):
    step = pl.program_id(0)
    rows = q0.shape[0]
    heads = w_ref.shape[1] // KV
    blocks = REACH + 2

    kept_copies = []
    for n, (all_e, all_g, all_k, all_run, all_top) in enumerate(kept_steps):
        copies = [
            pltpu.make_async_copy(all_e.at[0], local_e, kept_sems.at[0]),
            pltpu.make_async_copy(all_g.at[0], local_g, kept_sems.at[1]),
        ]
        kept_copies = kept_copies or copies

        @pl.when(step == n)
        def _():
            for copy in copies:
                copy.start()
            local_k[...] = all_k[0]
            local_run[...] = all_run[0]
            local_top[...] = all_top[0]

    core, chip = chip_place(index_ref)

    def active(j, t):
        block = chip + t - REACH
        last_doc = docs_sref[jnp.maximum(block, 0) * rows + rows - 1]
        return (block >= 0) & (last_doc >= docs_sref[(chip + j) * rows])

    def block_rows(t):
        return pl.ds(pl.multiple_of(t * rows, rows), rows)

    def piece_rows(t, part):
        size = part.stop - part.start
        return pl.ds(pl.multiple_of(t * rows + part.start, size), size)

    def loop(first, last, when, body):
        def visit(t, carry):
            @pl.when(when(t))
            def _():
                body(t)

            return carry

        lax.fori_loop(first, last, visit, 0)

    @pl.when(step == 0)
    def _():
        places = [(lat_far, 1 + core), (lat_swap, 2 - core), (lat_own, REACH + core),
                  (lat_other, REACH + 1 - core)]
        copies = [
            pltpu.make_async_copy(source, lat_t_ref.at[:, block_rows(t)], sems.at[i])
            for i, (source, t) in enumerate(places)
        ]
        first = lat_t_ref.at[:, block_rows(0)]
        oldest = pltpu.make_async_copy(lat_mixed, first, sems.at[4])
        passed = pltpu.make_async_copy(lat_passed, first, sems.at[4])
        for copy in copies:
            copy.start()
        pl.when(core == 0)(oldest.start)
        pl.when(core == 1)(passed.start)
        x_acc[...] = jnp.zeros_like(x_acc)
        for copy in copies:
            copy.wait()
        oldest.wait()
        for t in range(REACH):
            part = slice(t * rows, (t + 1) * rows)
            lat_ref[part, :] = lat_t_ref[:, part].T

    order_pair(q_ref, core, q0, q1)
    order_pair(do_ref, core, do0, do1)
    gw_acc[...] = jnp.zeros_like(gw_acc)
    dq_acc[...] = jnp.zeros_like(dq_acc)
    d_acc[...] = jnp.zeros_like(d_acc)

    def lift_block(t):
        def k_out(h, key):
            k_ref[h, block_rows(t), :] = key

        def v_out(h, value):
            v_ref[h, block_rows(t), :] = value

        lift(lat_ref[block_rows(t), :], w_ref, k_out, v_out)

    loop(0, REACH, lambda t: active(0, t) | active(1, t), lift_block)

    for j in range(2):
        for h in range(heads):
            run_ref[h] = local_run[j * heads + h]

        def first_pass(t):
            def keep(h, part, cols, weights, grads):
                e_ref[h, piece_rows(t, part), cols] = weights
                g_ref[h, piece_rows(t, part), cols] = grads

            score_block(
                lambda h: k_ref[h, block_rows(t), :], lambda h: v_ref[h, block_rows(t), :],
                q_ref.at[j], do_ref.at[j], query_bounds(start_ref, chip, j, t, rows), run_ref,
                raw_ref, graw_ref, keep,
            )
            for h in range(heads):
                top_ref[h, t] = run_ref[h]

        loop(j, REACH, lambda t: active(j, t), first_pass)
        for h in range(heads):
            inverse = 1.0 / run_ref[h, 1:2, :]
            end_ref[h, 0:1, :] = run_ref[h, 0:1, :]
            end_ref[h, 1:2, :] = inverse
            end_ref[h, 2:3, :] = run_ref[h, 2:3, :] * inverse
        q_t, do_t = q_ref[j].T, do_ref[j].T

        def add(t, part, kept, key, top):
            def r_add(rope):
                x_acc[LATENT:, part] += rope

            grad_block(
                kept, key, top, end_ref, q_t, do_t, low_ref, ds_ref, dq_acc.at[j], d_acc.at[t],
                r_add,
            )

        def second_pass(t):
            def kept(h, part, cols):
                return e_ref[h, piece_rows(t, part), cols], g_ref[h, piece_rows(t, part), cols]

            add(
                t, block_rows(t), kept, lambda h: k_ref[h, block_rows(t), :],
                lambda h: top_ref[h, t, 0:1, :],
            )

        loop(j, REACH, lambda t: active(j, t), second_pass)
        if j == 0:
            for copy in kept_copies:
                copy.wait()
        for n, (query, t) in enumerate(LOCAL):
            if query == j:
                add(
                    t, slice(t * rows, (t + 1) * rows),
                    lambda h, part, cols: (
                        local_e[n * heads + h, part, cols], local_g[n * heads + h, part, cols]
                    ),
                    lambda h: local_k[(t - REACH) * heads + h],
                    lambda h: local_top[n * heads + h, 0:1, :],
                )

    def project(t):
        part = block_rows(t)
        grads = d_acc[t].astype(jnp.bfloat16)
        x_acc[:LATENT, part] += dot(w_ref[...], grads)
        gw_acc[...] += dot(lat_t_ref[:LATENT, part], grads, NT)

    loop(0, blocks, lambda t: (t >= REACH) | active(0, t) | active(1, t), project)
    dq0_ref[...] = (dq_acc[core] * SCALE).T.astype(dq0_ref.dtype)
    dq1_ref[...] = (dq_acc[1 - core] * SCALE).T.astype(dq1_ref.dtype)

    share = 2 * (LATENT // ranks)
    own_x = lax.rem(index_ref[0] // 2, 2)
    for i in range(ranks // 4):
        for out, x in ((keep_ref, own_x), (send_ref, 1 - own_x)):
            source = pl.multiple_of((2 * i + x) * share, share)
            out[i * share : (i + 1) * share, :] = gw_acc[pl.ds(source, share), :].astype(out.dtype)

    @pl.when(step == pl.num_programs(0) - 1)
    def _():
        places = ((x_old, 0), (x_far, 1 + core), (x_swap, 2 - core), (x_own, REACH + core),
                  (x_other, REACH + 1 - core))
        copies = []
        for i, (out, t) in enumerate(places):
            part = block_rows(t)
            lat_t_ref[:, part] = x_acc[:, part].astype(lat_t_ref.dtype)
            copies.append(pltpu.make_async_copy(lat_t_ref.at[:, part], out, sems.at[i]))
            copies[-1].start()
        for copy in copies:
            copy.wait()


def step_cols(height, size):
    return pl.BlockSpec((height, size), lambda i, index: (0, i))


def core_cols(height, size, first):
    def place(i, index):
        return (0, first(i, lax.rem(index[0], 2)))

    return pl.BlockSpec((height, size), place)


def step_block(*shape):
    return pl.BlockSpec((1, *shape), lambda i, index: (i, 0, 0, 0))


def fixed(*shape):
    return pl.BlockSpec(shape, lambda i, index: (0,) * len(shape))


SCALARS = pl.BlockSpec(memory_space=pltpu.SMEM)
ANYWHERE = pl.BlockSpec(memory_space=pl.ANY)


def call(body, steps, flops, in_specs, outs, scratch, name):
    return pl.pallas_call(
        body,
        grid_spec=pltpu.PrefetchScalarGridSpec(
            num_scalar_prefetch=1,
            grid=(steps,),
            in_specs=in_specs,
            out_specs=[spec for spec, _, _ in outs],
            scratch_shapes=[
                pltpu.VMEM(*entry) if isinstance(entry, tuple) else entry for entry in scratch
            ],
        ),
        out_shape=[jax.ShapeDtypeStruct(shape, kind) for _, shape, kind in outs],
        compiler_params=pltpu.CompilerParams(
            dimension_semantics=("arbitrary",), vmem_limit_bytes=58 * 1024 * 1024
        ),
        cost_estimate=pl.CostEstimate(
            flops=flops, bytes_accessed=16 * 1024 * 1024, transcendentals=0
        ),
        name=name,
    )


def head_specs(rows, heads, steps, first, in_place):
    def received(i, core):
        return first + i

    def own(i, core):
        return (core * steps if in_place else 0) + first + i

    return [
        core_cols(rows, heads * QK, own), core_cols(rows, heads * VDIM, own),
        core_cols(rows, heads * QK, received), core_cols(rows, heads * VDIM, received),
        core_cols(LATENT, heads * KV, own),
    ]


def local_scores(index, docs, inputs, latents, heads, steps, step, in_place):
    rows = inputs[0].shape[0]
    low, full = jnp.bfloat16, jnp.float32
    count = len(LOCAL) * heads
    return call(
        local_kernel,
        1,
        2 * heads * rows * rows * (3 * (QK + VDIM) + 2 * KV),
        [
            fixed(1, docs.shape[1]), *head_specs(rows, heads, steps, step, in_place),
            fixed(WIDTH, rows), fixed(WIDTH, rows),
        ],
        [
            (step_block(count, rows, rows), (1, count, rows, rows), low),
            (step_block(count, rows, rows), (1, count, rows, rows), low),
            (step_block(2 * heads, rows, QK), (1, 2 * heads, rows, QK), low),
            (step_block(2 * heads, 8, rows), (1, 2 * heads, 8, rows), full),
            (step_block(count, 8, rows), (1, count, 8, rows), full),
            (fixed(2, 8, rows), (2, 8, rows), jnp.int32),
        ],
        [
            ((2, rows, heads * QK), low),
            ((2, rows, heads * VDIM), low),
            ((2, rows, WIDTH), low),
            ((2 * heads, rows, VDIM), low),
            ((heads, rows, rows), full),
            ((heads, rows, rows), full),
        ],
        "local_scores",
    )(index, docs, *inputs, *latents)


def attention(index, doc_ids, inputs, kept, starts, latents, heads, steps, ranks, in_place):
    rows = inputs[0].shape[0]
    low, full = jnp.bfloat16, jnp.float32
    count = len(LOCAL) * heads
    window = (REACH + 2) * rows
    far = REACH * rows
    half = (LATENT // 2, steps * heads * KV)
    every = [entry for part in kept for entry in part]
    return call(
        functools.partial(main_kernel, ranks, steps),
        steps,
        2 * steps * heads * rows * rows * (5 * (QK + VDIM) + 8 * (2 * QK + VDIM) + 13 * KV),
        [SCALARS, *head_specs(rows, heads, steps, 0, in_place)]
        + [
            ANYWHERE, ANYWHERE, fixed(1, 2 * heads, rows, QK), fixed(1, 2 * heads, 8, rows),
            fixed(1, count, 8, rows),
        ]
        * steps
        + [fixed(2, 8, rows)]
        + [ANYWHERE] * len(latents),
        [(step_cols(rows, heads * QK), (rows, steps * heads * QK), low)] * 2
        + [(step_cols(LATENT // 2, heads * KV), half, low)] * 2
        + [(ANYWHERE, (WIDTH, rows), low)] * (REACH + 2),
        [
            ((2, rows, heads * QK), low),
            ((2, rows, heads * VDIM), low),
            ((far, WIDTH), low),
            ((WIDTH, window), low),
            ((heads, far, rows), low),
            ((heads, far, rows), low),
            ((heads, far, QK), low),
            ((heads, far, VDIM), low),
            ((heads, REACH, 8, rows), full),
            ((heads, 8, rows), full),
            ((heads, 8, rows), full),
            ((heads, rows, rows), full),
            ((heads, rows, rows), full),
            ((heads, rows, rows), low),
            ((heads, rows, rows), low),
            ((2, heads * QK, rows), full),
            ((REACH + 2, heads * KV, rows), full),
            ((LATENT, heads * KV), full),
            ((WIDTH, window), full),
            ((count, rows, rows), low),
            ((count, rows, rows), low),
            ((2 * heads, rows, QK), low),
            ((2 * heads, 8, rows), full),
            ((count, 8, rows), full),
            pltpu.SemaphoreType.DMA((5,)),
            pltpu.SemaphoreType.DMA((2,)),
        ],
        "attention",
    )(index, doc_ids, *inputs, *every, starts, *latents)


def permute(value, axis, target):
    count = lax.axis_size(axis)
    pairs = [(s, target(s)) for s in range(count) if 0 <= target(s) < count]
    return lax.ppermute(value, axis, pairs)


def local(kv_latent, queries, grad_out, kv_up_weight, doc_ids):
    ranks = lax.axis_size("ctx")
    position = lax.axis_index("ctx").astype(jnp.int32)
    index, core = position[None], lax.rem(position, 2)
    low, full = jnp.bfloat16, jnp.float32
    docs = doc_ids[None]
    core_heads = kv_up_weight.shape[1] // KV // 2
    heads = min(2, core_heads)
    steps = core_heads // heads

    def own_heads(value, which):
        size = value.shape[1] // 2
        return lax.dynamic_slice_in_dim(value, which * size, size, axis=1)

    def across(value):
        return permute(value, "ctx", lambda s: s ^ 1)

    latent = kv_latent.T
    far = permute(latent, "ctx", lambda s: s + 2)
    mixed = permute(latent, "ctx", lambda s: s + 3 if s % 2 else -1)
    other = across(latent)
    in_place = heads * QK % 128 == 0
    inputs = (
        queries if in_place else own_heads(queries, core),
        grad_out if in_place else own_heads(grad_out, core),
        across(own_heads(queries, 1 - core)),
        across(own_heads(grad_out, 1 - core)),
        kv_up_weight if in_place else own_heads(kv_up_weight, core),
    )
    kept = []
    for step in range(steps):
        *parts, starts = local_scores(
            index, docs, inputs, (latent, other), heads, steps, step, in_place
        )
        kept.append(parts)
        if step == 0:
            far, mixed, parts[-1] = lax.optimization_barrier((far, mixed, parts[-1]))
            swapped = across(far)
            passed = permute(mixed, "ctx", lambda s: -1 if s % 2 else s + 1)

    dq_own, dq_other, keep, send, to_old, to_far, to_swap, mine, to_other = attention(
        index, doc_ids, inputs, kept, starts,
        (far, swapped, mixed, passed, latent, other), heads, steps, ranks, in_place,
    )

    from_x = permute(send, "ctx", lambda s: s ^ 2)
    from_swap = across(to_swap)
    from_other = across(to_other)
    from_old = permute(to_old, "ctx", lambda s: s - 1 if s % 2 else -1)
    far_sum = (to_far.astype(full) + from_swap.astype(full)).astype(low)
    old_sum = (to_old.astype(full) + from_old.astype(full)).astype(low)
    from_x, *_ = lax.optimization_barrier((from_x, far_sum, old_sum))
    from_far = permute(far_sum, "ctx", lambda s: s - 2)
    from_mixed = permute(old_sum, "ctx", lambda s: -1 if s % 2 else s - 3)
    plane = (keep.astype(full) + from_x.astype(full)).astype(low)
    columns = [list(range(first, ranks, 4)) for first in range(4)]
    pieces = lax.all_to_all(plane, "ctx", 0, 0, axis_index_groups=columns, tiled=True)
    share = LATENT // ranks
    summed = jnp.sum(pieces.reshape(ranks // 4, 2 * share, -1).astype(full), axis=0)

    def in_order(own, received):
        first = jnp.where(core == 0, own, received)
        second = jnp.where(core == 0, received, own)
        return jnp.concatenate([first, second], axis=1)

    rows_own = lax.dynamic_slice_in_dim(summed, core * share, share, axis=0)
    rows_other = lax.dynamic_slice_in_dim(summed, (1 - core) * share, share, axis=0)
    grad_weight = in_order(rows_own, across(rows_other))
    grad_queries = in_order(dq_own, across(dq_other))

    total = mine.astype(full) + from_other.astype(full)
    total = total + from_mixed.astype(full) + from_far.astype(full)
    mine = total.astype(low)
    size = lax.axis_size("head")
    for turn in range(1, size):
        other = lax.ppermute(mine, "head", [(s, (s + turn) % size) for s in range(size)])
        total = total + other.astype(full)
    return grad_queries, total.astype(low).T, grad_weight


def solution(mesh):
    return jax.shard_map(
        local,
        mesh=mesh,
        in_specs=(P("ctx", None), P("ctx", "head"), P("ctx", "head"), P(None, "head"), P()),
        out_specs=(P("ctx", "head"), P("ctx", None), P("ctx", "head")),
        check_vma=False,
    )
```

```python
import functools
import math

import jax
import jax.numpy as jnp
from jax import lax
from jax.experimental import pallas as pl
from jax.experimental.pallas import tpu as pltpu
from jax.sharding import PartitionSpec as P

NOPE = 128
ROPE = 64
VDIM = 128
LATENT = 512
REACH = 3
QK = NOPE + ROPE
KV = NOPE + VDIM
WIDTH = LATENT + ROPE
LANES = 128

MASKED = -1e30
FLOOR = -1e20
SCALE = 1.0 / math.sqrt(QK)
SCALE2 = SCALE * math.log2(math.e)

NT = (((1,), (1,)), ((), ()))
NN = (((1,), (0,)), ((), ()))


def dot(a, b, dims=NN):
    return lax.dot_general(a, b, dims, preferred_element_type=jnp.float32)


def head_cols(h, size):
    return slice(h * size, (h + 1) * size)


def fold(value, combine):
    return combine(value.reshape(-1, 8, value.shape[1]), axis=0)


def fold(value, combine):
    return combine(value.reshape(-1, 8, value.shape[1]), axis=0)


def lift(latent, w_ref, k_out, v_out):
    for h in range(w_ref.shape[1] // KV):
        lifted = dot(latent[:, :LATENT], w_ref[:, head_cols(h, KV)]).astype(jnp.bfloat16)
        k_out(h, jnp.concatenate([lifted[:, :NOPE], latent[:, LATENT:]], axis=1))
        v_out(h, lifted[:, NOPE:])


def score_block(key, value, q_ref, do_ref, bounds, run_ref, raw_ref, graw_ref, keep):
    rows = do_ref.shape[0]
    heads = range(do_ref.shape[1] // VDIM)
    lower, upper = bounds
    for h in heads:
        raw_ref[h] = dot(key(h), q_ref[:, head_cols(h, QK)], NT)
        graw_ref[h] = dot(value(h), do_ref[:, head_cols(h, VDIM)], NT)
    index = lax.broadcasted_iota(jnp.int32, (LANES, LANES), 0)
    pieces = [slice(r, r + LANES) for r in range(0, rows, LANES)]
    for h in heads:
        for c in range(0, rows, LANES):
            cols = slice(c, c + LANES)

            high = None
            for part in pieces:
                seen = index >= lower[:, cols] - part.start
                if upper is not None:
                    seen = seen & (index <= upper[:, cols] - part.start)
                scores = jnp.where(seen, raw_ref[h, part, cols] * SCALE2, MASKED)
                raw_ref[h, part, cols] = scores
                piece = fold(scores, jnp.max)
                high = piece if high is None else jnp.maximum(high, piece)
            old_top = run_ref[h, 0:1, cols]
            new_top = jnp.maximum(old_top, jnp.max(high, axis=0, keepdims=True))
            mass, cross = 0.0, 0.0
            for part in pieces:
                weights = jnp.exp2(raw_ref[h, part, cols] - new_top)
                grads = graw_ref[h, part, cols]
                keep(h, part, cols, weights.astype(jnp.bfloat16), grads.astype(jnp.bfloat16))
                mass = mass + fold(weights, jnp.sum)
                cross = cross + fold(weights * grads, jnp.sum)
            factor = jnp.exp2(old_top - new_top)
            run_ref[h, 0:1, cols] = new_top
            run_ref[h, 1:2, cols] = run_ref[h, 1:2, cols] * factor + jnp.sum(
                mass, axis=0, keepdims=True
            )
            run_ref[h, 2:3, cols] = run_ref[h, 2:3, cols] * factor + jnp.sum(
                cross, axis=0, keepdims=True
            )


def grad_block(kept, key, top, end_ref, q_t, do_t, low_ref, ds_ref, dq_acc, d_acc, r_acc, first_q, first_k):
    def put(ref, part, value, first):
        ref[part, :] = value if first else ref[part, :] + value

    rows = do_t.shape[1]
    heads = range(do_t.shape[0] // VDIM)
    for h in heads:
        factor = jnp.exp2(top(h) - end_ref[h, 0:1, :]) * end_ref[h, 1:2, :]
        delta = end_ref[h, 2:3, :]
        for c in range(0, rows, LANES):
            cols = slice(c, c + LANES)
            for r in range(0, rows, LANES):
                part = slice(r, r + LANES)
                weights, grads = kept(h, part, cols)
                probs = weights.astype(jnp.float32) * factor[:, cols]
                low_ref[h, part, cols] = probs.astype(jnp.bfloat16)
                ds_ref[h, part, cols] = (
                    probs * (grads.astype(jnp.float32) - delta[:, cols])
                ).astype(jnp.bfloat16)
    rope = 0.0
    for h in heads:
        dvalue = dot(do_t[head_cols(h, VDIM), :], low_ref[h], NT)
        dkey = dot(q_t[head_cols(h, QK), :], ds_ref[h], NT) * SCALE
        put(dq_acc, head_cols(h, QK), dot(key(h).T, ds_ref[h]), first_q)
        put(d_acc, slice(h * KV, h * KV + NOPE), dkey[:NOPE], first_k)
        put(d_acc, slice(h * KV + NOPE, (h + 1) * KV), dvalue, first_k)
        rope = rope + dkey[NOPE:]
    put(r_acc, slice(0, ROPE), rope, first_k)


def start_stats(run_ref):
    count, rows = run_ref.shape[0], run_ref.shape[2]
    for h in range(count):
        run_ref[h, 0:1, :] = jnp.full((1, rows), FLOOR, jnp.float32)
        run_ref[h, 1:8, :] = jnp.zeros((7, rows), jnp.float32)


def chip_place(index_ref):
    core = lax.rem(index_ref[0], 2)
    return core, index_ref[0] - core


def order_pair(out_ref, core, own, other):
    out_ref[core] = own[...]
    out_ref[1 - core] = other[...]


LOCAL = ((1, REACH), (0, REACH), (1, REACH + 1))


def query_bounds(start_ref, chip, j, t, rows):
    lower = start_ref[j, 0:1, :] - (chip + t - REACH) * rows
    own = isinstance(t, int) and t == j + REACH
    return lower, lax.broadcasted_iota(jnp.int32, (1, rows), 1) if own else None


def find_starts(docs_ref, start_ref, chip, rows):
    for j in range(2):
        block = chip + j
        my_docs = docs_ref[:, pl.ds(pl.multiple_of(block * rows, rows), rows)]
        first_doc = my_docs[:, :1]
        key_docs = jnp.broadcast_to(my_docs, (128, rows)).T[:, :1]
        inside = jnp.sum(jnp.where(key_docs < my_docs, 1.0, 0.0), axis=0, keepdims=True)
        before = jnp.zeros((1, rows), jnp.float32)
        for back in range(1, REACH + 1):
            earlier = jnp.maximum(block - back, 0)
            docs = docs_ref[:, pl.ds(pl.multiple_of(earlier * rows, rows), rows)]
            same = (docs == first_doc) & (block >= back)
            before = before + jnp.where(same, 1.0, 0.0)
        before = jnp.sum(before, axis=1, keepdims=True)
        start = jnp.where(my_docs == first_doc, -before, inside).astype(jnp.int32)
        start_ref[j, 0:1, :] = start + block * rows


def local_kernel(
    index_ref, docs_ref, q0, do0, q1, do1, w_ref, lat0, lat1,
    e_ref, g_ref, k_ref, run_ref, top_ref, start_ref,
    q_ref, do_ref, lat_ref, v_ref, raw_ref, graw_ref,
):
    rows = q0.shape[0]
    core, chip = chip_place(index_ref)
    heads = w_ref.shape[1] // KV

    @pl.when(pl.program_id(0) == 0)
    def _():
        lat_ref[core] = lat0[...].T
        lat_ref[1 - core] = lat1[...].T
        find_starts(docs_ref, start_ref, chip, rows)

    order_pair(q_ref, core, q0, q1)
    order_pair(do_ref, core, do0, do1)
    for j in range(2):

        def k_out(h, key):
            k_ref[0, j * heads + h] = key

        def v_out(h, value):
            v_ref[j * heads + h] = value

        lift(lat_ref[j], w_ref, k_out, v_out)
        start_stats(run_ref.at[0, pl.ds(j * heads, heads)])
    for n, (j, t) in enumerate(LOCAL):
        slot = t - REACH

        def keep(h, part, cols, weights, grads):
            e_ref[0, n * heads + h, part, cols] = weights
            g_ref[0, n * heads + h, part, cols] = grads

        run = run_ref.at[0, pl.ds(j * heads, heads)]
        score_block(
            lambda h: k_ref[0, slot * heads + h], lambda h: v_ref[slot * heads + h],
            q_ref.at[j], do_ref.at[j], query_bounds(start_ref, chip, j, t, rows), run,
            raw_ref, graw_ref, keep,
        )
        for h in range(heads):
            top_ref[0, n * heads + h] = run[h]


def main_kernel(
    ranks,
    index_ref, docs_sref, q0, do0, q1, do1, w_ref,
    all_e, all_g, local_k, local_run, local_top, start_ref,
    lat_far, lat_swap, lat_mixed, lat_passed, lat_own, lat_other,
    dq0_ref, dq1_ref, keep_ref, send_ref, x_old, x_far, x_swap, x_own, x_other,
    q_ref, do_ref, lat_ref, lat_t_ref, e_ref, g_ref, k_ref, v_ref, top_ref,
    run_ref, end_ref, raw_ref, graw_ref, low_ref, ds_ref, dq_acc, d_acc, gw_acc, x_acc,
    r_acc, local_e, local_g, sems, kept_sems,
):
    step = pl.program_id(0)
    rows = q0.shape[0]
    heads = w_ref.shape[1] // KV
    blocks = REACH + 2
    kept_copies = [
        pltpu.make_async_copy(all_e.at[step], local_e, kept_sems.at[0]),
        pltpu.make_async_copy(all_g.at[step], local_g, kept_sems.at[1]),
    ]
    for copy in kept_copies:
        copy.start()
    core, chip = chip_place(index_ref)

    def active(j, t):
        block = chip + t - REACH
        last_doc = docs_sref[jnp.maximum(block, 0) * rows + rows - 1]
        return (block >= 0) & (last_doc >= docs_sref[(chip + j) * rows])

    def block_rows(t):
        return pl.ds(pl.multiple_of(t * rows, rows), rows)

    def piece_rows(t, part):
        size = part.stop - part.start
        return pl.ds(pl.multiple_of(t * rows + part.start, size), size)

    def loop(first, last, when, body):
        def visit(t, carry):
            @pl.when(when(t))
            def _():
                body(t)

            return carry

        lax.fori_loop(first, last, visit, 0)

    @pl.when(step == 0)
    def _():
        places = [(lat_far, 1 + core), (lat_swap, 2 - core), (lat_own, REACH + core),
                  (lat_other, REACH + 1 - core)]
        copies = [
            pltpu.make_async_copy(source, lat_t_ref.at[:, block_rows(t)], sems.at[i])
            for i, (source, t) in enumerate(places)
        ]
        first = lat_t_ref.at[:, block_rows(0)]
        oldest = pltpu.make_async_copy(lat_mixed, first, sems.at[4])
        passed = pltpu.make_async_copy(lat_passed, first, sems.at[4])
        for copy in copies:
            copy.start()
        pl.when(core == 0)(oldest.start)
        pl.when(core == 1)(passed.start)
        for copy in copies:
            copy.wait()
        oldest.wait()
        for t in range(REACH):
            part = slice(t * rows, (t + 1) * rows)
            lat_ref[part, :] = lat_t_ref[:, part].T

    order_pair(q_ref, core, q0, q1)
    order_pair(do_ref, core, do0, do1)

    def lift_block(t):
        def k_out(h, key):
            k_ref[h, block_rows(t), :] = key

        def v_out(h, value):
            v_ref[h, block_rows(t), :] = value

        lift(lat_ref[block_rows(t), :], w_ref, k_out, v_out)

    loop(0, REACH, lambda t: active(0, t), lift_block)

    for j in range(2):
        for h in range(heads):
            run_ref[h] = local_run[0, j * heads + h]

        def first_pass(t):
            def keep(h, part, cols, weights, grads):
                e_ref[h, piece_rows(t, part), cols] = weights
                g_ref[h, piece_rows(t, part), cols] = grads

            score_block(
                lambda h: k_ref[h, block_rows(t), :], lambda h: v_ref[h, block_rows(t), :],
                q_ref.at[j], do_ref.at[j], query_bounds(start_ref, chip, j, t, rows), run_ref,
                raw_ref, graw_ref, keep,
            )
            for h in range(heads):
                top_ref[h, t] = run_ref[h]

        loop(j, REACH, lambda t: active(j, t), first_pass)
        for h in range(heads):
            inverse = 1.0 / run_ref[h, 1:2, :]
            end_ref[h, 0:1, :] = run_ref[h, 0:1, :]
            end_ref[h, 1:2, :] = inverse
            end_ref[h, 2:3, :] = run_ref[h, 2:3, :] * inverse
        q_t, do_t = q_ref[j].T, do_ref[j].T

        def add(t, kept, key, top, first_q, first_k):
            grad_block(
                kept, key, top, end_ref, q_t, do_t, low_ref, ds_ref, dq_acc.at[j], d_acc.at[t],
                r_acc.at[t], first_q, first_k,
            )

        def second_pass(t):
            def kept(h, part, cols):
                return e_ref[h, piece_rows(t, part), cols], g_ref[h, piece_rows(t, part), cols]

            add(
                t, kept, lambda h: k_ref[h, block_rows(t), :], lambda h: top_ref[h, t, 0:1, :],
                False, j == 0,
            )

        if j == 0:
            for copy in kept_copies:
                copy.wait()
        first_q = True
        for n, (query, t) in enumerate(LOCAL):
            if query == j:
                add(
                    t,
                    lambda h, part, cols: (
                        local_e[n * heads + h, part, cols], local_g[n * heads + h, part, cols]
                    ),
                    lambda h: local_k[0, (t - REACH) * heads + h],
                    lambda h: local_top[0, n * heads + h, 0:1, :],
                    first_q, t == REACH + j,
                )
                first_q = False
        loop(j, REACH, lambda t: active(j, t), second_pass)

    def seen(t):
        return (t >= REACH) | active(0, t)

    def project(t, first):
        part = block_rows(t)
        grads = d_acc[t].astype(jnp.bfloat16)
        weight_part = dot(lat_t_ref[:LATENT, part], grads, NT)
        gw_acc[...] = weight_part if first else gw_acc[...] + weight_part
        latent_part = dot(w_ref[...], grads)

        @pl.when(step == 0)
        def _():
            x_acc[:LATENT, part] = latent_part
            x_acc[LATENT:, part] = r_acc[t]

        @pl.when(step > 0)
        def _():
            x_acc[:LATENT, part] += latent_part
            x_acc[LATENT:, part] += r_acc[t]

    @pl.when(step == 0)
    def _():
        def clear(t):
            x_acc[:, block_rows(t)] = jnp.zeros((WIDTH, rows), jnp.float32)

        loop(0, REACH, lambda t: ~seen(t), clear)

    project(REACH, True)
    loop(0, blocks, lambda t: seen(t) & (t != REACH), lambda t: project(t, False))
    dq0_ref[...] = (dq_acc[core] * SCALE).T.astype(dq0_ref.dtype)
    dq1_ref[...] = (dq_acc[1 - core] * SCALE).T.astype(dq1_ref.dtype)

    share = 2 * (LATENT // ranks)
    own_x = lax.rem(index_ref[0] // 2, 2)
    for i in range(ranks // 4):
        for out, x in ((keep_ref, own_x), (send_ref, 1 - own_x)):
            source = pl.multiple_of((2 * i + x) * share, share)
            out[i * share : (i + 1) * share, :] = gw_acc[pl.ds(source, share), :].astype(out.dtype)

    @pl.when(step == pl.num_programs(0) - 1)
    def _():
        places = ((x_old, 0), (x_far, 1 + core), (x_swap, 2 - core), (x_own, REACH + core),
                  (x_other, REACH + 1 - core))
        copies = []
        for i, (out, t) in enumerate(places):
            part = block_rows(t)
            lat_t_ref[:, part] = x_acc[:, part].astype(lat_t_ref.dtype)
            copies.append(pltpu.make_async_copy(lat_t_ref.at[:, part], out, sems.at[i]))
            copies[-1].start()
        for copy in copies:
            copy.wait()


def step_cols(height, size):
    return pl.BlockSpec((height, size), lambda i, index: (0, i))


def core_cols(height, size, first):
    def place(i, index):
        return (0, first(i, lax.rem(index[0], 2)))

    return pl.BlockSpec((height, size), place)


def step_block(*shape):
    return pl.BlockSpec((1, *shape), lambda i, index: (i, 0, 0, 0))


def fixed(*shape):
    return pl.BlockSpec(shape, lambda i, index: (0,) * len(shape))


SCALARS = pl.BlockSpec(memory_space=pltpu.SMEM)
ANYWHERE = pl.BlockSpec(memory_space=pl.ANY)


def call(body, steps, flops, in_specs, outs, scratch, name):
    return pl.pallas_call(
        body,
        grid_spec=pltpu.PrefetchScalarGridSpec(
            num_scalar_prefetch=1,
            grid=(steps,),
            in_specs=in_specs,
            out_specs=[spec for spec, _, _ in outs],
            scratch_shapes=[
                pltpu.VMEM(*entry) if isinstance(entry, tuple) else entry for entry in scratch
            ],
        ),
        out_shape=[jax.ShapeDtypeStruct(shape, kind) for _, shape, kind in outs],
        compiler_params=pltpu.CompilerParams(
            dimension_semantics=("arbitrary",), vmem_limit_bytes=58 * 1024 * 1024
        ),
        cost_estimate=pl.CostEstimate(
            flops=flops, bytes_accessed=16 * 1024 * 1024, transcendentals=0
        ),
        name=name,
    )


def head_specs(rows, heads, steps, in_place):
    def received(i, core):
        return i

    def own(i, core):
        return core * steps + i if in_place else i

    return [
        core_cols(rows, heads * QK, own), core_cols(rows, heads * VDIM, own),
        core_cols(rows, heads * QK, received), core_cols(rows, heads * VDIM, received),
        core_cols(LATENT, heads * KV, own),
    ]


def local_scores(index, docs, inputs, latents, heads, steps, in_place):
    rows = inputs[0].shape[0]
    low, full = jnp.bfloat16, jnp.float32
    count = len(LOCAL) * heads
    return call(
        local_kernel,
        steps,
        2 * steps * heads * rows * rows * (3 * (QK + VDIM) + 2 * KV),
        [
            fixed(1, docs.shape[1]), *head_specs(rows, heads, steps, in_place),
            fixed(WIDTH, rows), fixed(WIDTH, rows),
        ],
        [
            (step_block(count, rows, rows), (steps, count, rows, rows), low),
            (step_block(count, rows, rows), (steps, count, rows, rows), low),
            (step_block(2 * heads, rows, QK), (steps, 2 * heads, rows, QK), low),
            (step_block(2 * heads, 8, rows), (steps, 2 * heads, 8, rows), full),
            (step_block(count, 8, rows), (steps, count, 8, rows), full),
            (fixed(2, 8, rows), (2, 8, rows), jnp.int32),
        ],
        [
            ((2, rows, heads * QK), low),
            ((2, rows, heads * VDIM), low),
            ((2, rows, WIDTH), low),
            ((2 * heads, rows, VDIM), low),
            ((heads, rows, rows), full),
            ((heads, rows, rows), full),
        ],
        "local_scores",
    )(index, docs, *inputs, *latents)


def attention(index, doc_ids, inputs, kept, latents, heads, steps, ranks, in_place):
    rows = inputs[0].shape[0]
    low, full = jnp.bfloat16, jnp.float32
    count = len(LOCAL) * heads
    window = (REACH + 2) * rows
    far = REACH * rows
    half = (LATENT // 2, steps * heads * KV)
    return call(
        functools.partial(main_kernel, ranks),
        steps,
        2 * steps * heads * rows * rows * (5 * (QK + VDIM) + 8 * (2 * QK + VDIM) + 13 * KV),
        [
            SCALARS, *head_specs(rows, heads, steps, in_place), ANYWHERE, ANYWHERE,
            step_block(2 * heads, rows, QK), step_block(2 * heads, 8, rows),
            step_block(count, 8, rows), fixed(2, 8, rows),
        ]
        + [ANYWHERE] * len(latents),
        [(step_cols(rows, heads * QK), (rows, steps * heads * QK), low)] * 2
        + [(step_cols(LATENT // 2, heads * KV), half, low)] * 2
        + [(ANYWHERE, (WIDTH, rows), low)] * (REACH + 2),
        [
            ((2, rows, heads * QK), low),
            ((2, rows, heads * VDIM), low),
            ((far, WIDTH), low),
            ((WIDTH, window), low),
            ((heads, far, rows), low),
            ((heads, far, rows), low),
            ((heads, far, QK), low),
            ((heads, far, VDIM), low),
            ((heads, REACH, 8, rows), full),
            ((heads, 8, rows), full),
            ((heads, 8, rows), full),
            ((heads, rows, rows), full),
            ((heads, rows, rows), full),
            ((heads, rows, rows), low),
            ((heads, rows, rows), low),
            ((2, heads * QK, rows), full),
            ((REACH + 2, heads * KV, rows), full),
            ((LATENT, heads * KV), full),
            ((WIDTH, window), full),
            ((REACH + 2, ROPE, rows), full),
            ((count, rows, rows), low),
            ((count, rows, rows), low),
            pltpu.SemaphoreType.DMA((5,)),
            pltpu.SemaphoreType.DMA((2,)),
        ],
        "attention",
    )(index, doc_ids, *inputs, *kept, *latents)


def permute(value, axis, target):
    count = lax.axis_size(axis)
    pairs = [(s, target(s)) for s in range(count) if 0 <= target(s) < count]
    return lax.ppermute(value, axis, pairs)


def local(kv_latent, queries, grad_out, kv_up_weight, doc_ids):
    ranks = lax.axis_size("ctx")
    position = lax.axis_index("ctx").astype(jnp.int32)
    index, core = position[None], lax.rem(position, 2)
    low, full = jnp.bfloat16, jnp.float32
    docs = doc_ids[None]
    core_heads = kv_up_weight.shape[1] // KV // 2
    heads = min(2, core_heads)
    steps = core_heads // heads

    def own_heads(value, which):
        size = value.shape[1] // 2
        return lax.dynamic_slice_in_dim(value, which * size, size, axis=1)

    def across(value):
        return permute(value, "ctx", lambda s: s ^ 1)

    latent = kv_latent.T
    far = permute(latent, "ctx", lambda s: s + 2)
    mixed = permute(latent, "ctx", lambda s: s + 3 if s % 2 else -1)
    other = across(latent)
    in_place = heads * QK % 128 == 0
    inputs = (
        queries if in_place else own_heads(queries, core),
        grad_out if in_place else own_heads(grad_out, core),
        across(own_heads(queries, 1 - core)),
        across(own_heads(grad_out, 1 - core)),
        kv_up_weight if in_place else own_heads(kv_up_weight, core),
    )
    *kept, starts = local_scores(index, docs, inputs, (latent, other), heads, steps, in_place)
    far, mixed, starts = lax.optimization_barrier((far, mixed, starts))
    swapped = across(far)
    passed = permute(mixed, "ctx", lambda s: -1 if s % 2 else s + 1)

    dq_own, dq_other, keep, send, to_old, to_far, to_swap, mine, to_other = attention(
        index, doc_ids, inputs, (*kept, starts),
        (far, swapped, mixed, passed, latent, other), heads, steps, ranks, in_place,
    )

    from_x = permute(send, "ctx", lambda s: s ^ 2)
    from_swap = across(to_swap)
    from_other = across(to_other)
    from_old = permute(to_old, "ctx", lambda s: s - 1 if s % 2 else -1)
    far_sum = (to_far.astype(full) + from_swap.astype(full)).astype(low)
    old_sum = (to_old.astype(full) + from_old.astype(full)).astype(low)
    from_x, *_ = lax.optimization_barrier((from_x, far_sum, old_sum))
    from_far = permute(far_sum, "ctx", lambda s: s - 2)
    from_mixed = permute(old_sum, "ctx", lambda s: -1 if s % 2 else s - 3)
    plane = (keep.astype(full) + from_x.astype(full)).astype(low)
    columns = [list(range(first, ranks, 4)) for first in range(4)]
    pieces = lax.all_to_all(plane, "ctx", 0, 0, axis_index_groups=columns, tiled=True)
    share = LATENT // ranks
    summed = jnp.sum(pieces.reshape(ranks // 4, 2 * share, -1).astype(full), axis=0)

    def in_order(own, received):
        first = jnp.where(core == 0, own, received)
        second = jnp.where(core == 0, received, own)
        return jnp.concatenate([first, second], axis=1)

    rows_own = lax.dynamic_slice_in_dim(summed, core * share, share, axis=0)
    rows_other = lax.dynamic_slice_in_dim(summed, (1 - core) * share, share, axis=0)
    grad_weight = in_order(rows_own, across(rows_other))
    grad_queries = in_order(dq_own, across(dq_other))

    total = mine.astype(full) + from_other.astype(full)
    total = total + from_mixed.astype(full) + from_far.astype(full)
    mine = total.astype(low)
    size = lax.axis_size("head")
    for turn in range(1, size):
        other = lax.ppermute(mine, "head", [(s, (s + turn) % size) for s in range(size)])
        total = total + other.astype(full)
    return grad_queries, total.astype(low).T, grad_weight


def solution(mesh):
    return jax.shard_map(
        local,
        mesh=mesh,
        in_specs=(P("ctx", None), P("ctx", "head"), P("ctx", "head"), P(None, "head"), P()),
        out_specs=(P("ctx", "head"), P("ctx", None), P("ctx", "head")),
        check_vma=False,
    )
```

```python
import functools
import math

import jax
import jax.numpy as jnp
from jax import lax
from jax.experimental import pallas as pl
from jax.experimental.pallas import tpu as pltpu
from jax.sharding import PartitionSpec as P

NOPE = 128
ROPE = 64
VDIM = 128
LATENT = 512
REACH = 3
QK = NOPE + ROPE
KV = NOPE + VDIM
WIDTH = LATENT + ROPE
LANES = 128
PIECE = 256

MASKED = -1e30
FLOOR = -1e20
SCALE = 1.0 / math.sqrt(QK)
SCALE2 = SCALE * math.log2(math.e)

NT = (((1,), (1,)), ((), ()))
NN = (((1,), (0,)), ((), ()))


def dot(a, b, dims=NN):
    return lax.dot_general(a, b, dims, preferred_element_type=jnp.float32)


def head_cols(h, size):
    return slice(h * size, (h + 1) * size)


def fold(value, combine):
    return combine(value.reshape(-1, 8, value.shape[1]), axis=0)


def fold(value, combine):
    return combine(value.reshape(-1, 8, value.shape[1]), axis=0)


def lift(latent, w_ref, k_out, v_out):
    for h in range(w_ref.shape[1] // KV):
        lifted = dot(latent[:, :LATENT], w_ref[:, head_cols(h, KV)]).astype(jnp.bfloat16)
        k_out(h, jnp.concatenate([lifted[:, :NOPE], latent[:, LATENT:]], axis=1))
        v_out(h, lifted[:, NOPE:])


def score_block(key, value, q_ref, do_ref, bounds, run_ref, raw_ref, graw_ref, keep):
    rows = do_ref.shape[0]
    lower, upper = bounds
    index = lax.broadcasted_iota(jnp.int32, (LANES, LANES), 0)
    parts = [slice(r, r + LANES) for r in range(0, rows, LANES)]

    def multiply(h, first):
        cols = slice(first, first + PIECE)
        raw_ref[h, :, cols] = dot(key(h), q_ref[cols, head_cols(h, QK)], NT)
        graw_ref[h, :, cols] = dot(value(h), do_ref[cols, head_cols(h, VDIM)], NT)

    def weigh(h, first):
        for c in range(first, first + PIECE, LANES):
            cols = slice(c, c + LANES)
            high = None
            for part in parts:
                seen = index >= lower[:, cols] - part.start
                if upper is not None:
                    seen = seen & (index <= upper[:, cols] - part.start)
                scores = jnp.where(seen, raw_ref[h, part, cols] * SCALE2, MASKED)
                raw_ref[h, part, cols] = scores
                piece = fold(scores, jnp.max)
                high = piece if high is None else jnp.maximum(high, piece)
            old_top = run_ref[h, 0:1, cols]
            new_top = jnp.maximum(old_top, jnp.max(high, axis=0, keepdims=True))
            mass, cross = 0.0, 0.0
            for part in parts:
                weights = jnp.exp2(raw_ref[h, part, cols] - new_top)
                grads = graw_ref[h, part, cols]
                keep(h, part, cols, weights.astype(jnp.bfloat16), grads.astype(jnp.bfloat16))
                mass = mass + fold(weights, jnp.sum)
                cross = cross + fold(weights * grads, jnp.sum)
            factor = jnp.exp2(old_top - new_top)
            run_ref[h, 0:1, cols] = new_top
            run_ref[h, 1:2, cols] = run_ref[h, 1:2, cols] * factor + jnp.sum(
                mass, axis=0, keepdims=True
            )
            run_ref[h, 2:3, cols] = run_ref[h, 2:3, cols] * factor + jnp.sum(
                cross, axis=0, keepdims=True
            )

    alternate(rows, do_ref.shape[1] // VDIM, multiply, weigh)


def alternate(rows, heads, first, second):
    pieces = [(h, c) for h in range(heads) for c in range(0, rows, PIECE)]
    first(*pieces[0])
    for now, following in zip(pieces, pieces[1:] + [None]):
        if following:
            first(*following)
        second(*now)


def grad_block(kept, key, top, end_ref, q_t, do_t, low_ref, ds_ref, dq_acc, d_acc, r_acc, first_q, first_k):
    def put(ref, part, value, first):
        ref[part, :] = value if first else ref[part, :] + value

    rows = do_t.shape[1]
    heads = do_t.shape[0] // VDIM
    sums = {}

    def weigh(h, first):
        for c in range(first, first + PIECE, LANES):
            cols = slice(c, c + LANES)
            factor = jnp.exp2(top(h)[:, cols] - end_ref[h, 0:1, cols]) * end_ref[h, 1:2, cols]
            delta = end_ref[h, 2:3, cols]
            for r in range(0, rows, LANES):
                part = slice(r, r + LANES)
                weights, grads = kept(h, part, cols)
                probs = weights.astype(jnp.float32) * factor
                low_ref[h, part, cols] = probs.astype(jnp.bfloat16)
                ds_ref[h, part, cols] = (
                    probs * (grads.astype(jnp.float32) - delta)
                ).astype(jnp.bfloat16)

    def multiply(h, first):
        cols = slice(first, first + PIECE)
        low, dscore = low_ref[h, :, cols], ds_ref[h, :, cols]
        dvalue = dot(do_t[head_cols(h, VDIM), cols], low, NT)
        dkey = dot(q_t[head_cols(h, QK), cols], dscore, NT)
        own = head_cols(h, QK)
        dq = dot(key(h).T, dscore)
        dq_acc[own, cols] = dq if first_q else dq_acc[own, cols] + dq
        if first:
            dvalue, dkey = sums[h][0] + dvalue, sums[h][1] + dkey
        sums[h] = dvalue, dkey
        if first + PIECE == rows:
            dkey = dkey * SCALE
            put(d_acc, slice(h * KV, h * KV + NOPE), dkey[:NOPE], first_k)
            put(d_acc, slice(h * KV + NOPE, (h + 1) * KV), dvalue, first_k)
            put(r_acc, slice(0, ROPE), dkey[NOPE:], first_k and h == 0)

    alternate(rows, heads, weigh, multiply)


def start_stats(run_ref):
    count, rows = run_ref.shape[0], run_ref.shape[2]
    for h in range(count):
        run_ref[h, 0:1, :] = jnp.full((1, rows), FLOOR, jnp.float32)
        run_ref[h, 1:8, :] = jnp.zeros((7, rows), jnp.float32)


def chip_place(index_ref):
    core = lax.rem(index_ref[0], 2)
    return core, index_ref[0] - core


def order_pair(out_ref, core, own, other):
    out_ref[core] = own[...]
    out_ref[1 - core] = other[...]


LOCAL = ((1, REACH), (0, REACH), (1, REACH + 1))


def query_bounds(start_ref, chip, j, t, rows):
    lower = start_ref[j, 0:1, :] - (chip + t - REACH) * rows
    own = isinstance(t, int) and t == j + REACH
    return lower, lax.broadcasted_iota(jnp.int32, (1, rows), 1) if own else None


def find_starts(docs_ref, start_ref, chip, rows):
    for j in range(2):
        block = chip + j
        my_docs = docs_ref[:, pl.ds(pl.multiple_of(block * rows, rows), rows)]
        first_doc = my_docs[:, :1]
        key_docs = jnp.broadcast_to(my_docs, (128, rows)).T[:, :1]
        inside = jnp.sum(jnp.where(key_docs < my_docs, 1.0, 0.0), axis=0, keepdims=True)
        before = jnp.zeros((1, rows), jnp.float32)
        for back in range(1, REACH + 1):
            earlier = jnp.maximum(block - back, 0)
            docs = docs_ref[:, pl.ds(pl.multiple_of(earlier * rows, rows), rows)]
            same = (docs == first_doc) & (block >= back)
            before = before + jnp.where(same, 1.0, 0.0)
        before = jnp.sum(before, axis=1, keepdims=True)
        start = jnp.where(my_docs == first_doc, -before, inside).astype(jnp.int32)
        start_ref[j, 0:1, :] = start + block * rows


def local_kernel(
    index_ref, docs_ref, q0, do0, q1, do1, w_ref, lat0, lat1,
    e_ref, g_ref, k_ref, run_ref, top_ref, start_ref,
    q_ref, do_ref, lat_ref, v_ref, raw_ref, graw_ref,
):
    rows = q0.shape[0]
    core, chip = chip_place(index_ref)
    heads = w_ref.shape[1] // KV

    @pl.when(pl.program_id(0) == 0)
    def _():
        lat_ref[core] = lat0[...].T
        lat_ref[1 - core] = lat1[...].T
        find_starts(docs_ref, start_ref, chip, rows)

    order_pair(q_ref, core, q0, q1)
    order_pair(do_ref, core, do0, do1)
    for j in range(2):

        def k_out(h, key):
            k_ref[0, j * heads + h] = key

        def v_out(h, value):
            v_ref[j * heads + h] = value

        lift(lat_ref[j], w_ref, k_out, v_out)
        start_stats(run_ref.at[0, pl.ds(j * heads, heads)])
    for n, (j, t) in enumerate(LOCAL):
        slot = t - REACH

        def keep(h, part, cols, weights, grads):
            e_ref[0, n * heads + h, part, cols] = weights
            g_ref[0, n * heads + h, part, cols] = grads

        run = run_ref.at[0, pl.ds(j * heads, heads)]
        score_block(
            lambda h: k_ref[0, slot * heads + h], lambda h: v_ref[slot * heads + h],
            q_ref.at[j], do_ref.at[j], query_bounds(start_ref, chip, j, t, rows), run,
            raw_ref, graw_ref, keep,
        )
        for h in range(heads):
            top_ref[0, n * heads + h] = run[h]


def main_kernel(
    ranks,
    index_ref, docs_sref, q0, do0, q1, do1, w_ref,
    all_e, all_g, local_k, local_run, local_top, start_ref,
    lat_far, lat_swap, lat_mixed, lat_passed, lat_own, lat_other,
    dq0_ref, dq1_ref, keep_ref, send_ref, x_old, x_far, x_swap, x_own, x_other,
    q_ref, do_ref, lat_ref, lat_t_ref, e_ref, g_ref, k_ref, v_ref, top_ref,
    run_ref, end_ref, raw_ref, graw_ref, low_ref, ds_ref, dq_acc, d_acc, gw_acc, x_acc,
    r_acc, local_e, local_g, sems, kept_sems,
):
    step = pl.program_id(0)
    rows = q0.shape[0]
    heads = w_ref.shape[1] // KV
    blocks = REACH + 2
    kept_copies = [
        pltpu.make_async_copy(all_e.at[step], local_e, kept_sems.at[0]),
        pltpu.make_async_copy(all_g.at[step], local_g, kept_sems.at[1]),
    ]
    for copy in kept_copies:
        copy.start()
    core, chip = chip_place(index_ref)

    def active(j, t):
        block = chip + t - REACH
        last_doc = docs_sref[jnp.maximum(block, 0) * rows + rows - 1]
        return (block >= 0) & (last_doc >= docs_sref[(chip + j) * rows])

    def block_rows(t):
        return pl.ds(pl.multiple_of(t * rows, rows), rows)

    def piece_rows(t, part):
        size = part.stop - part.start
        return pl.ds(pl.multiple_of(t * rows + part.start, size), size)

    def loop(first, last, when, body):
        def visit(t, carry):
            @pl.when(when(t))
            def _():
                body(t)

            return carry

        lax.fori_loop(first, last, visit, 0)

    @pl.when(step == 0)
    def _():
        places = [(lat_far, 1 + core), (lat_swap, 2 - core), (lat_own, REACH + core),
                  (lat_other, REACH + 1 - core)]
        copies = [
            pltpu.make_async_copy(source, lat_t_ref.at[:, block_rows(t)], sems.at[i])
            for i, (source, t) in enumerate(places)
        ]
        first = lat_t_ref.at[:, block_rows(0)]
        oldest = pltpu.make_async_copy(lat_mixed, first, sems.at[4])
        passed = pltpu.make_async_copy(lat_passed, first, sems.at[4])
        for copy in copies:
            copy.start()
        pl.when(core == 0)(oldest.start)
        pl.when(core == 1)(passed.start)
        for copy in copies:
            copy.wait()
        oldest.wait()
        for t in range(REACH):
            part = slice(t * rows, (t + 1) * rows)
            lat_ref[part, :] = lat_t_ref[:, part].T

    order_pair(q_ref, core, q0, q1)
    order_pair(do_ref, core, do0, do1)

    def lift_block(t):
        def k_out(h, key):
            k_ref[h, block_rows(t), :] = key

        def v_out(h, value):
            v_ref[h, block_rows(t), :] = value

        lift(lat_ref[block_rows(t), :], w_ref, k_out, v_out)

    loop(0, REACH, lambda t: active(0, t), lift_block)

    for j in range(2):
        for h in range(heads):
            run_ref[h] = local_run[0, j * heads + h]

        def first_pass(t):
            def keep(h, part, cols, weights, grads):
                e_ref[h, piece_rows(t, part), cols] = weights
                g_ref[h, piece_rows(t, part), cols] = grads

            score_block(
                lambda h: k_ref[h, block_rows(t), :], lambda h: v_ref[h, block_rows(t), :],
                q_ref.at[j], do_ref.at[j], query_bounds(start_ref, chip, j, t, rows), run_ref,
                raw_ref, graw_ref, keep,
            )
            for h in range(heads):
                top_ref[h, t] = run_ref[h]

        loop(j, REACH, lambda t: active(j, t), first_pass)
        for h in range(heads):
            inverse = 1.0 / run_ref[h, 1:2, :]
            end_ref[h, 0:1, :] = run_ref[h, 0:1, :]
            end_ref[h, 1:2, :] = inverse
            end_ref[h, 2:3, :] = run_ref[h, 2:3, :] * inverse
        q_t, do_t = q_ref[j].T, do_ref[j].T

        def add(t, kept, key, top, first_q, first_k):
            grad_block(
                kept, key, top, end_ref, q_t, do_t, low_ref, ds_ref, dq_acc.at[j], d_acc.at[t],
                r_acc.at[t], first_q, first_k,
            )

        def second_pass(t):
            def kept(h, part, cols):
                return e_ref[h, piece_rows(t, part), cols], g_ref[h, piece_rows(t, part), cols]

            add(
                t, kept, lambda h: k_ref[h, block_rows(t), :], lambda h: top_ref[h, t, 0:1, :],
                False, j == 0,
            )

        if j == 0:
            for copy in kept_copies:
                copy.wait()
        first_q = True
        for n, (query, t) in enumerate(LOCAL):
            if query == j:
                add(
                    t,
                    lambda h, part, cols: (
                        local_e[n * heads + h, part, cols], local_g[n * heads + h, part, cols]
                    ),
                    lambda h: local_k[0, (t - REACH) * heads + h],
                    lambda h: local_top[0, n * heads + h, 0:1, :],
                    first_q, t == REACH + j,
                )
                first_q = False
        loop(j, REACH, lambda t: active(j, t), second_pass)

    def seen(t):
        return (t >= REACH) | active(0, t)

    def project(t, first):
        part = block_rows(t)
        grads = d_acc[t].astype(jnp.bfloat16)
        weight_part = dot(lat_t_ref[:LATENT, part], grads, NT)
        gw_acc[...] = weight_part if first else gw_acc[...] + weight_part
        latent_part = dot(w_ref[...], grads)

        @pl.when(step == 0)
        def _():
            x_acc[:LATENT, part] = latent_part
            x_acc[LATENT:, part] = r_acc[t]

        @pl.when(step > 0)
        def _():
            x_acc[:LATENT, part] += latent_part
            x_acc[LATENT:, part] += r_acc[t]

    @pl.when(step == 0)
    def _():
        def clear(t):
            x_acc[:, block_rows(t)] = jnp.zeros((WIDTH, rows), jnp.float32)

        loop(0, REACH, lambda t: ~seen(t), clear)

    project(REACH, True)
    loop(0, blocks, lambda t: seen(t) & (t != REACH), lambda t: project(t, False))
    dq0_ref[...] = (dq_acc[core] * SCALE).T.astype(dq0_ref.dtype)
    dq1_ref[...] = (dq_acc[1 - core] * SCALE).T.astype(dq1_ref.dtype)

    share = 2 * (LATENT // ranks)
    own_x = lax.rem(index_ref[0] // 2, 2)
    for i in range(ranks // 4):
        for out, x in ((keep_ref, own_x), (send_ref, 1 - own_x)):
            source = pl.multiple_of((2 * i + x) * share, share)
            out[i * share : (i + 1) * share, :] = gw_acc[pl.ds(source, share), :].astype(out.dtype)

    @pl.when(step == pl.num_programs(0) - 1)
    def _():
        places = ((x_old, 0), (x_far, 1 + core), (x_swap, 2 - core), (x_own, REACH + core),
                  (x_other, REACH + 1 - core))
        copies = []
        for i, (out, t) in enumerate(places):
            part = block_rows(t)
            lat_t_ref[:, part] = x_acc[:, part].astype(lat_t_ref.dtype)
            copies.append(pltpu.make_async_copy(lat_t_ref.at[:, part], out, sems.at[i]))
            copies[-1].start()
        for copy in copies:
            copy.wait()


def step_cols(height, size):
    return pl.BlockSpec((height, size), lambda i, index: (0, i))


def core_cols(height, size, first):
    def place(i, index):
        return (0, first(i, lax.rem(index[0], 2)))

    return pl.BlockSpec((height, size), place)


def step_block(*shape):
    return pl.BlockSpec((1, *shape), lambda i, index: (i, 0, 0, 0))


def fixed(*shape):
    return pl.BlockSpec(shape, lambda i, index: (0,) * len(shape))


SCALARS = pl.BlockSpec(memory_space=pltpu.SMEM)
ANYWHERE = pl.BlockSpec(memory_space=pl.ANY)


def call(body, steps, flops, in_specs, outs, scratch, name):
    return pl.pallas_call(
        body,
        grid_spec=pltpu.PrefetchScalarGridSpec(
            num_scalar_prefetch=1,
            grid=(steps,),
            in_specs=in_specs,
            out_specs=[spec for spec, _, _ in outs],
            scratch_shapes=[
                pltpu.VMEM(*entry) if isinstance(entry, tuple) else entry for entry in scratch
            ],
        ),
        out_shape=[jax.ShapeDtypeStruct(shape, kind) for _, shape, kind in outs],
        compiler_params=pltpu.CompilerParams(
            dimension_semantics=("arbitrary",), vmem_limit_bytes=58 * 1024 * 1024
        ),
        cost_estimate=pl.CostEstimate(
            flops=flops, bytes_accessed=16 * 1024 * 1024, transcendentals=0
        ),
        name=name,
    )


def head_specs(rows, heads, steps, in_place):
    def received(i, core):
        return i

    def own(i, core):
        return core * steps + i if in_place else i

    return [
        core_cols(rows, heads * QK, own), core_cols(rows, heads * VDIM, own),
        core_cols(rows, heads * QK, received), core_cols(rows, heads * VDIM, received),
        core_cols(LATENT, heads * KV, own),
    ]


def local_scores(index, docs, inputs, latents, heads, steps, in_place):
    rows = inputs[0].shape[0]
    low, full = jnp.bfloat16, jnp.float32
    count = len(LOCAL) * heads
    return call(
        local_kernel,
        steps,
        2 * steps * heads * rows * rows * (3 * (QK + VDIM) + 2 * KV),
        [
            fixed(1, docs.shape[1]), *head_specs(rows, heads, steps, in_place),
            fixed(WIDTH, rows), fixed(WIDTH, rows),
        ],
        [
            (step_block(count, rows, rows), (steps, count, rows, rows), low),
            (step_block(count, rows, rows), (steps, count, rows, rows), low),
            (step_block(2 * heads, rows, QK), (steps, 2 * heads, rows, QK), low),
            (step_block(2 * heads, 8, rows), (steps, 2 * heads, 8, rows), full),
            (step_block(count, 8, rows), (steps, count, 8, rows), full),
            (fixed(2, 8, rows), (2, 8, rows), jnp.int32),
        ],
        [
            ((2, rows, heads * QK), low),
            ((2, rows, heads * VDIM), low),
            ((2, rows, WIDTH), low),
            ((2 * heads, rows, VDIM), low),
            ((heads, rows, rows), full),
            ((heads, rows, rows), full),
        ],
        "local_scores",
    )(index, docs, *inputs, *latents)


def attention(index, doc_ids, inputs, kept, latents, heads, steps, ranks, in_place):
    rows = inputs[0].shape[0]
    low, full = jnp.bfloat16, jnp.float32
    count = len(LOCAL) * heads
    window = (REACH + 2) * rows
    far = REACH * rows
    half = (LATENT // 2, steps * heads * KV)
    return call(
        functools.partial(main_kernel, ranks),
        steps,
        2 * steps * heads * rows * rows * (5 * (QK + VDIM) + 8 * (2 * QK + VDIM) + 13 * KV),
        [
            SCALARS, *head_specs(rows, heads, steps, in_place), ANYWHERE, ANYWHERE,
            step_block(2 * heads, rows, QK), step_block(2 * heads, 8, rows),
            step_block(count, 8, rows), fixed(2, 8, rows),
        ]
        + [ANYWHERE] * len(latents),
        [(step_cols(rows, heads * QK), (rows, steps * heads * QK), low)] * 2
        + [(step_cols(LATENT // 2, heads * KV), half, low)] * 2
        + [(ANYWHERE, (WIDTH, rows), low)] * (REACH + 2),
        [
            ((2, rows, heads * QK), low),
            ((2, rows, heads * VDIM), low),
            ((far, WIDTH), low),
            ((WIDTH, window), low),
            ((heads, far, rows), low),
            ((heads, far, rows), low),
            ((heads, far, QK), low),
            ((heads, far, VDIM), low),
            ((heads, REACH, 8, rows), full),
            ((heads, 8, rows), full),
            ((heads, 8, rows), full),
            ((heads, rows, rows), full),
            ((heads, rows, rows), full),
            ((heads, rows, rows), low),
            ((heads, rows, rows), low),
            ((2, heads * QK, rows), full),
            ((REACH + 2, heads * KV, rows), full),
            ((LATENT, heads * KV), full),
            ((WIDTH, window), full),
            ((REACH + 2, ROPE, rows), full),
            ((count, rows, rows), low),
            ((count, rows, rows), low),
            pltpu.SemaphoreType.DMA((5,)),
            pltpu.SemaphoreType.DMA((2,)),
        ],
        "attention",
    )(index, doc_ids, *inputs, *kept, *latents)


def permute(value, axis, target):
    count = lax.axis_size(axis)
    pairs = [(s, target(s)) for s in range(count) if 0 <= target(s) < count]
    return lax.ppermute(value, axis, pairs)


def local(kv_latent, queries, grad_out, kv_up_weight, doc_ids):
    ranks = lax.axis_size("ctx")
    position = lax.axis_index("ctx").astype(jnp.int32)
    index, core = position[None], lax.rem(position, 2)
    low, full = jnp.bfloat16, jnp.float32
    docs = doc_ids[None]
    core_heads = kv_up_weight.shape[1] // KV // 2
    heads = min(2, core_heads)
    steps = core_heads // heads

    def own_heads(value, which):
        size = value.shape[1] // 2
        return lax.dynamic_slice_in_dim(value, which * size, size, axis=1)

    def across(value):
        return permute(value, "ctx", lambda s: s ^ 1)

    latent = kv_latent.T
    far = permute(latent, "ctx", lambda s: s + 2)
    mixed = permute(latent, "ctx", lambda s: s + 3 if s % 2 else -1)
    other = across(latent)
    in_place = heads * QK % 128 == 0
    inputs = (
        queries if in_place else own_heads(queries, core),
        grad_out if in_place else own_heads(grad_out, core),
        across(own_heads(queries, 1 - core)),
        across(own_heads(grad_out, 1 - core)),
        kv_up_weight if in_place else own_heads(kv_up_weight, core),
    )
    *kept, starts = local_scores(index, docs, inputs, (latent, other), heads, steps, in_place)
    far, mixed, starts = lax.optimization_barrier((far, mixed, starts))
    swapped = across(far)
    passed = permute(mixed, "ctx", lambda s: -1 if s % 2 else s + 1)

    dq_own, dq_other, keep, send, to_old, to_far, to_swap, mine, to_other = attention(
        index, doc_ids, inputs, (*kept, starts),
        (far, swapped, mixed, passed, latent, other), heads, steps, ranks, in_place,
    )

    from_x = permute(send, "ctx", lambda s: s ^ 2)
    from_swap = across(to_swap)
    from_other = across(to_other)
    from_old = permute(to_old, "ctx", lambda s: s - 1 if s % 2 else -1)
    far_sum = (to_far.astype(full) + from_swap.astype(full)).astype(low)
    old_sum = (to_old.astype(full) + from_old.astype(full)).astype(low)
    from_x, *_ = lax.optimization_barrier((from_x, far_sum, old_sum))
    from_far = permute(far_sum, "ctx", lambda s: s - 2)
    from_mixed = permute(old_sum, "ctx", lambda s: -1 if s % 2 else s - 3)
    plane = (keep.astype(full) + from_x.astype(full)).astype(low)
    total = mine.astype(full) + from_other.astype(full)
    total = total + from_mixed.astype(full) + from_far.astype(full)
    mine = total.astype(low)
    plane, *_ = lax.optimization_barrier((plane, mine))
    columns = [list(range(first, ranks, 4)) for first in range(4)]
    pieces = lax.all_to_all(plane, "ctx", 0, 0, axis_index_groups=columns, tiled=True)
    share = LATENT // ranks
    summed = jnp.sum(pieces.reshape(ranks // 4, 2 * share, -1).astype(full), axis=0)

    def in_order(own, received):
        first = jnp.where(core == 0, own, received)
        second = jnp.where(core == 0, received, own)
        return jnp.concatenate([first, second], axis=1)

    rows_own = lax.dynamic_slice_in_dim(summed, core * share, share, axis=0)
    rows_other = lax.dynamic_slice_in_dim(summed, (1 - core) * share, share, axis=0)
    grad_weight = in_order(rows_own, across(rows_other))
    grad_queries = in_order(dq_own, across(dq_other))

    size = lax.axis_size("head")
    for turn in range(1, size):
        other = lax.ppermute(mine, "head", [(s, (s + turn) % size) for s in range(size)])
        total = total + other.astype(full)
    return grad_queries, total.astype(low).T, grad_weight


def solution(mesh):
    return jax.shard_map(
        local,
        mesh=mesh,
        in_specs=(P("ctx", None), P("ctx", "head"), P("ctx", "head"), P(None, "head"), P()),
        out_specs=(P("ctx", "head"), P("ctx", None), P("ctx", "head")),
        check_vma=False,
    )
```

```python
import functools
import math

import jax
import jax.numpy as jnp
from jax import lax
from jax.experimental import pallas as pl
from jax.experimental.pallas import tpu as pltpu
from jax.sharding import PartitionSpec as P

NOPE = 128
ROPE = 64
VDIM = 128
LATENT = 512
REACH = 3
QK = NOPE + ROPE
KV = NOPE + VDIM
WIDTH = LATENT + ROPE
LANES = 128
PIECE = 256

MASKED = -1e30
FLOOR = -1e20
SCALE = 1.0 / math.sqrt(QK)
SCALE2 = SCALE * math.log2(math.e)

NT = (((1,), (1,)), ((), ()))
NN = (((1,), (0,)), ((), ()))


def dot(a, b, dims=NN):
    return lax.dot_general(a, b, dims, preferred_element_type=jnp.float32)


def head_cols(h, size):
    return slice(h * size, (h + 1) * size)


def fold(value, combine):
    return combine(value.reshape(-1, 8, value.shape[1]), axis=0)


def fold(value, combine):
    return combine(value.reshape(-1, 8, value.shape[1]), axis=0)


def lift(latent, w_ref, k_out, v_out):
    for h in range(w_ref.shape[1] // KV):
        lifted = dot(latent[:, :LATENT], w_ref[:, head_cols(h, KV)]).astype(jnp.bfloat16)
        k_out(h, jnp.concatenate([lifted[:, :NOPE], latent[:, LATENT:]], axis=1))
        v_out(h, lifted[:, NOPE:])


def score_block(key, value, q_ref, do_ref, bounds, run_ref, raw_ref, graw_ref, keep):
    rows = do_ref.shape[0]
    lower, upper = bounds
    index = lax.broadcasted_iota(jnp.int32, (LANES, LANES), 0)
    parts = [slice(r, r + LANES) for r in range(0, rows, LANES)]

    def multiply(h, first):
        cols = slice(first, first + PIECE)
        raw_ref[h, :, cols] = dot(key(h), q_ref[cols, head_cols(h, QK)], NT)
        graw_ref[h, :, cols] = dot(value(h), do_ref[cols, head_cols(h, VDIM)], NT)

    def weigh(h, first):
        for c in range(first, first + PIECE, LANES):
            cols = slice(c, c + LANES)
            high = None
            for part in parts:
                seen = index >= lower[:, cols] - part.start
                if upper is not None:
                    seen = seen & (index <= upper[:, cols] - part.start)
                scores = jnp.where(seen, raw_ref[h, part, cols] * SCALE2, MASKED)
                raw_ref[h, part, cols] = scores
                piece = fold(scores, jnp.max)
                high = piece if high is None else jnp.maximum(high, piece)
            old_top = run_ref[h, 0:1, cols]
            new_top = jnp.maximum(old_top, jnp.max(high, axis=0, keepdims=True))
            mass, cross = 0.0, 0.0
            for part in parts:
                weights = jnp.exp2(raw_ref[h, part, cols] - new_top)
                grads = graw_ref[h, part, cols]
                keep(h, part, cols, weights.astype(jnp.bfloat16), grads.astype(jnp.bfloat16))
                mass = mass + fold(weights, jnp.sum)
                cross = cross + fold(weights * grads, jnp.sum)
            factor = jnp.exp2(old_top - new_top)
            run_ref[h, 0:1, cols] = new_top
            run_ref[h, 1:2, cols] = run_ref[h, 1:2, cols] * factor + jnp.sum(
                mass, axis=0, keepdims=True
            )
            run_ref[h, 2:3, cols] = run_ref[h, 2:3, cols] * factor + jnp.sum(
                cross, axis=0, keepdims=True
            )

    alternate(rows, do_ref.shape[1] // VDIM, multiply, weigh)


def alternate(rows, heads, first, second):
    pieces = [(h, c) for h in range(heads) for c in range(0, rows, PIECE)]
    first(*pieces[0])
    for now, following in zip(pieces, pieces[1:] + [None]):
        if following:
            first(*following)
        second(*now)


def grad_block(kept, key, top, end_ref, q_t, do_t, low_ref, ds_ref, dq_acc, d_acc, r_acc, first_q, first_k):
    def put(ref, part, value, first):
        ref[part, :] = value if first else ref[part, :] + value

    rows = do_t.shape[1]
    heads = do_t.shape[0] // VDIM
    sums = {}

    def weigh(h, first):
        for c in range(first, first + PIECE, LANES):
            cols = slice(c, c + LANES)
            factor = jnp.exp2(top(h)[:, cols] - end_ref[h, 0:1, cols]) * end_ref[h, 1:2, cols]
            delta = end_ref[h, 2:3, cols]
            for r in range(0, rows, LANES):
                part = slice(r, r + LANES)
                weights, grads = kept(h, part, cols)
                probs = weights.astype(jnp.float32) * factor
                low_ref[h, part, cols] = probs.astype(jnp.bfloat16)
                ds_ref[h, part, cols] = (
                    probs * (grads.astype(jnp.float32) - delta)
                ).astype(jnp.bfloat16)

    def multiply(h, first):
        cols = slice(first, first + PIECE)
        low, dscore = low_ref[h, :, cols], ds_ref[h, :, cols]
        dvalue = dot(do_t[head_cols(h, VDIM), cols], low, NT)
        dkey = dot(q_t[head_cols(h, QK), cols], dscore, NT)
        own = head_cols(h, QK)
        dq = dot(key(h).T, dscore)
        dq_acc[own, cols] = dq if first_q else dq_acc[own, cols] + dq
        if first:
            dvalue, dkey = sums[h][0] + dvalue, sums[h][1] + dkey
        sums[h] = dvalue, dkey
        if first + PIECE == rows:
            dkey = dkey * SCALE
            put(d_acc, slice(h * KV, h * KV + NOPE), dkey[:NOPE], first_k)
            put(d_acc, slice(h * KV + NOPE, (h + 1) * KV), dvalue, first_k)
            put(r_acc, slice(0, ROPE), dkey[NOPE:], first_k and h == 0)

    alternate(rows, heads, weigh, multiply)


def start_stats(run_ref):
    count, rows = run_ref.shape[0], run_ref.shape[2]
    for h in range(count):
        run_ref[h, 0:1, :] = jnp.full((1, rows), FLOOR, jnp.float32)
        run_ref[h, 1:8, :] = jnp.zeros((7, rows), jnp.float32)


def chip_place(index_ref):
    core = lax.rem(index_ref[0], 2)
    return core, index_ref[0] - core


def order_pair(out_ref, core, own, other):
    out_ref[core] = own[...]
    out_ref[1 - core] = other[...]


LOCAL = ((1, REACH), (0, REACH), (1, REACH + 1))


def query_bounds(start_ref, chip, j, t, rows):
    lower = start_ref[j, 0:1, :] - (chip + t - REACH) * rows
    own = isinstance(t, int) and t == j + REACH
    return lower, lax.broadcasted_iota(jnp.int32, (1, rows), 1) if own else None


def find_starts(docs_ref, start_ref, chip, rows):
    for j in range(2):
        block = chip + j
        my_docs = docs_ref[:, pl.ds(pl.multiple_of(block * rows, rows), rows)]
        first_doc = my_docs[:, :1]
        key_docs = jnp.broadcast_to(my_docs, (128, rows)).T[:, :1]
        inside = jnp.sum(jnp.where(key_docs < my_docs, 1.0, 0.0), axis=0, keepdims=True)
        before = jnp.zeros((1, rows), jnp.float32)
        for back in range(1, REACH + 1):
            earlier = jnp.maximum(block - back, 0)
            docs = docs_ref[:, pl.ds(pl.multiple_of(earlier * rows, rows), rows)]
            same = (docs == first_doc) & (block >= back)
            before = before + jnp.where(same, 1.0, 0.0)
        before = jnp.sum(before, axis=1, keepdims=True)
        start = jnp.where(my_docs == first_doc, -before, inside).astype(jnp.int32)
        start_ref[j, 0:1, :] = start + block * rows


def local_kernel(
    index_ref, docs_ref, q0, do0, q1, do1, w_ref, lat0, lat1,
    e_ref, g_ref, k_ref, run_ref, top_ref, start_ref,
    q_ref, do_ref, lat_ref, v_ref, raw_ref, graw_ref,
):
    rows = q0.shape[0]
    core, chip = chip_place(index_ref)
    heads = w_ref.shape[1] // KV

    @pl.when(pl.program_id(0) == 0)
    def _():
        lat_ref[core] = lat0[...].T
        lat_ref[1 - core] = lat1[...].T
        find_starts(docs_ref, start_ref, chip, rows)

    order_pair(q_ref, core, q0, q1)
    order_pair(do_ref, core, do0, do1)
    for j in range(2):

        def k_out(h, key):
            k_ref[0, j * heads + h] = key

        def v_out(h, value):
            v_ref[j * heads + h] = value

        lift(lat_ref[j], w_ref, k_out, v_out)
        start_stats(run_ref.at[0, pl.ds(j * heads, heads)])
    for n, (j, t) in enumerate(LOCAL):
        slot = t - REACH

        def keep(h, part, cols, weights, grads):
            e_ref[0, n * heads + h, part, cols] = weights
            g_ref[0, n * heads + h, part, cols] = grads

        run = run_ref.at[0, pl.ds(j * heads, heads)]
        score_block(
            lambda h: k_ref[0, slot * heads + h], lambda h: v_ref[slot * heads + h],
            q_ref.at[j], do_ref.at[j], query_bounds(start_ref, chip, j, t, rows), run,
            raw_ref, graw_ref, keep,
        )
        for h in range(heads):
            top_ref[0, n * heads + h] = run[h]


def main_kernel(
    ranks,
    index_ref, docs_sref, q0, do0, q1, do1, w_ref,
    all_e, all_g, local_k, local_run, local_top, start_ref,
    lat_far, lat_swap, lat_mixed, lat_passed, lat_own, lat_other,
    dq0_ref, dq1_ref, keep_ref, send_ref, x_old, x_far, x_swap, x_own, x_other,
    q_ref, do_ref, lat_ref, lat_t_ref, e_ref, g_ref, k_ref, v_ref, top_ref,
    run_ref, end_ref, raw_ref, graw_ref, low_ref, ds_ref, dq_acc, d_acc, gw_acc, x_acc,
    r_acc, local_e, local_g, sems, kept_sems,
):
    step = pl.program_id(0)
    rows = q0.shape[0]
    heads = w_ref.shape[1] // KV
    blocks = REACH + 2
    kept_copies = [
        pltpu.make_async_copy(all_e.at[step], local_e, kept_sems.at[0]),
        pltpu.make_async_copy(all_g.at[step], local_g, kept_sems.at[1]),
    ]
    for copy in kept_copies:
        copy.start()
    core, chip = chip_place(index_ref)

    def active(j, t):
        block = chip + t - REACH
        last_doc = docs_sref[jnp.maximum(block, 0) * rows + rows - 1]
        return (block >= 0) & (last_doc >= docs_sref[(chip + j) * rows])

    def block_rows(t):
        return pl.ds(pl.multiple_of(t * rows, rows), rows)

    def piece_rows(t, part):
        size = part.stop - part.start
        return pl.ds(pl.multiple_of(t * rows + part.start, size), size)

    def loop(first, last, when, body):
        def visit(t, carry):
            @pl.when(when(t))
            def _():
                body(t)

            return carry

        lax.fori_loop(first, last, visit, 0)

    @pl.when(step == 0)
    def _():
        places = [(lat_far, 1 + core), (lat_swap, 2 - core), (lat_own, REACH + core),
                  (lat_other, REACH + 1 - core)]
        copies = [
            pltpu.make_async_copy(source, lat_t_ref.at[:, block_rows(t)], sems.at[i])
            for i, (source, t) in enumerate(places)
        ]
        first = lat_t_ref.at[:, block_rows(0)]
        oldest = pltpu.make_async_copy(lat_mixed, first, sems.at[4])
        passed = pltpu.make_async_copy(lat_passed, first, sems.at[4])
        for copy in copies:
            copy.start()
        pl.when(core == 0)(oldest.start)
        pl.when(core == 1)(passed.start)
        for copy in copies:
            copy.wait()
        oldest.wait()
        for t in range(REACH):
            part = slice(t * rows, (t + 1) * rows)
            lat_ref[part, :] = lat_t_ref[:, part].T

    order_pair(q_ref, core, q0, q1)
    order_pair(do_ref, core, do0, do1)

    def lift_block(t):
        def k_out(h, key):
            k_ref[h, block_rows(t), :] = key

        def v_out(h, value):
            v_ref[h, block_rows(t), :] = value

        lift(lat_ref[block_rows(t), :], w_ref, k_out, v_out)

    loop(0, REACH, lambda t: active(0, t), lift_block)

    for j in range(2):
        for h in range(heads):
            run_ref[h] = local_run[0, j * heads + h]

        def first_pass(t):
            def keep(h, part, cols, weights, grads):
                e_ref[h, piece_rows(t, part), cols] = weights
                g_ref[h, piece_rows(t, part), cols] = grads

            score_block(
                lambda h: k_ref[h, block_rows(t), :], lambda h: v_ref[h, block_rows(t), :],
                q_ref.at[j], do_ref.at[j], query_bounds(start_ref, chip, j, t, rows), run_ref,
                raw_ref, graw_ref, keep,
            )
            for h in range(heads):
                top_ref[h, t] = run_ref[h]

        loop(j, REACH, lambda t: active(j, t), first_pass)
        for h in range(heads):
            inverse = 1.0 / run_ref[h, 1:2, :]
            end_ref[h, 0:1, :] = run_ref[h, 0:1, :]
            end_ref[h, 1:2, :] = inverse
            end_ref[h, 2:3, :] = run_ref[h, 2:3, :] * inverse
        q_t, do_t = q_ref[j].T, do_ref[j].T

        def add(t, kept, key, top, first_q, first_k):
            grad_block(
                kept, key, top, end_ref, q_t, do_t, low_ref, ds_ref, dq_acc.at[j], d_acc.at[t],
                r_acc.at[t], first_q, first_k,
            )

        def second_pass(t):
            def kept(h, part, cols):
                return e_ref[h, piece_rows(t, part), cols], g_ref[h, piece_rows(t, part), cols]

            add(
                t, kept, lambda h: k_ref[h, block_rows(t), :], lambda h: top_ref[h, t, 0:1, :],
                False, j == 0,
            )

        if j == 0:
            for copy in kept_copies:
                copy.wait()
        first_q = True
        for n, (query, t) in enumerate(LOCAL):
            if query == j:
                add(
                    t,
                    lambda h, part, cols: (
                        local_e[n * heads + h, part, cols], local_g[n * heads + h, part, cols]
                    ),
                    lambda h: local_k[0, (t - REACH) * heads + h],
                    lambda h: local_top[0, n * heads + h, 0:1, :],
                    first_q, t == REACH + j,
                )
                first_q = False
        loop(j, REACH, lambda t: active(j, t), second_pass)

    def seen(t):
        return (t >= REACH) | active(0, t)

    def project(t, first):
        part = block_rows(t)
        grads = d_acc[t].astype(jnp.bfloat16)
        weight_part = dot(lat_t_ref[:LATENT, part], grads, NT)
        gw_acc[...] = weight_part if first else gw_acc[...] + weight_part
        latent_part = dot(w_ref[...], grads)

        @pl.when(step == 0)
        def _():
            x_acc[:LATENT, part] = latent_part
            x_acc[LATENT:, part] = r_acc[t]

        @pl.when(step > 0)
        def _():
            x_acc[:LATENT, part] += latent_part
            x_acc[LATENT:, part] += r_acc[t]

    @pl.when(step == 0)
    def _():
        def clear(t):
            x_acc[:, block_rows(t)] = jnp.zeros((WIDTH, rows), jnp.float32)

        loop(0, REACH, lambda t: ~seen(t), clear)

    project(REACH, True)
    loop(0, blocks, lambda t: seen(t) & (t != REACH), lambda t: project(t, False))
    dq0_ref[...] = (dq_acc[core] * SCALE).T.astype(dq0_ref.dtype)
    dq1_ref[...] = (dq_acc[1 - core] * SCALE).T.astype(dq1_ref.dtype)

    share = 2 * (LATENT // ranks)
    own_x = lax.rem(index_ref[0] // 2, 2)
    for i in range(ranks // 4):
        for out, x in ((keep_ref, own_x), (send_ref, 1 - own_x)):
            source = pl.multiple_of((2 * i + x) * share, share)
            out[i * share : (i + 1) * share, :] = gw_acc[pl.ds(source, share), :].astype(out.dtype)

    @pl.when(step == pl.num_programs(0) - 1)
    def _():
        places = ((x_old, 0), (x_far, 1 + core), (x_swap, 2 - core), (x_own, REACH + core),
                  (x_other, REACH + 1 - core))
        copies = []
        for i, (out, t) in enumerate(places):
            part = block_rows(t)
            lat_t_ref[:, part] = x_acc[:, part].astype(lat_t_ref.dtype)
            copies.append(pltpu.make_async_copy(lat_t_ref.at[:, part], out, sems.at[i]))
            copies[-1].start()
        for copy in copies:
            copy.wait()


def step_cols(height, size):
    return pl.BlockSpec((height, size), lambda i, index: (0, i))


def core_cols(height, size, first):
    def place(i, index):
        return (0, first(i, lax.rem(index[0], 2)))

    return pl.BlockSpec((height, size), place)


def step_block(*shape):
    return pl.BlockSpec((1, *shape), lambda i, index: (i, 0, 0, 0))


def fixed(*shape):
    return pl.BlockSpec(shape, lambda i, index: (0,) * len(shape))


SCALARS = pl.BlockSpec(memory_space=pltpu.SMEM)
ANYWHERE = pl.BlockSpec(memory_space=pl.ANY)


def call(body, steps, flops, in_specs, outs, scratch, name):
    return pl.pallas_call(
        body,
        grid_spec=pltpu.PrefetchScalarGridSpec(
            num_scalar_prefetch=1,
            grid=(steps,),
            in_specs=in_specs,
            out_specs=[spec for spec, _, _ in outs],
            scratch_shapes=[
                pltpu.VMEM(*entry) if isinstance(entry, tuple) else entry for entry in scratch
            ],
        ),
        out_shape=[jax.ShapeDtypeStruct(shape, kind) for _, shape, kind in outs],
        compiler_params=pltpu.CompilerParams(
            dimension_semantics=("arbitrary",), vmem_limit_bytes=58 * 1024 * 1024
        ),
        cost_estimate=pl.CostEstimate(
            flops=flops, bytes_accessed=16 * 1024 * 1024, transcendentals=0
        ),
        name=name,
    )


def head_specs(rows, heads, steps, in_place):
    def received(i, core):
        return i

    def own(i, core):
        return core * steps + i if in_place else i

    return [
        core_cols(rows, heads * QK, own), core_cols(rows, heads * VDIM, own),
        core_cols(rows, heads * QK, received), core_cols(rows, heads * VDIM, received),
        core_cols(LATENT, heads * KV, own),
    ]


def local_scores(index, docs, inputs, latents, heads, steps, in_place):
    rows = inputs[0].shape[0]
    low, full = jnp.bfloat16, jnp.float32
    count = len(LOCAL) * heads
    return call(
        local_kernel,
        steps,
        steps * heads * rows * rows,
        [
            fixed(1, docs.shape[1]), *head_specs(rows, heads, steps, in_place),
            fixed(WIDTH, rows), fixed(WIDTH, rows),
        ],
        [
            (step_block(count, rows, rows), (steps, count, rows, rows), low),
            (step_block(count, rows, rows), (steps, count, rows, rows), low),
            (step_block(2 * heads, rows, QK), (steps, 2 * heads, rows, QK), low),
            (step_block(2 * heads, 8, rows), (steps, 2 * heads, 8, rows), full),
            (step_block(count, 8, rows), (steps, count, 8, rows), full),
            (fixed(2, 8, rows), (2, 8, rows), jnp.int32),
        ],
        [
            ((2, rows, heads * QK), low),
            ((2, rows, heads * VDIM), low),
            ((2, rows, WIDTH), low),
            ((2 * heads, rows, VDIM), low),
            ((heads, rows, rows), full),
            ((heads, rows, rows), full),
        ],
        "local_scores",
    )(index, docs, *inputs, *latents)


def attention(index, doc_ids, inputs, kept, latents, heads, steps, ranks, in_place):
    rows = inputs[0].shape[0]
    low, full = jnp.bfloat16, jnp.float32
    count = len(LOCAL) * heads
    window = (REACH + 2) * rows
    far = REACH * rows
    half = (LATENT // 2, steps * heads * KV)
    return call(
        functools.partial(main_kernel, ranks),
        steps,
        2 * steps * heads * rows * rows * (5 * (QK + VDIM) + 8 * (2 * QK + VDIM) + 13 * KV),
        [
            SCALARS, *head_specs(rows, heads, steps, in_place), ANYWHERE, ANYWHERE,
            step_block(2 * heads, rows, QK), step_block(2 * heads, 8, rows),
            step_block(count, 8, rows), fixed(2, 8, rows),
        ]
        + [ANYWHERE] * len(latents),
        [(step_cols(rows, heads * QK), (rows, steps * heads * QK), low)] * 2
        + [(step_cols(LATENT // 2, heads * KV), half, low)] * 2
        + [(ANYWHERE, (WIDTH, rows), low)] * (REACH + 2),
        [
            ((2, rows, heads * QK), low),
            ((2, rows, heads * VDIM), low),
            ((far, WIDTH), low),
            ((WIDTH, window), low),
            ((heads, far, rows), low),
            ((heads, far, rows), low),
            ((heads, far, QK), low),
            ((heads, far, VDIM), low),
            ((heads, REACH, 8, rows), full),
            ((heads, 8, rows), full),
            ((heads, 8, rows), full),
            ((heads, rows, rows), full),
            ((heads, rows, rows), full),
            ((heads, rows, rows), low),
            ((heads, rows, rows), low),
            ((2, heads * QK, rows), full),
            ((REACH + 2, heads * KV, rows), full),
            ((LATENT, heads * KV), full),
            ((WIDTH, window), full),
            ((REACH + 2, ROPE, rows), full),
            ((count, rows, rows), low),
            ((count, rows, rows), low),
            pltpu.SemaphoreType.DMA((5,)),
            pltpu.SemaphoreType.DMA((2,)),
        ],
        "attention",
    )(index, doc_ids, *inputs, *kept, *latents)


def permute(value, axis, target):
    count = lax.axis_size(axis)
    pairs = [(s, target(s)) for s in range(count) if 0 <= target(s) < count]
    return lax.ppermute(value, axis, pairs)


def local(kv_latent, queries, grad_out, kv_up_weight, doc_ids):
    ranks = lax.axis_size("ctx")
    position = lax.axis_index("ctx").astype(jnp.int32)
    index, core = position[None], lax.rem(position, 2)
    low, full = jnp.bfloat16, jnp.float32
    docs = doc_ids[None]
    core_heads = kv_up_weight.shape[1] // KV // 2
    heads = min(2, core_heads)
    steps = core_heads // heads

    def own_heads(value, which):
        size = value.shape[1] // 2
        return lax.dynamic_slice_in_dim(value, which * size, size, axis=1)

    def across(value):
        return permute(value, "ctx", lambda s: s ^ 1)

    latent = kv_latent.T
    far = permute(latent, "ctx", lambda s: s + 2)
    mixed = permute(latent, "ctx", lambda s: s + 3 if s % 2 else -1)
    other = across(latent)
    in_place = heads * QK % 128 == 0
    inputs = (
        queries if in_place else own_heads(queries, core),
        grad_out if in_place else own_heads(grad_out, core),
        across(own_heads(queries, 1 - core)),
        across(own_heads(grad_out, 1 - core)),
        kv_up_weight if in_place else own_heads(kv_up_weight, core),
    )
    *kept, starts = local_scores(index, docs, inputs, (latent, other), heads, steps, in_place)
    far, mixed, starts = lax.optimization_barrier((far, mixed, starts))
    swapped = across(far)
    passed = permute(mixed, "ctx", lambda s: -1 if s % 2 else s + 1)

    dq_own, dq_other, keep, send, to_old, to_far, to_swap, mine, to_other = attention(
        index, doc_ids, inputs, (*kept, starts),
        (far, swapped, mixed, passed, latent, other), heads, steps, ranks, in_place,
    )

    head, head_count = lax.axis_index("head"), lax.axis_size("head")
    share = WIDTH // head_count

    def turned(value, turn):
        turns = [(s, (s + turn) % head_count) for s in range(head_count)]
        return lax.ppermute(value, "head", turns)

    def head_share(value):
        def rows_of(which):
            return lax.dynamic_slice_in_dim(value, which * share, share, axis=0)

        total = rows_of(head).astype(full)
        for turn in range(1, head_count):
            target = lax.rem(head + turn, head_count)
            total = total + turned(rows_of(target), turn).astype(full)
        return total

    from_x = permute(send, "ctx", lambda s: s ^ 2)
    from_swap = across(to_swap)
    from_old = permute(to_old, "ctx", lambda s: s - 1 if s % 2 else -1)
    from_other = across(to_other)
    far_sum = head_share((to_far.astype(full) + from_swap.astype(full)).astype(low)).astype(low)
    old_sum = head_share((to_old.astype(full) + from_old.astype(full)).astype(low)).astype(low)
    from_far = permute(far_sum, "ctx", lambda s: s - 2)
    from_mixed = permute(old_sum, "ctx", lambda s: -1 if s % 2 else s - 3)
    total = head_share((mine.astype(full) + from_other.astype(full)).astype(low))

    from_x, *_ = lax.optimization_barrier((from_x, far_sum, old_sum))
    plane = (keep.astype(full) + from_x.astype(full)).astype(low)
    columns = [list(range(first, ranks, 4)) for first in range(4)]
    pieces = lax.all_to_all(plane, "ctx", 0, 0, axis_index_groups=columns, tiled=True)
    rows = LATENT // ranks
    summed = jnp.sum(pieces.reshape(ranks // 4, 2 * rows, -1).astype(full), axis=0)

    def in_order(own, received):
        first = jnp.where(core == 0, own, received)
        second = jnp.where(core == 0, received, own)
        return jnp.concatenate([first, second], axis=1)

    rows_own = lax.dynamic_slice_in_dim(summed, core * rows, rows, axis=0)
    rows_other = lax.dynamic_slice_in_dim(summed, (1 - core) * rows, rows, axis=0)
    grad_weight = in_order(rows_own, across(rows_other))
    grad_queries = in_order(dq_own, across(dq_other))

    total = (total + from_mixed.astype(full) + from_far.astype(full)).astype(low)
    shares = [total] + [turned(total, turn) for turn in range(1, head_count)]
    ordered = []
    for place in range(head_count):
        picked = shares[0]
        for turn in range(1, head_count):
            picked = jnp.where(lax.rem(head - place + head_count, head_count) == turn, shares[turn], picked)
        ordered.append(picked)
    return grad_queries, jnp.concatenate(ordered, axis=0).T, grad_weight


def solution(mesh):
    return jax.shard_map(
        local,
        mesh=mesh,
        in_specs=(P("ctx", None), P("ctx", "head"), P("ctx", "head"), P(None, "head"), P()),
        out_specs=(P("ctx", "head"), P("ctx", None), P("ctx", "head")),
        check_vma=False,
    )
```

```python
import functools
import math

import jax
import jax.numpy as jnp
from jax import lax
from jax.experimental import pallas as pl
from jax.experimental.pallas import tpu as pltpu
from jax.sharding import PartitionSpec as P

NOPE = 128
ROPE = 64
VDIM = 128
LATENT = 512
REACH = 3
QK = NOPE + ROPE
KV = NOPE + VDIM
WIDTH = LATENT + ROPE
LANES = 128
PIECE = 256

MASKED = -1e30
FLOOR = -1e20
SCALE = 1.0 / math.sqrt(QK)
SCALE2 = SCALE * math.log2(math.e)

NT = (((1,), (1,)), ((), ()))
NN = (((1,), (0,)), ((), ()))


def dot(a, b, dims=NN):
    return lax.dot_general(a, b, dims, preferred_element_type=jnp.float32)


def head_cols(h, size):
    return slice(h * size, (h + 1) * size)


def fold(value, combine):
    return combine(value.reshape(-1, 8, value.shape[1]), axis=0)


def fold(value, combine):
    return combine(value.reshape(-1, 8, value.shape[1]), axis=0)


def lift(latent, w_ref, k_out, v_out):
    for h in range(w_ref.shape[1] // KV):
        lifted = dot(latent[:, :LATENT], w_ref[:, head_cols(h, KV)]).astype(jnp.bfloat16)
        k_out(h, jnp.concatenate([lifted[:, :NOPE], latent[:, LATENT:]], axis=1))
        v_out(h, lifted[:, NOPE:])


def score_block(key, value, q_ref, do_ref, bounds, run_ref, raw_ref, graw_ref, keep):
    rows = do_ref.shape[0]
    lower, upper = bounds
    index = lax.broadcasted_iota(jnp.int32, (LANES, LANES), 0)
    parts = [slice(r, r + LANES) for r in range(0, rows, LANES)]

    def multiply(h, first):
        cols = slice(first, first + PIECE)
        raw_ref[h, :, cols] = dot(key(h), q_ref[cols, head_cols(h, QK)], NT)
        graw_ref[h, :, cols] = dot(value(h), do_ref[cols, head_cols(h, VDIM)], NT)

    def weigh(h, first):
        for c in range(first, first + PIECE, LANES):
            cols = slice(c, c + LANES)
            high = None
            for part in parts:
                seen = index >= lower[:, cols] - part.start
                if upper is not None:
                    seen = seen & (index <= upper[:, cols] - part.start)
                scores = jnp.where(seen, raw_ref[h, part, cols] * SCALE2, MASKED)
                raw_ref[h, part, cols] = scores
                piece = fold(scores, jnp.max)
                high = piece if high is None else jnp.maximum(high, piece)
            old_top = run_ref[h, 0:1, cols]
            new_top = jnp.maximum(old_top, jnp.max(high, axis=0, keepdims=True))
            mass, cross = 0.0, 0.0
            for part in parts:
                weights = jnp.exp2(raw_ref[h, part, cols] - new_top)
                grads = graw_ref[h, part, cols]
                keep(h, part, cols, weights.astype(jnp.bfloat16), grads.astype(jnp.bfloat16))
                mass = mass + fold(weights, jnp.sum)
                cross = cross + fold(weights * grads, jnp.sum)
            factor = jnp.exp2(old_top - new_top)
            run_ref[h, 0:1, cols] = new_top
            run_ref[h, 1:2, cols] = run_ref[h, 1:2, cols] * factor + jnp.sum(
                mass, axis=0, keepdims=True
            )
            run_ref[h, 2:3, cols] = run_ref[h, 2:3, cols] * factor + jnp.sum(
                cross, axis=0, keepdims=True
            )

    alternate(rows, do_ref.shape[1] // VDIM, multiply, weigh)


def alternate(rows, heads, first, second):
    pieces = [(h, c) for h in range(heads) for c in range(0, rows, PIECE)]
    first(*pieces[0])
    for now, following in zip(pieces, pieces[1:] + [None]):
        if following:
            first(*following)
        second(*now)


def grad_block(kept, key, top, end_ref, q_t, do_t, low_ref, ds_ref, dq_acc, d_acc, r_acc, first_q, first_k):
    def put(ref, part, value, first):
        ref[part, :] = value if first else ref[part, :] + value

    rows = do_t.shape[1]
    heads = do_t.shape[0] // VDIM
    sums = {}

    def weigh(h, first):
        for c in range(first, first + PIECE, LANES):
            cols = slice(c, c + LANES)
            factor = jnp.exp2(top(h)[:, cols] - end_ref[h, 0:1, cols]) * end_ref[h, 1:2, cols]
            delta = end_ref[h, 2:3, cols]
            for r in range(0, rows, LANES):
                part = slice(r, r + LANES)
                weights, grads = kept(h, part, cols)
                probs = weights.astype(jnp.float32) * factor
                low_ref[h, part, cols] = probs.astype(jnp.bfloat16)
                ds_ref[h, part, cols] = (
                    probs * (grads.astype(jnp.float32) - delta)
                ).astype(jnp.bfloat16)

    def multiply(h, first):
        cols = slice(first, first + PIECE)
        low, dscore = low_ref[h, :, cols], ds_ref[h, :, cols]
        dvalue = dot(do_t[head_cols(h, VDIM), cols], low, NT)
        dkey = dot(q_t[head_cols(h, QK), cols], dscore, NT)
        own = head_cols(h, QK)
        dq = dot(key(h).T, dscore)
        dq_acc[own, cols] = dq if first_q else dq_acc[own, cols] + dq
        if first:
            dvalue, dkey = sums[h][0] + dvalue, sums[h][1] + dkey
        sums[h] = dvalue, dkey
        if first + PIECE == rows:
            dkey = dkey * SCALE
            put(d_acc, slice(h * KV, h * KV + NOPE), dkey[:NOPE], first_k)
            put(d_acc, slice(h * KV + NOPE, (h + 1) * KV), dvalue, first_k)
            put(r_acc, slice(0, ROPE), dkey[NOPE:], first_k and h == 0)

    alternate(rows, heads, weigh, multiply)


def start_stats(run_ref):
    count, rows = run_ref.shape[0], run_ref.shape[2]
    for h in range(count):
        run_ref[h, 0:1, :] = jnp.full((1, rows), FLOOR, jnp.float32)
        run_ref[h, 1:8, :] = jnp.zeros((7, rows), jnp.float32)


def chip_place(index_ref):
    core = lax.rem(index_ref[0], 2)
    return core, index_ref[0] - core


def order_pair(out_ref, core, own, other):
    out_ref[core] = own[...]
    out_ref[1 - core] = other[...]


LOCAL = ((1, REACH), (0, REACH), (1, REACH + 1))


def query_bounds(start_ref, chip, j, t, rows):
    lower = start_ref[j, 0:1, :] - (chip + t - REACH) * rows
    own = isinstance(t, int) and t == j + REACH
    return lower, lax.broadcasted_iota(jnp.int32, (1, rows), 1) if own else None


def find_starts(docs_ref, start_ref, chip, rows):
    for j in range(2):
        block = chip + j
        my_docs = docs_ref[:, pl.ds(pl.multiple_of(block * rows, rows), rows)]
        first_doc = my_docs[:, :1]
        key_docs = jnp.broadcast_to(my_docs, (128, rows)).T[:, :1]
        inside = jnp.sum(jnp.where(key_docs < my_docs, 1.0, 0.0), axis=0, keepdims=True)
        before = jnp.zeros((1, rows), jnp.float32)
        for back in range(1, REACH + 1):
            earlier = jnp.maximum(block - back, 0)
            docs = docs_ref[:, pl.ds(pl.multiple_of(earlier * rows, rows), rows)]
            same = (docs == first_doc) & (block >= back)
            before = before + jnp.where(same, 1.0, 0.0)
        before = jnp.sum(before, axis=1, keepdims=True)
        start = jnp.where(my_docs == first_doc, -before, inside).astype(jnp.int32)
        start_ref[j, 0:1, :] = start + block * rows


def local_kernel(
    index_ref, docs_ref, q0, do0, q1, do1, w_ref, lat0, lat1,
    e_ref, g_ref, k_ref, run_ref, top_ref, start_ref,
    q_ref, do_ref, lat_ref, v_ref, raw_ref, graw_ref,
):
    rows = q0.shape[0]
    core, chip = chip_place(index_ref)
    heads = w_ref.shape[1] // KV

    @pl.when(pl.program_id(0) == 0)
    def _():
        lat_ref[core] = lat0[...].T
        lat_ref[1 - core] = lat1[...].T
        find_starts(docs_ref, start_ref, chip, rows)

    order_pair(q_ref, core, q0, q1)
    order_pair(do_ref, core, do0, do1)
    for j in range(2):

        def k_out(h, key):
            k_ref[0, j * heads + h] = key

        def v_out(h, value):
            v_ref[j * heads + h] = value

        lift(lat_ref[j], w_ref, k_out, v_out)
        start_stats(run_ref.at[0, pl.ds(j * heads, heads)])
    for n, (j, t) in enumerate(LOCAL):
        slot = t - REACH

        def keep(h, part, cols, weights, grads):
            e_ref[0, n * heads + h, part, cols] = weights
            g_ref[0, n * heads + h, part, cols] = grads

        run = run_ref.at[0, pl.ds(j * heads, heads)]
        score_block(
            lambda h: k_ref[0, slot * heads + h], lambda h: v_ref[slot * heads + h],
            q_ref.at[j], do_ref.at[j], query_bounds(start_ref, chip, j, t, rows), run,
            raw_ref, graw_ref, keep,
        )
        for h in range(heads):
            top_ref[0, n * heads + h] = run[h]


def main_kernel(
    ranks,
    index_ref, docs_sref, q0, do0, q1, do1, w_ref,
    all_e, all_g, local_k, local_run, local_top, start_ref,
    lat_far, lat_swap, lat_mixed, lat_passed, lat_own, lat_other,
    dq0_ref, dq1_ref, keep_ref, send_ref, x_old, x_far, x_swap, x_own, x_other,
    q_ref, do_ref, lat_ref, lat_t_ref, e_ref, g_ref, k_ref, v_ref, top_ref,
    run_ref, end_ref, raw_ref, graw_ref, low_ref, ds_ref, dq_acc, d_acc, gw_acc, x_acc,
    r_acc, local_e, local_g, sems, kept_sems,
):
    step = pl.program_id(0)
    rows = q0.shape[0]
    heads = w_ref.shape[1] // KV
    blocks = REACH + 2
    kept_copies = [
        pltpu.make_async_copy(all_e.at[step], local_e, kept_sems.at[0]),
        pltpu.make_async_copy(all_g.at[step], local_g, kept_sems.at[1]),
    ]
    for copy in kept_copies:
        copy.start()
    core, chip = chip_place(index_ref)

    def active(j, t):
        block = chip + t - REACH
        last_doc = docs_sref[jnp.maximum(block, 0) * rows + rows - 1]
        return (block >= 0) & (last_doc >= docs_sref[(chip + j) * rows])

    def block_rows(t):
        return pl.ds(pl.multiple_of(t * rows, rows), rows)

    def piece_rows(t, part):
        size = part.stop - part.start
        return pl.ds(pl.multiple_of(t * rows + part.start, size), size)

    def loop(first, last, when, body):
        def visit(t, carry):
            @pl.when(when(t))
            def _():
                body(t)

            return carry

        lax.fori_loop(first, last, visit, 0)

    @pl.when(step == 0)
    def _():
        places = [(lat_far, 1 + core), (lat_swap, 2 - core), (lat_own, REACH + core),
                  (lat_other, REACH + 1 - core)]
        copies = [
            pltpu.make_async_copy(source, lat_t_ref.at[:, block_rows(t)], sems.at[i])
            for i, (source, t) in enumerate(places)
        ]
        first = lat_t_ref.at[:, block_rows(0)]
        oldest = pltpu.make_async_copy(lat_mixed, first, sems.at[4])
        passed = pltpu.make_async_copy(lat_passed, first, sems.at[4])
        for copy in copies:
            copy.start()
        pl.when(core == 0)(oldest.start)
        pl.when(core == 1)(passed.start)
        for copy in copies:
            copy.wait()
        oldest.wait()
        for t in range(REACH):
            part = slice(t * rows, (t + 1) * rows)
            lat_ref[part, :] = lat_t_ref[:, part].T

    order_pair(q_ref, core, q0, q1)
    order_pair(do_ref, core, do0, do1)

    def lift_block(t):
        def k_out(h, key):
            k_ref[h, block_rows(t), :] = key

        def v_out(h, value):
            v_ref[h, block_rows(t), :] = value

        lift(lat_ref[block_rows(t), :], w_ref, k_out, v_out)

    loop(0, REACH, lambda t: active(0, t), lift_block)

    for j in range(2):
        for h in range(heads):
            run_ref[h] = local_run[0, j * heads + h]

        def first_pass(t):
            def keep(h, part, cols, weights, grads):
                e_ref[h, piece_rows(t, part), cols] = weights
                g_ref[h, piece_rows(t, part), cols] = grads

            score_block(
                lambda h: k_ref[h, block_rows(t), :], lambda h: v_ref[h, block_rows(t), :],
                q_ref.at[j], do_ref.at[j], query_bounds(start_ref, chip, j, t, rows), run_ref,
                raw_ref, graw_ref, keep,
            )
            for h in range(heads):
                top_ref[h, t] = run_ref[h]

        loop(j, REACH, lambda t: active(j, t), first_pass)
        for h in range(heads):
            inverse = 1.0 / run_ref[h, 1:2, :]
            end_ref[h, 0:1, :] = run_ref[h, 0:1, :]
            end_ref[h, 1:2, :] = inverse
            end_ref[h, 2:3, :] = run_ref[h, 2:3, :] * inverse
        q_t, do_t = q_ref[j].T, do_ref[j].T

        def add(t, kept, key, top, first_q, first_k):
            grad_block(
                kept, key, top, end_ref, q_t, do_t, low_ref, ds_ref, dq_acc.at[j], d_acc.at[t],
                r_acc.at[t], first_q, first_k,
            )

        def second_pass(t):
            def kept(h, part, cols):
                return e_ref[h, piece_rows(t, part), cols], g_ref[h, piece_rows(t, part), cols]

            add(
                t, kept, lambda h: k_ref[h, block_rows(t), :], lambda h: top_ref[h, t, 0:1, :],
                False, j == 0,
            )

        if j == 0:
            for copy in kept_copies:
                copy.wait()
        first_q = True
        for n, (query, t) in enumerate(LOCAL):
            if query == j:
                add(
                    t,
                    lambda h, part, cols: (
                        local_e[n * heads + h, part, cols], local_g[n * heads + h, part, cols]
                    ),
                    lambda h: local_k[0, (t - REACH) * heads + h],
                    lambda h: local_top[0, n * heads + h, 0:1, :],
                    first_q, t == REACH + j,
                )
                first_q = False
        loop(j, REACH, lambda t: active(j, t), second_pass)

    def seen(t):
        return (t >= REACH) | active(0, t)

    last = step == pl.num_programs(0) - 1
    outs = ((x_old, x_old), (x_far, x_swap), (x_swap, x_far), (x_own, x_other), (x_other, x_own))

    def out_copies(t):
        part = slice(t * rows, (t + 1) * rows)
        return [pltpu.make_async_copy(lat_t_ref.at[:, part], out, sems.at[t]) for out in outs[t]]

    def leave(t):
        part = slice(t * rows, (t + 1) * rows)
        lat_t_ref[:, part] = x_acc[:, part].astype(lat_t_ref.dtype)
        for parity, copy in enumerate(out_copies(t)):
            pl.when(core == parity)(copy.start)

    def project(t, first):
        part = slice(t * rows, (t + 1) * rows)
        grads = d_acc[t].astype(jnp.bfloat16)
        weight_part = dot(lat_t_ref[:LATENT, part], grads, NT)
        gw_acc[...] = weight_part if first else gw_acc[...] + weight_part
        latent_part = dot(w_ref[...], grads)

        @pl.when(step == 0)
        def _():
            x_acc[:LATENT, part] = latent_part
            x_acc[LATENT:, part] = r_acc[t]

        @pl.when(step > 0)
        def _():
            x_acc[:LATENT, part] += latent_part
            x_acc[LATENT:, part] += r_acc[t]

    def clear(t):
        x_acc[:, t * rows : (t + 1) * rows] = jnp.zeros((WIDTH, rows), jnp.float32)

    for n, t in enumerate((REACH, REACH + 1, *range(REACH))):
        if t >= REACH:
            project(t, n == 0)
        else:
            pl.when(seen(t))(functools.partial(project, t, False))
            pl.when(~seen(t) & (step == 0))(functools.partial(clear, t))
        pl.when(last)(functools.partial(leave, t))
    dq0_ref[...] = (dq_acc[core] * SCALE).astype(dq0_ref.dtype).T
    dq1_ref[...] = (dq_acc[1 - core] * SCALE).astype(dq1_ref.dtype).T

    share = 2 * (LATENT // ranks)
    own_x = lax.rem(index_ref[0] // 2, 2)
    for i in range(ranks // 4):
        for out, x in ((keep_ref, own_x), (send_ref, 1 - own_x)):
            source = pl.multiple_of((2 * i + x) * share, share)
            out[i * share : (i + 1) * share, :] = gw_acc[pl.ds(source, share), :].astype(out.dtype)

    @pl.when(last)
    def _():
        for t in range(blocks):
            out_copies(t)[0].wait()


def step_cols(height, size):
    return pl.BlockSpec((height, size), lambda i, index: (0, i))


def core_cols(height, size, first):
    def place(i, index):
        return (0, first(i, lax.rem(index[0], 2)))

    return pl.BlockSpec((height, size), place)


def step_block(*shape):
    return pl.BlockSpec((1, *shape), lambda i, index: (i, 0, 0, 0))


def fixed(*shape):
    return pl.BlockSpec(shape, lambda i, index: (0,) * len(shape))


SCALARS = pl.BlockSpec(memory_space=pltpu.SMEM)
ANYWHERE = pl.BlockSpec(memory_space=pl.ANY)


def call(body, steps, flops, in_specs, outs, scratch, name):
    return pl.pallas_call(
        body,
        grid_spec=pltpu.PrefetchScalarGridSpec(
            num_scalar_prefetch=1,
            grid=(steps,),
            in_specs=in_specs,
            out_specs=[spec for spec, _, _ in outs],
            scratch_shapes=[
                pltpu.VMEM(*entry) if isinstance(entry, tuple) else entry for entry in scratch
            ],
        ),
        out_shape=[jax.ShapeDtypeStruct(shape, kind) for _, shape, kind in outs],
        compiler_params=pltpu.CompilerParams(
            dimension_semantics=("arbitrary",), vmem_limit_bytes=58 * 1024 * 1024
        ),
        cost_estimate=pl.CostEstimate(
            flops=flops, bytes_accessed=16 * 1024 * 1024, transcendentals=0
        ),
        name=name,
    )


def head_specs(rows, heads, steps, in_place):
    def received(i, core):
        return i

    def own(i, core):
        return core * steps + i if in_place else i

    return [
        core_cols(rows, heads * QK, own), core_cols(rows, heads * VDIM, own),
        core_cols(rows, heads * QK, received), core_cols(rows, heads * VDIM, received),
        core_cols(LATENT, heads * KV, own),
    ]


def local_scores(index, docs, inputs, latents, heads, steps, in_place):
    rows = inputs[0].shape[0]
    low, full = jnp.bfloat16, jnp.float32
    count = len(LOCAL) * heads
    return call(
        local_kernel,
        steps,
        2 * steps * heads * rows * rows * (3 * (QK + VDIM) + 2 * KV),
        [
            fixed(1, docs.shape[1]), *head_specs(rows, heads, steps, in_place),
            fixed(WIDTH, rows), fixed(WIDTH, rows),
        ],
        [
            (step_block(count, rows, rows), (steps, count, rows, rows), low),
            (step_block(count, rows, rows), (steps, count, rows, rows), low),
            (step_block(2 * heads, rows, QK), (steps, 2 * heads, rows, QK), low),
            (step_block(2 * heads, 8, rows), (steps, 2 * heads, 8, rows), full),
            (step_block(count, 8, rows), (steps, count, 8, rows), full),
            (fixed(2, 8, rows), (2, 8, rows), jnp.int32),
        ],
        [
            ((2, rows, heads * QK), low),
            ((2, rows, heads * VDIM), low),
            ((2, rows, WIDTH), low),
            ((2 * heads, rows, VDIM), low),
            ((heads, rows, rows), full),
            ((heads, rows, rows), full),
        ],
        "local_scores",
    )(index, docs, *inputs, *latents)


def attention(index, doc_ids, inputs, kept, latents, heads, steps, ranks, in_place):
    rows = inputs[0].shape[0]
    low, full = jnp.bfloat16, jnp.float32
    count = len(LOCAL) * heads
    window = (REACH + 2) * rows
    far = REACH * rows
    half = (LATENT // 2, steps * heads * KV)
    return call(
        functools.partial(main_kernel, ranks),
        steps,
        2 * steps * heads * rows * rows * (5 * (QK + VDIM) + 8 * (2 * QK + VDIM) + 13 * KV),
        [
            SCALARS, *head_specs(rows, heads, steps, in_place), ANYWHERE, ANYWHERE,
            step_block(2 * heads, rows, QK), step_block(2 * heads, 8, rows),
            step_block(count, 8, rows), fixed(2, 8, rows),
        ]
        + [ANYWHERE] * len(latents),
        [(step_cols(rows, heads * QK), (rows, steps * heads * QK), low)] * 2
        + [(step_cols(LATENT // 2, heads * KV), half, low)] * 2
        + [(ANYWHERE, (WIDTH, rows), low)] * (REACH + 2),
        [
            ((2, rows, heads * QK), low),
            ((2, rows, heads * VDIM), low),
            ((far, WIDTH), low),
            ((WIDTH, window), low),
            ((heads, far, rows), low),
            ((heads, far, rows), low),
            ((heads, far, QK), low),
            ((heads, far, VDIM), low),
            ((heads, REACH, 8, rows), full),
            ((heads, 8, rows), full),
            ((heads, 8, rows), full),
            ((heads, rows, rows), full),
            ((heads, rows, rows), full),
            ((heads, rows, rows), low),
            ((heads, rows, rows), low),
            ((2, heads * QK, rows), full),
            ((REACH + 2, heads * KV, rows), full),
            ((LATENT, heads * KV), full),
            ((WIDTH, window), full),
            ((REACH + 2, ROPE, rows), full),
            ((count, rows, rows), low),
            ((count, rows, rows), low),
            pltpu.SemaphoreType.DMA((5,)),
            pltpu.SemaphoreType.DMA((2,)),
        ],
        "attention",
    )(index, doc_ids, *inputs, *kept, *latents)


def permute(value, axis, target):
    count = lax.axis_size(axis)
    pairs = [(s, target(s)) for s in range(count) if 0 <= target(s) < count]
    return lax.ppermute(value, axis, pairs)


def local(kv_latent, queries, grad_out, kv_up_weight, doc_ids):
    ranks = lax.axis_size("ctx")
    position = lax.axis_index("ctx").astype(jnp.int32)
    index, core = position[None], lax.rem(position, 2)
    low, full = jnp.bfloat16, jnp.float32
    docs = doc_ids[None]
    core_heads = kv_up_weight.shape[1] // KV // 2
    heads = min(2, core_heads)
    steps = core_heads // heads

    def own_heads(value, which):
        size = value.shape[1] // 2
        return lax.dynamic_slice_in_dim(value, which * size, size, axis=1)

    def across(value):
        return permute(value, "ctx", lambda s: s ^ 1)

    latent = kv_latent.T
    far = permute(latent, "ctx", lambda s: s + 2)
    mixed = permute(latent, "ctx", lambda s: s + 3 if s % 2 else -1)
    other = across(latent)
    in_place = heads * QK % 128 == 0
    inputs = (
        queries if in_place else own_heads(queries, core),
        grad_out if in_place else own_heads(grad_out, core),
        across(own_heads(queries, 1 - core)),
        across(own_heads(grad_out, 1 - core)),
        kv_up_weight if in_place else own_heads(kv_up_weight, core),
    )
    *kept, starts = local_scores(index, docs, inputs, (latent, other), heads, steps, in_place)
    far, mixed, starts = lax.optimization_barrier((far, mixed, starts))
    swapped = across(far)
    passed = permute(mixed, "ctx", lambda s: -1 if s % 2 else s + 1)

    dq_own, dq_other, keep, send, to_old, to_far, to_swap, mine, to_other = attention(
        index, doc_ids, inputs, (*kept, starts),
        (far, swapped, mixed, passed, latent, other), heads, steps, ranks, in_place,
    )

    head, head_count = lax.axis_index("head"), lax.axis_size("head")
    share = WIDTH // head_count

    def turned(value, turn, ctx=range(ranks)):
        turns = [
            (c * head_count + s, c * head_count + (s + turn) % head_count)
            for c in ctx
            for s in range(head_count)
        ]
        return lax.ppermute(value, ("ctx", "head"), turns)

    def head_share(value, ctx=range(ranks)):
        def rows_of(which):
            return lax.dynamic_slice_in_dim(value, which * share, share, axis=0)

        total = rows_of(head).astype(full)
        for turn in range(1, head_count):
            target = lax.rem(head + turn, head_count)
            total = total + turned(rows_of(target), turn, ctx).astype(full)
        return total

    from_x = permute(send, "ctx", lambda s: s ^ 2)
    from_swap = across(to_swap)
    from_old = permute(to_old, "ctx", lambda s: s - 1 if s % 2 else -1)
    from_other = across(to_other)
    far_sum = head_share((to_far.astype(full) + from_swap.astype(full)).astype(low)).astype(low)
    old_sum = (to_old.astype(full) + from_old.astype(full)).astype(low)
    old_sum = head_share(old_sum, range(0, ranks, 2)).astype(low)
    from_far = permute(far_sum, "ctx", lambda s: s - 2)
    from_mixed = permute(old_sum, "ctx", lambda s: -1 if s % 2 else s - 3)
    own_sum = (mine.astype(full) + from_other.astype(full)).astype(low)
    own_sum, *_ = lax.optimization_barrier((own_sum, far_sum))
    total = head_share(own_sum)

    from_x, *_ = lax.optimization_barrier((from_x, far_sum))
    plane = (keep.astype(full) + from_x.astype(full)).astype(low)
    columns = [list(range(first, ranks, 4)) for first in range(4)]
    pieces = lax.all_to_all(plane, "ctx", 0, 0, axis_index_groups=columns, tiled=True)
    rows = LATENT // ranks
    summed = jnp.sum(pieces.reshape(ranks // 4, 2 * rows, -1).astype(full), axis=0)

    def in_order(own, received):
        first = jnp.where(core == 0, own, received)
        second = jnp.where(core == 0, received, own)
        return jnp.concatenate([first, second], axis=1)

    rows_own = lax.dynamic_slice_in_dim(summed, core * rows, rows, axis=0)
    rows_other = lax.dynamic_slice_in_dim(summed, (1 - core) * rows, rows, axis=0)
    grad_weight = in_order(rows_own, across(rows_other))
    grad_queries = in_order(dq_own, across(dq_other))

    total = (total + from_mixed.astype(full) + from_far.astype(full)).astype(low)
    shares = [total] + [turned(total, turn) for turn in range(1, head_count)]
    ordered = []
    for place in range(head_count):
        picked = shares[0]
        for turn in range(1, head_count):
            picked = jnp.where(lax.rem(head - place + head_count, head_count) == turn, shares[turn], picked)
        ordered.append(picked)
    return grad_queries, jnp.concatenate(ordered, axis=0).T, grad_weight


def solution(mesh):
    return jax.shard_map(
        local,
        mesh=mesh,
        in_specs=(P("ctx", None), P("ctx", "head"), P("ctx", "head"), P(None, "head"), P()),
        out_specs=(P("ctx", "head"), P("ctx", None), P("ctx", "head")),
        check_vma=False,
    )
```

```python
import functools
import math

import jax
import jax.numpy as jnp
from jax import lax
from jax.experimental import pallas as pl
from jax.experimental.pallas import tpu as pltpu
from jax.sharding import PartitionSpec as P

NOPE = 128
ROPE = 64
VDIM = 128
LATENT = 512
REACH = 3
QK = NOPE + ROPE
KV = NOPE + VDIM
WIDTH = LATENT + ROPE
LANES = 128
PIECE = 256

MASKED = -1e30
FLOOR = -1e20
SCALE = 1.0 / math.sqrt(QK)
SCALE2 = SCALE * math.log2(math.e)

NT = (((1,), (1,)), ((), ()))
NN = (((1,), (0,)), ((), ()))


def dot(a, b, dims=NN):
    return lax.dot_general(a, b, dims, preferred_element_type=jnp.float32)


def head_cols(h, size):
    return slice(h * size, (h + 1) * size)


def fold(value, combine):
    return combine(value.reshape(-1, 8, value.shape[1]), axis=0)


def fold(value, combine):
    return combine(value.reshape(-1, 8, value.shape[1]), axis=0)


def lift(latent, w_ref, k_out, v_out):
    for h in range(w_ref.shape[1] // KV):
        lifted = dot(latent[:, :LATENT], w_ref[:, head_cols(h, KV)]).astype(jnp.bfloat16)
        k_out(h, jnp.concatenate([lifted[:, :NOPE], latent[:, LATENT:]], axis=1))
        v_out(h, lifted[:, NOPE:])


def score_block(key, value, q_ref, do_ref, bounds, run_ref, raw_ref, graw_ref, keep):
    rows = do_ref.shape[0]
    lower, upper = bounds
    index = lax.broadcasted_iota(jnp.int32, (LANES, LANES), 0)
    parts = [slice(r, r + LANES) for r in range(0, rows, LANES)]

    def multiply(h, first):
        cols = slice(first, first + PIECE)
        raw_ref[h, :, cols] = dot(key(h), q_ref[cols, head_cols(h, QK)], NT)
        graw_ref[h, :, cols] = dot(value(h), do_ref[cols, head_cols(h, VDIM)], NT)

    def weigh(h, first):
        for c in range(first, first + PIECE, LANES):
            cols = slice(c, c + LANES)
            high = None
            for part in parts:
                seen = index >= lower[:, cols] - part.start
                if upper is not None:
                    seen = seen & (index <= upper[:, cols] - part.start)
                scores = jnp.where(seen, raw_ref[h, part, cols] * SCALE2, MASKED)
                raw_ref[h, part, cols] = scores
                piece = fold(scores, jnp.max)
                high = piece if high is None else jnp.maximum(high, piece)
            old_top = run_ref[h, 0:1, cols]
            new_top = jnp.maximum(old_top, jnp.max(high, axis=0, keepdims=True))
            mass, cross = 0.0, 0.0
            for part in parts:
                weights = jnp.exp2(raw_ref[h, part, cols] - new_top)
                grads = graw_ref[h, part, cols]
                keep(h, part, cols, weights.astype(jnp.bfloat16), grads.astype(jnp.bfloat16))
                mass = mass + fold(weights, jnp.sum)
                cross = cross + fold(weights * grads, jnp.sum)
            factor = jnp.exp2(old_top - new_top)
            run_ref[h, 0:1, cols] = new_top
            run_ref[h, 1:2, cols] = run_ref[h, 1:2, cols] * factor + jnp.sum(
                mass, axis=0, keepdims=True
            )
            run_ref[h, 2:3, cols] = run_ref[h, 2:3, cols] * factor + jnp.sum(
                cross, axis=0, keepdims=True
            )

    alternate(rows, do_ref.shape[1] // VDIM, multiply, weigh)


def alternate(rows, heads, first, second):
    pieces = [(h, c) for h in range(heads) for c in range(0, rows, PIECE)]
    first(*pieces[0])
    for now, following in zip(pieces, pieces[1:] + [None]):
        if following:
            first(*following)
        second(*now)


def grad_block(kept, key, top, end_ref, q_ref, do_ref, low_ref, ds_ref, dq_acc, d_acc, r_acc, first_q, first_k):
    def put(ref, part, value, first):
        ref[:, part] = value if first else ref[:, part] + value

    rows = do_ref.shape[0]
    heads = do_ref.shape[1] // VDIM
    sums, turned = {}, {}

    def weigh(h, first):
        for c in range(first, first + PIECE, LANES):
            cols = slice(c, c + LANES)
            factor = jnp.exp2(top(h)[:, cols] - end_ref[h, 0:1, cols]) * end_ref[h, 1:2, cols]
            delta = end_ref[h, 2:3, cols]
            for r in range(0, rows, LANES):
                part = slice(r, r + LANES)
                weights, grads = kept(h, part, cols)
                probs = weights.astype(jnp.float32) * factor
                low_ref[h, part, cols] = probs.astype(jnp.bfloat16)
                ds_ref[h, part, cols] = (
                    probs * (grads.astype(jnp.float32) - delta)
                ).astype(jnp.bfloat16)

    def multiply(h, first):
        cols = slice(first, first + PIECE)
        low, dscore = low_ref[h, :, cols], ds_ref[h, :, cols]
        dvalue = dot(low, do_ref[cols, head_cols(h, VDIM)])
        dkey = dot(dscore, q_ref[cols, head_cols(h, QK)])
        own = head_cols(h, QK)
        if not first:
            turned[h] = key(h).T
        dq = dot(turned[h], dscore)
        dq_acc[own, cols] = dq if first_q else dq_acc[own, cols] + dq
        if first:
            dvalue, dkey = sums[h][0] + dvalue, sums[h][1] + dkey
        sums[h] = dvalue, dkey
        if first + PIECE == rows:
            dkey = dkey * SCALE
            put(d_acc, slice(h * KV, h * KV + NOPE), dkey[:, :NOPE], first_k)
            put(d_acc, slice(h * KV + NOPE, (h + 1) * KV), dvalue, first_k)
            put(r_acc, slice(0, ROPE), dkey[:, NOPE:], first_k and h == 0)

    alternate(rows, heads, weigh, multiply)


def start_stats(run_ref):
    count, rows = run_ref.shape[0], run_ref.shape[2]
    for h in range(count):
        run_ref[h, 0:1, :] = jnp.full((1, rows), FLOOR, jnp.float32)
        run_ref[h, 1:8, :] = jnp.zeros((7, rows), jnp.float32)


def chip_place(index_ref):
    core = lax.rem(index_ref[0], 2)
    return core, index_ref[0] - core


def order_pair(out_ref, core, own, other):
    out_ref[core] = own[...]
    out_ref[1 - core] = other[...]


LOCAL = ((1, REACH), (0, REACH), (1, REACH + 1))


def query_bounds(start_ref, chip, j, t, rows):
    lower = start_ref[j, 0:1, :] - (chip + t - REACH) * rows
    own = isinstance(t, int) and t == j + REACH
    return lower, lax.broadcasted_iota(jnp.int32, (1, rows), 1) if own else None


def find_starts(docs_ref, start_ref, chip, rows):
    for j in range(2):
        block = chip + j
        my_docs = docs_ref[:, pl.ds(pl.multiple_of(block * rows, rows), rows)]
        first_doc = my_docs[:, :1]
        key_docs = jnp.broadcast_to(my_docs, (128, rows)).T[:, :1]
        inside = jnp.sum(jnp.where(key_docs < my_docs, 1.0, 0.0), axis=0, keepdims=True)
        before = jnp.zeros((1, rows), jnp.float32)
        for back in range(1, REACH + 1):
            earlier = jnp.maximum(block - back, 0)
            docs = docs_ref[:, pl.ds(pl.multiple_of(earlier * rows, rows), rows)]
            same = (docs == first_doc) & (block >= back)
            before = before + jnp.where(same, 1.0, 0.0)
        before = jnp.sum(before, axis=1, keepdims=True)
        start = jnp.where(my_docs == first_doc, -before, inside).astype(jnp.int32)
        start_ref[j, 0:1, :] = start + block * rows


def local_kernel(
    index_ref, docs_ref, q0, do0, q1, do1, w_ref, lat0, lat1,
    e_ref, g_ref, k_ref, run_ref, top_ref, start_ref,
    q_ref, do_ref, lat_ref, v_ref, raw_ref, graw_ref,
):
    rows = q0.shape[0]
    core, chip = chip_place(index_ref)
    heads = w_ref.shape[1] // KV

    @pl.when(pl.program_id(0) == 0)
    def _():
        lat_ref[core] = lat0[...].T
        lat_ref[1 - core] = lat1[...].T
        find_starts(docs_ref, start_ref, chip, rows)

    order_pair(q_ref, core, q0, q1)
    order_pair(do_ref, core, do0, do1)
    for j in range(2):

        def k_out(h, key):
            k_ref[0, j * heads + h] = key

        def v_out(h, value):
            v_ref[j * heads + h] = value

        lift(lat_ref[j], w_ref, k_out, v_out)
        start_stats(run_ref.at[0, pl.ds(j * heads, heads)])
    for n, (j, t) in enumerate(LOCAL):
        slot = t - REACH

        def keep(h, part, cols, weights, grads):
            e_ref[0, n * heads + h, part, cols] = weights
            g_ref[0, n * heads + h, part, cols] = grads

        run = run_ref.at[0, pl.ds(j * heads, heads)]
        score_block(
            lambda h: k_ref[0, slot * heads + h], lambda h: v_ref[slot * heads + h],
            q_ref.at[j], do_ref.at[j], query_bounds(start_ref, chip, j, t, rows), run,
            raw_ref, graw_ref, keep,
        )
        for h in range(heads):
            top_ref[0, n * heads + h] = run[h]


def main_kernel(
    ranks,
    index_ref, docs_sref, q0, do0, q1, do1, w_ref,
    all_e, all_g, local_k, local_run, local_top, start_ref,
    lat_far, lat_swap, lat_mixed, lat_passed, lat_own, lat_other,
    dq0_ref, dq1_ref, keep_ref, send_ref, x_old, x_far, x_swap, x_own, x_other,
    q_ref, do_ref, lat_ref, lat_t_ref, e_ref, g_ref, k_ref, v_ref, top_ref,
    run_ref, end_ref, raw_ref, graw_ref, low_ref, ds_ref, dq_acc, d_acc, gw_acc, x_acc,
    r_acc, local_e, local_g, sems, kept_sems,
):
    step = pl.program_id(0)
    rows = q0.shape[0]
    heads = w_ref.shape[1] // KV
    blocks = REACH + 2
    kept_copies = [
        pltpu.make_async_copy(all_e.at[step], local_e, kept_sems.at[0]),
        pltpu.make_async_copy(all_g.at[step], local_g, kept_sems.at[1]),
    ]
    core, chip = chip_place(index_ref)

    def active(j, t):
        block = chip + t - REACH
        last_doc = docs_sref[jnp.maximum(block, 0) * rows + rows - 1]
        return (block >= 0) & (last_doc >= docs_sref[(chip + j) * rows])

    def block_rows(t):
        return pl.ds(pl.multiple_of(t * rows, rows), rows)

    def piece_rows(t, part):
        size = part.stop - part.start
        return pl.ds(pl.multiple_of(t * rows + part.start, size), size)

    def loop(first, last, when, body):
        def visit(t, carry):
            @pl.when(when(t))
            def _():
                body(t)

            return carry

        lax.fori_loop(first, last, visit, 0)

    @pl.when(step == 0)
    def _():
        places = [(lat_far, 1 + core), (lat_swap, 2 - core), (lat_own, REACH + core),
                  (lat_other, REACH + 1 - core)]
        copies = [
            pltpu.make_async_copy(source, lat_t_ref.at[:, block_rows(t)], sems.at[i])
            for i, (source, t) in enumerate(places)
        ]
        first = lat_t_ref.at[:, block_rows(0)]
        oldest = pltpu.make_async_copy(lat_mixed, first, sems.at[4])
        passed = pltpu.make_async_copy(lat_passed, first, sems.at[4])
        for copy in copies:
            copy.start()
        pl.when(core == 0)(oldest.start)
        pl.when(core == 1)(passed.start)
        for copy in kept_copies:
            copy.start()
        for copy in copies:
            copy.wait()
        oldest.wait()
        for t in range(REACH):
            part = slice(t * rows, (t + 1) * rows)
            lat_ref[part, :] = lat_t_ref[:, part].T

    @pl.when(step > 0)
    def _():
        for copy in kept_copies:
            copy.start()

    order_pair(q_ref, core, q0, q1)
    order_pair(do_ref, core, do0, do1)

    def lift_block(t):
        def k_out(h, key):
            k_ref[h, block_rows(t), :] = key

        def v_out(h, value):
            v_ref[h, block_rows(t), :] = value

        lift(lat_ref[block_rows(t), :], w_ref, k_out, v_out)

    loop(0, REACH, lambda t: active(0, t), lift_block)

    for j in range(2):
        for h in range(heads):
            run_ref[h] = local_run[0, j * heads + h]

        def first_pass(t):
            def keep(h, part, cols, weights, grads):
                e_ref[h, piece_rows(t, part), cols] = weights
                g_ref[h, piece_rows(t, part), cols] = grads

            score_block(
                lambda h: k_ref[h, block_rows(t), :], lambda h: v_ref[h, block_rows(t), :],
                q_ref.at[j], do_ref.at[j], query_bounds(start_ref, chip, j, t, rows), run_ref,
                raw_ref, graw_ref, keep,
            )
            for h in range(heads):
                top_ref[h, t] = run_ref[h]

        loop(j, REACH, lambda t: active(j, t), first_pass)
        for h in range(heads):
            inverse = 1.0 / run_ref[h, 1:2, :]
            end_ref[h, 0:1, :] = run_ref[h, 0:1, :]
            end_ref[h, 1:2, :] = inverse
            end_ref[h, 2:3, :] = run_ref[h, 2:3, :] * inverse

        def add(t, kept, key, top, first_q, first_k):
            grad_block(
                kept, key, top, end_ref, q_ref.at[j], do_ref.at[j], low_ref, ds_ref, dq_acc.at[j], d_acc.at[t],
                r_acc.at[t], first_q, first_k,
            )

        def second_pass(t):
            def kept(h, part, cols):
                return e_ref[h, piece_rows(t, part), cols], g_ref[h, piece_rows(t, part), cols]

            add(
                t, kept, lambda h: k_ref[h, block_rows(t), :], lambda h: top_ref[h, t, 0:1, :],
                False, j == 0,
            )

        if j == 0:
            for copy in kept_copies:
                copy.wait()
        first_q = True
        for n, (query, t) in enumerate(LOCAL):
            if query == j:
                add(
                    t,
                    lambda h, part, cols: (
                        local_e[n * heads + h, part, cols], local_g[n * heads + h, part, cols]
                    ),
                    lambda h: local_k[0, (t - REACH) * heads + h],
                    lambda h: local_top[0, n * heads + h, 0:1, :],
                    first_q, t == REACH + j,
                )
                first_q = False
        loop(j, REACH, lambda t: active(j, t), second_pass)

    def seen(t):
        return (t >= REACH) | active(0, t)

    last = step == pl.num_programs(0) - 1
    outs = ((x_old, x_old), (x_far, x_swap), (x_swap, x_far), (x_own, x_other), (x_other, x_own))

    def out_copies(t):
        part = slice(t * rows, (t + 1) * rows)
        return [pltpu.make_async_copy(lat_t_ref.at[:, part], out, sems.at[t]) for out in outs[t]]

    def leave(t):
        part = slice(t * rows, (t + 1) * rows)
        lat_t_ref[:, part] = x_acc[:, part].astype(lat_t_ref.dtype)
        for parity, copy in enumerate(out_copies(t)):
            pl.when(core == parity)(copy.start)

    def project(t, first):
        part = slice(t * rows, (t + 1) * rows)
        grads = d_acc[t].astype(jnp.bfloat16)
        weight_part = dot(lat_t_ref[:LATENT, part], grads)
        gw_acc[...] = weight_part if first else gw_acc[...] + weight_part
        latent_part = dot(w_ref[...], grads, NT)
        rope_part = r_acc[t].T

        @pl.when(step == 0)
        def _():
            x_acc[:LATENT, part] = latent_part
            x_acc[LATENT:, part] = rope_part

        @pl.when(step > 0)
        def _():
            x_acc[:LATENT, part] += latent_part
            x_acc[LATENT:, part] += rope_part

    def clear(t):
        x_acc[:, t * rows : (t + 1) * rows] = jnp.zeros((WIDTH, rows), jnp.float32)

    for n, t in enumerate((REACH, REACH + 1, *range(REACH))):
        if t >= REACH:
            project(t, n == 0)
        else:
            pl.when(seen(t))(functools.partial(project, t, False))
            pl.when(~seen(t) & (step == 0))(functools.partial(clear, t))
        pl.when(last)(functools.partial(leave, t))
    dq0_ref[...] = (dq_acc[core] * SCALE).astype(dq0_ref.dtype).T
    dq1_ref[...] = (dq_acc[1 - core] * SCALE).astype(dq1_ref.dtype).T

    share = 2 * (LATENT // ranks)
    own_x = lax.rem(index_ref[0] // 2, 2)
    for i in range(ranks // 4):
        for out, x in ((keep_ref, own_x), (send_ref, 1 - own_x)):
            source = pl.multiple_of((2 * i + x) * share, share)
            out[i * share : (i + 1) * share, :] = gw_acc[pl.ds(source, share), :].astype(out.dtype)

    @pl.when(last)
    def _():
        for t in range(blocks):
            out_copies(t)[0].wait()


def step_cols(height, size):
    return pl.BlockSpec((height, size), lambda i, index: (0, i))


def core_cols(height, size, first):
    def place(i, index):
        return (0, first(i, lax.rem(index[0], 2)))

    return pl.BlockSpec((height, size), place)


def step_block(*shape):
    return pl.BlockSpec((1, *shape), lambda i, index: (i, 0, 0, 0))


def fixed(*shape):
    return pl.BlockSpec(shape, lambda i, index: (0,) * len(shape))


SCALARS = pl.BlockSpec(memory_space=pltpu.SMEM)
ANYWHERE = pl.BlockSpec(memory_space=pl.ANY)


def call(body, steps, flops, in_specs, outs, scratch, name):
    return pl.pallas_call(
        body,
        grid_spec=pltpu.PrefetchScalarGridSpec(
            num_scalar_prefetch=1,
            grid=(steps,),
            in_specs=in_specs,
            out_specs=[spec for spec, _, _ in outs],
            scratch_shapes=[
                pltpu.VMEM(*entry) if isinstance(entry, tuple) else entry for entry in scratch
            ],
        ),
        out_shape=[jax.ShapeDtypeStruct(shape, kind) for _, shape, kind in outs],
        compiler_params=pltpu.CompilerParams(
            dimension_semantics=("arbitrary",), vmem_limit_bytes=58 * 1024 * 1024
        ),
        cost_estimate=pl.CostEstimate(
            flops=flops, bytes_accessed=16 * 1024 * 1024, transcendentals=0
        ),
        name=name,
    )


def head_specs(rows, heads, steps, in_place):
    def received(i, core):
        return i

    def own(i, core):
        return core * steps + i if in_place else i

    return [
        core_cols(rows, heads * QK, own), core_cols(rows, heads * VDIM, own),
        core_cols(rows, heads * QK, received), core_cols(rows, heads * VDIM, received),
        core_cols(LATENT, heads * KV, own),
    ]


def local_scores(index, docs, inputs, latents, heads, steps, in_place):
    rows = inputs[0].shape[0]
    low, full = jnp.bfloat16, jnp.float32
    count = len(LOCAL) * heads
    return call(
        local_kernel,
        steps,
        2 * steps * heads * rows * rows * (3 * (QK + VDIM) + 2 * KV),
        [
            fixed(1, docs.shape[1]), *head_specs(rows, heads, steps, in_place),
            fixed(WIDTH, rows), fixed(WIDTH, rows),
        ],
        [
            (step_block(count, rows, rows), (steps, count, rows, rows), low),
            (step_block(count, rows, rows), (steps, count, rows, rows), low),
            (step_block(2 * heads, rows, QK), (steps, 2 * heads, rows, QK), low),
            (step_block(2 * heads, 8, rows), (steps, 2 * heads, 8, rows), full),
            (step_block(count, 8, rows), (steps, count, 8, rows), full),
            (fixed(2, 8, rows), (2, 8, rows), jnp.int32),
        ],
        [
            ((2, rows, heads * QK), low),
            ((2, rows, heads * VDIM), low),
            ((2, rows, WIDTH), low),
            ((2 * heads, rows, VDIM), low),
            ((heads, rows, rows), full),
            ((heads, rows, rows), full),
        ],
        "local_scores",
    )(index, docs, *inputs, *latents)


def attention(index, doc_ids, inputs, kept, latents, heads, steps, ranks, in_place):
    rows = inputs[0].shape[0]
    low, full = jnp.bfloat16, jnp.float32
    count = len(LOCAL) * heads
    window = (REACH + 2) * rows
    far = REACH * rows
    half = (LATENT // 2, steps * heads * KV)
    return call(
        functools.partial(main_kernel, ranks),
        steps,
        2 * steps * heads * rows * rows * (5 * (QK + VDIM) + 8 * (2 * QK + VDIM) + 13 * KV),
        [
            SCALARS, *head_specs(rows, heads, steps, in_place), ANYWHERE, ANYWHERE,
            step_block(2 * heads, rows, QK), step_block(2 * heads, 8, rows),
            step_block(count, 8, rows), fixed(2, 8, rows),
        ]
        + [ANYWHERE] * len(latents),
        [(step_cols(rows, heads * QK), (rows, steps * heads * QK), low)] * 2
        + [(step_cols(LATENT // 2, heads * KV), half, low)] * 2
        + [(ANYWHERE, (WIDTH, rows), low)] * (REACH + 2),
        [
            ((2, rows, heads * QK), low),
            ((2, rows, heads * VDIM), low),
            ((far, WIDTH), low),
            ((WIDTH, window), low),
            ((heads, far, rows), low),
            ((heads, far, rows), low),
            ((heads, far, QK), low),
            ((heads, far, VDIM), low),
            ((heads, REACH, 8, rows), full),
            ((heads, 8, rows), full),
            ((heads, 8, rows), full),
            ((heads, rows, rows), full),
            ((heads, rows, rows), full),
            ((heads, rows, rows), low),
            ((heads, rows, rows), low),
            ((2, heads * QK, rows), full),
            ((REACH + 2, rows, heads * KV), full),
            ((LATENT, heads * KV), full),
            ((WIDTH, window), full),
            ((REACH + 2, rows, ROPE), full),
            ((count, rows, rows), low),
            ((count, rows, rows), low),
            pltpu.SemaphoreType.DMA((5,)),
            pltpu.SemaphoreType.DMA((2,)),
        ],
        "attention",
    )(index, doc_ids, *inputs, *kept, *latents)


def permute(value, axis, target):
    count = lax.axis_size(axis)
    pairs = [(s, target(s)) for s in range(count) if 0 <= target(s) < count]
    return lax.ppermute(value, axis, pairs)


def local(kv_latent, queries, grad_out, kv_up_weight, doc_ids):
    ranks = lax.axis_size("ctx")
    position = lax.axis_index("ctx").astype(jnp.int32)
    index, core = position[None], lax.rem(position, 2)
    low, full = jnp.bfloat16, jnp.float32
    docs = doc_ids[None]
    core_heads = kv_up_weight.shape[1] // KV // 2
    heads = min(2, core_heads)
    steps = core_heads // heads

    def own_heads(value, which):
        size = value.shape[1] // 2
        return lax.dynamic_slice_in_dim(value, which * size, size, axis=1)

    def across(value):
        return permute(value, "ctx", lambda s: s ^ 1)

    latent = kv_latent.T
    far = permute(latent, "ctx", lambda s: s + 2)
    mixed = permute(latent, "ctx", lambda s: s + 3 if s % 2 else -1)
    other = across(latent)
    in_place = heads * QK % 128 == 0
    inputs = (
        queries if in_place else own_heads(queries, core),
        grad_out if in_place else own_heads(grad_out, core),
        across(own_heads(queries, 1 - core)),
        across(own_heads(grad_out, 1 - core)),
        kv_up_weight if in_place else own_heads(kv_up_weight, core),
    )
    *kept, starts = local_scores(index, docs, inputs, (latent, other), heads, steps, in_place)
    far, mixed, starts = lax.optimization_barrier((far, mixed, starts))
    swapped = across(far)
    passed = permute(mixed, "ctx", lambda s: -1 if s % 2 else s + 1)

    dq_own, dq_other, keep, send, to_old, to_far, to_swap, mine, to_other = attention(
        index, doc_ids, inputs, (*kept, starts),
        (far, swapped, mixed, passed, latent, other), heads, steps, ranks, in_place,
    )

    head, head_count = lax.axis_index("head"), lax.axis_size("head")
    share = WIDTH // head_count

    def turned(value, turn, ctx=range(ranks)):
        turns = [
            (c * head_count + s, c * head_count + (s + turn) % head_count)
            for c in ctx
            for s in range(head_count)
        ]
        return lax.ppermute(value, ("ctx", "head"), turns)

    def head_share(value, ctx=range(ranks)):
        def rows_of(which):
            return lax.dynamic_slice_in_dim(value, which * share, share, axis=0)

        total = rows_of(head).astype(full)
        for turn in range(1, head_count):
            target = lax.rem(head + turn, head_count)
            total = total + turned(rows_of(target), turn, ctx).astype(full)
        return total

    from_x = permute(send, "ctx", lambda s: s ^ 2)
    from_swap = across(to_swap)
    from_old = permute(to_old, "ctx", lambda s: s - 1 if s % 2 else -1)
    from_other = across(to_other)
    far_sum = head_share((to_far.astype(full) + from_swap.astype(full)).astype(low)).astype(low)
    old_sum = (to_old.astype(full) + from_old.astype(full)).astype(low)
    old_sum = head_share(old_sum, range(0, ranks, 2)).astype(low)
    from_far = permute(far_sum, "ctx", lambda s: s - 2)
    from_mixed = permute(old_sum, "ctx", lambda s: -1 if s % 2 else s - 3)
    own_sum = (mine.astype(full) + from_other.astype(full)).astype(low)
    own_sum, *_ = lax.optimization_barrier((own_sum, far_sum))
    total = head_share(own_sum)

    from_x, *_ = lax.optimization_barrier((from_x, far_sum, old_sum))
    plane = (keep.astype(full) + from_x.astype(full)).astype(low)
    columns = [list(range(first, ranks, 4)) for first in range(4)]
    pieces = lax.all_to_all(plane, "ctx", 0, 0, axis_index_groups=columns, tiled=True)
    rows = LATENT // ranks
    summed = jnp.sum(pieces.reshape(ranks // 4, 2 * rows, -1).astype(full), axis=0)

    def in_order(own, received):
        first = jnp.where(core == 0, own, received)
        second = jnp.where(core == 0, received, own)
        return jnp.concatenate([first, second], axis=1)

    rows_own = lax.dynamic_slice_in_dim(summed, core * rows, rows, axis=0)
    rows_other = lax.dynamic_slice_in_dim(summed, (1 - core) * rows, rows, axis=0)
    grad_weight = in_order(rows_own, across(rows_other))
    grad_queries = in_order(dq_own, across(dq_other))

    total = (total + from_mixed.astype(full) + from_far.astype(full)).astype(low)
    shares = [total] + [turned(total, turn) for turn in range(1, head_count)]
    ordered = []
    for place in range(head_count):
        picked = shares[0]
        for turn in range(1, head_count):
            picked = jnp.where(lax.rem(head - place + head_count, head_count) == turn, shares[turn], picked)
        ordered.append(picked)
    return grad_queries, jnp.concatenate(ordered, axis=0).T, grad_weight


def solution(mesh):
    return jax.shard_map(
        local,
        mesh=mesh,
        in_specs=(P("ctx", None), P("ctx", "head"), P("ctx", "head"), P(None, "head"), P()),
        out_specs=(P("ctx", "head"), P("ctx", None), P("ctx", "head")),
        check_vma=False,
    )
```

```python
import functools
import math

import jax
import jax.numpy as jnp
from jax import lax
from jax.experimental import pallas as pl
from jax.experimental.pallas import tpu as pltpu
from jax.sharding import PartitionSpec as P

NOPE = 128
ROPE = 64
VDIM = 128
LATENT = 512
REACH = 3
QK = NOPE + ROPE
KV = NOPE + VDIM
WIDTH = LATENT + ROPE
LANES = 128
PIECE = 256

MASKED = -1e30
FLOOR = -1e20
SCALE = 1.0 / math.sqrt(QK)
SCALE2 = SCALE * math.log2(math.e)

NT = (((1,), (1,)), ((), ()))
NN = (((1,), (0,)), ((), ()))


def dot(a, b, dims=NN):
    return lax.dot_general(a, b, dims, preferred_element_type=jnp.float32)


def head_cols(h, size):
    return slice(h * size, (h + 1) * size)


def fold(value, combine):
    return combine(value.reshape(-1, 8, value.shape[1]), axis=0)


def fold(value, combine):
    return combine(value.reshape(-1, 8, value.shape[1]), axis=0)


def lift(latent, w_ref, k_out, v_out):
    for h in range(w_ref.shape[1] // KV):
        lifted = dot(latent[:, :LATENT], w_ref[:, head_cols(h, KV)]).astype(jnp.bfloat16)
        k_out(h, jnp.concatenate([lifted[:, :NOPE], latent[:, LATENT:]], axis=1))
        v_out(h, lifted[:, NOPE:])


def score_block(key, value, qt_ref, dot_ref, bounds, run_ref, raw_ref, graw_ref, keep):
    rows = dot_ref.shape[1]
    lower, upper = bounds
    index = lax.broadcasted_iota(jnp.int32, (LANES, LANES), 0)
    parts = [slice(r, r + LANES) for r in range(0, rows, LANES)]

    def multiply(h, first):
        cols = slice(first, first + PIECE)
        raw_ref[h, :, cols] = dot(key(h), qt_ref[head_cols(h, QK), cols])
        graw_ref[h, :, cols] = dot(value(h), dot_ref[head_cols(h, VDIM), cols])

    def weigh(h, first):
        for c in range(first, first + PIECE, LANES):
            cols = slice(c, c + LANES)
            high = None
            for part in parts:
                seen = index >= lower[:, cols] - part.start
                if upper is not None:
                    seen = seen & (index <= upper[:, cols] - part.start)
                scores = jnp.where(seen, raw_ref[h, part, cols] * SCALE2, MASKED)
                raw_ref[h, part, cols] = scores
                piece = fold(scores, jnp.max)
                high = piece if high is None else jnp.maximum(high, piece)
            old_top = run_ref[h, 0:1, cols]
            new_top = jnp.maximum(old_top, jnp.max(high, axis=0, keepdims=True))
            mass, cross = 0.0, 0.0
            for part in parts:
                weights = jnp.exp2(raw_ref[h, part, cols] - new_top)
                grads = graw_ref[h, part, cols]
                keep(h, part, cols, weights.astype(jnp.bfloat16), grads.astype(jnp.bfloat16))
                mass = mass + fold(weights, jnp.sum)
                cross = cross + fold(weights * grads, jnp.sum)
            factor = jnp.exp2(old_top - new_top)
            run_ref[h, 0:1, cols] = new_top
            run_ref[h, 1:2, cols] = run_ref[h, 1:2, cols] * factor + jnp.sum(
                mass, axis=0, keepdims=True
            )
            run_ref[h, 2:3, cols] = run_ref[h, 2:3, cols] * factor + jnp.sum(
                cross, axis=0, keepdims=True
            )

    alternate(rows, dot_ref.shape[0] // VDIM, multiply, weigh)


def alternate(rows, heads, first, second):
    pieces = [(h, c) for h in range(heads) for c in range(0, rows, PIECE)]
    first(*pieces[0])
    for now, following in zip(pieces, pieces[1:] + [None]):
        if following:
            first(*following)
        second(*now)


def grad_block(kept, key, top, end_ref, q_ref, do_ref, low_ref, ds_ref, dq_acc, d_acc, r_acc, first_q, first_k):
    def put(ref, part, value, first):
        ref[:, part] = value if first else ref[:, part] + value

    rows = do_ref.shape[0]
    heads = do_ref.shape[1] // VDIM
    sums, turned = {}, {}

    def weigh(h, first):
        for c in range(first, first + PIECE, LANES):
            cols = slice(c, c + LANES)
            factor = jnp.exp2(top(h)[:, cols] - end_ref[h, 0:1, cols]) * end_ref[h, 1:2, cols]
            delta = end_ref[h, 2:3, cols]
            for r in range(0, rows, LANES):
                part = slice(r, r + LANES)
                weights, grads = kept(h, part, cols)
                probs = weights.astype(jnp.float32) * factor
                low_ref[h, part, cols] = probs.astype(jnp.bfloat16)
                ds_ref[h, part, cols] = (
                    probs * (grads.astype(jnp.float32) - delta)
                ).astype(jnp.bfloat16)

    def multiply(h, first):
        cols = slice(first, first + PIECE)
        low, dscore = low_ref[h, :, cols], ds_ref[h, :, cols]
        dvalue = dot(low, do_ref[cols, head_cols(h, VDIM)])
        dkey = dot(dscore, q_ref[cols, head_cols(h, QK)])
        own = head_cols(h, QK)
        if not first:
            turned[h] = key(h).T
        dq = dot(turned[h], dscore)
        dq_acc[own, cols] = dq if first_q else dq_acc[own, cols] + dq
        if first:
            dvalue, dkey = sums[h][0] + dvalue, sums[h][1] + dkey
        sums[h] = dvalue, dkey
        if first + PIECE == rows:
            dkey = dkey * SCALE
            put(d_acc, slice(h * KV, h * KV + NOPE), dkey[:, :NOPE], first_k)
            put(d_acc, slice(h * KV + NOPE, (h + 1) * KV), dvalue, first_k)
            put(r_acc, slice(0, ROPE), dkey[:, NOPE:], first_k and h == 0)

    alternate(rows, heads, weigh, multiply)


def start_stats(run_ref):
    count, rows = run_ref.shape[0], run_ref.shape[2]
    for h in range(count):
        run_ref[h, 0:1, :] = jnp.full((1, rows), FLOOR, jnp.float32)
        run_ref[h, 1:8, :] = jnp.zeros((7, rows), jnp.float32)


def chip_place(index_ref):
    core = lax.rem(index_ref[0], 2)
    return core, index_ref[0] - core


def order_pair(out_ref, core, own, other):
    out_ref[core] = own[...]
    out_ref[1 - core] = other[...]


def turn_pair(out_ref, core, own, other):
    out_ref[core] = own[...].T
    out_ref[1 - core] = other[...].T


LOCAL = ((1, REACH), (0, REACH), (1, REACH + 1))


def query_bounds(start_ref, chip, j, t, rows):
    lower = start_ref[j, 0:1, :] - (chip + t - REACH) * rows
    own = isinstance(t, int) and t == j + REACH
    return lower, lax.broadcasted_iota(jnp.int32, (1, rows), 1) if own else None


def find_starts(docs_ref, start_ref, chip, rows):
    for j in range(2):
        block = chip + j
        my_docs = docs_ref[:, pl.ds(pl.multiple_of(block * rows, rows), rows)]
        first_doc = my_docs[:, :1]
        key_docs = jnp.broadcast_to(my_docs, (128, rows)).T[:, :1]
        inside = jnp.sum(jnp.where(key_docs < my_docs, 1.0, 0.0), axis=0, keepdims=True)
        before = jnp.zeros((1, rows), jnp.float32)
        for back in range(1, REACH + 1):
            earlier = jnp.maximum(block - back, 0)
            docs = docs_ref[:, pl.ds(pl.multiple_of(earlier * rows, rows), rows)]
            same = (docs == first_doc) & (block >= back)
            before = before + jnp.where(same, 1.0, 0.0)
        before = jnp.sum(before, axis=1, keepdims=True)
        start = jnp.where(my_docs == first_doc, -before, inside).astype(jnp.int32)
        start_ref[j, 0:1, :] = start + block * rows


def local_kernel(
    index_ref, docs_ref, q0, do0, q1, do1, w_ref, lat0, lat1,
    e_ref, g_ref, k_ref, run_ref, top_ref, start_ref,
    qt_ref, dot_ref, lat_ref, v_ref, raw_ref, graw_ref,
):
    rows = q0.shape[0]
    core, chip = chip_place(index_ref)
    heads = w_ref.shape[1] // KV

    @pl.when(pl.program_id(0) == 0)
    def _():
        lat_ref[core] = lat0[...].T
        lat_ref[1 - core] = lat1[...].T
        find_starts(docs_ref, start_ref, chip, rows)

    turn_pair(qt_ref, core, q0, q1)
    turn_pair(dot_ref, core, do0, do1)
    for j in range(2):

        def k_out(h, key):
            k_ref[0, j * heads + h] = key

        def v_out(h, value):
            v_ref[j * heads + h] = value

        lift(lat_ref[j], w_ref, k_out, v_out)
        start_stats(run_ref.at[0, pl.ds(j * heads, heads)])
    for n, (j, t) in enumerate(LOCAL):
        slot = t - REACH

        def keep(h, part, cols, weights, grads):
            e_ref[0, n * heads + h, part, cols] = weights
            g_ref[0, n * heads + h, part, cols] = grads

        run = run_ref.at[0, pl.ds(j * heads, heads)]
        score_block(
            lambda h: k_ref[0, slot * heads + h], lambda h: v_ref[slot * heads + h],
            qt_ref.at[j], dot_ref.at[j], query_bounds(start_ref, chip, j, t, rows), run,
            raw_ref, graw_ref, keep,
        )
        for h in range(heads):
            top_ref[0, n * heads + h] = run[h]


def main_kernel(
    ranks,
    index_ref, docs_sref, q0, do0, q1, do1, w_ref,
    all_e, all_g, local_k, local_run, local_top, start_ref,
    lat_far, lat_swap, lat_mixed, lat_passed, lat_own, lat_other,
    dq0_ref, dq1_ref, keep_ref, send_ref, x_old, x_far, x_swap, x_own, x_other,
    q_ref, do_ref, qt_ref, dot_ref, lat_ref, lat_t_ref, e_ref, g_ref, k_ref, v_ref, top_ref,
    run_ref, end_ref, raw_ref, graw_ref, low_ref, ds_ref, dq_acc, d_acc, gw_acc, x_acc,
    r_acc, local_e, local_g, sems, kept_sems,
):
    step = pl.program_id(0)
    rows = q0.shape[0]
    heads = w_ref.shape[1] // KV
    blocks = REACH + 2
    kept_copies = [
        pltpu.make_async_copy(all_e.at[step], local_e, kept_sems.at[0]),
        pltpu.make_async_copy(all_g.at[step], local_g, kept_sems.at[1]),
    ]
    core, chip = chip_place(index_ref)

    def active(j, t):
        block = chip + t - REACH
        last_doc = docs_sref[jnp.maximum(block, 0) * rows + rows - 1]
        return (block >= 0) & (last_doc >= docs_sref[(chip + j) * rows])

    def block_rows(t):
        return pl.ds(pl.multiple_of(t * rows, rows), rows)

    def piece_rows(t, part):
        size = part.stop - part.start
        return pl.ds(pl.multiple_of(t * rows + part.start, size), size)

    def loop(first, last, when, body):
        def visit(t, carry):
            @pl.when(when(t))
            def _():
                body(t)

            return carry

        lax.fori_loop(first, last, visit, 0)

    @pl.when(step == 0)
    def _():
        places = [(lat_far, 1 + core), (lat_swap, 2 - core), (lat_own, REACH + core),
                  (lat_other, REACH + 1 - core)]
        copies = [
            pltpu.make_async_copy(source, lat_t_ref.at[:, block_rows(t)], sems.at[i])
            for i, (source, t) in enumerate(places)
        ]
        first = lat_t_ref.at[:, block_rows(0)]
        oldest = pltpu.make_async_copy(lat_mixed, first, sems.at[4])
        passed = pltpu.make_async_copy(lat_passed, first, sems.at[4])
        for copy in copies:
            copy.start()
        pl.when(core == 0)(oldest.start)
        pl.when(core == 1)(passed.start)
        for copy in kept_copies:
            copy.start()
        for copy in copies:
            copy.wait()
        oldest.wait()
        for t in range(REACH):
            part = slice(t * rows, (t + 1) * rows)
            lat_ref[part, :] = lat_t_ref[:, part].T

    @pl.when(step > 0)
    def _():
        for copy in kept_copies:
            copy.start()

    order_pair(q_ref, core, q0, q1)
    order_pair(do_ref, core, do0, do1)
    turn_pair(qt_ref, core, q0, q1)
    turn_pair(dot_ref, core, do0, do1)

    def lift_block(t):
        def k_out(h, key):
            k_ref[h, block_rows(t), :] = key

        def v_out(h, value):
            v_ref[h, block_rows(t), :] = value

        lift(lat_ref[block_rows(t), :], w_ref, k_out, v_out)

    loop(0, REACH, lambda t: active(0, t), lift_block)

    for j in range(2):
        for h in range(heads):
            run_ref[h] = local_run[0, j * heads + h]

        def first_pass(t):
            def keep(h, part, cols, weights, grads):
                e_ref[h, piece_rows(t, part), cols] = weights
                g_ref[h, piece_rows(t, part), cols] = grads

            score_block(
                lambda h: k_ref[h, block_rows(t), :], lambda h: v_ref[h, block_rows(t), :],
                qt_ref.at[j], dot_ref.at[j], query_bounds(start_ref, chip, j, t, rows), run_ref,
                raw_ref, graw_ref, keep,
            )
            for h in range(heads):
                top_ref[h, t] = run_ref[h]

        loop(j, REACH, lambda t: active(j, t), first_pass)
        for h in range(heads):
            inverse = 1.0 / run_ref[h, 1:2, :]
            end_ref[h, 0:1, :] = run_ref[h, 0:1, :]
            end_ref[h, 1:2, :] = inverse
            end_ref[h, 2:3, :] = run_ref[h, 2:3, :] * inverse

        def add(t, kept, key, top, first_q, first_k):
            grad_block(
                kept, key, top, end_ref, q_ref.at[j], do_ref.at[j], low_ref, ds_ref, dq_acc.at[j], d_acc.at[t],
                r_acc.at[t], first_q, first_k,
            )

        def second_pass(t):
            def kept(h, part, cols):
                return e_ref[h, piece_rows(t, part), cols], g_ref[h, piece_rows(t, part), cols]

            add(
                t, kept, lambda h: k_ref[h, block_rows(t), :], lambda h: top_ref[h, t, 0:1, :],
                False, j == 0,
            )

        if j == 0:
            for copy in kept_copies:
                copy.wait()
        first_q = True
        for n, (query, t) in enumerate(LOCAL):
            if query == j:
                add(
                    t,
                    lambda h, part, cols: (
                        local_e[n * heads + h, part, cols], local_g[n * heads + h, part, cols]
                    ),
                    lambda h: local_k[0, (t - REACH) * heads + h],
                    lambda h: local_top[0, n * heads + h, 0:1, :],
                    first_q, t == REACH + j,
                )
                first_q = False
        loop(j, REACH, lambda t: active(j, t), second_pass)

    def seen(t):
        return (t >= REACH) | active(0, t)

    last = step == pl.num_programs(0) - 1
    outs = ((x_old, x_old), (x_far, x_swap), (x_swap, x_far), (x_own, x_other), (x_other, x_own))

    def out_copies(t):
        part = slice(t * rows, (t + 1) * rows)
        return [pltpu.make_async_copy(lat_t_ref.at[:, part], out, sems.at[t]) for out in outs[t]]

    def leave(t):
        part = slice(t * rows, (t + 1) * rows)
        lat_t_ref[:, part] = x_acc[:, part].astype(lat_t_ref.dtype)
        for parity, copy in enumerate(out_copies(t)):
            pl.when(core == parity)(copy.start)

    def project(t, first):
        part = slice(t * rows, (t + 1) * rows)
        grads = d_acc[t].astype(jnp.bfloat16)
        weight_part = dot(lat_t_ref[:LATENT, part], grads)
        gw_acc[...] = weight_part if first else gw_acc[...] + weight_part
        latent_part = dot(w_ref[...], grads, NT)
        rope_part = r_acc[t].T

        @pl.when(step == 0)
        def _():
            x_acc[:LATENT, part] = latent_part
            x_acc[LATENT:, part] = rope_part

        @pl.when(step > 0)
        def _():
            x_acc[:LATENT, part] += latent_part
            x_acc[LATENT:, part] += rope_part

    def clear(t):
        x_acc[:, t * rows : (t + 1) * rows] = jnp.zeros((WIDTH, rows), jnp.float32)

    for n, t in enumerate((REACH, REACH + 1, *range(REACH))):
        if t >= REACH:
            project(t, n == 0)
        else:
            pl.when(seen(t))(functools.partial(project, t, False))
            pl.when(~seen(t) & (step == 0))(functools.partial(clear, t))
        pl.when(last)(functools.partial(leave, t))
    dq0_ref[...] = (dq_acc[core] * SCALE).astype(dq0_ref.dtype).T
    dq1_ref[...] = (dq_acc[1 - core] * SCALE).astype(dq1_ref.dtype).T

    share = 2 * (LATENT // ranks)
    own_x = lax.rem(index_ref[0] // 2, 2)
    for i in range(ranks // 4):
        for out, x in ((keep_ref, own_x), (send_ref, 1 - own_x)):
            source = pl.multiple_of((2 * i + x) * share, share)
            out[i * share : (i + 1) * share, :] = gw_acc[pl.ds(source, share), :].astype(out.dtype)

    @pl.when(last)
    def _():
        for t in range(blocks):
            out_copies(t)[0].wait()


def step_cols(height, size):
    return pl.BlockSpec((height, size), lambda i, index: (0, i))


def core_cols(height, size, first):
    def place(i, index):
        return (0, first(i, lax.rem(index[0], 2)))

    return pl.BlockSpec((height, size), place)


def step_block(*shape):
    return pl.BlockSpec((1, *shape), lambda i, index: (i, 0, 0, 0))


def fixed(*shape):
    return pl.BlockSpec(shape, lambda i, index: (0,) * len(shape))


SCALARS = pl.BlockSpec(memory_space=pltpu.SMEM)
ANYWHERE = pl.BlockSpec(memory_space=pl.ANY)


def call(body, steps, flops, in_specs, outs, scratch, name):
    return pl.pallas_call(
        body,
        grid_spec=pltpu.PrefetchScalarGridSpec(
            num_scalar_prefetch=1,
            grid=(steps,),
            in_specs=in_specs,
            out_specs=[spec for spec, _, _ in outs],
            scratch_shapes=[
                pltpu.VMEM(*entry) if isinstance(entry, tuple) else entry for entry in scratch
            ],
        ),
        out_shape=[jax.ShapeDtypeStruct(shape, kind) for _, shape, kind in outs],
        compiler_params=pltpu.CompilerParams(
            dimension_semantics=("arbitrary",), vmem_limit_bytes=58 * 1024 * 1024
        ),
        cost_estimate=pl.CostEstimate(
            flops=flops, bytes_accessed=16 * 1024 * 1024, transcendentals=0
        ),
        name=name,
    )


def head_specs(rows, heads, steps, in_place):
    def received(i, core):
        return i

    def own(i, core):
        return core * steps + i if in_place else i

    return [
        core_cols(rows, heads * QK, own), core_cols(rows, heads * VDIM, own),
        core_cols(rows, heads * QK, received), core_cols(rows, heads * VDIM, received),
        core_cols(LATENT, heads * KV, own),
    ]


def local_scores(index, docs, inputs, latents, heads, steps, in_place):
    rows = inputs[0].shape[0]
    low, full = jnp.bfloat16, jnp.float32
    count = len(LOCAL) * heads
    return call(
        local_kernel,
        steps,
        2 * steps * heads * rows * rows * (3 * (QK + VDIM) + 2 * KV),
        [
            fixed(1, docs.shape[1]), *head_specs(rows, heads, steps, in_place),
            fixed(WIDTH, rows), fixed(WIDTH, rows),
        ],
        [
            (step_block(count, rows, rows), (steps, count, rows, rows), low),
            (step_block(count, rows, rows), (steps, count, rows, rows), low),
            (step_block(2 * heads, rows, QK), (steps, 2 * heads, rows, QK), low),
            (step_block(2 * heads, 8, rows), (steps, 2 * heads, 8, rows), full),
            (step_block(count, 8, rows), (steps, count, 8, rows), full),
            (fixed(2, 8, rows), (2, 8, rows), jnp.int32),
        ],
        [
            ((2, heads * QK, rows), low),
            ((2, heads * VDIM, rows), low),
            ((2, rows, WIDTH), low),
            ((2 * heads, rows, VDIM), low),
            ((heads, rows, rows), full),
            ((heads, rows, rows), full),
        ],
        "local_scores",
    )(index, docs, *inputs, *latents)


def attention(index, doc_ids, inputs, kept, latents, heads, steps, ranks, in_place):
    rows = inputs[0].shape[0]
    low, full = jnp.bfloat16, jnp.float32
    count = len(LOCAL) * heads
    window = (REACH + 2) * rows
    far = REACH * rows
    half = (LATENT // 2, steps * heads * KV)
    return call(
        functools.partial(main_kernel, ranks),
        steps,
        2 * steps * heads * rows * rows * (5 * (QK + VDIM) + 8 * (2 * QK + VDIM) + 13 * KV),
        [
            SCALARS, *head_specs(rows, heads, steps, in_place), ANYWHERE, ANYWHERE,
            step_block(2 * heads, rows, QK), step_block(2 * heads, 8, rows),
            step_block(count, 8, rows), fixed(2, 8, rows),
        ]
        + [ANYWHERE] * len(latents),
        [(step_cols(rows, heads * QK), (rows, steps * heads * QK), low)] * 2
        + [(step_cols(LATENT // 2, heads * KV), half, low)] * 2
        + [(ANYWHERE, (WIDTH, rows), low)] * (REACH + 2),
        [
            ((2, rows, heads * QK), low),
            ((2, rows, heads * VDIM), low),
            ((2, heads * QK, rows), low),
            ((2, heads * VDIM, rows), low),
            ((far, WIDTH), low),
            ((WIDTH, window), low),
            ((heads, far, rows), low),
            ((heads, far, rows), low),
            ((heads, far, QK), low),
            ((heads, far, VDIM), low),
            ((heads, REACH, 8, rows), full),
            ((heads, 8, rows), full),
            ((heads, 8, rows), full),
            ((heads, rows, rows), full),
            ((heads, rows, rows), full),
            ((heads, rows, rows), low),
            ((heads, rows, rows), low),
            ((2, heads * QK, rows), full),
            ((REACH + 2, rows, heads * KV), full),
            ((LATENT, heads * KV), full),
            ((WIDTH, window), full),
            ((REACH + 2, rows, ROPE), full),
            ((count, rows, rows), low),
            ((count, rows, rows), low),
            pltpu.SemaphoreType.DMA((5,)),
            pltpu.SemaphoreType.DMA((2,)),
        ],
        "attention",
    )(index, doc_ids, *inputs, *kept, *latents)


def permute(value, axis, target):
    count = lax.axis_size(axis)
    pairs = [(s, target(s)) for s in range(count) if 0 <= target(s) < count]
    return lax.ppermute(value, axis, pairs)


def local(kv_latent, queries, grad_out, kv_up_weight, doc_ids):
    ranks = lax.axis_size("ctx")
    position = lax.axis_index("ctx").astype(jnp.int32)
    index, core = position[None], lax.rem(position, 2)
    low, full = jnp.bfloat16, jnp.float32
    docs = doc_ids[None]
    core_heads = kv_up_weight.shape[1] // KV // 2
    heads = min(2, core_heads)
    steps = core_heads // heads

    def own_heads(value, which):
        size = value.shape[1] // 2
        return lax.dynamic_slice_in_dim(value, which * size, size, axis=1)

    def across(value):
        return permute(value, "ctx", lambda s: s ^ 1)

    latent = kv_latent.T
    far = permute(latent, "ctx", lambda s: s + 2)
    mixed = permute(latent, "ctx", lambda s: s + 3 if s % 2 else -1)
    other = across(latent)
    in_place = heads * QK % 128 == 0
    inputs = (
        queries if in_place else own_heads(queries, core),
        grad_out if in_place else own_heads(grad_out, core),
        across(own_heads(queries, 1 - core)),
        across(own_heads(grad_out, 1 - core)),
        kv_up_weight if in_place else own_heads(kv_up_weight, core),
    )
    *kept, starts = local_scores(index, docs, inputs, (latent, other), heads, steps, in_place)
    far, mixed, starts = lax.optimization_barrier((far, mixed, starts))
    swapped = across(far)
    passed = permute(mixed, "ctx", lambda s: -1 if s % 2 else s + 1)

    dq_own, dq_other, keep, send, to_old, to_far, to_swap, mine, to_other = attention(
        index, doc_ids, inputs, (*kept, starts),
        (far, swapped, mixed, passed, latent, other), heads, steps, ranks, in_place,
    )

    head, head_count = lax.axis_index("head"), lax.axis_size("head")
    share = WIDTH // head_count

    def turned(value, turn, ctx=range(ranks)):
        turns = [
            (c * head_count + s, c * head_count + (s + turn) % head_count)
            for c in ctx
            for s in range(head_count)
        ]
        return lax.ppermute(value, ("ctx", "head"), turns)

    arrived = []

    def head_share(value, ctx=range(ranks), after=()):
        def rows_of(which):
            return lax.dynamic_slice_in_dim(value, which * share, share, axis=0)

        total = rows_of(head).astype(full)
        for turn in range(1, head_count):
            target = lax.rem(head + turn, head_count)
            received, *_ = lax.optimization_barrier((turned(rows_of(target), turn, ctx), *after))
            arrived.append(received)
            total = total + received.astype(full)
        return total

    from_x = permute(send, "ctx", lambda s: s ^ 2)
    from_swap = across(to_swap)
    from_old = permute(to_old, "ctx", lambda s: s - 1 if s % 2 else -1)
    from_other = across(to_other)
    far_sum = head_share((to_far.astype(full) + from_swap.astype(full)).astype(low)).astype(low)
    old_sum = (to_old.astype(full) + from_old.astype(full)).astype(low)
    old_sum = head_share(old_sum, range(0, ranks, 2), (far_sum,)).astype(low)
    from_far = permute(far_sum, "ctx", lambda s: s - 2)
    from_mixed = permute(old_sum, "ctx", lambda s: -1 if s % 2 else s - 3)
    own_sum = (mine.astype(full) + from_other.astype(full)).astype(low)
    own_sum, *_ = lax.optimization_barrier((own_sum, far_sum))
    total = head_share(own_sum)

    from_x, *_ = lax.optimization_barrier((from_x, far_sum, old_sum, arrived[-1]))
    plane = (keep.astype(full) + from_x.astype(full)).astype(low)
    columns = [list(range(first, ranks, 4)) for first in range(4)]
    pieces = lax.all_to_all(plane, "ctx", 0, 0, axis_index_groups=columns, tiled=True)
    rows = LATENT // ranks
    summed = jnp.sum(pieces.reshape(ranks // 4, 2 * rows, -1).astype(full), axis=0)

    def in_order(own, received):
        first = jnp.where(core == 0, own, received)
        second = jnp.where(core == 0, received, own)
        return jnp.concatenate([first, second], axis=1)

    rows_own = lax.dynamic_slice_in_dim(summed, core * rows, rows, axis=0)
    rows_other = lax.dynamic_slice_in_dim(summed, (1 - core) * rows, rows, axis=0)
    grad_weight = in_order(rows_own, across(rows_other))
    grad_queries = in_order(dq_own, across(dq_other))

    total = (total + from_mixed.astype(full) + from_far.astype(full)).astype(low)
    shares = [total] + [turned(total, turn) for turn in range(1, head_count)]
    ordered = []
    for place in range(head_count):
        picked = shares[0]
        for turn in range(1, head_count):
            picked = jnp.where(lax.rem(head - place + head_count, head_count) == turn, shares[turn], picked)
        ordered.append(picked)
    return grad_queries, jnp.concatenate(ordered, axis=0).T, grad_weight


def solution(mesh):
    return jax.shard_map(
        local,
        mesh=mesh,
        in_specs=(P("ctx", None), P("ctx", "head"), P("ctx", "head"), P(None, "head"), P()),
        out_specs=(P("ctx", "head"), P("ctx", None), P("ctx", "head")),
        check_vma=False,
    )
```

```python
import functools
import math

import jax
import jax.numpy as jnp
from jax import lax
from jax.experimental import pallas as pl
from jax.experimental.pallas import tpu as pltpu
from jax.sharding import PartitionSpec as P

NOPE = 128
ROPE = 64
VDIM = 128
LATENT = 512
REACH = 3
QK = NOPE + ROPE
KV = NOPE + VDIM
WIDTH = LATENT + ROPE
LANES = 128
PIECE = 256

MASKED = -1e30
FLOOR = -1e20
SCALE = 1.0 / math.sqrt(QK)
SCALE2 = SCALE * math.log2(math.e)

NT = (((1,), (1,)), ((), ()))
NN = (((1,), (0,)), ((), ()))


def dot(a, b, dims=NN):
    return lax.dot_general(a, b, dims, preferred_element_type=jnp.float32)


def head_cols(h, size):
    return slice(h * size, (h + 1) * size)


def fold(value, combine):
    return combine(value.reshape(-1, 8, value.shape[1]), axis=0)


def fold(value, combine):
    return combine(value.reshape(-1, 8, value.shape[1]), axis=0)


def lift(latent, w_ref, k_out, v_out):
    for h in range(w_ref.shape[1] // KV):
        lifted = dot(latent[:, :LATENT], w_ref[:, head_cols(h, KV)]).astype(jnp.bfloat16)
        k_out(h, jnp.concatenate([lifted[:, :NOPE], latent[:, LATENT:]], axis=1))
        v_out(h, lifted[:, NOPE:])


def score_block(key, value, q_ref, do_ref, bounds, run_ref, raw_ref, graw_ref, keep, limit):
    rows = do_ref.shape[0]
    lower, upper = bounds
    index = lax.broadcasted_iota(jnp.int32, (LANES, LANES), 0)
    parts = [slice(r, r + LANES) for r in range(0, rows, LANES)]

    def multiply(h, first):
        cols = slice(first, first + PIECE)
        raw_ref[h, :, cols] = dot(key(h), q_ref[cols, head_cols(h, QK)], NT)
        graw_ref[h, :, cols] = dot(value(h), do_ref[cols, head_cols(h, VDIM)], NT)

    def weigh(h, first):
        for c in range(first, first + PIECE, LANES):
            cols = slice(c, c + LANES)
            high = None
            for part in parts:
                seen = index >= lower[:, cols] - part.start
                if upper is not None:
                    seen = seen & (index <= upper[:, cols] - part.start)
                scores = jnp.where(seen, raw_ref[h, part, cols] * SCALE2, MASKED)
                raw_ref[h, part, cols] = scores
                piece = fold(scores, jnp.max)
                high = piece if high is None else jnp.maximum(high, piece)
            old_top = run_ref[h, 0:1, cols]
            new_top = jnp.maximum(old_top, jnp.max(high, axis=0, keepdims=True))
            mass, cross = 0.0, 0.0
            for part in parts:
                weights = jnp.exp2(raw_ref[h, part, cols] - new_top)
                grads = graw_ref[h, part, cols]
                keep(h, part, cols, weights.astype(jnp.bfloat16), grads.astype(jnp.bfloat16))
                mass = mass + fold(weights, jnp.sum)
                cross = cross + fold(weights * grads, jnp.sum)
            factor = jnp.exp2(old_top - new_top)
            run_ref[h, 0:1, cols] = new_top
            run_ref[h, 1:2, cols] = run_ref[h, 1:2, cols] * factor + jnp.sum(
                mass, axis=0, keepdims=True
            )
            run_ref[h, 2:3, cols] = run_ref[h, 2:3, cols] * factor + jnp.sum(
                cross, axis=0, keepdims=True
            )

    alternate(limit, do_ref.shape[1] // VDIM, multiply, weigh)


def alternate(limit, heads, first, second):
    pieces = [(h, c) for h in range(heads) for c in range(0, limit, PIECE)]
    first(*pieces[0])
    for now, following in zip(pieces, pieces[1:] + [None]):
        if following:
            first(*following)
        second(*now)


def grad_block(kept, key, top, end_ref, q_ref, do_ref, low_ref, ds_ref, dq_acc, d_acc, r_acc, first_q, first_k, limit):
    def put(ref, part, value, first):
        ref[:, part] = value if first else ref[:, part] + value

    rows = do_ref.shape[0]
    heads = do_ref.shape[1] // VDIM
    sums, turned = {}, {}

    def weigh(h, first):
        for c in range(first, first + PIECE, LANES):
            cols = slice(c, c + LANES)
            factor = jnp.exp2(top(h)[:, cols] - end_ref[h, 0:1, cols]) * end_ref[h, 1:2, cols]
            delta = end_ref[h, 2:3, cols]
            for r in range(0, rows, LANES):
                part = slice(r, r + LANES)
                weights, grads = kept(h, part, cols)
                probs = weights.astype(jnp.float32) * factor
                low_ref[h, part, cols] = probs.astype(jnp.bfloat16)
                ds_ref[h, part, cols] = (
                    probs * (grads.astype(jnp.float32) - delta)
                ).astype(jnp.bfloat16)

    def multiply(h, first):
        cols = slice(first, first + PIECE)
        low, dscore = low_ref[h, :, cols], ds_ref[h, :, cols]
        dvalue = dot(low, do_ref[cols, head_cols(h, VDIM)])
        dkey = dot(dscore, q_ref[cols, head_cols(h, QK)])
        own = head_cols(h, QK)
        if not first:
            turned[h] = key(h).T
        dq = dot(turned[h], dscore)
        dq_acc[own, cols] = dq if first_q else dq_acc[own, cols] + dq
        if first:
            dvalue, dkey = sums[h][0] + dvalue, sums[h][1] + dkey
        sums[h] = dvalue, dkey
        if first + PIECE == limit:
            dkey = dkey * SCALE
            put(d_acc, slice(h * KV, h * KV + NOPE), dkey[:, :NOPE], first_k)
            put(d_acc, slice(h * KV + NOPE, (h + 1) * KV), dvalue, first_k)
            put(r_acc, slice(0, ROPE), dkey[:, NOPE:], first_k and h == 0)

    alternate(limit, heads, weigh, multiply)


def start_stats(run_ref):
    count, rows = run_ref.shape[0], run_ref.shape[2]
    for h in range(count):
        run_ref[h, 0:1, :] = jnp.full((1, rows), FLOOR, jnp.float32)
        run_ref[h, 1:8, :] = jnp.zeros((7, rows), jnp.float32)


def chip_place(index_ref):
    core = lax.rem(index_ref[0], 2)
    return core, index_ref[0] - core


def order_pair(out_ref, core, own, other):
    out_ref[core] = own[...]
    out_ref[1 - core] = other[...]


LOCAL = ((1, REACH), (0, REACH), (1, REACH + 1))


def query_bounds(start_ref, chip, j, t, rows):
    lower = start_ref[j, 0:1, :] - (chip + t - REACH) * rows
    own = isinstance(t, int) and t == j + REACH
    return lower, lax.broadcasted_iota(jnp.int32, (1, rows), 1) if own else None


def find_starts(docs_ref, start_ref, chip, rows):
    for j in range(2):
        block = chip + j
        my_docs = docs_ref[:, pl.ds(pl.multiple_of(block * rows, rows), rows)]
        first_doc = my_docs[:, :1]
        key_docs = jnp.broadcast_to(my_docs, (128, rows)).T[:, :1]
        inside = jnp.sum(jnp.where(key_docs < my_docs, 1.0, 0.0), axis=0, keepdims=True)
        before = jnp.zeros((1, rows), jnp.float32)
        for back in range(1, REACH + 1):
            earlier = jnp.maximum(block - back, 0)
            docs = docs_ref[:, pl.ds(pl.multiple_of(earlier * rows, rows), rows)]
            same = (docs == first_doc) & (block >= back)
            before = before + jnp.where(same, 1.0, 0.0)
        before = jnp.sum(before, axis=1, keepdims=True)
        start = jnp.where(my_docs == first_doc, -before, inside).astype(jnp.int32)
        start_ref[j, 0:1, :] = start + block * rows


def local_kernel(
    index_ref, docs_ref, q0, do0, q1, do1, w_ref, lat0, lat1,
    e_ref, g_ref, k_ref, run_ref, top_ref, start_ref,
    q_ref, do_ref, lat_ref, v_ref, raw_ref, graw_ref,
):
    rows = q0.shape[0]
    core, chip = chip_place(index_ref)
    heads = w_ref.shape[1] // KV

    @pl.when(pl.program_id(0) == 0)
    def _():
        lat_ref[core] = lat0[...].T
        lat_ref[1 - core] = lat1[...].T
        find_starts(docs_ref, start_ref, chip, rows)

    order_pair(q_ref, core, q0, q1)
    order_pair(do_ref, core, do0, do1)
    for j in range(2):

        def k_out(h, key):
            k_ref[0, j * heads + h] = key

        def v_out(h, value):
            v_ref[j * heads + h] = value

        lift(lat_ref[j], w_ref, k_out, v_out)
        start_stats(run_ref.at[0, pl.ds(j * heads, heads)])
    for n, (j, t) in enumerate(LOCAL):
        slot = t - REACH

        def keep(h, part, cols, weights, grads):
            e_ref[0, n * heads + h, part, cols] = weights
            g_ref[0, n * heads + h, part, cols] = grads

        run = run_ref.at[0, pl.ds(j * heads, heads)]
        score_block(
            lambda h: k_ref[0, slot * heads + h], lambda h: v_ref[slot * heads + h],
            q_ref.at[j], do_ref.at[j], query_bounds(start_ref, chip, j, t, rows), run,
            raw_ref, graw_ref, keep, rows,
        )
        for h in range(heads):
            top_ref[0, n * heads + h] = run[h]


def main_kernel(
    ranks,
    index_ref, docs_sref, q0, do0, q1, do1, w_ref,
    all_e, all_g, local_k, local_run, local_top, start_ref,
    lat_far, lat_swap, lat_mixed, lat_passed, lat_own, lat_other,
    dq0_ref, dq1_ref, keep_ref, send_ref, x_old, x_far, x_swap, x_own, x_other,
    q_ref, do_ref, lat_ref, lat_t_ref, e_ref, g_ref, k_ref, v_ref, top_ref,
    run_ref, end_ref, raw_ref, graw_ref, low_ref, ds_ref, dq_acc, d_acc, gw_acc, x_acc,
    r_acc, local_e, local_g, sems, kept_sems,
):
    step = pl.program_id(0)
    rows = q0.shape[0]
    heads = w_ref.shape[1] // KV
    blocks = REACH + 2
    kept_copies = [
        pltpu.make_async_copy(all_e.at[step], local_e, kept_sems.at[0]),
        pltpu.make_async_copy(all_g.at[step], local_g, kept_sems.at[1]),
    ]
    core, chip = chip_place(index_ref)

    def active(j, t):
        block = chip + t - REACH
        last_doc = docs_sref[jnp.maximum(block, 0) * rows + rows - 1]
        return (block >= 0) & (last_doc >= docs_sref[(chip + j) * rows])

    def wide(j, t):
        last_doc = docs_sref[jnp.maximum(chip + t - REACH, 0) * rows + rows - 1]
        return last_doc >= docs_sref[(chip + j) * rows + PIECE]

    def by_width(j, t, body):
        pl.when(wide(j, t))(lambda: body(t, rows))
        pl.when(~wide(j, t))(lambda: body(t, PIECE))

    def block_rows(t):
        return pl.ds(pl.multiple_of(t * rows, rows), rows)

    def piece_rows(t, part):
        size = part.stop - part.start
        return pl.ds(pl.multiple_of(t * rows + part.start, size), size)

    def loop(first, last, when, body):
        def visit(t, carry):
            @pl.when(when(t))
            def _():
                body(t)

            return carry

        lax.fori_loop(first, last, visit, 0)

    @pl.when(step == 0)
    def _():
        places = [(lat_far, 1 + core), (lat_swap, 2 - core), (lat_own, REACH + core),
                  (lat_other, REACH + 1 - core)]
        copies = [
            pltpu.make_async_copy(source, lat_t_ref.at[:, block_rows(t)], sems.at[i])
            for i, (source, t) in enumerate(places)
        ]
        first = lat_t_ref.at[:, block_rows(0)]
        oldest = pltpu.make_async_copy(lat_mixed, first, sems.at[4])
        passed = pltpu.make_async_copy(lat_passed, first, sems.at[4])
        for copy in copies:
            copy.start()
        pl.when(core == 0)(oldest.start)
        pl.when(core == 1)(passed.start)
        for copy in kept_copies:
            copy.start()
        for copy in copies:
            copy.wait()
        oldest.wait()
        for t in range(REACH):
            part = slice(t * rows, (t + 1) * rows)
            lat_ref[part, :] = lat_t_ref[:, part].T

    @pl.when(step > 0)
    def _():
        for copy in kept_copies:
            copy.start()

    order_pair(q_ref, core, q0, q1)
    order_pair(do_ref, core, do0, do1)

    def lift_block(t):
        def k_out(h, key):
            k_ref[h, block_rows(t), :] = key

        def v_out(h, value):
            v_ref[h, block_rows(t), :] = value

        lift(lat_ref[block_rows(t), :], w_ref, k_out, v_out)

    loop(0, REACH, lambda t: active(0, t), lift_block)

    for j in range(2):
        for h in range(heads):
            run_ref[h] = local_run[0, j * heads + h]

        def first_pass(t, limit):
            def keep(h, part, cols, weights, grads):
                e_ref[h, piece_rows(t, part), cols] = weights
                g_ref[h, piece_rows(t, part), cols] = grads

            score_block(
                lambda h: k_ref[h, block_rows(t), :], lambda h: v_ref[h, block_rows(t), :],
                q_ref.at[j], do_ref.at[j], query_bounds(start_ref, chip, j, t, rows), run_ref,
                raw_ref, graw_ref, keep, limit,
            )
            for h in range(heads):
                top_ref[h, t] = run_ref[h]

        loop(j, REACH, lambda t: active(j, t), lambda t: by_width(j, t, first_pass))
        for h in range(heads):
            inverse = 1.0 / run_ref[h, 1:2, :]
            end_ref[h, 0:1, :] = run_ref[h, 0:1, :]
            end_ref[h, 1:2, :] = inverse
            end_ref[h, 2:3, :] = run_ref[h, 2:3, :] * inverse

        def add(t, kept, key, top, first_q, first_k, limit=rows):
            grad_block(
                kept, key, top, end_ref, q_ref.at[j], do_ref.at[j], low_ref, ds_ref, dq_acc.at[j], d_acc.at[t],
                r_acc.at[t], first_q, first_k, limit,
            )

        def second_pass(t, limit):
            def kept(h, part, cols):
                return e_ref[h, piece_rows(t, part), cols], g_ref[h, piece_rows(t, part), cols]

            add(
                t, kept, lambda h: k_ref[h, block_rows(t), :], lambda h: top_ref[h, t, 0:1, :],
                False, j == 0, limit,
            )

        if j == 0:
            for copy in kept_copies:
                copy.wait()
        first_q = True
        for n, (query, t) in enumerate(LOCAL):
            if query == j:
                add(
                    t,
                    lambda h, part, cols: (
                        local_e[n * heads + h, part, cols], local_g[n * heads + h, part, cols]
                    ),
                    lambda h: local_k[0, (t - REACH) * heads + h],
                    lambda h: local_top[0, n * heads + h, 0:1, :],
                    first_q, t == REACH + j,
                )
                first_q = False
        loop(j, REACH, lambda t: active(j, t), lambda t: by_width(j, t, second_pass))

    def seen(t):
        return (t >= REACH) | active(0, t)

    last = step == pl.num_programs(0) - 1
    outs = ((x_old, x_old), (x_far, x_swap), (x_swap, x_far), (x_own, x_other), (x_other, x_own))

    def out_copies(t):
        part = slice(t * rows, (t + 1) * rows)
        return [pltpu.make_async_copy(lat_t_ref.at[:, part], out, sems.at[t]) for out in outs[t]]

    def leave(t):
        part = slice(t * rows, (t + 1) * rows)
        lat_t_ref[:, part] = x_acc[:, part].astype(lat_t_ref.dtype)
        for parity, copy in enumerate(out_copies(t)):
            pl.when(core == parity)(copy.start)

    def project(t, first):
        part = slice(t * rows, (t + 1) * rows)
        grads = d_acc[t].astype(jnp.bfloat16)
        weight_part = dot(lat_t_ref[:LATENT, part], grads)
        gw_acc[...] = weight_part if first else gw_acc[...] + weight_part
        latent_part = dot(w_ref[...], grads, NT)
        rope_part = r_acc[t].T

        @pl.when(step == 0)
        def _():
            x_acc[:LATENT, part] = latent_part
            x_acc[LATENT:, part] = rope_part

        @pl.when(step > 0)
        def _():
            x_acc[:LATENT, part] += latent_part
            x_acc[LATENT:, part] += rope_part

    def clear(t):
        x_acc[:, t * rows : (t + 1) * rows] = jnp.zeros((WIDTH, rows), jnp.float32)

    for n, t in enumerate((REACH, REACH + 1, *range(REACH))):
        if t >= REACH:
            project(t, n == 0)
        else:
            pl.when(seen(t))(functools.partial(project, t, False))
            pl.when(~seen(t) & (step == 0))(functools.partial(clear, t))
        pl.when(last)(functools.partial(leave, t))
    dq0_ref[...] = (dq_acc[core] * SCALE).astype(dq0_ref.dtype).T
    dq1_ref[...] = (dq_acc[1 - core] * SCALE).astype(dq1_ref.dtype).T

    share = 2 * (LATENT // ranks)
    own_x = lax.rem(index_ref[0] // 2, 2)
    for i in range(ranks // 4):
        for out, x in ((keep_ref, own_x), (send_ref, 1 - own_x)):
            source = pl.multiple_of((2 * i + x) * share, share)
            out[i * share : (i + 1) * share, :] = gw_acc[pl.ds(source, share), :].astype(out.dtype)

    @pl.when(last)
    def _():
        for t in range(blocks):
            out_copies(t)[0].wait()


def step_cols(height, size):
    return pl.BlockSpec((height, size), lambda i, index: (0, i))


def core_cols(height, size, first):
    def place(i, index):
        return (0, first(i, lax.rem(index[0], 2)))

    return pl.BlockSpec((height, size), place)


def step_block(*shape):
    return pl.BlockSpec((1, *shape), lambda i, index: (i, 0, 0, 0))


def fixed(*shape):
    return pl.BlockSpec(shape, lambda i, index: (0,) * len(shape))


SCALARS = pl.BlockSpec(memory_space=pltpu.SMEM)
ANYWHERE = pl.BlockSpec(memory_space=pl.ANY)


def call(body, steps, flops, in_specs, outs, scratch, name):
    return pl.pallas_call(
        body,
        grid_spec=pltpu.PrefetchScalarGridSpec(
            num_scalar_prefetch=1,
            grid=(steps,),
            in_specs=in_specs,
            out_specs=[spec for spec, _, _ in outs],
            scratch_shapes=[
                pltpu.VMEM(*entry) if isinstance(entry, tuple) else entry for entry in scratch
            ],
        ),
        out_shape=[jax.ShapeDtypeStruct(shape, kind) for _, shape, kind in outs],
        compiler_params=pltpu.CompilerParams(
            dimension_semantics=("arbitrary",), vmem_limit_bytes=58 * 1024 * 1024
        ),
        cost_estimate=pl.CostEstimate(
            flops=flops, bytes_accessed=16 * 1024 * 1024, transcendentals=0
        ),
        name=name,
    )


def head_specs(rows, heads, steps, in_place):
    def received(i, core):
        return i

    def own(i, core):
        return core * steps + i if in_place else i

    return [
        core_cols(rows, heads * QK, own), core_cols(rows, heads * VDIM, own),
        core_cols(rows, heads * QK, received), core_cols(rows, heads * VDIM, received),
        core_cols(LATENT, heads * KV, own),
    ]


def local_scores(index, docs, inputs, latents, heads, steps, in_place):
    rows = inputs[0].shape[0]
    low, full = jnp.bfloat16, jnp.float32
    count = len(LOCAL) * heads
    return call(
        local_kernel,
        steps,
        2 * steps * heads * rows * rows * (3 * (QK + VDIM) + 2 * KV),
        [
            fixed(1, docs.shape[1]), *head_specs(rows, heads, steps, in_place),
            fixed(WIDTH, rows), fixed(WIDTH, rows),
        ],
        [
            (step_block(count, rows, rows), (steps, count, rows, rows), low),
            (step_block(count, rows, rows), (steps, count, rows, rows), low),
            (step_block(2 * heads, rows, QK), (steps, 2 * heads, rows, QK), low),
            (step_block(2 * heads, 8, rows), (steps, 2 * heads, 8, rows), full),
            (step_block(count, 8, rows), (steps, count, 8, rows), full),
            (fixed(2, 8, rows), (2, 8, rows), jnp.int32),
        ],
        [
            ((2, rows, heads * QK), low),
            ((2, rows, heads * VDIM), low),
            ((2, rows, WIDTH), low),
            ((2 * heads, rows, VDIM), low),
            ((heads, rows, rows), full),
            ((heads, rows, rows), full),
        ],
        "local_scores",
    )(index, docs, *inputs, *latents)


def attention(index, doc_ids, inputs, kept, latents, heads, steps, ranks, in_place):
    rows = inputs[0].shape[0]
    low, full = jnp.bfloat16, jnp.float32
    count = len(LOCAL) * heads
    window = (REACH + 2) * rows
    far = REACH * rows
    half = (LATENT // 2, steps * heads * KV)
    return call(
        functools.partial(main_kernel, ranks),
        steps,
        2 * steps * heads * rows * rows * (5 * (QK + VDIM) + 8 * (2 * QK + VDIM) + 13 * KV),
        [
            SCALARS, *head_specs(rows, heads, steps, in_place), ANYWHERE, ANYWHERE,
            step_block(2 * heads, rows, QK), step_block(2 * heads, 8, rows),
            step_block(count, 8, rows), fixed(2, 8, rows),
        ]
        + [ANYWHERE] * len(latents),
        [(step_cols(rows, heads * QK), (rows, steps * heads * QK), low)] * 2
        + [(step_cols(LATENT // 2, heads * KV), half, low)] * 2
        + [(ANYWHERE, (WIDTH, rows), low)] * (REACH + 2),
        [
            ((2, rows, heads * QK), low),
            ((2, rows, heads * VDIM), low),
            ((far, WIDTH), low),
            ((WIDTH, window), low),
            ((heads, far, rows), low),
            ((heads, far, rows), low),
            ((heads, far, QK), low),
            ((heads, far, VDIM), low),
            ((heads, REACH, 8, rows), full),
            ((heads, 8, rows), full),
            ((heads, 8, rows), full),
            ((heads, rows, rows), full),
            ((heads, rows, rows), full),
            ((heads, rows, rows), low),
            ((heads, rows, rows), low),
            ((2, heads * QK, rows), full),
            ((REACH + 2, rows, heads * KV), full),
            ((LATENT, heads * KV), full),
            ((WIDTH, window), full),
            ((REACH + 2, rows, ROPE), full),
            ((count, rows, rows), low),
            ((count, rows, rows), low),
            pltpu.SemaphoreType.DMA((5,)),
            pltpu.SemaphoreType.DMA((2,)),
        ],
        "attention",
    )(index, doc_ids, *inputs, *kept, *latents)


def permute(value, axis, target):
    count = lax.axis_size(axis)
    pairs = [(s, target(s)) for s in range(count) if 0 <= target(s) < count]
    return lax.ppermute(value, axis, pairs)


def local(kv_latent, queries, grad_out, kv_up_weight, doc_ids):
    ranks = lax.axis_size("ctx")
    position = lax.axis_index("ctx").astype(jnp.int32)
    index, core = position[None], lax.rem(position, 2)
    low, full = jnp.bfloat16, jnp.float32
    docs = doc_ids[None]
    core_heads = kv_up_weight.shape[1] // KV // 2
    heads = min(2, core_heads)
    steps = core_heads // heads

    def own_heads(value, which):
        size = value.shape[1] // 2
        return lax.dynamic_slice_in_dim(value, which * size, size, axis=1)

    def across(value):
        return permute(value, "ctx", lambda s: s ^ 1)

    latent = kv_latent.T
    far = permute(latent, "ctx", lambda s: s + 2)
    mixed = permute(latent, "ctx", lambda s: s + 3 if s % 2 else -1)
    other = across(latent)
    in_place = heads * QK % 128 == 0
    inputs = (
        queries if in_place else own_heads(queries, core),
        grad_out if in_place else own_heads(grad_out, core),
        across(own_heads(queries, 1 - core)),
        across(own_heads(grad_out, 1 - core)),
        kv_up_weight if in_place else own_heads(kv_up_weight, core),
    )
    *kept, starts = local_scores(index, docs, inputs, (latent, other), heads, steps, in_place)
    far, mixed, starts = lax.optimization_barrier((far, mixed, starts))
    swapped = across(far)
    passed = permute(mixed, "ctx", lambda s: -1 if s % 2 else s + 1)

    dq_own, dq_other, keep, send, to_old, to_far, to_swap, mine, to_other = attention(
        index, doc_ids, inputs, (*kept, starts),
        (far, swapped, mixed, passed, latent, other), heads, steps, ranks, in_place,
    )

    head, head_count = lax.axis_index("head"), lax.axis_size("head")
    share = WIDTH // head_count

    def turned(value, turn, ctx=range(ranks)):
        turns = [
            (c * head_count + s, c * head_count + (s + turn) % head_count)
            for c in ctx
            for s in range(head_count)
        ]
        return lax.ppermute(value, ("ctx", "head"), turns)

    def head_share(value, ctx=range(ranks)):
        def rows_of(which):
            return lax.dynamic_slice_in_dim(value, which * share, share, axis=0)

        total = rows_of(head).astype(full)
        for turn in range(1, head_count):
            target = lax.rem(head + turn, head_count)
            total = total + turned(rows_of(target), turn, ctx).astype(full)
        return total

    from_x = permute(send, "ctx", lambda s: s ^ 2)
    from_swap = across(to_swap)
    from_old = permute(to_old, "ctx", lambda s: s - 1 if s % 2 else -1)
    from_other = across(to_other)
    far_sum = head_share((to_far.astype(full) + from_swap.astype(full)).astype(low)).astype(low)
    old_sum = (to_old.astype(full) + from_old.astype(full)).astype(low)
    old_sum = head_share(old_sum, range(0, ranks, 2)).astype(low)
    from_far = permute(far_sum, "ctx", lambda s: s - 2)
    from_mixed = permute(old_sum, "ctx", lambda s: -1 if s % 2 else s - 3)
    own_sum = (mine.astype(full) + from_other.astype(full)).astype(low)
    own_sum, *_ = lax.optimization_barrier((own_sum, far_sum))
    total = head_share(own_sum)

    from_x, *_ = lax.optimization_barrier((from_x, far_sum, old_sum))
    plane = (keep.astype(full) + from_x.astype(full)).astype(low)
    columns = [list(range(first, ranks, 4)) for first in range(4)]
    pieces = lax.all_to_all(plane, "ctx", 0, 0, axis_index_groups=columns, tiled=True)
    rows = LATENT // ranks
    summed = jnp.sum(pieces.reshape(ranks // 4, 2 * rows, -1).astype(full), axis=0)

    def in_order(own, received):
        first = jnp.where(core == 0, own, received)
        second = jnp.where(core == 0, received, own)
        return jnp.concatenate([first, second], axis=1)

    rows_own = lax.dynamic_slice_in_dim(summed, core * rows, rows, axis=0)
    rows_other = lax.dynamic_slice_in_dim(summed, (1 - core) * rows, rows, axis=0)
    grad_weight = in_order(rows_own, across(rows_other))
    grad_queries = in_order(dq_own, across(dq_other))

    total = (total + from_mixed.astype(full) + from_far.astype(full)).astype(low)
    shares = [total] + [turned(total, turn) for turn in range(1, head_count)]
    ordered = []
    for place in range(head_count):
        picked = shares[0]
        for turn in range(1, head_count):
            picked = jnp.where(lax.rem(head - place + head_count, head_count) == turn, shares[turn], picked)
        ordered.append(picked)
    return grad_queries, jnp.concatenate(ordered, axis=0).T, grad_weight


def solution(mesh):
    return jax.shard_map(
        local,
        mesh=mesh,
        in_specs=(P("ctx", None), P("ctx", "head"), P("ctx", "head"), P(None, "head"), P()),
        out_specs=(P("ctx", "head"), P("ctx", None), P("ctx", "head")),
        check_vma=False,
    )
```

```python
import functools
import math

import jax
import jax.numpy as jnp
from jax import lax
from jax.experimental import pallas as pl
from jax.experimental.pallas import tpu as pltpu
from jax.sharding import PartitionSpec as P

NOPE = 128
ROPE = 64
VDIM = 128
LATENT = 512
REACH = 3
QK = NOPE + ROPE
KV = NOPE + VDIM
WIDTH = LATENT + ROPE
LANES = 128
PIECE = 256

MASKED = -1e30
FLOOR = -1e20
SCALE = 1.0 / math.sqrt(QK)
SCALE2 = SCALE * math.log2(math.e)

NT = (((1,), (1,)), ((), ()))
NN = (((1,), (0,)), ((), ()))


def dot(a, b, dims=NN):
    return lax.dot_general(a, b, dims, preferred_element_type=jnp.float32)


def head_cols(h, size):
    return slice(h * size, (h + 1) * size)


def fold(value, combine):
    return combine(value.reshape(-1, 8, value.shape[1]), axis=0)


def fold(value, combine):
    return combine(value.reshape(-1, 8, value.shape[1]), axis=0)


def lift(latent, w_ref, k_out, v_out):
    for h in range(w_ref.shape[1] // KV):
        lifted = dot(latent[:, :LATENT], w_ref[:, head_cols(h, KV)]).astype(jnp.bfloat16)
        k_out(h, jnp.concatenate([lifted[:, :NOPE], latent[:, LATENT:]], axis=1))
        v_out(h, lifted[:, NOPE:])


def score_block(key, value, q_ref, do_ref, bounds, run_ref, raw_ref, graw_ref, keep):
    rows = do_ref.shape[0]
    lower, upper = bounds
    index = lax.broadcasted_iota(jnp.int32, (LANES, LANES), 0)
    parts = [slice(r, r + LANES) for r in range(0, rows, LANES)]

    def multiply(h, first):
        cols = slice(first, first + PIECE)
        raw_ref[h, :, cols] = dot(key(h), q_ref[cols, head_cols(h, QK)], NT)
        graw_ref[h, :, cols] = dot(value(h), do_ref[cols, head_cols(h, VDIM)], NT)

    def weigh(h, first):
        for c in range(first, first + PIECE, LANES):
            cols = slice(c, c + LANES)
            high = None
            for part in parts:
                seen = index >= lower[:, cols] - part.start
                if upper is not None:
                    seen = seen & (index <= upper[:, cols] - part.start)
                scores = jnp.where(seen, raw_ref[h, part, cols] * SCALE2, MASKED)
                raw_ref[h, part, cols] = scores
                piece = fold(scores, jnp.max)
                high = piece if high is None else jnp.maximum(high, piece)
            old_top = run_ref[h, 0:1, cols]
            new_top = jnp.maximum(old_top, jnp.max(high, axis=0, keepdims=True))
            mass, cross = 0.0, 0.0
            for part in parts:
                weights = jnp.exp2(raw_ref[h, part, cols] - new_top)
                grads = graw_ref[h, part, cols]
                keep(h, part, cols, weights.astype(jnp.bfloat16), grads.astype(jnp.bfloat16))
                mass = mass + fold(weights, jnp.sum)
                cross = cross + fold(weights * grads, jnp.sum)
            factor = jnp.exp2(old_top - new_top)
            run_ref[h, 0:1, cols] = new_top
            run_ref[h, 1:2, cols] = run_ref[h, 1:2, cols] * factor + jnp.sum(
                mass, axis=0, keepdims=True
            )
            run_ref[h, 2:3, cols] = run_ref[h, 2:3, cols] * factor + jnp.sum(
                cross, axis=0, keepdims=True
            )

    alternate(rows, do_ref.shape[1] // VDIM, multiply, weigh)


def alternate(rows, heads, first, second):
    pieces = [(h, c) for h in range(heads) for c in range(0, rows, PIECE)]
    first(*pieces[0])
    for now, following in zip(pieces, pieces[1:] + [None]):
        if following:
            first(*following)
        second(*now)


def grad_block(kept, key, top, end_ref, q_ref, do_ref, low_ref, ds_ref, dq_acc, d_acc, r_acc, first_q, first_k):
    def put(ref, part, value, first):
        ref[:, part] = value if first else ref[:, part] + value

    rows = do_ref.shape[0]
    heads = do_ref.shape[1] // VDIM
    sums, turned = {}, {}

    def weigh(h, first):
        for c in range(first, first + PIECE, LANES):
            cols = slice(c, c + LANES)
            factor = jnp.exp2(top(h)[:, cols] - end_ref[h, 0:1, cols]) * end_ref[h, 1:2, cols]
            delta = end_ref[h, 2:3, cols]
            for r in range(0, rows, LANES):
                part = slice(r, r + LANES)
                weights, grads = kept(h, part, cols)
                probs = weights.astype(jnp.float32) * factor
                low_ref[h, part, cols] = probs.astype(jnp.bfloat16)
                ds_ref[h, part, cols] = (
                    probs * (grads.astype(jnp.float32) - delta)
                ).astype(jnp.bfloat16)

    def multiply(h, first):
        cols = slice(first, first + PIECE)
        low, dscore = low_ref[h, :, cols], ds_ref[h, :, cols]
        dvalue = dot(low, do_ref[cols, head_cols(h, VDIM)])
        dkey = dot(dscore, q_ref[cols, head_cols(h, QK)])
        own = head_cols(h, QK)
        if not first:
            turned[h] = key(h).T
        dq = dot(turned[h], dscore)
        dq_acc[own, cols] = dq if first_q else dq_acc[own, cols] + dq
        if first:
            dvalue, dkey = sums[h][0] + dvalue, sums[h][1] + dkey
        sums[h] = dvalue, dkey
        if first + PIECE == rows:
            dkey = dkey * SCALE
            put(d_acc, slice(h * KV, h * KV + NOPE), dkey[:, :NOPE], first_k)
            put(d_acc, slice(h * KV + NOPE, (h + 1) * KV), dvalue, first_k)
            put(r_acc, slice(0, ROPE), dkey[:, NOPE:], first_k and h == 0)

    alternate(rows, heads, weigh, multiply)


def start_stats(run_ref):
    count, rows = run_ref.shape[0], run_ref.shape[2]
    for h in range(count):
        run_ref[h, 0:1, :] = jnp.full((1, rows), FLOOR, jnp.float32)
        run_ref[h, 1:8, :] = jnp.zeros((7, rows), jnp.float32)


def chip_place(index_ref):
    core = lax.rem(index_ref[0], 2)
    return core, index_ref[0] - core


def order_pair(out_ref, core, own, other):
    out_ref[core] = own[...]
    out_ref[1 - core] = other[...]


LOCAL = ((1, REACH), (0, REACH), (1, REACH + 1))


def query_bounds(start_ref, chip, j, t, rows):
    lower = start_ref[j, 0:1, :] - (chip + t - REACH) * rows
    own = isinstance(t, int) and t == j + REACH
    return lower, lax.broadcasted_iota(jnp.int32, (1, rows), 1) if own else None


def find_starts(docs_ref, start_ref, chip, rows):
    for j in range(2):
        block = chip + j
        my_docs = docs_ref[:, pl.ds(pl.multiple_of(block * rows, rows), rows)]
        first_doc = my_docs[:, :1]
        key_docs = jnp.broadcast_to(my_docs, (128, rows)).T[:, :1]
        inside = jnp.sum(jnp.where(key_docs < my_docs, 1.0, 0.0), axis=0, keepdims=True)
        before = jnp.zeros((1, rows), jnp.float32)
        for back in range(1, REACH + 1):
            earlier = jnp.maximum(block - back, 0)
            docs = docs_ref[:, pl.ds(pl.multiple_of(earlier * rows, rows), rows)]
            same = (docs == first_doc) & (block >= back)
            before = before + jnp.where(same, 1.0, 0.0)
        before = jnp.sum(before, axis=1, keepdims=True)
        start = jnp.where(my_docs == first_doc, -before, inside).astype(jnp.int32)
        start_ref[j, 0:1, :] = start + block * rows


def local_kernel(
    index_ref, docs_ref, q0, do0, q1, do1, w_ref, lat0, lat1,
    e_ref, g_ref, k_ref, run_ref, top_ref, start_ref,
    q_ref, do_ref, lat_ref, v_ref, raw_ref, graw_ref,
):
    rows = q0.shape[0]
    core, chip = chip_place(index_ref)
    heads = w_ref.shape[1] // KV

    @pl.when(pl.program_id(0) == 0)
    def _():
        lat_ref[core] = lat0[...].T
        lat_ref[1 - core] = lat1[...].T
        find_starts(docs_ref, start_ref, chip, rows)

    order_pair(q_ref, core, q0, q1)
    order_pair(do_ref, core, do0, do1)
    for j in range(2):

        def k_out(h, key):
            k_ref[0, j * heads + h] = key

        def v_out(h, value):
            v_ref[j * heads + h] = value

        lift(lat_ref[j], w_ref, k_out, v_out)
        start_stats(run_ref.at[0, pl.ds(j * heads, heads)])
    for n, (j, t) in enumerate(LOCAL):
        slot = t - REACH

        def keep(h, part, cols, weights, grads):
            e_ref[0, n * heads + h, part, cols] = weights
            g_ref[0, n * heads + h, part, cols] = grads

        run = run_ref.at[0, pl.ds(j * heads, heads)]
        score_block(
            lambda h: k_ref[0, slot * heads + h], lambda h: v_ref[slot * heads + h],
            q_ref.at[j], do_ref.at[j], query_bounds(start_ref, chip, j, t, rows), run,
            raw_ref, graw_ref, keep,
        )
        for h in range(heads):
            top_ref[0, n * heads + h] = run[h]


def main_kernel(
    ranks,
    index_ref, docs_sref, q0, do0, q1, do1, w_ref,
    all_e, all_g, local_k, local_run, local_top, start_ref,
    lat_far, lat_swap, lat_mixed, lat_passed, lat_own, lat_other,
    dq0_ref, dq1_ref, keep_ref, send_ref, x_old, x_far, x_swap, x_own, x_other,
    q_ref, do_ref, lat_ref, lat_t_ref, e_ref, g_ref, k_ref, v_ref, top_ref,
    run_ref, end_ref, raw_ref, graw_ref, low_ref, ds_ref, dq_acc, d_acc, gw_acc, x_acc,
    r_acc, local_e, local_g, sems, kept_sems,
):
    step = pl.program_id(0)
    rows = q0.shape[0]
    heads = w_ref.shape[1] // KV
    blocks = REACH + 2
    kept_copies = [
        pltpu.make_async_copy(all_e.at[step], local_e, kept_sems.at[0]),
        pltpu.make_async_copy(all_g.at[step], local_g, kept_sems.at[1]),
    ]
    core, chip = chip_place(index_ref)

    def active(j, t):
        block = chip + t - REACH
        last_doc = docs_sref[jnp.maximum(block, 0) * rows + rows - 1]
        return (block >= 0) & (last_doc >= docs_sref[(chip + j) * rows])

    def block_rows(t):
        return pl.ds(pl.multiple_of(t * rows, rows), rows)

    def piece_rows(t, part):
        size = part.stop - part.start
        return pl.ds(pl.multiple_of(t * rows + part.start, size), size)

    def loop(first, last, when, body):
        def visit(t, carry):
            @pl.when(when(t))
            def _():
                body(t)

            return carry

        lax.fori_loop(first, last, visit, 0)

    @pl.when(step == 0)
    def _():
        places = [(lat_far, 1 + core), (lat_swap, 2 - core), (lat_own, REACH + core),
                  (lat_other, REACH + 1 - core)]
        copies = [
            pltpu.make_async_copy(source, lat_t_ref.at[:, block_rows(t)], sems.at[i])
            for i, (source, t) in enumerate(places)
        ]
        first = lat_t_ref.at[:, block_rows(0)]
        oldest = pltpu.make_async_copy(lat_mixed, first, sems.at[4])
        passed = pltpu.make_async_copy(lat_passed, first, sems.at[4])
        for copy in copies:
            copy.start()
        pl.when(core == 0)(oldest.start)
        pl.when(core == 1)(passed.start)
        for copy in kept_copies:
            copy.start()
        for copy in copies:
            copy.wait()
        oldest.wait()
        for t in range(REACH):
            part = slice(t * rows, (t + 1) * rows)
            lat_ref[part, :] = lat_t_ref[:, part].T

    @pl.when(step > 0)
    def _():
        for copy in kept_copies:
            copy.start()

    order_pair(q_ref, core, q0, q1)
    order_pair(do_ref, core, do0, do1)

    def lift_block(t):
        def k_out(h, key):
            k_ref[h, block_rows(t), :] = key

        def v_out(h, value):
            v_ref[h, block_rows(t), :] = value

        lift(lat_ref[block_rows(t), :], w_ref, k_out, v_out)

    loop(0, REACH, lambda t: active(0, t), lift_block)

    for j in range(2):
        for h in range(heads):
            run_ref[h] = local_run[0, j * heads + h]

        def first_pass(t):
            def keep(h, part, cols, weights, grads):
                e_ref[h, piece_rows(t, part), cols] = weights
                g_ref[h, piece_rows(t, part), cols] = grads

            score_block(
                lambda h: k_ref[h, block_rows(t), :], lambda h: v_ref[h, block_rows(t), :],
                q_ref.at[j], do_ref.at[j], query_bounds(start_ref, chip, j, t, rows), run_ref,
                raw_ref, graw_ref, keep,
            )
            for h in range(heads):
                top_ref[h, t] = run_ref[h]

        loop(j, REACH, lambda t: active(j, t), first_pass)
        for h in range(heads):
            inverse = 1.0 / run_ref[h, 1:2, :]
            end_ref[h, 0:1, :] = run_ref[h, 0:1, :]
            end_ref[h, 1:2, :] = inverse
            end_ref[h, 2:3, :] = run_ref[h, 2:3, :] * inverse

        def add(t, kept, key, top, first_q, first_k):
            grad_block(
                kept, key, top, end_ref, q_ref.at[j], do_ref.at[j], low_ref, ds_ref, dq_acc.at[j], d_acc.at[t],
                r_acc.at[t], first_q, first_k,
            )

        def second_pass(t):
            def kept(h, part, cols):
                return e_ref[h, piece_rows(t, part), cols], g_ref[h, piece_rows(t, part), cols]

            add(
                t, kept, lambda h: k_ref[h, block_rows(t), :], lambda h: top_ref[h, t, 0:1, :],
                False, j == 0,
            )

        if j == 0:
            for copy in kept_copies:
                copy.wait()
        first_q = True
        for n, (query, t) in enumerate(LOCAL):
            if query == j:
                add(
                    t,
                    lambda h, part, cols: (
                        local_e[n * heads + h, part, cols], local_g[n * heads + h, part, cols]
                    ),
                    lambda h: local_k[0, (t - REACH) * heads + h],
                    lambda h: local_top[0, n * heads + h, 0:1, :],
                    first_q, t == REACH + j,
                )
                first_q = False
        loop(j, REACH, lambda t: active(j, t), second_pass)

    def seen(t):
        return (t >= REACH) | active(0, t)

    last = step == pl.num_programs(0) - 1
    outs = ((x_old, x_old), (x_far, x_swap), (x_swap, x_far), (x_own, x_other), (x_other, x_own))

    def out_copies(t):
        part = slice(t * rows, (t + 1) * rows)
        return [pltpu.make_async_copy(lat_t_ref.at[:, part], out, sems.at[t]) for out in outs[t]]

    def leave(t):
        part = slice(t * rows, (t + 1) * rows)
        lat_t_ref[:, part] = x_acc[:, part].astype(lat_t_ref.dtype)
        for parity, copy in enumerate(out_copies(t)):
            pl.when(core == parity)(copy.start)

    def project(t, first):
        part = slice(t * rows, (t + 1) * rows)
        grads = d_acc[t].astype(jnp.bfloat16)
        weight_part = dot(lat_t_ref[:LATENT, part], grads)
        gw_acc[...] = weight_part if first else gw_acc[...] + weight_part
        latent_part = dot(w_ref[...], grads, NT)
        rope_part = r_acc[t].T

        @pl.when(step == 0)
        def _():
            x_acc[:LATENT, part] = latent_part
            x_acc[LATENT:, part] = rope_part

        @pl.when(step > 0)
        def _():
            x_acc[:LATENT, part] += latent_part
            x_acc[LATENT:, part] += rope_part

    def clear(t):
        x_acc[:, t * rows : (t + 1) * rows] = jnp.zeros((WIDTH, rows), jnp.float32)

    for n, t in enumerate((REACH, REACH + 1, *range(REACH))):
        if t >= REACH:
            project(t, n == 0)
        else:
            pl.when(seen(t))(functools.partial(project, t, False))
            pl.when(~seen(t) & (step == 0))(functools.partial(clear, t))
        pl.when(last)(functools.partial(leave, t))
    dq0_ref[...] = (dq_acc[core] * SCALE).astype(dq0_ref.dtype).T
    dq1_ref[...] = (dq_acc[1 - core] * SCALE).astype(dq1_ref.dtype).T

    share = 2 * (LATENT // ranks)
    own_x = lax.rem(index_ref[0] // 2, 2)
    for i in range(ranks // 4):
        for out, x in ((keep_ref, own_x), (send_ref, 1 - own_x)):
            source = pl.multiple_of((2 * i + x) * share, share)
            out[i * share : (i + 1) * share, :] = gw_acc[pl.ds(source, share), :].astype(out.dtype)

    @pl.when(last)
    def _():
        for t in range(blocks):
            out_copies(t)[0].wait()


def step_cols(height, size):
    return pl.BlockSpec((height, size), lambda i, index: (0, i))


def core_cols(height, size, first):
    def place(i, index):
        return (0, first(i, lax.rem(index[0], 2)))

    return pl.BlockSpec((height, size), place)


def step_block(*shape):
    return pl.BlockSpec((1, *shape), lambda i, index: (i, 0, 0, 0))


def fixed(*shape):
    return pl.BlockSpec(shape, lambda i, index: (0,) * len(shape))


SCALARS = pl.BlockSpec(memory_space=pltpu.SMEM)
ANYWHERE = pl.BlockSpec(memory_space=pl.ANY)


def call(body, steps, flops, in_specs, outs, scratch, name):
    return pl.pallas_call(
        body,
        grid_spec=pltpu.PrefetchScalarGridSpec(
            num_scalar_prefetch=1,
            grid=(steps,),
            in_specs=in_specs,
            out_specs=[spec for spec, _, _ in outs],
            scratch_shapes=[
                pltpu.VMEM(*entry) if isinstance(entry, tuple) else entry for entry in scratch
            ],
        ),
        out_shape=[jax.ShapeDtypeStruct(shape, kind) for _, shape, kind in outs],
        compiler_params=pltpu.CompilerParams(
            dimension_semantics=("arbitrary",), vmem_limit_bytes=58 * 1024 * 1024
        ),
        cost_estimate=pl.CostEstimate(
            flops=flops, bytes_accessed=16 * 1024 * 1024, transcendentals=0
        ),
        name=name,
    )


def head_specs(rows, heads, steps, in_place):
    def received(i, core):
        return i

    def own(i, core):
        return core * steps + i if in_place else i

    return [
        core_cols(rows, heads * QK, own), core_cols(rows, heads * VDIM, own),
        core_cols(rows, heads * QK, received), core_cols(rows, heads * VDIM, received),
        core_cols(LATENT, heads * KV, own),
    ]


def local_scores(index, docs, inputs, latents, heads, steps, in_place):
    rows = inputs[0].shape[0]
    low, full = jnp.bfloat16, jnp.float32
    count = len(LOCAL) * heads
    return call(
        local_kernel,
        steps,
        2 * steps * heads * rows * rows * (3 * (QK + VDIM) + 2 * KV),
        [
            fixed(1, docs.shape[1]), *head_specs(rows, heads, steps, in_place),
            fixed(WIDTH, rows), fixed(WIDTH, rows),
        ],
        [
            (step_block(count, rows, rows), (steps, count, rows, rows), low),
            (step_block(count, rows, rows), (steps, count, rows, rows), low),
            (step_block(2 * heads, rows, QK), (steps, 2 * heads, rows, QK), low),
            (step_block(2 * heads, 8, rows), (steps, 2 * heads, 8, rows), full),
            (step_block(count, 8, rows), (steps, count, 8, rows), full),
            (fixed(2, 8, rows), (2, 8, rows), jnp.int32),
        ],
        [
            ((2, rows, heads * QK), low),
            ((2, rows, heads * VDIM), low),
            ((2, rows, WIDTH), low),
            ((2 * heads, rows, VDIM), low),
            ((heads, rows, rows), full),
            ((heads, rows, rows), full),
        ],
        "local_scores",
    )(index, docs, *inputs, *latents)


def attention(index, doc_ids, inputs, kept, latents, heads, steps, ranks, in_place):
    rows = inputs[0].shape[0]
    low, full = jnp.bfloat16, jnp.float32
    count = len(LOCAL) * heads
    window = (REACH + 2) * rows
    far = REACH * rows
    half = (LATENT // 2, steps * heads * KV)
    return call(
        functools.partial(main_kernel, ranks),
        steps,
        2 * steps * heads * rows * rows * (5 * (QK + VDIM) + 8 * (2 * QK + VDIM) + 13 * KV),
        [
            SCALARS, *head_specs(rows, heads, steps, in_place), ANYWHERE, ANYWHERE,
            step_block(2 * heads, rows, QK), step_block(2 * heads, 8, rows),
            step_block(count, 8, rows), fixed(2, 8, rows),
        ]
        + [ANYWHERE] * len(latents),
        [(step_cols(rows, heads * QK), (rows, steps * heads * QK), low)] * 2
        + [(step_cols(LATENT // 2, heads * KV), half, low)] * 2
        + [(ANYWHERE, (WIDTH, rows), low)] * (REACH + 2),
        [
            ((2, rows, heads * QK), low),
            ((2, rows, heads * VDIM), low),
            ((far, WIDTH), low),
            ((WIDTH, window), low),
            ((heads, far, rows), low),
            ((heads, far, rows), low),
            ((heads, far, QK), low),
            ((heads, far, VDIM), low),
            ((heads, REACH, 8, rows), full),
            ((heads, 8, rows), full),
            ((heads, 8, rows), full),
            ((heads, rows, rows), full),
            ((heads, rows, rows), full),
            ((heads, rows, rows), low),
            ((heads, rows, rows), low),
            ((2, heads * QK, rows), full),
            ((REACH + 2, rows, heads * KV), full),
            ((LATENT, heads * KV), full),
            ((WIDTH, window), full),
            ((REACH + 2, rows, ROPE), full),
            ((count, rows, rows), low),
            ((count, rows, rows), low),
            pltpu.SemaphoreType.DMA((5,)),
            pltpu.SemaphoreType.DMA((2,)),
        ],
        "attention",
    )(index, doc_ids, *inputs, *kept, *latents)


def permute(value, axis, target):
    count = lax.axis_size(axis)
    pairs = [(s, target(s)) for s in range(count) if 0 <= target(s) < count]
    return lax.ppermute(value, axis, pairs)


def local(kv_latent, queries, grad_out, kv_up_weight, doc_ids):
    ranks = lax.axis_size("ctx")
    position = lax.axis_index("ctx").astype(jnp.int32)
    index, core = position[None], lax.rem(position, 2)
    low, full = jnp.bfloat16, jnp.float32
    docs = doc_ids[None]
    core_heads = kv_up_weight.shape[1] // KV // 2
    heads = min(2, core_heads)
    steps = core_heads // heads

    def own_heads(value, which):
        size = value.shape[1] // 2
        return lax.dynamic_slice_in_dim(value, which * size, size, axis=1)

    def across(value):
        return permute(value, "ctx", lambda s: s ^ 1)

    latent = kv_latent.T
    far = permute(latent, "ctx", lambda s: s + 2)
    mixed = permute(latent, "ctx", lambda s: s + 3 if s % 2 else -1)
    other = across(latent)
    in_place = heads * QK % 128 == 0
    inputs = (
        queries if in_place else own_heads(queries, core),
        grad_out if in_place else own_heads(grad_out, core),
        across(own_heads(queries, 1 - core)),
        across(own_heads(grad_out, 1 - core)),
        kv_up_weight if in_place else own_heads(kv_up_weight, core),
    )
    *kept, starts = local_scores(index, docs, inputs, (latent, other), heads, steps, in_place)
    far, mixed, starts = lax.optimization_barrier((far, mixed, starts))
    swapped = across(far)
    passed = permute(mixed, "ctx", lambda s: -1 if s % 2 else s + 1)

    dq_own, dq_other, keep, send, to_old, to_far, to_swap, mine, to_other = attention(
        index, doc_ids, inputs, (*kept, starts),
        (far, swapped, mixed, passed, latent, other), heads, steps, ranks, in_place,
    )

    head, head_count = lax.axis_index("head"), lax.axis_size("head")
    share = WIDTH // head_count

    def turned(value, turn, ctx=range(ranks)):
        turns = [
            (c * head_count + s, c * head_count + (s + turn) % head_count)
            for c in ctx
            for s in range(head_count)
        ]
        return lax.ppermute(value, ("ctx", "head"), turns)

    def head_share(value, ctx=range(ranks), after=()):
        def rows_of(which):
            return lax.dynamic_slice_in_dim(value, which * share, share, axis=0)

        total = rows_of(head).astype(full)
        for turn in range(1, head_count):
            target = lax.rem(head + turn, head_count)
            received, *_ = lax.optimization_barrier((turned(rows_of(target), turn, ctx), *after))
            total = total + received.astype(full)
        return total

    from_x = permute(send, "ctx", lambda s: s ^ 2)
    from_swap = across(to_swap)
    from_old = permute(to_old, "ctx", lambda s: s - 1 if s % 2 else -1)
    from_other = across(to_other)
    far_sum = head_share((to_far.astype(full) + from_swap.astype(full)).astype(low)).astype(low)
    old_sum = (to_old.astype(full) + from_old.astype(full)).astype(low)
    old_sum = head_share(old_sum, range(0, ranks, 2), (far_sum,)).astype(low)
    from_far = permute(far_sum, "ctx", lambda s: s - 2)
    from_mixed = permute(old_sum, "ctx", lambda s: -1 if s % 2 else s - 3)
    own_sum = (mine.astype(full) + from_other.astype(full)).astype(low)
    own_sum, *_ = lax.optimization_barrier((own_sum, far_sum))
    if head_count == 2:
        kept_half = lax.dynamic_slice_in_dim(own_sum, head * share, share, axis=0)
        sent_half = lax.dynamic_slice_in_dim(own_sum, (1 - head) * share, share, axis=0)
        received_half = turned(sent_half, 1)
        total = kept_half.astype(full)
    else:
        total = head_share(own_sum)

    from_x, *_ = lax.optimization_barrier((from_x, far_sum, old_sum))
    plane = (keep.astype(full) + from_x.astype(full)).astype(low)
    columns = [list(range(first, ranks, 4)) for first in range(4)]
    pieces = lax.all_to_all(plane, "ctx", 0, 0, axis_index_groups=columns, tiled=True)
    rows = LATENT // ranks
    summed = jnp.sum(pieces.reshape(ranks // 4, 2 * rows, -1).astype(full), axis=0)

    def in_order(own, received):
        first = jnp.where(core == 0, own, received)
        second = jnp.where(core == 0, received, own)
        return jnp.concatenate([first, second], axis=1)

    rows_own = lax.dynamic_slice_in_dim(summed, core * rows, rows, axis=0)
    rows_other = lax.dynamic_slice_in_dim(summed, (1 - core) * rows, rows, axis=0)
    grad_weight = in_order(rows_own, across(rows_other))
    grad_queries = in_order(dq_own, across(dq_other))

    total = (total + from_mixed.astype(full) + from_far.astype(full)).astype(low)
    shares = [total] + [turned(total, turn) for turn in range(1, head_count)]
    if head_count == 2:
        shares = [
            (whole.astype(full) + part.astype(full)).astype(low)
            for whole, part in zip(shares, (received_half, sent_half))
        ]
    ordered = []
    for place in range(head_count):
        picked = shares[0]
        for turn in range(1, head_count):
            picked = jnp.where(lax.rem(head - place + head_count, head_count) == turn, shares[turn], picked)
        ordered.append(picked)
    return grad_queries, jnp.concatenate(ordered, axis=0).T, grad_weight


def solution(mesh):
    return jax.shard_map(
        local,
        mesh=mesh,
        in_specs=(P("ctx", None), P("ctx", "head"), P("ctx", "head"), P(None, "head"), P()),
        out_specs=(P("ctx", "head"), P("ctx", None), P("ctx", "head")),
        check_vma=False,
    )
```

```python
import functools
import math

import jax
import jax.numpy as jnp
from jax import lax
from jax.experimental import pallas as pl
from jax.experimental.pallas import tpu as pltpu
from jax.sharding import PartitionSpec as P

NOPE = 128
ROPE = 64
VDIM = 128
LATENT = 512
REACH = 3
QK = NOPE + ROPE
KV = NOPE + VDIM
WIDTH = LATENT + ROPE
LANES = 128
PIECE = 256

MASKED = -1e30
FLOOR = -1e20
SCALE = 1.0 / math.sqrt(QK)
SCALE2 = SCALE * math.log2(math.e)

NT = (((1,), (1,)), ((), ()))
NN = (((1,), (0,)), ((), ()))


def dot(a, b, dims=NN):
    return lax.dot_general(a, b, dims, preferred_element_type=jnp.float32)


def head_cols(h, size):
    return slice(h * size, (h + 1) * size)


def fold(value, combine):
    return combine(value.reshape(-1, 8, value.shape[1]), axis=0)


def fold(value, combine):
    return combine(value.reshape(-1, 8, value.shape[1]), axis=0)


def lift(latent, w_ref, k_out, v_out):
    for h in range(w_ref.shape[1] // KV):
        lifted = dot(latent[:, :LATENT], w_ref[:, head_cols(h, KV)]).astype(jnp.bfloat16)
        k_out(h, jnp.concatenate([lifted[:, :NOPE], latent[:, LATENT:]], axis=1))
        v_out(h, lifted[:, NOPE:])


def score_block(key, value, q_ref, do_ref, bounds, run_ref, raw_ref, graw_ref, keep):
    rows = do_ref.shape[0]
    lower, upper = bounds
    index = lax.broadcasted_iota(jnp.int32, (LANES, LANES), 0)
    parts = [slice(r, r + LANES) for r in range(0, rows, LANES)]

    def multiply(h, first):
        cols = slice(first, first + PIECE)
        raw_ref[h, :, cols] = dot(key(h), q_ref[cols, head_cols(h, QK)], NT)
        graw_ref[h, :, cols] = dot(value(h), do_ref[cols, head_cols(h, VDIM)], NT)

    def weigh(h, first):
        for c in range(first, first + PIECE, LANES):
            cols = slice(c, c + LANES)
            high = None
            for part in parts:
                seen = index >= lower[:, cols] - part.start
                if upper is not None:
                    seen = seen & (index <= upper[:, cols] - part.start)
                scores = jnp.where(seen, raw_ref[h, part, cols] * SCALE2, MASKED)
                raw_ref[h, part, cols] = scores
                piece = fold(scores, jnp.max)
                high = piece if high is None else jnp.maximum(high, piece)
            old_top = run_ref[h, 0:1, cols]
            new_top = jnp.maximum(old_top, jnp.max(high, axis=0, keepdims=True))
            mass, cross = 0.0, 0.0
            for part in parts:
                weights = jnp.exp2(raw_ref[h, part, cols] - new_top)
                grads = graw_ref[h, part, cols]
                keep(h, part, cols, weights.astype(jnp.bfloat16), grads.astype(jnp.bfloat16))
                mass = mass + fold(weights, jnp.sum)
                cross = cross + fold(weights * grads, jnp.sum)
            factor = jnp.exp2(old_top - new_top)
            run_ref[h, 0:1, cols] = new_top
            run_ref[h, 1:2, cols] = run_ref[h, 1:2, cols] * factor + jnp.sum(
                mass, axis=0, keepdims=True
            )
            run_ref[h, 2:3, cols] = run_ref[h, 2:3, cols] * factor + jnp.sum(
                cross, axis=0, keepdims=True
            )

    alternate(rows, do_ref.shape[1] // VDIM, multiply, weigh)


def alternate(rows, heads, first, second):
    pieces = [(h, c) for h in range(heads) for c in range(0, rows, PIECE)]
    first(*pieces[0])
    for now, following in zip(pieces, pieces[1:] + [None]):
        if following:
            first(*following)
        second(*now)


def grad_block(kept, key, top, end_ref, q_ref, do_ref, low_ref, ds_ref, dq_acc, d_acc, r_acc, first_q, first_k):
    def put(ref, part, value, first):
        ref[:, part] = value if first else ref[:, part] + value

    rows = do_ref.shape[0]
    heads = do_ref.shape[1] // VDIM
    sums, turned = {}, {}

    def weigh(h, first):
        for c in range(first, first + PIECE, LANES):
            cols = slice(c, c + LANES)
            factor = jnp.exp2(top(h)[:, cols] - end_ref[h, 0:1, cols]) * end_ref[h, 1:2, cols]
            delta = end_ref[h, 2:3, cols]
            for r in range(0, rows, LANES):
                part = slice(r, r + LANES)
                weights, grads = kept(h, part, cols)
                probs = weights.astype(jnp.float32) * factor
                low_ref[h, part, cols] = probs.astype(jnp.bfloat16)
                ds_ref[h, part, cols] = (
                    probs * (grads.astype(jnp.float32) - delta)
                ).astype(jnp.bfloat16)

    def multiply(h, first):
        cols = slice(first, first + PIECE)
        low, dscore = low_ref[h, :, cols], ds_ref[h, :, cols]
        dvalue = dot(low, do_ref[cols, head_cols(h, VDIM)])
        dkey = dot(dscore, q_ref[cols, head_cols(h, QK)])
        own = head_cols(h, QK)
        if not first:
            turned[h] = key(h).T
        dq = dot(turned[h], dscore)
        dq_acc[own, cols] = dq if first_q else dq_acc[own, cols] + dq
        if first:
            dvalue, dkey = sums[h][0] + dvalue, sums[h][1] + dkey
        sums[h] = dvalue, dkey
        if first + PIECE == rows:
            dkey = dkey * SCALE
            put(d_acc, slice(h * KV, h * KV + NOPE), dkey[:, :NOPE], first_k)
            put(d_acc, slice(h * KV + NOPE, (h + 1) * KV), dvalue, first_k)
            put(r_acc, slice(0, ROPE), dkey[:, NOPE:], first_k and h == 0)

    alternate(rows, heads, weigh, multiply)


def start_stats(run_ref):
    count, rows = run_ref.shape[0], run_ref.shape[2]
    for h in range(count):
        run_ref[h, 0:1, :] = jnp.full((1, rows), FLOOR, jnp.float32)
        run_ref[h, 1:8, :] = jnp.zeros((7, rows), jnp.float32)


def chip_place(index_ref):
    core = lax.rem(index_ref[0], 2)
    return core, index_ref[0] - core


def order_pair(out_ref, core, own, other):
    out_ref[core] = own[...]
    out_ref[1 - core] = other[...]


LOCAL = ((1, REACH), (0, REACH), (1, REACH + 1))


def query_bounds(start_ref, chip, j, t, rows):
    lower = start_ref[j, 0:1, :] - (chip + t - REACH) * rows
    own = isinstance(t, int) and t == j + REACH
    return lower, lax.broadcasted_iota(jnp.int32, (1, rows), 1) if own else None


def find_starts(docs_ref, start_ref, chip, rows):
    for j in range(2):
        block = chip + j
        my_docs = docs_ref[:, pl.ds(pl.multiple_of(block * rows, rows), rows)]
        first_doc = my_docs[:, :1]
        key_docs = jnp.broadcast_to(my_docs, (128, rows)).T[:, :1]
        inside = jnp.sum(jnp.where(key_docs < my_docs, 1.0, 0.0), axis=0, keepdims=True)
        before = jnp.zeros((1, rows), jnp.float32)
        for back in range(1, REACH + 1):
            earlier = jnp.maximum(block - back, 0)
            docs = docs_ref[:, pl.ds(pl.multiple_of(earlier * rows, rows), rows)]
            same = (docs == first_doc) & (block >= back)
            before = before + jnp.where(same, 1.0, 0.0)
        before = jnp.sum(before, axis=1, keepdims=True)
        start = jnp.where(my_docs == first_doc, -before, inside).astype(jnp.int32)
        start_ref[j, 0:1, :] = start + block * rows


def local_kernel(
    index_ref, docs_ref, q0, do0, q1, do1, w_ref, lat0, lat1,
    e_ref, g_ref, k_ref, run_ref, top_ref, start_ref,
    q_ref, do_ref, lat_ref, v_ref, raw_ref, graw_ref,
):
    rows = q0.shape[0]
    core, chip = chip_place(index_ref)
    heads = w_ref.shape[1] // KV

    @pl.when(pl.program_id(0) == 0)
    def _():
        lat_ref[core] = lat0[...].T
        lat_ref[1 - core] = lat1[...].T
        find_starts(docs_ref, start_ref, chip, rows)

    order_pair(q_ref, core, q0, q1)
    order_pair(do_ref, core, do0, do1)
    for j in range(2):

        def k_out(h, key):
            k_ref[0, j * heads + h] = key

        def v_out(h, value):
            v_ref[j * heads + h] = value

        lift(lat_ref[j], w_ref, k_out, v_out)
        start_stats(run_ref.at[0, pl.ds(j * heads, heads)])
    for n, (j, t) in enumerate(LOCAL):
        slot = t - REACH

        def keep(h, part, cols, weights, grads):
            e_ref[0, n * heads + h, part, cols] = weights
            g_ref[0, n * heads + h, part, cols] = grads

        run = run_ref.at[0, pl.ds(j * heads, heads)]
        score_block(
            lambda h: k_ref[0, slot * heads + h], lambda h: v_ref[slot * heads + h],
            q_ref.at[j], do_ref.at[j], query_bounds(start_ref, chip, j, t, rows), run,
            raw_ref, graw_ref, keep,
        )
        for h in range(heads):
            top_ref[0, n * heads + h] = run[h]


def main_kernel(
    ranks,
    index_ref, docs_sref, q0, do0, q1, do1, w_ref,
    all_e, all_g, local_k, local_run, local_top, start_ref,
    lat_far, lat_swap, lat_mixed, lat_passed, lat_own, lat_other,
    dq0_ref, dq1_ref, keep_ref, send_ref, x_old, x_far, x_swap, x_own, x_other,
    q_ref, do_ref, lat_ref, lat_t_ref, e_ref, g_ref, k_ref, v_ref, top_ref,
    run_ref, end_ref, raw_ref, graw_ref, low_ref, ds_ref, dq_acc, d_acc, gw_acc, x_acc,
    r_acc, local_e, local_g, sems, kept_sems,
):
    step = pl.program_id(0)
    rows = q0.shape[0]
    heads = w_ref.shape[1] // KV
    blocks = REACH + 2
    kept_copies = [
        pltpu.make_async_copy(all_e.at[step], local_e, kept_sems.at[0]),
        pltpu.make_async_copy(all_g.at[step], local_g, kept_sems.at[1]),
    ]
    core, chip = chip_place(index_ref)

    def active(j, t):
        block = chip + t - REACH
        last_doc = docs_sref[jnp.maximum(block, 0) * rows + rows - 1]
        return (block >= 0) & (last_doc >= docs_sref[(chip + j) * rows])

    def block_rows(t):
        return pl.ds(pl.multiple_of(t * rows, rows), rows)

    def piece_rows(t, part):
        size = part.stop - part.start
        return pl.ds(pl.multiple_of(t * rows + part.start, size), size)

    def loop(first, last, when, body):
        def visit(t, carry):
            @pl.when(when(t))
            def _():
                body(t)

            return carry

        lax.fori_loop(first, last, visit, 0)

    @pl.when(step == 0)
    def _():
        places = [(lat_far, 1 + core), (lat_swap, 2 - core), (lat_own, REACH + core),
                  (lat_other, REACH + 1 - core)]
        copies = [
            pltpu.make_async_copy(source, lat_t_ref.at[:, block_rows(t)], sems.at[i])
            for i, (source, t) in enumerate(places)
        ]
        first = lat_t_ref.at[:, block_rows(0)]
        oldest = pltpu.make_async_copy(lat_mixed, first, sems.at[4])
        passed = pltpu.make_async_copy(lat_passed, first, sems.at[4])
        for copy in copies:
            copy.start()
        pl.when(core == 0)(oldest.start)
        pl.when(core == 1)(passed.start)
        for copy in kept_copies:
            copy.start()
        for copy in copies:
            copy.wait()
        oldest.wait()
        for t in range(REACH):
            part = slice(t * rows, (t + 1) * rows)
            lat_ref[part, :] = lat_t_ref[:, part].T

    @pl.when(step > 0)
    def _():
        for copy in kept_copies:
            copy.start()

    order_pair(q_ref, core, q0, q1)
    order_pair(do_ref, core, do0, do1)

    def lift_block(t):
        def k_out(h, key):
            k_ref[h, block_rows(t), :] = key

        def v_out(h, value):
            v_ref[h, block_rows(t), :] = value

        lift(lat_ref[block_rows(t), :], w_ref, k_out, v_out)

    loop(0, REACH, lambda t: active(0, t), lift_block)

    for j in range(2):
        for h in range(heads):
            run_ref[h] = local_run[0, j * heads + h]

        def first_pass(t):
            def keep(h, part, cols, weights, grads):
                e_ref[h, piece_rows(t, part), cols] = weights
                g_ref[h, piece_rows(t, part), cols] = grads

            score_block(
                lambda h: k_ref[h, block_rows(t), :], lambda h: v_ref[h, block_rows(t), :],
                q_ref.at[j], do_ref.at[j], query_bounds(start_ref, chip, j, t, rows), run_ref,
                raw_ref, graw_ref, keep,
            )
            for h in range(heads):
                top_ref[h, t] = run_ref[h]

        loop(j, REACH, lambda t: active(j, t), first_pass)
        for h in range(heads):
            inverse = 1.0 / run_ref[h, 1:2, :]
            end_ref[h, 0:1, :] = run_ref[h, 0:1, :]
            end_ref[h, 1:2, :] = inverse
            end_ref[h, 2:3, :] = run_ref[h, 2:3, :] * inverse

        def add(t, kept, key, top, first_q, first_k):
            grad_block(
                kept, key, top, end_ref, q_ref.at[j], do_ref.at[j], low_ref, ds_ref, dq_acc.at[j], d_acc.at[t],
                r_acc.at[t], first_q, first_k,
            )

        def second_pass(t):
            def kept(h, part, cols):
                return e_ref[h, piece_rows(t, part), cols], g_ref[h, piece_rows(t, part), cols]

            add(
                t, kept, lambda h: k_ref[h, block_rows(t), :], lambda h: top_ref[h, t, 0:1, :],
                False, j == 0,
            )

        if j == 0:
            for copy in kept_copies:
                copy.wait()
        first_q = True
        for n, (query, t) in enumerate(LOCAL):
            if query == j:
                add(
                    t,
                    lambda h, part, cols: (
                        local_e[n * heads + h, part, cols], local_g[n * heads + h, part, cols]
                    ),
                    lambda h: local_k[0, (t - REACH) * heads + h],
                    lambda h: local_top[0, n * heads + h, 0:1, :],
                    first_q, t == REACH + j,
                )
                first_q = False
        loop(j, REACH, lambda t: active(j, t), second_pass)

    def seen(t):
        return (t >= REACH) | active(0, t)

    last = step == pl.num_programs(0) - 1
    outs = ((x_old, x_old), (x_far, x_swap), (x_swap, x_far), (x_own, x_other), (x_other, x_own))

    def out_copies(t):
        part = slice(t * rows, (t + 1) * rows)
        return [pltpu.make_async_copy(lat_t_ref.at[:, part], out, sems.at[t]) for out in outs[t]]

    def leave(t):
        part = slice(t * rows, (t + 1) * rows)
        lat_t_ref[:, part] = x_acc[:, part].astype(lat_t_ref.dtype)
        for parity, copy in enumerate(out_copies(t)):
            pl.when(core == parity)(copy.start)

    def project(t, first):
        part = slice(t * rows, (t + 1) * rows)
        grads = d_acc[t].astype(jnp.bfloat16)
        weight_part = dot(lat_t_ref[:LATENT, part], grads)
        gw_acc[...] = weight_part if first else gw_acc[...] + weight_part
        latent_part = dot(w_ref[...], grads, NT)
        rope_part = r_acc[t].T

        @pl.when(step == 0)
        def _():
            x_acc[:LATENT, part] = latent_part
            x_acc[LATENT:, part] = rope_part

        @pl.when(step > 0)
        def _():
            x_acc[:LATENT, part] += latent_part
            x_acc[LATENT:, part] += rope_part

    def clear(t):
        x_acc[:, t * rows : (t + 1) * rows] = jnp.zeros((WIDTH, rows), jnp.float32)

    for n, t in enumerate((REACH, REACH + 1, *range(REACH))):
        if t >= REACH:
            project(t, n == 0)
        else:
            pl.when(seen(t))(functools.partial(project, t, False))
            pl.when(~seen(t) & (step == 0))(functools.partial(clear, t))
        pl.when(last)(functools.partial(leave, t))
    dq0_ref[...] = (dq_acc[core] * SCALE).astype(dq0_ref.dtype).T
    dq1_ref[...] = (dq_acc[1 - core] * SCALE).astype(dq1_ref.dtype).T

    share = 2 * (LATENT // ranks)
    own_x = lax.rem(index_ref[0] // 2, 2)
    for i in range(ranks // 4):
        for out, x in ((keep_ref, own_x), (send_ref, 1 - own_x)):
            source = pl.multiple_of((2 * i + x) * share, share)
            out[i * share : (i + 1) * share, :] = gw_acc[pl.ds(source, share), :].astype(out.dtype)

    @pl.when(last)
    def _():
        for t in range(blocks):
            out_copies(t)[0].wait()


def step_cols(height, size):
    return pl.BlockSpec((height, size), lambda i, index: (0, i))


def core_cols(height, size, first):
    def place(i, index):
        return (0, first(i, lax.rem(index[0], 2)))

    return pl.BlockSpec((height, size), place)


def step_block(*shape):
    return pl.BlockSpec((1, *shape), lambda i, index: (i, 0, 0, 0))


def fixed(*shape):
    return pl.BlockSpec(shape, lambda i, index: (0,) * len(shape))


SCALARS = pl.BlockSpec(memory_space=pltpu.SMEM)
ANYWHERE = pl.BlockSpec(memory_space=pl.ANY)


def call(body, steps, flops, in_specs, outs, scratch, name):
    return pl.pallas_call(
        body,
        grid_spec=pltpu.PrefetchScalarGridSpec(
            num_scalar_prefetch=1,
            grid=(steps,),
            in_specs=in_specs,
            out_specs=[spec for spec, _, _ in outs],
            scratch_shapes=[
                pltpu.VMEM(*entry) if isinstance(entry, tuple) else entry for entry in scratch
            ],
        ),
        out_shape=[jax.ShapeDtypeStruct(shape, kind) for _, shape, kind in outs],
        compiler_params=pltpu.CompilerParams(
            dimension_semantics=("arbitrary",), vmem_limit_bytes=58 * 1024 * 1024
        ),
        cost_estimate=pl.CostEstimate(
            flops=flops, bytes_accessed=16 * 1024 * 1024, transcendentals=0
        ),
        name=name,
    )


def head_specs(rows, heads, steps, in_place):
    def received(i, core):
        return i

    def own(i, core):
        return core * steps + i if in_place else i

    return [
        core_cols(rows, heads * QK, own), core_cols(rows, heads * VDIM, own),
        core_cols(rows, heads * QK, received), core_cols(rows, heads * VDIM, received),
        core_cols(LATENT, heads * KV, own),
    ]


def local_scores(index, docs, inputs, latents, heads, steps, in_place):
    rows = inputs[0].shape[0]
    low, full = jnp.bfloat16, jnp.float32
    count = len(LOCAL) * heads
    return call(
        local_kernel,
        steps,
        2 * steps * heads * rows * rows * (3 * (QK + VDIM) + 2 * KV),
        [
            fixed(1, docs.shape[1]), *head_specs(rows, heads, steps, in_place),
            fixed(WIDTH, rows), fixed(WIDTH, rows),
        ],
        [
            (step_block(count, rows, rows), (steps, count, rows, rows), low),
            (step_block(count, rows, rows), (steps, count, rows, rows), low),
            (step_block(2 * heads, rows, QK), (steps, 2 * heads, rows, QK), low),
            (step_block(2 * heads, 8, rows), (steps, 2 * heads, 8, rows), full),
            (step_block(count, 8, rows), (steps, count, 8, rows), full),
            (fixed(2, 8, rows), (2, 8, rows), jnp.int32),
        ],
        [
            ((2, rows, heads * QK), low),
            ((2, rows, heads * VDIM), low),
            ((2, rows, WIDTH), low),
            ((2 * heads, rows, VDIM), low),
            ((heads, rows, rows), full),
            ((heads, rows, rows), full),
        ],
        "local_scores",
    )(index, docs, *inputs, *latents)


def attention(index, doc_ids, inputs, kept, latents, heads, steps, ranks, in_place):
    rows = inputs[0].shape[0]
    low, full = jnp.bfloat16, jnp.float32
    count = len(LOCAL) * heads
    window = (REACH + 2) * rows
    far = REACH * rows
    half = (LATENT // 2, steps * heads * KV)
    return call(
        functools.partial(main_kernel, ranks),
        steps,
        2 * steps * heads * rows * rows * (5 * (QK + VDIM) + 8 * (2 * QK + VDIM) + 13 * KV),
        [
            SCALARS, *head_specs(rows, heads, steps, in_place), ANYWHERE, ANYWHERE,
            step_block(2 * heads, rows, QK), step_block(2 * heads, 8, rows),
            step_block(count, 8, rows), fixed(2, 8, rows),
        ]
        + [ANYWHERE] * len(latents),
        [(step_cols(rows, heads * QK), (rows, steps * heads * QK), low)] * 2
        + [(step_cols(LATENT // 2, heads * KV), half, low)] * 2
        + [(ANYWHERE, (WIDTH, rows), low)] * (REACH + 2),
        [
            ((2, rows, heads * QK), low),
            ((2, rows, heads * VDIM), low),
            ((far, WIDTH), low),
            ((WIDTH, window), low),
            ((heads, far, rows), low),
            ((heads, far, rows), low),
            ((heads, far, QK), low),
            ((heads, far, VDIM), low),
            ((heads, REACH, 8, rows), full),
            ((heads, 8, rows), full),
            ((heads, 8, rows), full),
            ((heads, rows, rows), full),
            ((heads, rows, rows), full),
            ((heads, rows, rows), low),
            ((heads, rows, rows), low),
            ((2, heads * QK, rows), full),
            ((REACH + 2, rows, heads * KV), full),
            ((LATENT, heads * KV), full),
            ((WIDTH, window), full),
            ((REACH + 2, rows, ROPE), full),
            ((count, rows, rows), low),
            ((count, rows, rows), low),
            pltpu.SemaphoreType.DMA((5,)),
            pltpu.SemaphoreType.DMA((2,)),
        ],
        "attention",
    )(index, doc_ids, *inputs, *kept, *latents)


def permute(value, axis, target):
    count = lax.axis_size(axis)
    pairs = [(s, target(s)) for s in range(count) if 0 <= target(s) < count]
    return lax.ppermute(value, axis, pairs)


def local(kv_latent, queries, grad_out, kv_up_weight, doc_ids):
    ranks = lax.axis_size("ctx")
    position = lax.axis_index("ctx").astype(jnp.int32)
    index, core = position[None], lax.rem(position, 2)
    low, full = jnp.bfloat16, jnp.float32
    docs = doc_ids[None]
    core_heads = kv_up_weight.shape[1] // KV // 2
    heads = min(2, core_heads)
    steps = core_heads // heads

    def own_heads(value, which):
        size = value.shape[1] // 2
        return lax.dynamic_slice_in_dim(value, which * size, size, axis=1)

    def across(value):
        return permute(value, "ctx", lambda s: s ^ 1)

    latent = kv_latent.T
    far = permute(latent, "ctx", lambda s: s + 2)
    mixed = permute(latent, "ctx", lambda s: s + 3 if s % 2 else -1)
    other = across(latent)
    in_place = heads * QK % 128 == 0
    inputs = (
        queries if in_place else own_heads(queries, core),
        grad_out if in_place else own_heads(grad_out, core),
        across(own_heads(queries, 1 - core)),
        across(own_heads(grad_out, 1 - core)),
        kv_up_weight if in_place else own_heads(kv_up_weight, core),
    )
    *kept, starts = local_scores(index, docs, inputs, (latent, other), heads, steps, in_place)
    far, mixed, starts = lax.optimization_barrier((far, mixed, starts))
    swapped = across(far)
    passed = permute(mixed, "ctx", lambda s: -1 if s % 2 else s + 1)

    dq_own, dq_other, keep, send, to_old, to_far, to_swap, mine, to_other = attention(
        index, doc_ids, inputs, (*kept, starts),
        (far, swapped, mixed, passed, latent, other), heads, steps, ranks, in_place,
    )

    head, head_count = lax.axis_index("head"), lax.axis_size("head")
    share = WIDTH // head_count

    def turned(value, turn, ctx=range(ranks)):
        turns = [
            (c * head_count + s, c * head_count + (s + turn) % head_count)
            for c in ctx
            for s in range(head_count)
        ]
        return lax.ppermute(value, ("ctx", "head"), turns)

    def head_share(value, ctx=range(ranks), after=()):
        def rows_of(which):
            return lax.dynamic_slice_in_dim(value, which * share, share, axis=0)

        total = rows_of(head).astype(full)
        for turn in range(1, head_count):
            target = lax.rem(head + turn, head_count)
            received, *_ = lax.optimization_barrier((turned(rows_of(target), turn, ctx), *after))
            total = total + received.astype(full)
        return total

    from_x = permute(send, "ctx", lambda s: s ^ 2)
    from_swap = across(to_swap)
    from_old = permute(to_old, "ctx", lambda s: s - 1 if s % 2 else -1)
    from_other = across(to_other)
    far_sum = head_share((to_far.astype(full) + from_swap.astype(full)).astype(low)).astype(low)
    old_sum = (to_old.astype(full) + from_old.astype(full)).astype(low)
    old_sum = head_share(old_sum, range(0, ranks, 2), (far_sum,)).astype(low)
    from_far = permute(far_sum, "ctx", lambda s: s - 2)
    from_mixed = permute(old_sum, "ctx", lambda s: -1 if s % 2 else s - 3)
    own_sum = (mine.astype(full) + from_other.astype(full)).astype(low)
    own_sum, *_ = lax.optimization_barrier((own_sum, far_sum))
    if head_count == 2:
        kept_half = lax.dynamic_slice_in_dim(own_sum, head * share, share, axis=0)
        sent_half = lax.dynamic_slice_in_dim(own_sum, (1 - head) * share, share, axis=0)
        received_half = turned(sent_half, 1)
        total = kept_half.astype(full)
    else:
        total = head_share(own_sum)

    from_x, *_ = lax.optimization_barrier((from_x, far_sum))
    plane = (keep.astype(full) + from_x.astype(full)).astype(low)
    columns = [list(range(first, ranks, 4)) for first in range(4)]
    pieces = lax.all_to_all(plane, "ctx", 0, 0, axis_index_groups=columns, tiled=True)
    rows = LATENT // ranks
    summed = jnp.sum(pieces.reshape(ranks // 4, 2 * rows, -1).astype(full), axis=0)

    def in_order(own, received):
        first = jnp.where(core == 0, own, received)
        second = jnp.where(core == 0, received, own)
        return jnp.concatenate([first, second], axis=1)

    rows_own = lax.dynamic_slice_in_dim(summed, core * rows, rows, axis=0)
    rows_other = lax.dynamic_slice_in_dim(summed, (1 - core) * rows, rows, axis=0)
    grad_weight = in_order(rows_own, across(rows_other))
    grad_queries = in_order(dq_own, across(dq_other))

    total = (total + from_mixed.astype(full) + from_far.astype(full)).astype(low)
    shares = [total] + [turned(total, turn) for turn in range(1, head_count)]
    if head_count == 2:
        shares = [
            (whole.astype(full) + part.astype(full)).astype(low)
            for whole, part in zip(shares, (received_half, sent_half))
        ]
    ordered = []
    for place in range(head_count):
        picked = shares[0]
        for turn in range(1, head_count):
            picked = jnp.where(lax.rem(head - place + head_count, head_count) == turn, shares[turn], picked)
        ordered.append(picked)
    return grad_queries, jnp.concatenate(ordered, axis=0).T, grad_weight


def solution(mesh):
    return jax.shard_map(
        local,
        mesh=mesh,
        in_specs=(P("ctx", None), P("ctx", "head"), P("ctx", "head"), P(None, "head"), P()),
        out_specs=(P("ctx", "head"), P("ctx", None), P("ctx", "head")),
        check_vma=False,
    )
```
